32 devices in a mesh: grp: 2 (over y), ops: 4 (over z), sec: 2 (over x), rep: 2 (over core).
Axes of the slice: x: 2, y: 2, z: 4, core: 2. Of those that a mesh axis runs over, the one named last changes fastest.
Arguments:
- wavefunction: bfloat16 [4, 512, 512], P(('grp', 'sec'), 'rep'), parts along dimension 0, may hold values from -135 to 135
- sector_sizes: int32 [4, 2], P('grp'), parts along dimension 0, may hold values from 256 to 512, as said below
- left_blocks: bfloat16 [32, 512, 512], P(('grp', 'ops')), parts along dimension 0, may hold values from -0.25 to 0.25
- right_blocks: bfloat16 [32, 512, 512], P(('grp', 'ops')), parts along dimension 0, may hold values from -0.25 to 0.25
- sector_pairs: int32 [32, 8, 2], P(('grp', 'ops')), parts along dimension 0, may hold values from 0 to 1, as said below
- pair_weights: float32 [32, 8], P(('grp', 'ops')), parts along dimension 0, may hold values from -0.6 to 0.6
Outputs:
- second_wave: bfloat16 [4, 512, 512], P(('grp', 'sec'), 'rep'), parts along dimension 0
- second_sigma: float32 [4, 512, 512], P(('grp', 'sec'), 'rep'), parts along dimension 0
The draws below stay inside these ranges and needn't reach their ends.
There are 2 independent parts, one for each index of `grp`. The reference program is written for one: setup_inputs(seed, part) draws one part's arguments, and reference() takes and returns one part's arrays. A program takes and returns all parts, laid end to end along the dimension named above; each array names one. Nothing has to cross between parts.
Inputs may be any that keep to these rules, and one draw needn't show every extreme that they name: `sector_sizes`: each row holds the live left and right dimension of a sector; some sector has both equal to 512. `sector_pairs`: each row names the input sector and the output sector that the term maps it to.
All inputs are finite; a program needn't handle non-finite values.
Results may differ from the reference program's by a relative error of at most 0.0058.
Values may be sent and summed in bfloat16 or wider, within the bound.
No kernel may reach another device: no remote copies, remote signals or barrier semaphores. Data moves between devices by JAX's collectives and lax.ppermute only.
A program may use at most 64 MiB of HBM per device.

```python
import math
import jax
import jax.numpy as jnp
from jax import lax

B = 512
PAIRS = 8
SECT = 2
TERMS = 16


def draw_wavefunction(key, part):
    key = jax.random.fold_in(key, 11)
    base_key, row_key, column_key = jax.random.split(key, 3)
    sector_ramp = 1.0 + 2.0 * jnp.arange(SECT, dtype=jnp.float32) / (SECT - 1)
    row_scale = jnp.exp(jax.random.uniform(row_key, (SECT, B, 1), jnp.float32, math.log(0.3), math.log(3.0)))
    column_scale = jnp.exp(jax.random.uniform(column_key, (SECT, 1, B), jnp.float32, math.log(0.3), math.log(3.0)))
    base_values = jnp.clip(jax.random.normal(base_key, (SECT, B, B), jnp.float32), -5.0, 5.0)
    return (base_values * row_scale * column_scale * sector_ramp[:, None, None]).astype(jnp.bfloat16)


def draw_sector_sizes(key, part):
    key = jax.random.fold_in(key, 23)
    size_key, pick_key = jax.random.split(key, 2)
    drawn_sizes = jax.random.randint(size_key, (SECT, 2), B // 2, B + 1, dtype=jnp.int32)
    chosen_sector = jax.random.randint(pick_key, (), 0, SECT, dtype=jnp.int32)
    sector_index = jnp.arange(SECT, dtype=jnp.int32)[:, None]
    return jnp.where(sector_index == chosen_sector, jnp.int32(B), drawn_sizes)


def draw_sector_pairs(key, part):
    key = jax.random.fold_in(key, 37)
    draw_keys = jax.random.split(key, 5)
    source_sector = jax.random.randint(draw_keys[0], (TERMS, PAIRS), 0, SECT, dtype=jnp.int32)
    first_pick = jax.random.randint(draw_keys[1], (TERMS, PAIRS), 0, SECT, dtype=jnp.int32)
    second_pick = jax.random.randint(draw_keys[2], (TERMS, PAIRS), 0, SECT, dtype=jnp.int32)
    third_pick = jax.random.randint(draw_keys[3], (TERMS, PAIRS), 0, SECT, dtype=jnp.int32)
    lowest_pick = jnp.minimum(jnp.minimum(first_pick, second_pick), third_pick)
    sector_order = jax.random.permutation(draw_keys[4], SECT).astype(jnp.int32)
    target_sector = jnp.take(sector_order, lowest_pick)
    source_sector = source_sector.at[0, 0].set(SECT - 1).at[0, 1].set(0)
    target_sector = target_sector.at[0, 0].set(SECT - 1).at[0, 1].set(0)
    return jnp.stack([source_sector, target_sector], axis=-1).astype(jnp.int32)


def level_of(key, dims, pieces, low, high):
    def one(axis_at, blocks):
        steps = jax.random.uniform(jax.random.fold_in(jax.random.fold_in(key, 6), axis_at), (blocks,), jnp.float32, low / len(pieces), high / len(pieces))
        return jnp.repeat(jnp.exp(steps), dims[axis_at] // blocks).reshape((-1,) + (1,) * (len(dims) - axis_at - 1))

    gain = one(*pieces[0])
    for cut in pieces[1:]:
        gain = gain * one(*cut)
    return gain


def centred(key, shape, spread, limit, cuts=(), held_as=jnp.bfloat16):
    values = spread * jax.random.normal(key, shape, jnp.float32)
    if cuts:
        values = values * level_of(key, shape, cuts, -0.22, 0.18)
    return jnp.clip(values, -limit, limit).astype(held_as)


def setup_inputs(seed: int = 0, part: int = 0) -> dict:
    arg_keys = jax.random.split(jax.random.key(seed), 7)
    part_splits = jax.random.split(jax.random.fold_in(arg_keys[6], part), 7)
    return {
        "wavefunction": draw_wavefunction(jax.random.fold_in(jax.random.fold_in(arg_keys[6], part), 71), part),
        "sector_sizes": draw_sector_sizes(jax.random.fold_in(jax.random.fold_in(arg_keys[6], part), 71), part),
        "left_blocks": centred(part_splits[2], (TERMS, B, B), B ** -0.5, 0.25, ((0, 4),)),
        "right_blocks": centred(part_splits[3], (TERMS, B, B), B ** -0.5, 0.25, ((0, 4),)),
        "sector_pairs": draw_sector_pairs(jax.random.fold_in(jax.random.fold_in(arg_keys[6], part), 71), part),
        "pair_weights": centred(part_splits[5], (TERMS, PAIRS), 0.1, 0.6, ((0, 4),), jnp.float32),
    }


def sector_mask(sector_sizes):
    rows = lax.broadcasted_iota(jnp.int32, (SECT, B, B), 1)
    cols = lax.broadcasted_iota(jnp.int32, (SECT, B, B), 2)
    left_live = sector_sizes[:, 0].astype(jnp.int32)[:, None, None]
    right_live = sector_sizes[:, 1].astype(jnp.int32)[:, None, None]
    return (rows < left_live) & (cols < right_live)

def mixing_matrix(term_pairs, term_weights):
    sectors = jnp.arange(SECT, dtype=jnp.int32)
    source_hot = (term_pairs[:, 0][:, None] == sectors[None, :]).astype(jnp.float32)
    target_hot = (term_pairs[:, 1][:, None] == sectors[None, :]).astype(jnp.float32) * term_weights[:, None]
    return jnp.dot(target_hot.T, source_hot, precision=lax.Precision.HIGHEST, preferred_element_type=jnp.float32)

def apply_terms(wave, left_blocks, right_blocks, sector_pairs, pair_weights):
    wave_float = wave.astype(jnp.float32)

    def visit(running, term_index):
        left_float = left_blocks[term_index].astype(jnp.float32)
        left_product = jnp.einsum('ik,akj->aij', left_float, wave_float, precision=lax.Precision.HIGHEST)
        mixing = mixing_matrix(sector_pairs[term_index], pair_weights[term_index])
        combined = jnp.einsum('ba,aij->bij', mixing, left_product, precision=lax.Precision.HIGHEST).astype(jnp.bfloat16)
        right_float = right_blocks[term_index].astype(jnp.float32)
        contribution = jnp.einsum('bij,kj->bik', combined.astype(jnp.float32), right_float, precision=lax.Precision.HIGHEST)
        return (running + contribution, None)
    start = jnp.zeros((SECT, B, B), jnp.float32)
    return lax.scan(visit, start, jnp.arange(TERMS, dtype=jnp.int32))[0]

def reference(wavefunction, sector_sizes, left_blocks, right_blocks, sector_pairs, pair_weights):
    live_mask = sector_mask(sector_sizes)
    first_wave = jnp.where(live_mask, wavefunction, jnp.zeros_like(wavefunction))
    first_sigma = jnp.where(live_mask, apply_terms(first_wave, left_blocks, right_blocks, sector_pairs, pair_weights), jnp.zeros((), jnp.float32))
    wave_float = first_wave.astype(jnp.float32)
    rayleigh = jnp.sum(wave_float * first_sigma) / jnp.sum(wave_float * wave_float)
    residual = first_sigma - rayleigh * wave_float
    live_count = jnp.sum(sector_sizes[:, 0].astype(jnp.float32) * sector_sizes[:, 1].astype(jnp.float32))
    second_wave = (residual / jnp.sqrt(jnp.sum(residual * residual) / live_count + 1e-06)).astype(jnp.bfloat16)
    second_sigma = jnp.where(live_mask, apply_terms(second_wave, left_blocks, right_blocks, sector_pairs, pair_weights), jnp.zeros((), jnp.float32))
    return (second_wave, second_sigma)
```

```python
import jax
import jax.numpy as jnp
from jax import lax
from jax.experimental import pallas as pl
from jax.experimental.pallas import tpu as pltpu
from jax.sharding import PartitionSpec as P

epsilon = 1e-06
vmem_bytes = 40 * 1024 * 1024


def mixing_scalars(pairs_ref, weights_ref, target, terms, sectors):
    table = []
    for term in range(terms):
        row = [jnp.float32(0.0)] * sectors
        for pair in range(weights_ref.shape[1]):
            source = pairs_ref[term, pair, 0]
            hit = pairs_ref[term, pair, 1] == target
            weight = weights_ref[term, pair]
            for sector in range(sectors):
                row[sector] = row[sector] + jnp.where(
                    hit & (source == sector), weight, jnp.float32(0.0)
                )
        table.append(row)
    return table


def apply_operators(mixing, vector, left, right, arrived):
    total = None
    for term in range(left.shape[0]):
        arrived(term)
        combined = None
        for sector, weight in enumerate(mixing[term]):
            product = weight * jnp.dot(
                left[term], vector[sector], preferred_element_type=jnp.float32
            )
            combined = product if combined is None else combined + product
        part = lax.dot_general(
            combined.astype(jnp.bfloat16),
            right[term],
            (((1,), (1,)), ((), ())),
            preferred_element_type=jnp.float32,
        )
        total = part if total is None else total + part
    return total


def live_cells(sizes_ref, sector, row_start, rows, columns):
    row = row_start + lax.broadcasted_iota(jnp.int32, (rows, columns), 0)
    column = lax.broadcasted_iota(jnp.int32, (rows, columns), 1)
    return (row < sizes_ref[sector, 0]) & (column < sizes_ref[sector, 1])


def operator_copies(left_ref, right_ref, left, right, sems, row_start):
    rows = left.shape[1]
    copies = []
    for term in range(left.shape[0]):
        copies.append(
            (
                pltpu.make_async_copy(
                    left_ref.at[term, pl.ds(row_start, rows)], left.at[term], sems.at[0, term]
                ),
                pltpu.make_async_copy(right_ref.at[term], right.at[term], sems.at[1, term]),
            )
        )
    return copies


def first_kernel(
    sizes_ref, pairs_ref, weights_ref, left_ref, right_ref, wave_ref,
    masked_ref, partial_ref,
    left, right, vector, operator_sems, wave_sem, masked_sem,
):
    sectors, columns = vector.shape[0], vector.shape[2]
    rows = partial_ref.shape[0]
    target = lax.axis_index("sec")
    row_start = pl.multiple_of(lax.axis_index("rep") * rows, rows)
    wave_copy = pltpu.make_async_copy(wave_ref, vector, wave_sem)
    wave_copy.start()
    copies = operator_copies(left_ref, right_ref, left, right, operator_sems, row_start)
    for pair in copies:
        for copy in pair:
            copy.start()
    mixing = mixing_scalars(pairs_ref, weights_ref, target, left.shape[0], sectors)
    wave_copy.wait()
    step = 32

    for sector in range(sectors):

        def mask_rows(block, carry):
            start = pl.multiple_of(block * step, step)
            live = live_cells(sizes_ref, sector, start, step, columns)
            values = vector[sector, pl.ds(start, step), :].astype(jnp.float32)
            vector[sector, pl.ds(start, step), :] = jnp.where(live, values, 0.0).astype(
                jnp.bfloat16
            )
            return carry

        lax.fori_loop(0, vector.shape[1] // step, mask_rows, 0)
    masked_copy = pltpu.make_async_copy(vector, masked_ref, masked_sem)
    masked_copy.start()

    def arrived(term):
        for copy in copies[term]:
            copy.wait()

    total = apply_operators(mixing, vector, left, right, arrived)
    live = live_cells(sizes_ref, target, row_start, rows, columns)
    partial_ref[...] = jnp.where(live, total, 0.0).astype(partial_ref.dtype)
    masked_copy.wait()


def second_kernel(
    sizes_ref, pairs_ref, weights_ref, left_ref, right_ref, wave_ref, sigma_ref,
    second_ref, partial_ref,
    left, right, wave, sigma, operator_sems, wave_sem, sigma_sem, second_sem,
):
    sectors, columns = wave.shape[0], wave.shape[2]
    rows = partial_ref.shape[0]
    target = lax.axis_index("sec")
    row_start = pl.multiple_of(lax.axis_index("rep") * rows, rows)
    wave_copy = pltpu.make_async_copy(wave_ref, wave, wave_sem)
    sigma_copy = pltpu.make_async_copy(sigma_ref, sigma, sigma_sem)
    wave_copy.start()
    sigma_copy.start()
    copies = operator_copies(left_ref, right_ref, left, right, operator_sems, row_start)
    for pair in copies:
        for copy in pair:
            copy.start()
    mixing = mixing_scalars(pairs_ref, weights_ref, target, left.shape[0], sectors)
    live_count = jnp.float32(0.0)
    for sector in range(sectors):
        live_count = live_count + sizes_ref[sector, 0].astype(jnp.float32) * sizes_ref[
            sector, 1
        ].astype(jnp.float32)
    wave_copy.wait()
    sigma_copy.wait()
    step = 16
    blocks = wave.shape[1] // step
    sums = (jnp.zeros((step, columns), jnp.float32),) * 3

    for sector in range(sectors):

        def add_rows(block, carry):
            start = pl.multiple_of(block * step, step)
            w = wave[sector, pl.ds(start, step), :].astype(jnp.float32)
            s = sigma[sector, pl.ds(start, step), :].astype(jnp.float32)
            return (carry[0] + w * s, carry[1] + w * w, carry[2] + s * s)

        sums = lax.fori_loop(0, blocks, add_rows, sums)
    correlation, norm_square, sigma_square = (jnp.sum(x, keepdims=True) for x in sums)
    rayleigh = correlation / norm_square
    residual_square = (
        sigma_square - 2.0 * rayleigh * correlation + rayleigh * rayleigh * norm_square
    )
    residual_square = jnp.maximum(residual_square, 0.0)
    scale = 1.0 / jnp.sqrt(residual_square / jnp.full((1, 1), live_count) + epsilon)
    wave_scale = jnp.broadcast_to(rayleigh * scale, (step, columns))
    sigma_scale = jnp.broadcast_to(scale, (step, columns))

    for sector in range(sectors):

        def make_rows(block, carry):
            start = pl.multiple_of(block * step, step)
            w = wave[sector, pl.ds(start, step), :].astype(jnp.float32)
            s = sigma[sector, pl.ds(start, step), :].astype(jnp.float32)
            sigma[sector, pl.ds(start, step), :] = (sigma_scale * s - wave_scale * w).astype(
                jnp.bfloat16
            )
            return carry

        lax.fori_loop(0, blocks, make_rows, 0)
    second_copy = pltpu.make_async_copy(
        sigma.at[target, pl.ds(row_start, rows)], second_ref.at[0], second_sem
    )
    second_copy.start()

    def arrived(term):
        for copy in copies[term]:
            copy.wait()

    total = apply_operators(mixing, sigma, left, right, arrived)
    live = live_cells(sizes_ref, target, row_start, rows, columns)
    partial_ref[...] = jnp.where(live, total, 0.0).astype(partial_ref.dtype)
    second_copy.wait()


def kernel_specs(count):
    smem = pl.BlockSpec(memory_space=pltpu.SMEM)
    anywhere = pl.BlockSpec(memory_space=pl.ANY)
    return [smem] * 3 + [anywhere] * count


def local(wavefunction, sector_sizes, left_blocks, right_blocks, sector_pairs, pair_weights):
    sectors = sector_sizes.shape[0]
    ops_count = lax.axis_size("ops")
    _, rows, columns = wavefunction.shape
    terms, side = left_blocks.shape[0], left_blocks.shape[1]
    share = rows // ops_count
    operators = (sector_sizes, sector_pairs, pair_weights, left_blocks, right_blocks)
    bf16, f32 = jnp.bfloat16, jnp.float32
    operator_scratch = [
        pltpu.VMEM((terms, rows, side), bf16),
        pltpu.VMEM((terms, columns, columns), bf16),
    ]
    anywhere = pl.BlockSpec(memory_space=pl.ANY)
    inside = pl.BlockSpec(memory_space=pltpu.VMEM)
    full = jax.ShapeDtypeStruct((sectors, side, columns), bf16)
    partial = jax.ShapeDtypeStruct((rows, columns), bf16)
    params = pltpu.CompilerParams(vmem_limit_bytes=vmem_bytes)

    def summed(piece):
        pieces = lax.all_to_all(
            piece.reshape(ops_count, share, columns), "ops", 0, 0, tiled=True
        )
        return jnp.sum(pieces.astype(f32), axis=0).astype(bf16)

    gathered = lax.all_gather(wavefunction, ("sec", "rep"), axis=1, tiled=True)
    masked, first_part = pl.pallas_call(
        first_kernel,
        out_shape=(full, partial),
        in_specs=kernel_specs(3),
        out_specs=(anywhere, inside),
        scratch_shapes=operator_scratch
        + [
            pltpu.VMEM((sectors, side, columns), bf16),
            pltpu.SemaphoreType.DMA((2, terms)),
            pltpu.SemaphoreType.DMA,
            pltpu.SemaphoreType.DMA,
        ],
        compiler_params=params,
        name="first_sigma_terms",
    )(*operators, gathered.reshape(sectors, side, columns))
    first_sigma = lax.all_gather(summed(first_part), ("sec", "rep", "ops"), axis=0, tiled=True)
    second_wave, second_part = pl.pallas_call(
        second_kernel,
        out_shape=(jax.ShapeDtypeStruct((1, rows, columns), bf16), partial),
        in_specs=kernel_specs(4),
        out_specs=(anywhere, inside),
        scratch_shapes=operator_scratch
        + [
            pltpu.VMEM((sectors, side, columns), bf16),
            pltpu.VMEM((sectors, side, columns), bf16),
            pltpu.SemaphoreType.DMA((2, terms)),
            pltpu.SemaphoreType.DMA,
            pltpu.SemaphoreType.DMA,
            pltpu.SemaphoreType.DMA,
        ],
        compiler_params=params,
        name="second_sigma_terms",
    )(*operators, masked, first_sigma.reshape(sectors, side, columns))
    second_sigma = lax.all_gather(summed(second_part), "ops", axis=0, tiled=True)
    return (second_wave, second_sigma.astype(f32)[None])


def solution(mesh):
    return jax.shard_map(
        local,
        mesh=mesh,
        in_specs=(
            P(("grp", "sec"), "rep", None),
            P("grp", None),
            P(("grp", "ops"), None, None),
            P(("grp", "ops"), None, None),
            P(("grp", "ops"), None, None),
            P(("grp", "ops"), None),
        ),
        out_specs=(P(("grp", "sec"), "rep", None), P(("grp", "sec"), "rep", None)),
        check_vma=False,
    )
```

```python
import jax
import jax.numpy as jnp
from jax import lax
from jax.experimental import pallas as pl
from jax.experimental.pallas import tpu as pltpu
from jax.sharding import PartitionSpec as P

epsilon = 1e-06
vmem_bytes = 24 * 1024 * 1024


def mixing_scalars(pairs_ref, weights_ref, target, terms, sectors):
    table = []
    for term in range(terms):
        row = [jnp.float32(0.0)] * sectors
        for pair in range(weights_ref.shape[1]):
            source = pairs_ref[term, pair, 0]
            hit = pairs_ref[term, pair, 1] == target
            weight = weights_ref[term, pair]
            for sector in range(sectors):
                row[sector] = row[sector] + jnp.where(
                    hit & (source == sector), weight, jnp.float32(0.0)
                )
        table.append(row)
    return table


def apply_operators(mixing, vector, left, right):
    total = None
    for term in range(left.shape[0]):
        combined = None
        for sector, weight in enumerate(mixing[term]):
            product = weight * jnp.dot(
                left[term], vector[sector], preferred_element_type=jnp.float32
            )
            combined = product if combined is None else combined + product
        part = lax.dot_general(
            combined.astype(jnp.bfloat16),
            right[term],
            (((1,), (1,)), ((), ())),
            preferred_element_type=jnp.float32,
        )
        total = part if total is None else total + part
    return total


def live_cells(sizes_ref, sector, row_start, rows, columns):
    row = row_start + lax.broadcasted_iota(jnp.int32, (rows, columns), 0)
    column = lax.broadcasted_iota(jnp.int32, (rows, columns), 1)
    return (row < sizes_ref[sector, 0]) & (column < sizes_ref[sector, 1])


def load_kernel(left_ref, right_ref, left, right, sems):
    rows = left.shape[1]
    row_start = pl.multiple_of(lax.axis_index("rep") * rows, rows)
    copies = [
        pltpu.make_async_copy(left_ref.at[:, pl.ds(row_start, rows)], left, sems.at[0]),
        pltpu.make_async_copy(right_ref, right, sems.at[1]),
    ]
    for copy in copies:
        copy.start()
    for copy in copies:
        copy.wait()


def place_pieces(pieces, spots, vector, sems):
    copies = []
    for index, (piece, (sector, row)) in enumerate(zip(pieces, spots)):
        rows = piece.shape[0]
        start = pl.multiple_of(row, rows)
        copies.append(
            pltpu.make_async_copy(piece, vector.at[sector, pl.ds(start, rows)], sems.at[index])
        )
    for copy in copies:
        copy.start()
    return copies


def give_shares(total, live, held, own_ref, send_refs):
    held[...] = jnp.where(live, total, 0.0)
    share = own_ref.shape[0]
    place = lax.axis_index("ops")
    own_ref[...] = held[pl.ds(pl.multiple_of(place * share, share), share), :]
    for step, send_ref in enumerate(send_refs, 1):
        start = pl.multiple_of((place ^ step) * share, share)
        send_ref[...] = held[pl.ds(start, share), :].astype(send_ref.dtype)


def first_kernel(counts, *refs):
    pieces_count, sends = counts
    sizes_ref, pairs_ref, weights_ref, left, right = refs[:5]
    pieces = refs[5 : 5 + pieces_count]
    masked, own_ref = refs[5 + pieces_count : 7 + pieces_count]
    send_refs = refs[7 + pieces_count : 7 + pieces_count + sends]
    held, sems = refs[7 + pieces_count + sends :]
    sectors, columns = masked.shape[0], masked.shape[2]
    rows = held.shape[0]
    target = lax.axis_index("sec")
    core = lax.axis_index("rep")
    spots = [
        (target ^ (index // 2), (core ^ (index % 2)) * rows) for index in range(pieces_count)
    ]
    copies = place_pieces([piece.at[0] for piece in pieces], spots, masked, sems)
    mixing = mixing_scalars(pairs_ref, weights_ref, target, left.shape[0], sectors)
    for copy in copies:
        copy.wait()
    step = 32

    for sector in range(sectors):

        def mask_rows(block, carry):
            start = pl.multiple_of(block * step, step)
            live = live_cells(sizes_ref, sector, start, step, columns)
            values = masked[sector, pl.ds(start, step), :].astype(jnp.float32)
            masked[sector, pl.ds(start, step), :] = jnp.where(live, values, 0.0).astype(
                jnp.bfloat16
            )
            return carry

        lax.fori_loop(0, masked.shape[1] // step, mask_rows, 0)
    total = apply_operators(mixing, masked, left, right)
    live = live_cells(sizes_ref, target, core * rows, rows, columns)
    give_shares(total, live, held, own_ref, send_refs)


def second_kernel(counts, *refs):
    pieces_count, sends = counts
    sizes_ref, pairs_ref, weights_ref, left, right, wave = refs[:6]
    pieces = refs[6 : 6 + pieces_count]
    second_ref, own_ref = refs[6 + pieces_count : 8 + pieces_count]
    send_refs = refs[8 + pieces_count : 8 + pieces_count + sends]
    sigma, held, sems, second_sem = refs[8 + pieces_count + sends :]
    sectors, columns = wave.shape[0], wave.shape[2]
    rows, share = held.shape[0], own_ref.shape[0]
    target = lax.axis_index("sec")
    core = lax.axis_index("rep")
    place = lax.axis_index("ops")
    spots = [
        (
            target ^ ((index // 2) % sectors),
            (core ^ (index % 2)) * rows + (place ^ (index // (2 * sectors))) * share,
        )
        for index in range(pieces_count)
    ]
    copies = place_pieces(pieces, spots, sigma, sems)
    mixing = mixing_scalars(pairs_ref, weights_ref, target, left.shape[0], sectors)
    live_count = jnp.float32(0.0)
    for sector in range(sectors):
        live_count = live_count + sizes_ref[sector, 0].astype(jnp.float32) * sizes_ref[
            sector, 1
        ].astype(jnp.float32)
    for copy in copies:
        copy.wait()
    step = 16
    blocks = wave.shape[1] // step
    sums = (jnp.zeros((step, columns), jnp.float32),) * 3

    for sector in range(sectors):

        def add_rows(block, carry):
            start = pl.multiple_of(block * step, step)
            w = wave[sector, pl.ds(start, step), :].astype(jnp.float32)
            s = sigma[sector, pl.ds(start, step), :].astype(jnp.float32)
            return (carry[0] + w * s, carry[1] + w * w, carry[2] + s * s)

        sums = lax.fori_loop(0, blocks, add_rows, sums)
    correlation, norm_square, sigma_square = (jnp.sum(x, keepdims=True) for x in sums)
    rayleigh = correlation / norm_square
    residual_square = (
        sigma_square - 2.0 * rayleigh * correlation + rayleigh * rayleigh * norm_square
    )
    residual_square = jnp.maximum(residual_square, 0.0)
    scale = 1.0 / jnp.sqrt(residual_square / jnp.full((1, 1), live_count) + epsilon)
    wave_scale = jnp.broadcast_to(rayleigh * scale, (step, columns))
    sigma_scale = jnp.broadcast_to(scale, (step, columns))

    for sector in range(sectors):

        def make_rows(block, carry):
            start = pl.multiple_of(block * step, step)
            w = wave[sector, pl.ds(start, step), :].astype(jnp.float32)
            s = sigma[sector, pl.ds(start, step), :].astype(jnp.float32)
            sigma[sector, pl.ds(start, step), :] = (sigma_scale * s - wave_scale * w).astype(
                jnp.bfloat16
            )
            return carry

        lax.fori_loop(0, blocks, make_rows, 0)
    second_copy = pltpu.make_async_copy(
        sigma.at[target, pl.ds(pl.multiple_of(core * rows, rows), rows)], second_ref.at[0], second_sem
    )
    second_copy.start()

    total = apply_operators(mixing, sigma, left, right)
    live = live_cells(sizes_ref, target, core * rows, rows, columns)
    give_shares(total, live, held, own_ref, send_refs)
    second_copy.wait()


def sum_kernel(own_ref, *refs):
    total = own_ref[...]
    for piece in refs[:-1]:
        total = total + piece[...].astype(jnp.float32)
    refs[-1][...] = total.astype(refs[-1].dtype)


def join_kernel(*refs):
    out_ref = refs[-1]
    share = refs[0].shape[0]
    place = lax.axis_index("ops")
    for step, piece in enumerate(refs[:-1]):
        start = pl.multiple_of((place ^ step) * share, share)
        out_ref[0, pl.ds(start, share), :] = piece[...].astype(out_ref.dtype)


def partner(value, axis, step):
    if step == 0:
        return value
    count = lax.axis_size(axis)
    return lax.ppermute(value, axis, [(i, i ^ step) for i in range(count)])


def local(wavefunction, sector_sizes, left_blocks, right_blocks, sector_pairs, pair_weights):
    sectors = sector_sizes.shape[0]
    ops_count, cores = lax.axis_size("ops"), lax.axis_size("rep")
    _, rows, columns = wavefunction.shape
    terms, side = left_blocks.shape[0], left_blocks.shape[1]
    share = rows // ops_count
    bf16, f32 = jnp.bfloat16, jnp.float32
    smem = pl.BlockSpec(memory_space=pltpu.SMEM)
    anywhere = pl.BlockSpec(memory_space=pl.ANY)
    inside = pl.BlockSpec(memory_space=pltpu.VMEM)
    full = jax.ShapeDtypeStruct((sectors, side, columns), bf16)
    shares = [jax.ShapeDtypeStruct((share, columns), f32)] + [
        jax.ShapeDtypeStruct((share, columns), bf16)
    ] * (ops_count - 1)
    params = pltpu.CompilerParams(vmem_limit_bytes=vmem_bytes)

    left_rows, right = pl.pallas_call(
        load_kernel,
        out_shape=(
            jax.ShapeDtypeStruct((terms, rows, side), bf16),
            jax.ShapeDtypeStruct(right_blocks.shape, bf16),
        ),
        in_specs=[anywhere] * 2,
        out_specs=(inside, inside),
        scratch_shapes=[pltpu.SemaphoreType.DMA((2,))],
        compiler_params=params,
        name="load_operators",
    )(left_blocks, right_blocks)
    operators = (sector_sizes, sector_pairs, pair_weights, left_rows, right)
    operator_specs = [smem] * 3 + [inside] * 2

    def summed(own, *sends):
        received = [partner(send, "ops", step) for step, send in enumerate(sends, 1)]
        return pl.pallas_call(
            sum_kernel,
            out_shape=jax.ShapeDtypeStruct((share, columns), bf16),
            in_specs=[inside] * ops_count,
            out_specs=inside,
            compiler_params=params,
            name="sum_over_terms",
        )(own, *received)

    pieces = []
    for sector in range(sectors):
        piece = partner(wavefunction, "sec", sector)
        pieces += [partner(piece, "rep", core) for core in range(cores)]
    masked, *first_shares = pl.pallas_call(
        lambda *refs: first_kernel((len(pieces), ops_count - 1), *refs),
        out_shape=[full] + shares,
        in_specs=operator_specs + [anywhere] * len(pieces),
        out_specs=[inside] * (1 + ops_count),
        scratch_shapes=[
            pltpu.VMEM((rows, columns), f32),
            pltpu.SemaphoreType.DMA((len(pieces),)),
        ],
        compiler_params=params,
        name="first_sigma_terms",
    )(*operators, *pieces)
    first_sum = summed(*first_shares)
    pieces = []
    for step in range(ops_count):
        along_ops = partner(first_sum, "ops", step)
        for sector in range(sectors):
            piece = partner(along_ops, "sec", sector)
            pieces += [partner(piece, "rep", core) for core in range(cores)]
    second_wave, *second_shares = pl.pallas_call(
        lambda *refs: second_kernel((len(pieces), ops_count - 1), *refs),
        out_shape=[jax.ShapeDtypeStruct((1, rows, columns), bf16)] + shares,
        in_specs=operator_specs + [inside] + [anywhere] * len(pieces),
        out_specs=[anywhere] + [inside] * ops_count,
        scratch_shapes=[
            pltpu.VMEM((sectors, side, columns), bf16),
            pltpu.VMEM((rows, columns), f32),
            pltpu.SemaphoreType.DMA((len(pieces),)),
            pltpu.SemaphoreType.DMA,
        ],
        compiler_params=params,
        name="second_sigma_terms",
    )(*operators, masked, *pieces)
    second_sum = summed(*second_shares)
    second_sigma = pl.pallas_call(
        join_kernel,
        out_shape=jax.ShapeDtypeStruct((1, rows, columns), f32),
        in_specs=[inside] * ops_count,
        out_specs=inside,
        compiler_params=params,
        name="join_second_sigma",
    )(*[partner(second_sum, "ops", step) for step in range(ops_count)])
    return (second_wave, second_sigma)


def solution(mesh):
    return jax.shard_map(
        local,
        mesh=mesh,
        in_specs=(
            P(("grp", "sec"), "rep", None),
            P("grp", None),
            P(("grp", "ops"), None, None),
            P(("grp", "ops"), None, None),
            P(("grp", "ops"), None, None),
            P(("grp", "ops"), None),
        ),
        out_specs=(P(("grp", "sec"), "rep", None), P(("grp", "sec"), "rep", None)),
        check_vma=False,
    )
```

```python
import jax
import jax.numpy as jnp
from jax import lax
from jax.experimental import pallas as pl
from jax.experimental.pallas import tpu as pltpu
from jax.sharding import PartitionSpec as P

epsilon = 1e-06
vmem_bytes = 24 * 1024 * 1024


def mixing_scalar(pairs_ref, weights_ref, term, target, source):
    value = jnp.float32(0.0)
    for pair in range(weights_ref.shape[1]):
        hit = (pairs_ref[term, pair, 1] == target) & (pairs_ref[term, pair, 0] == source)
        value = value + jnp.where(hit, weights_ref[term, pair], jnp.float32(0.0))
    return value


def live_cells(sizes_ref, sector, row_start, rows, columns):
    row = row_start + lax.broadcasted_iota(jnp.int32, (rows, columns), 0)
    column = lax.broadcasted_iota(jnp.int32, (rows, columns), 1)
    return (row < sizes_ref[sector, 0]) & (column < sizes_ref[sector, 1])


def masked(values, live):
    return jnp.where(live, values.astype(jnp.float32), 0.0).astype(values.dtype)


def left_times(left_own, left_other, term, own, other):
    return jnp.dot(left_own[term], own, preferred_element_type=jnp.float32) + jnp.dot(
        left_other[term], other, preferred_element_type=jnp.float32
    )


def times_right(values, right, term):
    return lax.dot_general(
        values.astype(jnp.bfloat16),
        right[term],
        (((1,), (1,)), ((), ())),
        preferred_element_type=jnp.float32,
    )


def load_kernel(
    sizes_ref, left_ref, right_ref, wave_ref,
    left_own, left_other, right, wave_own,
    sems,
):
    rows, columns = wave_own.shape
    core = lax.axis_index("rep")
    own = pl.multiple_of(core * rows, rows)
    other = pl.multiple_of((core ^ 1) * rows, rows)
    copies = [
        pltpu.make_async_copy(wave_ref.at[0], wave_own, sems.at[0]),
        pltpu.make_async_copy(
            left_ref.at[:, pl.ds(own, rows), pl.ds(own, rows)], left_own, sems.at[1]
        ),
        pltpu.make_async_copy(
            left_ref.at[:, pl.ds(own, rows), pl.ds(other, rows)], left_other, sems.at[2]
        ),
        pltpu.make_async_copy(right_ref, right, sems.at[3]),
    ]
    for copy in copies:
        copy.start()
    copies[0].wait()
    live = live_cells(sizes_ref, lax.axis_index("sec"), own, rows, columns)
    wave_own[...] = masked(wave_own[...], live)
    for copy in copies[1:]:
        copy.wait()


def first_kernel(sectors, *refs):
    sizes_ref, pairs_ref, weights_ref, left_own, left_other, right, own, arrived = refs[:8]
    other, *shares = refs[8:-1]
    held = refs[-1]
    rows, columns = own.shape
    share = shares[0].shape[0]
    sector = lax.axis_index("sec")
    core = lax.axis_index("rep")
    place = lax.axis_index("ops")
    live = live_cells(sizes_ref, sector, (core ^ 1) * rows, rows, columns)
    other[...] = masked(arrived[0], live)
    totals = [None] * sectors
    for term in range(right.shape[0]):
        product = left_times(left_own, left_other, term, own[...], other[...])
        product = times_right(product, right, term)
        for step in range(sectors):
            weight = mixing_scalar(pairs_ref, weights_ref, term, sector ^ step, sector)
            part = weight * product
            totals[step] = part if totals[step] is None else totals[step] + part
    for step in range(sectors):
        live = live_cells(sizes_ref, sector ^ step, core * rows, rows, columns)
        held[step] = jnp.where(live, totals[step], 0.0)
    for index, out in enumerate(shares):
        along, across = index // sectors, index % sectors
        start = pl.multiple_of((place ^ along) * share, share)
        out[...] = held[across, pl.ds(start, share), :].astype(out.dtype)


def sum_kernel(own_ref, *refs):
    total = own_ref[...]
    for piece in refs[:-1]:
        total = total + piece[...].astype(jnp.float32)
    refs[-1][...] = total.astype(refs[-1].dtype)


def join_halves_kernel(*refs):
    pieces, half = refs[:-1], refs[-1]
    sectors = half.shape[0]
    share = pieces[0].shape[0]
    sector = lax.axis_index("sec")
    place = lax.axis_index("ops")
    for index, piece in enumerate(pieces):
        along, across = index // sectors, index % sectors
        start = pl.multiple_of((place ^ along) * share, share)
        half[sector ^ across, pl.ds(start, share), :] = piece[...]


def second_kernel(
    sizes_ref, pairs_ref, weights_ref, left_own, left_other, right, own, other, *refs
):
    shares, held = refs[:-1], refs[-1]
    sectors, rows, columns = own.shape
    share = shares[0].shape[0]
    target = lax.axis_index("sec")
    core = lax.axis_index("rep")
    place = lax.axis_index("ops")
    total = None
    for term in range(right.shape[0]):
        combined = None
        for source in range(sectors):
            weight = mixing_scalar(pairs_ref, weights_ref, term, target, source)
            part = weight * left_times(left_own, left_other, term, own[source], other[source])
            combined = part if combined is None else combined + part
        part = times_right(combined, right, term)
        total = part if total is None else total + part
    live = live_cells(sizes_ref, target, core * rows, rows, columns)
    held[...] = jnp.where(live, total, 0.0)
    for step, out in enumerate(shares):
        start = pl.multiple_of((place ^ step) * share, share)
        out[...] = held[pl.ds(start, share), :].astype(out.dtype)


def sums_kernel(wave_own, wave_other, sigma_own, sigma_other, out):
    sector = lax.axis_index("sec")
    step, columns = 16, wave_own.shape[1]
    sums = (jnp.zeros((step, columns), jnp.float32),) * 3
    for wave, sigma in ((wave_own, sigma_own), (wave_other, sigma_other)):

        def add_rows(block, carry):
            start = pl.multiple_of(block * step, step)
            w = wave[pl.ds(start, step), :].astype(jnp.float32)
            s = sigma[sector, pl.ds(start, step), :].astype(jnp.float32)
            return (carry[0] + w * s, carry[1] + w * w, carry[2] + s * s)

        sums = lax.fori_loop(0, wave.shape[0] // step, add_rows, sums, unroll=2)
    for index, value in enumerate(sums):
        out[index] = jnp.broadcast_to(jnp.sum(value, keepdims=True), out.shape[1:])


def wave_kernel(sizes_ref, wave_own, sigma_own, *refs):
    sums, (second, factors) = refs[:-2], refs[-2:]
    rows, columns = wave_own.shape
    live_count = jnp.float32(0.0)
    for sector in range(sizes_ref.shape[0]):
        live_count = live_count + sizes_ref[sector, 0].astype(jnp.float32) * sizes_ref[
            sector, 1
        ].astype(jnp.float32)
    total = sums[0][...]
    for other in sums[1:]:
        total = total + other[...]
    correlation, norm_square, sigma_square = total[0], total[1], total[2]
    rayleigh = correlation / norm_square
    residual_square = (
        sigma_square - 2.0 * rayleigh * correlation + rayleigh * rayleigh * norm_square
    )
    residual_square = jnp.maximum(residual_square, 0.0)
    scale = 1.0 / jnp.sqrt(residual_square / live_count + epsilon)
    factors[0] = scale
    factors[1] = rayleigh * scale
    sigma_factor = jnp.broadcast_to(scale[:1, :1], (rows, columns))
    wave_factor = jnp.broadcast_to((rayleigh * scale)[:1, :1], (rows, columns))
    sigma = sigma_own[lax.axis_index("sec")].astype(jnp.float32)
    wave = wave_own[...].astype(jnp.float32)
    second[0] = (sigma_factor * sigma - wave_factor * wave).astype(second.dtype)


def join_kernel(factors, sigma_own, *refs):
    pieces, out = refs[:-1], refs[-1]
    share, columns = pieces[0].shape
    sector = lax.axis_index("sec")
    place = lax.axis_index("ops")
    scale = jnp.broadcast_to(factors[0][:1, :1], (share, columns))
    shift = jnp.broadcast_to(factors[1][:1, :1], (share, columns))
    for step, piece in enumerate(pieces):
        start = pl.multiple_of((place ^ step) * share, share)
        sigma = sigma_own[sector, pl.ds(start, share), :].astype(jnp.float32)
        out[0, pl.ds(start, share), :] = scale * piece[...].astype(jnp.float32) - shift * sigma


def partner(value, steps):
    steps = {axis: step for axis, step in steps.items() if step}
    if not steps:
        return value
    axes = tuple(steps)
    places = [()]
    for axis in axes:
        places = [place + (i,) for place in places for i in range(lax.axis_size(axis))]
    index = {place: i for i, place in enumerate(places)}
    pairs = [
        (index[tuple(i ^ steps[axis] for i, axis in zip(place, axes))], index[place])
        for place in places
    ]
    return lax.ppermute(value, axes, pairs)


def local(wavefunction, sector_sizes, left_blocks, right_blocks, sector_pairs, pair_weights):
    sectors = sector_sizes.shape[0]
    ops_count = lax.axis_size("ops")
    _, rows, columns = wavefunction.shape
    terms, side = left_blocks.shape[0], left_blocks.shape[1]
    share = rows // ops_count
    bf16, f32 = jnp.bfloat16, jnp.float32
    smem = pl.BlockSpec(memory_space=pltpu.SMEM)
    outside = pl.BlockSpec(memory_space=pltpu.HBM)
    inside = pl.BlockSpec(memory_space=pltpu.VMEM)

    def shape(*dims, dtype=bf16):
        return jax.ShapeDtypeStruct(dims, dtype)

    def call(kernel, name, out_shape, in_specs, *operands, scratch=()):
        return pl.pallas_call(
            kernel,
            out_shape=out_shape,
            in_specs=list(in_specs) + [inside] * (len(operands) - len(in_specs)),
            out_specs=jax.tree.map(lambda _: inside, out_shape),
            scratch_shapes=list(scratch),
            compiler_params=pltpu.CompilerParams(vmem_limit_bytes=vmem_bytes),
            name=name,
        )(*operands)

    def share_shapes(count):
        return [shape(share, columns, dtype=f32)] + [shape(share, columns)] * (count - 1)

    arrived = partner(wavefunction, {"rep": 1})
    left_own, left_other, right, wave_own = call(
        load_kernel,
        "load_operators",
        [
            shape(terms, rows, rows),
            shape(terms, rows, side - rows),
            shape(*right_blocks.shape),
            shape(rows, columns),
        ],
        [smem] + [outside] * 3,
        sector_sizes,
        left_blocks,
        right_blocks,
        wavefunction,
        scratch=[pltpu.SemaphoreType.DMA((4,))],
    )
    operators = (sector_sizes, sector_pairs, pair_weights, left_own, left_other, right)

    wave_other, *shares = call(
        lambda *refs: first_kernel(sectors, *refs),
        "first_sigma_terms",
        [shape(rows, columns)] + share_shapes(ops_count * sectors),
        [smem] * 3,
        *operators,
        wave_own,
        arrived,
        scratch=[pltpu.VMEM((sectors, rows, columns), f32)],
    )
    received = [
        partner(shares[index], {"ops": index // sectors, "sec": index % sectors})
        for index in reversed(range(1, ops_count * sectors))
    ]
    first_share = call(
        sum_kernel, "sum_first_sigma", shape(share, columns), [], shares[0], *received
    )
    along = [None] * ops_count
    for step in reversed(range(ops_count)):
        along[step] = partner(first_share, {"ops": step})
    pieces = [
        partner(along[step], {"sec": across})
        for step in range(ops_count)
        for across in range(sectors)
    ]
    sigma_own = call(
        join_halves_kernel, "join_first_sigma", shape(sectors, rows, columns), [], *pieces
    )
    sigma_other = partner(sigma_own, {"rep": 1})

    shares = call(
        second_kernel,
        "second_sigma_terms",
        share_shapes(ops_count),
        [smem] * 3,
        *operators,
        sigma_own,
        sigma_other,
        scratch=[pltpu.VMEM((rows, columns), f32)],
    )
    received = [partner(shares[step], {"ops": step}) for step in reversed(range(1, ops_count))]
    sums = call(
        sums_kernel,
        "sums_for_rayleigh",
        shape(3, 8, 128, dtype=f32),
        [],
        wave_own,
        wave_other,
        sigma_own,
        sigma_other,
    )
    second_wave, factors = call(
        wave_kernel,
        "second_wave",
        [shape(1, rows, columns), shape(2, 8, 128, dtype=f32)],
        [smem],
        sector_sizes,
        wave_own,
        sigma_own,
        *[partner(sums, {"sec": step}) for step in range(sectors)],
    )
    second_share = call(
        sum_kernel, "sum_second_sigma", shape(share, columns), [], shares[0], *received
    )
    pieces = [None] * ops_count
    for step in reversed(range(ops_count)):
        pieces[step] = partner(second_share, {"ops": step})
    second_sigma = call(
        join_kernel,
        "join_second_sigma",
        shape(1, rows, columns, dtype=f32),
        [],
        factors,
        sigma_own,
        *pieces,
    )
    return (second_wave, second_sigma)


def solution(mesh):
    return jax.shard_map(
        local,
        mesh=mesh,
        in_specs=(
            P(("grp", "sec"), "rep", None),
            P("grp", None),
            P(("grp", "ops"), None, None),
            P(("grp", "ops"), None, None),
            P(("grp", "ops"), None, None),
            P(("grp", "ops"), None),
        ),
        out_specs=(P(("grp", "sec"), "rep", None), P(("grp", "sec"), "rep", None)),
        check_vma=False,
    )
```

```python
import jax
import jax.numpy as jnp
from jax import lax
from jax.experimental import pallas as pl
from jax.experimental.pallas import tpu as pltpu
from jax.sharding import PartitionSpec as P

epsilon = 1e-06
mebibyte = 1024 * 1024


def mixing_scalar(pairs_ref, weights_ref, term, target, source):
    value = jnp.float32(0.0)
    for pair in range(weights_ref.shape[1]):
        hit = (pairs_ref[term, 1, pair] == target) & (pairs_ref[term, 0, pair] == source)
        value = value + jnp.where(hit, weights_ref[term, pair], jnp.float32(0.0))
    return value


def live_cells(sizes_ref, sector, row_start, rows, columns):
    row = row_start + lax.broadcasted_iota(jnp.int32, (rows, columns), 0)
    column = lax.broadcasted_iota(jnp.int32, (rows, columns), 1)
    return (row < sizes_ref[sector, 0]) & (column < sizes_ref[sector, 1])


def masked(values, live):
    return jnp.where(live, values.astype(jnp.float32), 0.0).astype(values.dtype)


def times_right(values, right):
    return lax.dot_general(
        values.astype(jnp.bfloat16),
        right,
        (((1,), (1,)), ((), ())),
        preferred_element_type=jnp.float32,
    )


def start_operators(left_ref, right_ref, left, right, sems):
    rows = left.shape[1]
    start = pl.multiple_of(lax.axis_index("rep") * rows, rows)
    copies = []
    for term in range(left.shape[0]):
        pair = (
            pltpu.make_async_copy(
                left_ref.at[term, pl.ds(start, rows)], left.at[term], sems.at[0, term]
            ),
            pltpu.make_async_copy(right_ref.at[term], right.at[term], sems.at[1, term]),
        )
        for copy in pair:
            copy.start()
        copies.append(pair)
    return copies


def halves(rows):
    half = rows // 2
    kept = pl.multiple_of((lax.axis_index("ops") & 1) * half, half)
    given = pl.multiple_of(((lax.axis_index("ops") & 1) ^ 1) * half, half)
    return kept, given


def first_kernel(sectors, *refs):
    sizes_ref, pairs_ref, weights_ref, left_ref, right_ref, own_ref, arrived = refs[:7]
    wave, *parts = refs[7 : 8 + 2 * sectors]
    left, right, held, sems, own, own_sem = refs[8 + 2 * sectors :]
    rows, columns = own.shape[1:]
    half = rows // 2
    own_copy = pltpu.make_async_copy(own_ref, own, own_sem)
    own_copy.start()
    copies = start_operators(left_ref, right_ref, left, right, sems)
    sector = lax.axis_index("sec")
    core = lax.axis_index("rep")
    for piece, place in ((arrived, core ^ 1), (own, core)):
        if piece is own:
            own_copy.wait()
        start = pl.multiple_of(place * rows, rows)
        live = live_cells(sizes_ref, sector, start, rows, columns)
        wave[pl.ds(start, rows), :] = masked(piece[0], live)
    totals = [None] * sectors
    for term in range(right.shape[0]):
        copies[term][0].wait()
        product = jnp.dot(left[term], wave[...], preferred_element_type=jnp.float32)
        copies[term][1].wait()
        product = times_right(product, right[term])
        for step in range(sectors):
            weight = mixing_scalar(pairs_ref, weights_ref, term, sector ^ step, sector)
            part = weight * product
            totals[step] = part if totals[step] is None else totals[step] + part
    for step in range(sectors):
        live = live_cells(sizes_ref, sector ^ step, core * rows, rows, columns)
        held[step] = jnp.where(live, totals[step], 0.0)
    for index, out in enumerate(parts):
        start = halves(rows)[index // sectors]
        out[...] = held[index % sectors, pl.ds(start, half), :].astype(out.dtype)


def sum_kernel(count, *refs):
    total = refs[0][...].astype(jnp.float32)
    for piece in refs[1:count]:
        total = total + piece[...].astype(jnp.float32)
    refs[-1][...] = total.astype(refs[-1].dtype)


def join_halves_kernel(*refs):
    pieces, joined = refs[:-1], refs[-1]
    sectors, rows, _ = joined.shape
    sector = lax.axis_index("sec")
    starts = halves(rows)
    for index, piece in enumerate(pieces):
        along, across = index // sectors, index % sectors
        joined[sector ^ across, pl.ds(starts[along], rows // 2), :] = piece[...]


def second_kernel(
    sizes_ref, pairs_ref, weights_ref, left_ref, right_ref, own, arrived,
    sigma, kept, given,
    left, right, held, sems,
):
    sectors, rows, columns = own.shape
    copies = start_operators(left_ref, right_ref, left, right, sems)
    target = lax.axis_index("sec")
    core = lax.axis_index("rep")
    for piece, place in ((own, core), (arrived, core ^ 1)):
        sigma[:, pl.ds(pl.multiple_of(place * rows, rows), rows), :] = piece[...]
    total = None
    for term in range(right.shape[0]):
        combined = None
        copies[term][0].wait()
        for source in range(sectors):
            weight = mixing_scalar(pairs_ref, weights_ref, term, target, source)
            part = weight * jnp.dot(
                left[term], sigma[source], preferred_element_type=jnp.float32
            )
            combined = part if combined is None else combined + part
        copies[term][1].wait()
        part = times_right(combined, right[term])
        total = part if total is None else total + part
    live = live_cells(sizes_ref, target, core * rows, rows, columns)
    held[...] = jnp.where(live, total, 0.0)
    for out, start in zip((kept, given), halves(rows)):
        out[...] = held[pl.ds(start, rows // 2), :].astype(out.dtype)


def sums_kernel(wave, sigma, out):
    sector = lax.axis_index("sec")
    step, columns = 16, wave.shape[1]

    def add_rows(block, carry):
        start = pl.multiple_of(block * step, step)
        w = wave[pl.ds(start, step), :].astype(jnp.float32)
        s = sigma[sector, pl.ds(start, step), :].astype(jnp.float32)
        return (carry[0] + w * s, carry[1] + w * w, carry[2] + s * s)

    sums = (jnp.zeros((step, columns), jnp.float32),) * 3
    sums = lax.fori_loop(0, wave.shape[0] // step, add_rows, sums, unroll=2)
    for index, value in enumerate(sums):
        out[index] = jnp.broadcast_to(jnp.sum(value, keepdims=True), out.shape[1:])


def wave_kernel(sizes_ref, wave, sigma, *refs):
    sums, (second, factors) = refs[:-2], refs[-2:]
    rows, columns = second.shape[1:]
    live_count = jnp.float32(0.0)
    for sector in range(sizes_ref.shape[0]):
        live_count = live_count + sizes_ref[sector, 0].astype(jnp.float32) * sizes_ref[
            sector, 1
        ].astype(jnp.float32)
    total = sums[0][...]
    for other in sums[1:]:
        total = total + other[...]
    correlation, norm_square, sigma_square = total[0], total[1], total[2]
    rayleigh = correlation / norm_square
    residual_square = (
        sigma_square - 2.0 * rayleigh * correlation + rayleigh * rayleigh * norm_square
    )
    residual_square = jnp.maximum(residual_square, 0.0)
    scale = 1.0 / jnp.sqrt(residual_square / live_count + epsilon)
    factors[0] = scale
    factors[1] = rayleigh * scale
    sigma_factor = jnp.broadcast_to(scale[:1, :1], (rows, columns))
    wave_factor = jnp.broadcast_to((rayleigh * scale)[:1, :1], (rows, columns))
    mine = pl.ds(pl.multiple_of(lax.axis_index("rep") * rows, rows), rows)
    values = sigma_factor * sigma[lax.axis_index("sec"), mine, :].astype(jnp.float32)
    values = values - wave_factor * wave[mine, :].astype(jnp.float32)
    second[0] = values.astype(second.dtype)


def join_kernel(factors, sigma, *refs):
    pieces, out = refs[:-1], refs[-1]
    rows, columns = out.shape[1:]
    half = rows // 2
    sector = lax.axis_index("sec")
    first = lax.axis_index("rep") * rows
    scale = jnp.broadcast_to(factors[0][:1, :1], (half, columns))
    shift = jnp.broadcast_to(factors[1][:1, :1], (half, columns))
    for start, piece in zip(halves(rows), pieces):
        mine = pl.ds(pl.multiple_of(first + start, half), half)
        moved = shift * sigma[sector, mine, :].astype(jnp.float32)
        out[0, pl.ds(start, half), :] = scale * piece[...].astype(jnp.float32) - moved


def partner(value, steps):
    steps = {axis: step for axis, step in steps.items() if step}
    if not steps:
        return value
    axes = tuple(steps)
    places = [()]
    for axis in axes:
        places = [place + (i,) for place in places for i in range(lax.axis_size(axis))]
    index = {place: i for i, place in enumerate(places)}
    pairs = [
        (index[tuple(i ^ steps[axis] for i, axis in zip(place, axes))], index[place])
        for place in places
    ]
    return lax.ppermute(value, axes, pairs)


def local(wavefunction, sector_sizes, left_blocks, right_blocks, sector_pairs, pair_weights):
    sectors = sector_sizes.shape[0]
    ops_count = lax.axis_size("ops")
    _, rows, columns = wavefunction.shape
    terms, side = left_blocks.shape[0], left_blocks.shape[1]
    half = rows // 2
    bf16, f32 = jnp.bfloat16, jnp.float32
    smem = pl.BlockSpec(memory_space=pltpu.SMEM)
    outside = pl.BlockSpec(memory_space=pltpu.HBM)
    inside = pl.BlockSpec(memory_space=pltpu.VMEM)

    def shape(*dims, dtype=bf16):
        return jax.ShapeDtypeStruct(dims, dtype)

    def call(kernel, name, out_shape, in_specs, *operands, scratch=(), vmem=4):
        return pl.pallas_call(
            kernel,
            out_shape=out_shape,
            in_specs=list(in_specs) + [inside] * (len(operands) - len(in_specs)),
            out_specs=jax.tree.map(lambda _: inside, out_shape),
            scratch_shapes=list(scratch),
            compiler_params=pltpu.CompilerParams(vmem_limit_bytes=vmem * mebibyte),
            name=name,
        )(*operands)

    def summed(name, *pieces, after=()):
        count = len(pieces)
        return call(
            lambda *refs: sum_kernel(count, *refs), name, shape(half, columns), [], *pieces, *after
        )

    def doubled(name, value, after=()):
        step = 2
        while step < ops_count:
            value = summed(name, value, partner(value, {"ops": step}), after=after)
            step *= 2
        return value

    pairs = jnp.swapaxes(sector_pairs, 1, 2)
    operators = (sector_sizes, pairs, pair_weights, left_blocks, right_blocks)
    operator_specs = [smem] * 3 + [outside] * 2
    operator_scratch = [pltpu.VMEM((terms, rows, side), bf16), pltpu.VMEM(right_blocks.shape, bf16)]
    copy_sems = pltpu.SemaphoreType.DMA((2, terms))
    exact, sent = shape(half, columns, dtype=f32), shape(half, columns)

    wave, kept, *rest = call(
        lambda *refs: first_kernel(sectors, *refs),
        "first_sigma_terms",
        [shape(side, columns)] + ([exact] + [sent] * (sectors - 1)) * 2,
        operator_specs + [outside],
        *operators,
        wavefunction,
        partner(wavefunction, {"rep": 1}),
        scratch=operator_scratch + [
            pltpu.VMEM((sectors, rows, columns), f32),
            copy_sems,
            pltpu.VMEM((1, rows, columns), bf16),
            pltpu.SemaphoreType.DMA,
        ],
        vmem=51,
    )
    kept_parts, given, given_parts = rest[: sectors - 1], rest[sectors - 1], rest[sectors:]
    given_parts = [partner(part, {"sec": i}) for i, part in enumerate(given_parts, 1)]
    kept_parts = [partner(part, {"sec": i}) for i, part in enumerate(kept_parts, 1)]
    given = summed("sum_sectors", given, *given_parts)
    total = summed("sum_neighbours", kept, *kept_parts, partner(given, {"ops": 1}))
    total = doubled("sum_first_sigma", total)
    pieces = [
        partner(total, {"ops": along, "sec": across})
        for along in range(2)
        for across in range(sectors)
    ]
    joined = call(
        join_halves_kernel, "join_first_sigma", shape(sectors, rows, columns), [], *pieces
    )

    sigma, kept, given = call(
        second_kernel,
        "second_sigma_terms",
        [shape(sectors, side, columns), exact, sent],
        operator_specs,
        *operators,
        joined,
        partner(joined, {"rep": 1}),
        scratch=operator_scratch + [pltpu.VMEM((rows, columns), f32), copy_sems],
        vmem=51,
    )
    sums = call(sums_kernel, "sums_for_rayleigh", shape(3, 8, 128, dtype=f32), [], wave, sigma)
    second_wave, factors = call(
        wave_kernel,
        "second_wave",
        [shape(1, rows, columns), shape(2, 8, 128, dtype=f32)],
        [smem],
        sector_sizes,
        wave,
        sigma,
        *[partner(sums, {"sec": step}) for step in range(sectors)],
    )
    total = summed("sum_neighbours", kept, partner(given, {"ops": 1}), after=(sums,))
    total = doubled("sum_second_sigma", total, after=(factors,))
    second_sigma = call(
        join_kernel,
        "join_second_sigma",
        shape(1, rows, columns, dtype=f32),
        [],
        factors,
        sigma,
        total,
        partner(total, {"ops": 1}),
    )
    return (second_wave, second_sigma)


def solution(mesh):
    return jax.shard_map(
        local,
        mesh=mesh,
        in_specs=(
            P(("grp", "sec"), "rep", None),
            P("grp", None),
            P(("grp", "ops"), None, None),
            P(("grp", "ops"), None, None),
            P(("grp", "ops"), None, None),
            P(("grp", "ops"), None),
        ),
        out_specs=(P(("grp", "sec"), "rep", None), P(("grp", "sec"), "rep", None)),
        check_vma=False,
    )
```

```python
import jax
import jax.numpy as jnp
from jax import lax
from jax.experimental import pallas as pl
from jax.experimental.pallas import tpu as pltpu
from jax.sharding import PartitionSpec as P

epsilon = 1e-06
mebibyte = 1024 * 1024


def mixing_scalar(pairs_ref, weights_ref, term, target, source):
    value = jnp.float32(0.0)
    for pair in range(weights_ref.shape[1]):
        hit = (pairs_ref[term, 1, pair] == target) & (pairs_ref[term, 0, pair] == source)
        value = value + jnp.where(hit, weights_ref[term, pair], jnp.float32(0.0))
    return value


def live_cells(sizes_ref, sector, row_start, rows, columns):
    row = row_start + lax.broadcasted_iota(jnp.int32, (rows, columns), 0)
    column = lax.broadcasted_iota(jnp.int32, (rows, columns), 1)
    return (row < sizes_ref[sector, 0]) & (column < sizes_ref[sector, 1])


def masked(values, live):
    return jnp.where(live, values.astype(jnp.float32), 0.0).astype(values.dtype)


def left_times(left_own, left_other, term, own, other):
    return jnp.dot(left_own[term], own, preferred_element_type=jnp.float32) + jnp.dot(
        left_other[term], other, preferred_element_type=jnp.float32
    )


def times_right(values, right, term):
    return lax.dot_general(
        values.astype(jnp.bfloat16),
        right[term],
        (((1,), (1,)), ((), ())),
        preferred_element_type=jnp.float32,
    )


def load_kernel(left_ref, right_ref, left_own, left_other, right, sems):
    rows = left_own.shape[1]
    core = lax.axis_index("rep")
    own = pl.multiple_of(core * rows, rows)
    other = pl.multiple_of((core ^ 1) * rows, rows)
    mine = left_ref.at[:, pl.ds(own, rows)]
    copies = [
        pltpu.make_async_copy(mine.at[:, :, pl.ds(own, rows)], left_own, sems.at[0]),
        pltpu.make_async_copy(mine.at[:, :, pl.ds(other, rows)], left_other, sems.at[1]),
        pltpu.make_async_copy(right_ref, right, sems.at[2]),
    ]
    for copy in copies:
        copy.start()
    for copy in copies:
        copy.wait()


def first_kernel(sectors, *refs):
    sizes_ref, pairs_ref, weights_ref, left_own, left_other, right, wave, arrived = refs[:8]
    own, other, *parts = refs[8:-1]
    held = refs[-1]
    rows, columns = own.shape
    share = parts[0].shape[1]
    sector = lax.axis_index("sec")
    core = lax.axis_index("rep")
    place = lax.axis_index("ops")
    live = live_cells(sizes_ref, sector, core * rows, rows, columns)
    own[...] = masked(wave[0], live)
    live = live_cells(sizes_ref, sector, (core ^ 1) * rows, rows, columns)
    other[...] = masked(arrived[0], live)
    totals = [None] * sectors
    for term in range(right.shape[0]):
        product = left_times(left_own, left_other, term, own[...], other[...])
        product = times_right(product, right, term)
        for step in range(sectors):
            weight = mixing_scalar(pairs_ref, weights_ref, term, sector ^ step, sector)
            part = weight * product
            totals[step] = part if totals[step] is None else totals[step] + part
    for step in range(sectors):
        live = live_cells(sizes_ref, sector ^ step, core * rows, rows, columns)
        held[step] = jnp.where(live, totals[step], 0.0)
    for index, out in enumerate(parts):
        first = 2 * (index // sectors)
        for step in range(out.shape[0]):
            start = pl.multiple_of((place ^ (first + step)) * share, share)
            out[step] = held[index % sectors, pl.ds(start, share), :].astype(out.dtype)


def far_kernel(sectors, *refs):
    far, near = refs[:sectors], refs[sectors : 2 * sectors - 1]
    sums, handed = refs[2 * sectors - 1 : -(sectors - 1)], refs[-(sectors - 1) :]
    for step, out in enumerate(sums):
        total = far[0][step]
        for part in far[1:]:
            total = total + part[step].astype(jnp.float32)
        out[...] = total.astype(out.dtype)
    for part, out in zip(near, handed):
        out[...] = part[...]


def near_kernel(*refs):
    parts, (kept, given) = refs[:-2], refs[-2:]
    total = parts[0][...]
    for part in parts[1:]:
        total = total + part[...].astype(jnp.float32)
    kept[...] = total[0]
    given[...] = total[1].astype(given.dtype)


def sum_kernel(count, own_ref, *refs):
    total = own_ref[...]
    for piece in refs[:count]:
        total = total + piece[...].astype(jnp.float32)
    refs[-1][...] = total.astype(refs[-1].dtype)


def join_halves_kernel(*refs):
    pieces, half = refs[:-1], refs[-1]
    sectors = half.shape[0]
    share = pieces[0].shape[0]
    sector = lax.axis_index("sec")
    place = lax.axis_index("ops")
    for index, piece in enumerate(reversed(pieces)):
        along, across = index // sectors, index % sectors
        start = pl.multiple_of((place ^ along) * share, share)
        half[sector ^ across, pl.ds(start, share), :] = piece[...]


def second_kernel(
    sizes_ref, pairs_ref, weights_ref, left_own, left_other, right, own, other, *refs
):
    shares, held = refs[:-1], refs[-1]
    sectors, rows, columns = own.shape
    share = shares[0].shape[0]
    target = lax.axis_index("sec")
    core = lax.axis_index("rep")
    place = lax.axis_index("ops")
    total = None
    for term in range(right.shape[0]):
        combined = None
        for source in range(sectors):
            weight = mixing_scalar(pairs_ref, weights_ref, term, target, source)
            part = weight * left_times(left_own, left_other, term, own[source], other[source])
            combined = part if combined is None else combined + part
        part = times_right(combined, right, term)
        total = part if total is None else total + part
    live = live_cells(sizes_ref, target, core * rows, rows, columns)
    held[...] = jnp.where(live, total, 0.0)
    for step, out in enumerate(shares):
        start = pl.multiple_of((place ^ step) * share, share)
        out[...] = held[pl.ds(start, share), :].astype(out.dtype)


def sums_kernel(wave_own, wave_other, sigma_own, sigma_other, out):
    sector = lax.axis_index("sec")
    step, columns = 16, wave_own.shape[1]
    sums = (jnp.zeros((step, columns), jnp.float32),) * 3
    for wave, sigma in ((wave_own, sigma_own), (wave_other, sigma_other)):

        def add_rows(block, carry):
            start = pl.multiple_of(block * step, step)
            w = wave[pl.ds(start, step), :].astype(jnp.float32)
            s = sigma[sector, pl.ds(start, step), :].astype(jnp.float32)
            return (carry[0] + w * s, carry[1] + w * w, carry[2] + s * s)

        sums = lax.fori_loop(0, wave.shape[0] // step, add_rows, sums, unroll=2)
    for index, value in enumerate(sums):
        out[index] = jnp.broadcast_to(jnp.sum(value, keepdims=True), out.shape[1:])


def wave_kernel(sizes_ref, wave_own, sigma_own, *refs):
    sums, (second, factors) = refs[:-2], refs[-2:]
    rows, columns = wave_own.shape
    live_count = jnp.float32(0.0)
    for sector in range(sizes_ref.shape[0]):
        live_count = live_count + sizes_ref[sector, 0].astype(jnp.float32) * sizes_ref[
            sector, 1
        ].astype(jnp.float32)
    total = sums[0][...]
    for other in sums[1:]:
        total = total + other[...]
    correlation, norm_square, sigma_square = total[0], total[1], total[2]
    rayleigh = correlation / norm_square
    residual_square = (
        sigma_square - 2.0 * rayleigh * correlation + rayleigh * rayleigh * norm_square
    )
    residual_square = jnp.maximum(residual_square, 0.0)
    scale = 1.0 / jnp.sqrt(residual_square / live_count + epsilon)
    factors[0] = scale
    factors[1] = rayleigh * scale
    sigma_factor = jnp.broadcast_to(scale[:1, :1], (rows, columns))
    wave_factor = jnp.broadcast_to((rayleigh * scale)[:1, :1], (rows, columns))
    sigma = sigma_own[lax.axis_index("sec")].astype(jnp.float32)
    wave = wave_own[...].astype(jnp.float32)
    second[0] = (sigma_factor * sigma - wave_factor * wave).astype(second.dtype)


def join_kernel(factors, sigma_own, *refs):
    pieces, out = refs[:-1], refs[-1]
    share, columns = pieces[0].shape
    sector = lax.axis_index("sec")
    place = lax.axis_index("ops")
    scale = jnp.broadcast_to(factors[0][:1, :1], (share, columns))
    shift = jnp.broadcast_to(factors[1][:1, :1], (share, columns))
    for step, piece in enumerate(reversed(pieces)):
        start = pl.multiple_of((place ^ step) * share, share)
        sigma = sigma_own[sector, pl.ds(start, share), :].astype(jnp.float32)
        out[0, pl.ds(start, share), :] = scale * piece[...].astype(jnp.float32) - shift * sigma


def partner(value, steps):
    steps = {axis: step for axis, step in steps.items() if step}
    if not steps:
        return value
    axes = tuple(steps)
    places = [()]
    for axis in axes:
        places = [place + (i,) for place in places for i in range(lax.axis_size(axis))]
    index = {place: i for i, place in enumerate(places)}
    pairs = [
        (index[tuple(i ^ steps[axis] for i, axis in zip(place, axes))], index[place])
        for place in places
    ]
    return lax.ppermute(value, axes, pairs)


def local(wavefunction, sector_sizes, left_blocks, right_blocks, sector_pairs, pair_weights):
    sectors = sector_sizes.shape[0]
    ops_count = lax.axis_size("ops")
    _, rows, columns = wavefunction.shape
    terms, side = left_blocks.shape[0], left_blocks.shape[1]
    share = rows // ops_count
    bf16, f32 = jnp.bfloat16, jnp.float32
    smem = pl.BlockSpec(memory_space=pltpu.SMEM)
    outside = pl.BlockSpec(memory_space=pltpu.HBM)
    inside = pl.BlockSpec(memory_space=pltpu.VMEM)

    def shape(*dims, dtype=bf16):
        return jax.ShapeDtypeStruct(dims, dtype)

    def call(kernel, name, out_shape, in_specs, *operands, scratch=(), vmem=16):
        return pl.pallas_call(
            kernel,
            out_shape=out_shape,
            in_specs=list(in_specs) + [inside] * (len(operands) - len(in_specs)),
            out_specs=jax.tree.map(lambda _: inside, out_shape),
            scratch_shapes=list(scratch),
            compiler_params=pltpu.CompilerParams(vmem_limit_bytes=vmem * mebibyte),
            name=name,
        )(*operands)

    def summed(name, own, *pieces, after=()):
        count = len(pieces)
        return call(
            lambda *refs: sum_kernel(count, *refs),
            name,
            shape(share, columns),
            [],
            own,
            *pieces,
            *after,
        )

    def parts(count):
        return [shape(count, share, columns, dtype=f32)] + [shape(count, share, columns)] * (
            sectors - 1
        )

    def across(values):
        return [partner(value, {"sec": step}) for step, value in enumerate(values, 1)]

    farthest_first = list(reversed(range(ops_count)))
    far_steps = farthest_first[:-2]
    arrived = partner(wavefunction, {"rep": 1})
    left_own, left_other, right = call(
        load_kernel,
        "load_operators",
        [
            shape(terms, rows, rows),
            shape(terms, rows, side - rows),
            shape(*right_blocks.shape),
        ],
        [outside] * 2,
        left_blocks,
        right_blocks,
        scratch=[pltpu.SemaphoreType.DMA((3,))],
        vmem=49,
    )
    pairs = jnp.swapaxes(sector_pairs, 1, 2)
    operators = (sector_sizes, pairs, pair_weights, left_own, left_other, right)

    wave_own, wave_other, *rest = call(
        lambda *refs: first_kernel(sectors, *refs),
        "first_sigma_terms",
        [shape(rows, columns)] * 2 + parts(2) + parts(ops_count - 2),
        [smem] * 3,
        *operators,
        wavefunction,
        arrived,
        scratch=[pltpu.VMEM((sectors, rows, columns), f32)],
    )
    near, far = rest[:sectors], rest[sectors:]
    sums = call(
        lambda *refs: far_kernel(sectors, *refs),
        "sum_far_shares",
        [shape(share, columns)] * (ops_count - 2) + parts(2)[1:],
        [],
        far[0],
        *across(far[1:]),
        *near[1:],
    )
    far_sums, handed = sums[: ops_count - 2], sums[ops_count - 2 :]
    kept, given = call(
        near_kernel,
        "sum_near_shares",
        [shape(share, columns, dtype=f32), shape(share, columns)],
        [],
        near[0],
        *across(handed),
    )
    received = [partner(far_sums[step - 2], {"ops": step}) for step in far_steps]
    first_share = summed("sum_first_sigma", kept, *received, partner(given, {"ops": 1}))
    pieces = []
    for step in farthest_first:
        along = partner(first_share, {"ops": step})
        pieces += [partner(along, {"sec": i}) for i in reversed(range(sectors))]
    sigma_own = call(
        join_halves_kernel, "join_first_sigma", shape(sectors, rows, columns), [], *pieces
    )
    sigma_other = partner(sigma_own, {"rep": 1})

    shares = call(
        second_kernel,
        "second_sigma_terms",
        [shape(share, columns, dtype=f32)] + [shape(share, columns)] * (ops_count - 1),
        [smem] * 3,
        *operators,
        sigma_own,
        sigma_other,
        scratch=[pltpu.VMEM((rows, columns), f32)],
    )
    received = [partner(shares[step], {"ops": step}) for step in farthest_first[:-1]]
    sums = call(
        sums_kernel,
        "sums_for_rayleigh",
        shape(3, 8, 128, dtype=f32),
        [],
        wave_own,
        wave_other,
        sigma_own,
        sigma_other,
    )
    second_share = summed("sum_second_sigma", shares[0], *received, after=(sums,))
    second_wave, factors = call(
        wave_kernel,
        "second_wave",
        [shape(1, rows, columns), shape(2, 8, 128, dtype=f32)],
        [smem],
        sector_sizes,
        wave_own,
        sigma_own,
        *[partner(sums, {"sec": step}) for step in range(sectors)],
    )
    second_sigma = call(
        join_kernel,
        "join_second_sigma",
        shape(1, rows, columns, dtype=f32),
        [],
        factors,
        sigma_own,
        *[partner(second_share, {"ops": step}) for step in farthest_first],
    )
    return (second_wave, second_sigma)


def solution(mesh):
    return jax.shard_map(
        local,
        mesh=mesh,
        in_specs=(
            P(("grp", "sec"), "rep", None),
            P("grp", None),
            P(("grp", "ops"), None, None),
            P(("grp", "ops"), None, None),
            P(("grp", "ops"), None, None),
            P(("grp", "ops"), None),
        ),
        out_specs=(P(("grp", "sec"), "rep", None), P(("grp", "sec"), "rep", None)),
        check_vma=False,
    )
```

```python
import jax
import jax.numpy as jnp
from jax import lax
from jax.experimental import pallas as pl
from jax.experimental.pallas import tpu as pltpu
from jax.sharding import PartitionSpec as P

epsilon = 1e-06
mebibyte = 1024 * 1024


def mixing_scalar(pairs_ref, weights_ref, term, target, source):
    value = jnp.float32(0.0)
    for pair in range(weights_ref.shape[1]):
        hit = (pairs_ref[term, 1, pair] == target) & (pairs_ref[term, 0, pair] == source)
        value = value + jnp.where(hit, weights_ref[term, pair], jnp.float32(0.0))
    return value


def live_cells(sizes_ref, sector, row_start, rows, columns):
    row = row_start + lax.broadcasted_iota(jnp.int32, (rows, columns), 0)
    column = lax.broadcasted_iota(jnp.int32, (rows, columns), 1)
    return (row < sizes_ref[sector, 0]) & (column < sizes_ref[sector, 1])


def masked(values, live):
    return jnp.where(live, values.astype(jnp.float32), 0.0).astype(values.dtype)


def left_times(left_own, left_other, term, own, other):
    return jnp.dot(left_own[term], own, preferred_element_type=jnp.float32) + jnp.dot(
        left_other[term], other, preferred_element_type=jnp.float32
    )


def times_right(values, right, term):
    return lax.dot_general(
        values.astype(jnp.bfloat16),
        right[term],
        (((1,), (1,)), ((), ())),
        preferred_element_type=jnp.float32,
    )


def load_kernel(left_ref, right_ref, left_own, left_other, right, sems):
    rows = left_own.shape[1]
    core = lax.axis_index("rep")
    own = pl.multiple_of(core * rows, rows)
    other = pl.multiple_of((core ^ 1) * rows, rows)
    mine = left_ref.at[:, pl.ds(own, rows)]
    copies = [
        pltpu.make_async_copy(mine.at[:, :, pl.ds(own, rows)], left_own, sems.at[0]),
        pltpu.make_async_copy(mine.at[:, :, pl.ds(other, rows)], left_other, sems.at[1]),
        pltpu.make_async_copy(right_ref, right, sems.at[2]),
    ]
    for copy in copies:
        copy.start()
    for copy in copies:
        copy.wait()


def first_kernel(shares, *refs):
    sizes_ref, pairs_ref, weights_ref, left_own, left_other, right, wave, arrived = refs[:8]
    own, other, *parts = refs[8:-1]
    held = refs[-1]
    rows, columns = own.shape
    share = parts[0].shape[0]
    sectors = held.shape[0]
    sector = lax.axis_index("sec")
    core = lax.axis_index("rep")
    place = lax.axis_index("ops")
    live = live_cells(sizes_ref, sector, core * rows, rows, columns)
    own[...] = masked(wave[0], live)
    live = live_cells(sizes_ref, sector, (core ^ 1) * rows, rows, columns)
    other[...] = masked(arrived[0], live)
    totals = [None] * sectors
    for term in range(right.shape[0]):
        product = left_times(left_own, left_other, term, own[...], other[...])
        product = times_right(product, right, term)
        for step in range(sectors):
            weight = mixing_scalar(pairs_ref, weights_ref, term, sector ^ step, sector)
            part = weight * product
            totals[step] = part if totals[step] is None else totals[step] + part
    for step in range(sectors):
        live = live_cells(sizes_ref, sector ^ step, core * rows, rows, columns)
        held[step] = jnp.where(live, totals[step], 0.0)
    for (along, across), out in zip(shares, parts):
        start = pl.multiple_of((place ^ along) * share, share)
        out[...] = held[across, pl.ds(start, share), :].astype(out.dtype)


def sum_kernel(count, own_ref, *refs):
    total = own_ref[...]
    for piece in refs[:count]:
        total = total + piece[...].astype(jnp.float32)
    refs[-1][...] = total.astype(refs[-1].dtype)


def place_kernel(spots, *refs):
    pieces, half = refs[:-1], refs[-1]
    share = pieces[0].shape[0]
    place = lax.axis_index("ops")
    for (along, index), piece in zip(spots, pieces):
        start = pl.multiple_of((place ^ along) * share, share)
        half[index, pl.ds(start, share), :] = piece[...]


def left_kernel(left_own, left_other, own, other, out):
    for term in range(out.shape[0]):
        out[term] = left_times(left_own, left_other, term, own[0], other[0])


def second_kernel(
    sizes_ref, pairs_ref, weights_ref, left_own, left_other, right, products, own, other, *refs
):
    shares, held = refs[:-1], refs[-1]
    rows, columns = own.shape[1:]
    share = shares[0].shape[0]
    target = lax.axis_index("sec")
    core = lax.axis_index("rep")
    place = lax.axis_index("ops")
    total = None
    for term in range(right.shape[0]):
        weight = mixing_scalar(pairs_ref, weights_ref, term, target, target)
        combined = weight * products[term]
        for step in range(own.shape[0]):
            weight = mixing_scalar(pairs_ref, weights_ref, term, target, target ^ (step + 1))
            combined = combined + weight * left_times(
                left_own, left_other, term, own[step], other[step]
            )
        part = times_right(combined, right, term)
        total = part if total is None else total + part
    live = live_cells(sizes_ref, target, core * rows, rows, columns)
    held[...] = jnp.where(live, total, 0.0)
    for step, out in enumerate(shares):
        start = pl.multiple_of((place ^ step) * share, share)
        out[...] = held[pl.ds(start, share), :].astype(out.dtype)


def sums_kernel(wave_own, wave_other, sigma_own, sigma_other, out):
    step, columns = 16, wave_own.shape[1]
    sums = (jnp.zeros((step, columns), jnp.float32),) * 3
    for wave, sigma in ((wave_own, sigma_own), (wave_other, sigma_other)):

        def add_rows(block, carry):
            start = pl.multiple_of(block * step, step)
            w = wave[pl.ds(start, step), :].astype(jnp.float32)
            s = sigma[0, pl.ds(start, step), :].astype(jnp.float32)
            return (carry[0] + w * s, carry[1] + w * w, carry[2] + s * s)

        sums = lax.fori_loop(0, wave.shape[0] // step, add_rows, sums, unroll=2)
    for index, value in enumerate(sums):
        out[index] = jnp.broadcast_to(jnp.sum(value, keepdims=True), out.shape[1:])


def wave_kernel(sizes_ref, wave_own, sigma_own, *refs):
    sums, (second, factors) = refs[:-2], refs[-2:]
    rows, columns = wave_own.shape
    live_count = jnp.float32(0.0)
    for sector in range(sizes_ref.shape[0]):
        live_count = live_count + sizes_ref[sector, 0].astype(jnp.float32) * sizes_ref[
            sector, 1
        ].astype(jnp.float32)
    total = sums[0][...]
    for other in sums[1:]:
        total = total + other[...]
    correlation, norm_square, sigma_square = total[0], total[1], total[2]
    rayleigh = correlation / norm_square
    residual_square = (
        sigma_square - 2.0 * rayleigh * correlation + rayleigh * rayleigh * norm_square
    )
    residual_square = jnp.maximum(residual_square, 0.0)
    scale = 1.0 / jnp.sqrt(residual_square / live_count + epsilon)
    factors[0] = scale
    factors[1] = rayleigh * scale
    sigma_factor = jnp.broadcast_to(scale[:1, :1], (rows, columns))
    wave_factor = jnp.broadcast_to((rayleigh * scale)[:1, :1], (rows, columns))
    sigma = sigma_own[0].astype(jnp.float32)
    wave = wave_own[...].astype(jnp.float32)
    second[0] = (sigma_factor * sigma - wave_factor * wave).astype(second.dtype)


def join_kernel(factors, sigma_own, *refs):
    pieces, out = refs[:-1], refs[-1]
    share, columns = pieces[0].shape
    place = lax.axis_index("ops")
    scale = jnp.broadcast_to(factors[0][:1, :1], (share, columns))
    shift = jnp.broadcast_to(factors[1][:1, :1], (share, columns))
    for step, piece in enumerate(reversed(pieces)):
        start = pl.multiple_of((place ^ step) * share, share)
        sigma = sigma_own[0, pl.ds(start, share), :].astype(jnp.float32)
        out[0, pl.ds(start, share), :] = scale * piece[...].astype(jnp.float32) - shift * sigma


def partner(value, steps):
    steps = {axis: step for axis, step in steps.items() if step}
    if not steps:
        return value
    axes = tuple(steps)
    places = [()]
    for axis in axes:
        places = [place + (i,) for place in places for i in range(lax.axis_size(axis))]
    index = {place: i for i, place in enumerate(places)}
    pairs = [
        (index[tuple(i ^ steps[axis] for i, axis in zip(place, axes))], index[place])
        for place in places
    ]
    return lax.ppermute(value, axes, pairs)


def local(wavefunction, sector_sizes, left_blocks, right_blocks, sector_pairs, pair_weights):
    sectors = sector_sizes.shape[0]
    ops_count = lax.axis_size("ops")
    _, rows, columns = wavefunction.shape
    terms, side = left_blocks.shape[0], left_blocks.shape[1]
    share = rows // ops_count
    bf16, f32 = jnp.bfloat16, jnp.float32
    smem = pl.BlockSpec(memory_space=pltpu.SMEM)
    outside = pl.BlockSpec(memory_space=pltpu.HBM)
    inside = pl.BlockSpec(memory_space=pltpu.VMEM)

    def shape(*dims, dtype=bf16):
        return jax.ShapeDtypeStruct(dims, dtype)

    def call(kernel, name, out_shape, in_specs, *operands, scratch=(), vmem=16):
        return pl.pallas_call(
            kernel,
            out_shape=out_shape,
            in_specs=list(in_specs) + [inside] * (len(operands) - len(in_specs)),
            out_specs=jax.tree.map(lambda _: inside, out_shape),
            scratch_shapes=list(scratch),
            compiler_params=pltpu.CompilerParams(vmem_limit_bytes=vmem * mebibyte),
            name=name,
        )(*operands)

    def summed(name, own, *pieces, after=()):
        count = len(pieces)
        return call(
            lambda *refs: sum_kernel(count, *refs),
            name,
            shape(share, columns),
            [],
            own,
            *pieces,
            *after,
        )

    farthest_first = list(reversed(range(ops_count)))
    far_steps = farthest_first[:-2]
    arrived = partner(wavefunction, {"rep": 1})
    left_own, left_other, right = call(
        load_kernel,
        "load_operators",
        [
            shape(terms, rows, rows),
            shape(terms, rows, side - rows),
            shape(*right_blocks.shape),
        ],
        [outside] * 2,
        left_blocks,
        right_blocks,
        scratch=[pltpu.SemaphoreType.DMA((3,))],
        vmem=49,
    )
    pairs = jnp.swapaxes(sector_pairs, 1, 2)
    operators = (sector_sizes, pairs, pair_weights, left_own, left_other, right)

    spots = [(along, across) for along in farthest_first for across in range(sectors)]
    wave_own, wave_other, *rest = call(
        lambda *refs: first_kernel(spots, *refs),
        "first_sigma_terms",
        [shape(rows, columns)] * 2
        + [
            shape(share, columns, dtype=f32 if across == 0 and along != 1 else bf16)
            for along, across in spots
        ],
        [smem] * 3,
        *operators,
        wavefunction,
        arrived,
        scratch=[pltpu.VMEM((sectors, rows, columns), f32)],
    )
    rest = dict(zip(spots, rest))
    received = []
    for along in far_steps:
        parts = [partner(rest[along, across], {"sec": across}) for across in range(sectors)]
        received.append(partner(summed("sum_far_share", *parts), {"ops": along}))
    received += [
        partner(rest[along, across], {"ops": along, "sec": across})
        for along in (1, 0)
        for across in range(sectors)
        if along or across
    ]
    first_share = summed("sum_first_sigma", rest[0, 0], *received)
    along_ops = {along: partner(first_share, {"ops": along}) for along in farthest_first}
    sigma_own = call(
        lambda *refs: place_kernel([(along, 0) for along in farthest_first], *refs),
        "place_own_sector",
        shape(1, rows, columns),
        [],
        *along_ops.values(),
    )
    sigma_other = partner(sigma_own, {"rep": 1})
    spots = [(along, across) for along in farthest_first for across in range(1, sectors)]
    pieces = [
        partner(first_share, {"ops": along, "sec": across})
        if along < 2
        else partner(along_ops[along], {"sec": across})
        for along, across in spots
    ]
    across_own = call(
        lambda *refs: place_kernel([(along, across - 1) for along, across in spots], *refs),
        "place_other_sectors",
        shape(sectors - 1, rows, columns),
        [],
        *pieces,
    )
    across_other = partner(across_own, {"rep": 1})

    products = call(
        left_kernel,
        "left_products",
        shape(terms, rows, columns, dtype=f32),
        [],
        left_own,
        left_other,
        sigma_own,
        sigma_other,
    )
    shares = call(
        second_kernel,
        "second_sigma_terms",
        [shape(share, columns, dtype=f32)] + [shape(share, columns)] * (ops_count - 1),
        [smem] * 3,
        *operators,
        products,
        across_own,
        across_other,
        scratch=[pltpu.VMEM((rows, columns), f32)],
    )
    received = [partner(shares[step], {"ops": step}) for step in farthest_first[:-1]]
    sums = call(
        sums_kernel,
        "sums_for_rayleigh",
        shape(3, 8, 128, dtype=f32),
        [],
        wave_own,
        wave_other,
        sigma_own,
        sigma_other,
    )
    sums = [partner(sums, {"sec": step}) for step in range(sectors)]
    second_share = summed("sum_second_sigma", shares[0], *received, after=sums)
    second_wave, factors = call(
        wave_kernel,
        "second_wave",
        [shape(1, rows, columns), shape(2, 8, 128, dtype=f32)],
        [smem],
        sector_sizes,
        wave_own,
        sigma_own,
        *sums,
    )
    second_sigma = call(
        join_kernel,
        "join_second_sigma",
        shape(1, rows, columns, dtype=f32),
        [],
        factors,
        sigma_own,
        *[partner(second_share, {"ops": step}) for step in farthest_first],
    )
    return (second_wave, second_sigma)


def solution(mesh):
    return jax.shard_map(
        local,
        mesh=mesh,
        in_specs=(
            P(("grp", "sec"), "rep", None),
            P("grp", None),
            P(("grp", "ops"), None, None),
            P(("grp", "ops"), None, None),
            P(("grp", "ops"), None, None),
            P(("grp", "ops"), None),
        ),
        out_specs=(P(("grp", "sec"), "rep", None), P(("grp", "sec"), "rep", None)),
        check_vma=False,
    )
```

```python
import jax
import jax.numpy as jnp
from jax import lax
from jax.experimental import pallas as pl
from jax.experimental.pallas import tpu as pltpu
from jax.sharding import PartitionSpec as P

epsilon = 1e-06
mebibyte = 1024 * 1024


def mixing_scalar(pairs_ref, weights_ref, term, target, source):
    value = jnp.float32(0.0)
    for pair in range(weights_ref.shape[1]):
        hit = (pairs_ref[term, 1, pair] == target) & (pairs_ref[term, 0, pair] == source)
        value = value + jnp.where(hit, weights_ref[term, pair], jnp.float32(0.0))
    return value


def live_cells(sizes_ref, sector, row_start, rows, columns):
    row = row_start + lax.broadcasted_iota(jnp.int32, (rows, columns), 0)
    column = lax.broadcasted_iota(jnp.int32, (rows, columns), 1)
    return (row < sizes_ref[sector, 0]) & (column < sizes_ref[sector, 1])


def masked(values, live):
    return jnp.where(live, values.astype(jnp.float32), 0.0).astype(values.dtype)


def left_times(left_own, left_other, term, own, other):
    return jnp.dot(left_own[term], own, preferred_element_type=jnp.float32) + jnp.dot(
        left_other[term], other, preferred_element_type=jnp.float32
    )


def times_right(values, right, term):
    return lax.dot_general(
        values.astype(jnp.bfloat16),
        right[term],
        (((1,), (1,)), ((), ())),
        preferred_element_type=jnp.float32,
    )


def load_kernel(left_ref, left_own, left_other, sems):
    rows = left_own.shape[1]
    core = lax.axis_index("rep")
    copies = []
    for index, (half, place) in enumerate(((left_own, core), (left_other, core ^ 1))):
        mine = pl.ds(pl.multiple_of(core * rows, rows), rows)
        columns = pl.ds(pl.multiple_of(place * rows, rows), rows)
        copies.append(pltpu.make_async_copy(left_ref.at[:, mine, columns], half, sems.at[index]))
    for copy in copies:
        copy.start()
    for copy in copies:
        copy.wait()


def first_kernel(shares, *refs):
    sizes_ref, pairs_ref, weights_ref, left_own, left_other, right_ref, wave, arrived = refs[:8]
    right, own, other, *parts = refs[8:-2]
    held, sems = refs[-2:]
    rows, columns = own.shape
    share = parts[0].shape[-2]
    copies = [
        pltpu.make_async_copy(right_ref.at[term], right.at[term], sems.at[term])
        for term in range(right.shape[0])
    ]
    for copy in copies:
        copy.start()
    sectors = held.shape[0]
    sector = lax.axis_index("sec")
    core = lax.axis_index("rep")
    place = lax.axis_index("ops")
    live = live_cells(sizes_ref, sector, core * rows, rows, columns)
    own[...] = masked(wave[0], live)
    live = live_cells(sizes_ref, sector, (core ^ 1) * rows, rows, columns)
    other[...] = masked(arrived[0], live)
    totals = [None] * sectors
    for term in range(right.shape[0]):
        product = left_times(left_own, left_other, term, own[...], other[...])
        copies[term].wait()
        product = times_right(product, right, term)
        for step in range(sectors):
            weight = mixing_scalar(pairs_ref, weights_ref, term, sector ^ step, sector)
            part = weight * product
            totals[step] = part if totals[step] is None else totals[step] + part
    for step in range(sectors):
        live = live_cells(sizes_ref, sector ^ step, core * rows, rows, columns)
        held[step] = jnp.where(live, totals[step], 0.0)
    for (steps, across), out in zip(shares, parts):
        for index, along in enumerate(steps):
            start = pl.multiple_of((place ^ along) * share, share)
            out[index] = held[across, pl.ds(start, share), :].astype(out.dtype)


def sum_kernel(indices, *refs):
    total = refs[0][indices[0]].astype(jnp.float32)
    for index, piece in zip(indices[1:], refs[1:]):
        total = total + piece[index].astype(jnp.float32)
    refs[-1][0] = total.astype(refs[-1].dtype)


def place_kernel(spots, *refs):
    pieces, half = refs[:-1], refs[-1]
    share = pieces[0].shape[1]
    place = lax.axis_index("ops")
    for (along, index), piece in zip(spots, pieces):
        start = pl.multiple_of((place ^ along) * share, share)
        half[index, pl.ds(start, share), :] = piece[0]


def left_kernel(left_own, left_other, own, other, out):
    for term in range(out.shape[0]):
        out[term] = left_times(left_own, left_other, term, own[0], other[0])


def second_kernel(
    sizes_ref, pairs_ref, weights_ref, left_own, left_other, right, products, own, other, *refs
):
    shares, held = refs[:-1], refs[-1]
    rows, columns = own.shape[1:]
    share = shares[0].shape[1]
    target = lax.axis_index("sec")
    core = lax.axis_index("rep")
    place = lax.axis_index("ops")
    total = None
    for term in range(right.shape[0]):
        weight = mixing_scalar(pairs_ref, weights_ref, term, target, target)
        combined = weight * products[term]
        for step in range(own.shape[0]):
            weight = mixing_scalar(pairs_ref, weights_ref, term, target, target ^ (step + 1))
            combined = combined + weight * left_times(
                left_own, left_other, term, own[step], other[step]
            )
        part = times_right(combined, right, term)
        total = part if total is None else total + part
    live = live_cells(sizes_ref, target, core * rows, rows, columns)
    held[...] = jnp.where(live, total, 0.0)
    for step, out in enumerate(shares):
        start = pl.multiple_of((place ^ step) * share, share)
        out[0] = held[pl.ds(start, share), :].astype(out.dtype)


def sums_kernel(wave_own, wave_other, sigma_own, sigma_other, out):
    step, columns = 16, wave_own.shape[1]
    sums = (jnp.zeros((step, columns), jnp.float32),) * 3
    for wave, sigma in ((wave_own, sigma_own), (wave_other, sigma_other)):

        def add_rows(block, carry):
            start = pl.multiple_of(block * step, step)
            w = wave[pl.ds(start, step), :].astype(jnp.float32)
            s = sigma[0, pl.ds(start, step), :].astype(jnp.float32)
            return (carry[0] + w * s, carry[1] + w * w, carry[2] + s * s)

        sums = lax.fori_loop(0, wave.shape[0] // step, add_rows, sums, unroll=2)
    for index, value in enumerate(sums):
        out[index] = jnp.broadcast_to(jnp.sum(value, keepdims=True), out.shape[1:])


def wave_kernel(sizes_ref, wave_own, sigma_own, *refs):
    sums, (second, factors) = refs[:-2], refs[-2:]
    rows, columns = wave_own.shape
    live_count = jnp.float32(0.0)
    for sector in range(sizes_ref.shape[0]):
        live_count = live_count + sizes_ref[sector, 0].astype(jnp.float32) * sizes_ref[
            sector, 1
        ].astype(jnp.float32)
    total = sums[0][...]
    for other in sums[1:]:
        total = total + other[...]
    correlation, norm_square, sigma_square = total[0], total[1], total[2]
    rayleigh = correlation / norm_square
    residual_square = (
        sigma_square - 2.0 * rayleigh * correlation + rayleigh * rayleigh * norm_square
    )
    residual_square = jnp.maximum(residual_square, 0.0)
    scale = 1.0 / jnp.sqrt(residual_square / live_count + epsilon)
    factors[0] = scale
    factors[1] = rayleigh * scale
    sigma_factor = jnp.broadcast_to(scale[:1, :1], (rows, columns))
    wave_factor = jnp.broadcast_to((rayleigh * scale)[:1, :1], (rows, columns))
    sigma = sigma_own[0].astype(jnp.float32)
    wave = wave_own[...].astype(jnp.float32)
    second[0] = (sigma_factor * sigma - wave_factor * wave).astype(second.dtype)


def join_kernel(factors, sigma_own, *refs):
    pieces, (out, held, sems) = refs[:-3], refs[-3:]
    _, share, columns = pieces[0].shape
    place = lax.axis_index("ops")
    scale = jnp.broadcast_to(factors[0][:1, :1], (share, columns))
    shift = jnp.broadcast_to(factors[1][:1, :1], (share, columns))
    copies = []
    for step, piece in enumerate(pieces):
        rows = pl.ds(pl.multiple_of((place ^ step) * share, share), share)
        moved = shift * sigma_own[0, rows, :].astype(jnp.float32)
        held[step] = scale * piece[0].astype(jnp.float32) - moved
        copies.append(pltpu.make_async_copy(held.at[step], out.at[0, rows], sems.at[step]))
        copies[-1].start()
    for copy in copies:
        copy.wait()


def partner(value, steps):
    steps = {axis: step for axis, step in steps.items() if step}
    if not steps:
        return value
    axes = tuple(steps)
    places = [()]
    for axis in axes:
        places = [place + (i,) for place in places for i in range(lax.axis_size(axis))]
    index = {place: i for i, place in enumerate(places)}
    pairs = [
        (index[tuple(i ^ steps[axis] for i, axis in zip(place, axes))], index[place])
        for place in places
    ]
    return lax.ppermute(value, axes, pairs)


def local(wavefunction, sector_sizes, left_blocks, right_blocks, sector_pairs, pair_weights):
    sectors = sector_sizes.shape[0]
    ops_count = lax.axis_size("ops")
    _, rows, columns = wavefunction.shape
    terms, side = left_blocks.shape[0], left_blocks.shape[1]
    share = rows // ops_count
    bf16, f32 = jnp.bfloat16, jnp.float32
    smem = pl.BlockSpec(memory_space=pltpu.SMEM)
    outside = pl.BlockSpec(memory_space=pltpu.HBM)
    inside = pl.BlockSpec(memory_space=pltpu.VMEM)

    def shape(*dims, dtype=bf16):
        return jax.ShapeDtypeStruct(dims, dtype)

    def call(kernel, name, out_shape, in_specs, *operands, scratch=(), vmem=16, out=inside):
        return pl.pallas_call(
            kernel,
            out_shape=out_shape,
            in_specs=list(in_specs) + [inside] * (len(operands) - len(in_specs)),
            out_specs=jax.tree.map(lambda _: out, out_shape),
            scratch_shapes=list(scratch),
            compiler_params=pltpu.CompilerParams(vmem_limit_bytes=vmem * mebibyte),
            name=name,
        )(*operands)

    def summed(name, *pieces, after=()):
        pieces = [piece if isinstance(piece, tuple) else (piece, 0) for piece in pieces]
        arrays, indices = zip(*pieces)
        return call(
            lambda *refs: sum_kernel(indices, *refs),
            name,
            shape(1, share, columns),
            [],
            *arrays,
            *after,
        )

    farthest_first = list(reversed(range(ops_count)))
    arrived = partner(wavefunction, {"rep": 1})
    left_own, left_other = call(
        load_kernel,
        "load_operators",
        [shape(terms, rows, rows), shape(terms, rows, side - rows)],
        [outside],
        left_blocks,
        scratch=[pltpu.SemaphoreType.DMA((2,))],
        vmem=51,
    )
    pairs = jnp.swapaxes(sector_pairs, 1, 2)
    scalars = (sector_sizes, pairs, pair_weights)

    far = ops_count - 1
    direct = [(along,) for along in farthest_first[1:-1]]
    spots = [((far, 0), across) for across in range(sectors)]
    spots += [(along, across) for along in direct for across in range(sectors)]
    right, wave_own, wave_other, *rest = call(
        lambda *refs: first_kernel(spots, *refs),
        "first_sigma_terms",
        [shape(*right_blocks.shape), shape(rows, columns), shape(rows, columns)]
        + [
            shape(len(along), share, columns, dtype=f32 if along == (far, 0) and across == 0 else bf16)
            for along, across in spots
        ],
        [smem] * 3 + [inside] * 2 + [outside],
        *scalars,
        left_own,
        left_other,
        right_blocks,
        wavefunction,
        arrived,
        scratch=[
            pltpu.VMEM((sectors, rows, columns), f32),
            pltpu.SemaphoreType.DMA((terms,)),
        ],
        vmem=49,
    )
    operators = scalars + (left_own, left_other, right)
    rest = dict(zip(spots, rest))
    met = [partner(rest[(far, 0), across], {"sec": across}) for across in range(sectors)]
    received = [partner(summed("sum_far_share", *met), {"ops": far})]
    received += [
        partner(rest[along, across], {"ops": along[0], "sec": across})
        for along in direct
        for across in range(sectors)
    ]
    first_share = summed("sum_first_sigma", *[(piece, 1) for piece in met], *received)
    along_ops = {along: partner(first_share, {"ops": along}) for along in farthest_first}
    sigma_own = call(
        lambda *refs: place_kernel([(along, 0) for along in farthest_first], *refs),
        "place_own_sector",
        shape(1, rows, columns),
        [],
        *along_ops.values(),
    )
    sigma_other = partner(sigma_own, {"rep": 1})
    spots = [(along, across) for along in farthest_first for across in range(1, sectors)]
    pieces = [
        partner(first_share, {"ops": along, "sec": across})
        if along < 2
        else partner(along_ops[along], {"sec": across})
        for along, across in spots
    ]
    across_own = call(
        lambda *refs: place_kernel([(along, across - 1) for along, across in spots], *refs),
        "place_other_sectors",
        shape(sectors - 1, rows, columns),
        [],
        *pieces,
    )
    across_other = partner(across_own, {"rep": 1})

    products = call(
        left_kernel,
        "left_products",
        shape(terms, rows, columns, dtype=f32),
        [],
        left_own,
        left_other,
        sigma_own,
        sigma_other,
    )
    shares = call(
        second_kernel,
        "second_sigma_terms",
        [shape(1, share, columns, dtype=f32)] + [shape(1, share, columns)] * (ops_count - 1),
        [smem] * 3,
        *operators,
        products,
        across_own,
        across_other,
        scratch=[pltpu.VMEM((rows, columns), f32)],
    )
    received = [partner(shares[step], {"ops": step}) for step in farthest_first[:-1]]
    sums = call(
        sums_kernel,
        "sums_for_rayleigh",
        shape(3, 8, 128, dtype=f32),
        [],
        wave_own,
        wave_other,
        sigma_own,
        sigma_other,
    )
    sums = [partner(sums, {"sec": step}) for step in range(sectors)]
    second_share = summed("sum_second_sigma", shares[0], *received, after=sums)
    second_wave, factors = call(
        wave_kernel,
        "second_wave",
        [shape(1, rows, columns), shape(2, 8, 128, dtype=f32)],
        [smem],
        sector_sizes,
        wave_own,
        sigma_own,
        *sums,
    )
    second_sigma = call(
        join_kernel,
        "join_second_sigma",
        shape(1, rows, columns, dtype=f32),
        [],
        factors,
        sigma_own,
        *[partner(second_share, {"ops": step}) for step in range(ops_count)],
        scratch=[
            pltpu.VMEM((ops_count, share, columns), f32),
            pltpu.SemaphoreType.DMA((ops_count,)),
        ],
        out=outside,
    )
    return (second_wave, second_sigma)


def solution(mesh):
    return jax.shard_map(
        local,
        mesh=mesh,
        in_specs=(
            P(("grp", "sec"), "rep", None),
            P("grp", None),
            P(("grp", "ops"), None, None),
            P(("grp", "ops"), None, None),
            P(("grp", "ops"), None, None),
            P(("grp", "ops"), None),
        ),
        out_specs=(P(("grp", "sec"), "rep", None), P(("grp", "sec"), "rep", None)),
        check_vma=False,
    )
```

```python
import jax
import jax.numpy as jnp
from jax import lax
from jax.experimental import pallas as pl
from jax.experimental.pallas import tpu as pltpu
from jax.sharding import PartitionSpec as P

epsilon = 1e-06
mebibyte = 1024 * 1024


def mixing_scalar(pairs_ref, weights_ref, term, target, source):
    value = jnp.float32(0.0)
    for pair in range(weights_ref.shape[1]):
        hit = (pairs_ref[term, 1, pair] == target) & (pairs_ref[term, 0, pair] == source)
        value = value + jnp.where(hit, weights_ref[term, pair], jnp.float32(0.0))
    return value


def live_cells(sizes_ref, sector, row_start, rows, columns):
    row = row_start + lax.broadcasted_iota(jnp.int32, (rows, columns), 0)
    column = lax.broadcasted_iota(jnp.int32, (rows, columns), 1)
    return (row < sizes_ref[sector, 0]) & (column < sizes_ref[sector, 1])


def masked(values, live):
    return jnp.where(live, values.astype(jnp.float32), 0.0).astype(values.dtype)


def left_times(left_own, left_other, term, own, other):
    return jnp.dot(left_own[term], own, preferred_element_type=jnp.float32) + jnp.dot(
        left_other[term], other, preferred_element_type=jnp.float32
    )


def times_right(values, right):
    return lax.dot_general(
        values.astype(jnp.bfloat16),
        right,
        (((1,), (1,)), ((), ())),
        preferred_element_type=jnp.float32,
    )


def load_kernel(left_ref, right_ref, left_own, left_other, right, sems):
    rows = left_own.shape[1]
    core = lax.axis_index("rep")
    copies = []
    for index, (half, place) in enumerate(((left_own, core), (left_other, core ^ 1))):
        mine = pl.ds(pl.multiple_of(core * rows, rows), rows)
        columns = pl.ds(pl.multiple_of(place * rows, rows), rows)
        copies.append(pltpu.make_async_copy(left_ref.at[:, mine, columns], half, sems.at[index]))
    loaded = right_ref.at[pl.ds(0, right.shape[0])]
    copies.append(pltpu.make_async_copy(loaded, right, sems.at[2]))
    for copy in copies:
        copy.start()
    for copy in copies:
        copy.wait()


def first_kernel(shares, *refs):
    sizes_ref, pairs_ref, weights_ref, left_own, left_other, loaded, right_ref = refs[:7]
    wave, arrived, right, own, other, *parts = refs[7:-2]
    held, sems = refs[-2:]
    early = loaded.shape[0]
    rows, columns = own.shape
    share = parts[0].shape[-2]
    copies = [
        pltpu.make_async_copy(right_ref.at[early + term], right.at[term], sems.at[term])
        for term in range(right.shape[0])
    ]
    for copy in copies:
        copy.start()
    sectors = held.shape[0]
    sector = lax.axis_index("sec")
    core = lax.axis_index("rep")
    place = lax.axis_index("ops")
    live = live_cells(sizes_ref, sector, core * rows, rows, columns)
    own[...] = masked(wave[0], live)
    live = live_cells(sizes_ref, sector, (core ^ 1) * rows, rows, columns)
    other[...] = masked(arrived[0], live)
    totals = [None] * sectors
    for term in range(left_own.shape[0]):
        product = left_times(left_own, left_other, term, own[...], other[...])
        if term < early:
            product = times_right(product, loaded[term])
        else:
            copies[term - early].wait()
            product = times_right(product, right[term - early])
        for step in range(sectors):
            weight = mixing_scalar(pairs_ref, weights_ref, term, sector ^ step, sector)
            part = weight * product
            totals[step] = part if totals[step] is None else totals[step] + part
    for step in range(sectors):
        live = live_cells(sizes_ref, sector ^ step, core * rows, rows, columns)
        held[step] = jnp.where(live, totals[step], 0.0)
    for (steps, across), out in zip(shares, parts):
        for index, along in enumerate(steps):
            start = pl.multiple_of((place ^ along) * share, share)
            out[index] = held[across, pl.ds(start, share), :].astype(out.dtype)


def sum_kernel(indices, handed, *refs):
    total = refs[0][indices[0]].astype(jnp.float32)
    for index, piece in zip(indices[1:], refs[1:]):
        total = total + piece[index].astype(jnp.float32)
    out, *copies = refs[len(refs) - handed - 1 :]
    out[0] = total.astype(out.dtype)
    for array, copy in zip(refs[len(indices) :], copies):
        copy[...] = array[...]


def place_kernel(spots, *refs):
    pieces, half = refs[:-1], refs[-1]
    share = pieces[0].shape[1]
    place = lax.axis_index("ops")
    for (along, index), piece in zip(spots, pieces):
        start = pl.multiple_of((place ^ along) * share, share)
        half[index, pl.ds(start, share), :] = piece[0]


def left_kernel(pairs_ref, weights_ref, left_own, left_other, own, other, across_own, out):
    target = lax.axis_index("sec")
    for term in range(out.shape[0]):
        weight = mixing_scalar(pairs_ref, weights_ref, term, target, target)
        total = weight * left_times(left_own, left_other, term, own[0], other[0])
        for step in range(across_own.shape[0]):
            weight = mixing_scalar(pairs_ref, weights_ref, term, target, target ^ (step + 1))
            total = total + weight * jnp.dot(
                left_own[term], across_own[step], preferred_element_type=jnp.float32
            )
        out[term] = total


def second_kernel(side, steps, *refs):
    sizes_ref, pairs_ref, weights_ref, left_other, loaded, right, products, across = refs[:8]
    shares, held = refs[8:-1], refs[-1]
    half, columns = held.shape
    share = shares[0].shape[1]
    target = lax.axis_index("sec")
    place = lax.axis_index("ops")
    count = lax.axis_size("ops") // 2
    first = pl.multiple_of(((place // count) ^ side) * half, half)
    mine = pl.ds(first, half)
    total = None
    for term in range(products.shape[0]):
        combined = products[term, mine, :]
        for step in range(across.shape[0]):
            weight = mixing_scalar(pairs_ref, weights_ref, term, target, target ^ (step + 1))
            combined = combined + weight * jnp.dot(
                left_other[term, mine, :], across[step], preferred_element_type=jnp.float32
            )
        early = loaded.shape[0]
        block = loaded[term] if term < early else right[term - early]
        part = times_right(combined, block)
        total = part if total is None else total + part
    row_start = lax.axis_index("rep") * (2 * half) + first
    live = live_cells(sizes_ref, target, row_start, half, columns)
    held[...] = jnp.where(live, total, 0.0)
    for step, out in zip(steps, shares):
        start = pl.multiple_of((place ^ step) % count * share, share)
        out[0] = held[pl.ds(start, share), :].astype(out.dtype)


def sums_kernel(wave_own, wave_other, sigma_own, sigma_other, out):
    step, columns = 16, wave_own.shape[1]
    sums = (jnp.zeros((step, columns), jnp.float32),) * 3
    for wave, sigma in ((wave_own, sigma_own), (wave_other, sigma_other)):

        def add_rows(block, carry):
            start = pl.multiple_of(block * step, step)
            w = wave[pl.ds(start, step), :].astype(jnp.float32)
            s = sigma[0, pl.ds(start, step), :].astype(jnp.float32)
            return (carry[0] + w * s, carry[1] + w * w, carry[2] + s * s)

        sums = lax.fori_loop(0, wave.shape[0] // step, add_rows, sums, unroll=2)
    for index, value in enumerate(sums):
        out[index] = jnp.broadcast_to(jnp.sum(value, keepdims=True), out.shape[1:])


def wave_kernel(sizes_ref, wave_own, sigma_own, *refs):
    sums, (second, factors) = refs[:-2], refs[-2:]
    rows, columns = wave_own.shape
    live_count = jnp.float32(0.0)
    for sector in range(sizes_ref.shape[0]):
        live_count = live_count + sizes_ref[sector, 0].astype(jnp.float32) * sizes_ref[
            sector, 1
        ].astype(jnp.float32)
    total = sums[0][...]
    for other in sums[1:]:
        total = total + other[...]
    correlation, norm_square, sigma_square = total[0], total[1], total[2]
    rayleigh = correlation / norm_square
    residual_square = (
        sigma_square - 2.0 * rayleigh * correlation + rayleigh * rayleigh * norm_square
    )
    residual_square = jnp.maximum(residual_square, 0.0)
    scale = 1.0 / jnp.sqrt(residual_square / live_count + epsilon)
    factors[0] = scale
    factors[1] = rayleigh * scale
    sigma_factor = jnp.broadcast_to(scale[:1, :1], (rows, columns))
    wave_factor = jnp.broadcast_to((rayleigh * scale)[:1, :1], (rows, columns))
    sigma = sigma_own[0].astype(jnp.float32)
    wave = wave_own[...].astype(jnp.float32)
    second[0] = (sigma_factor * sigma - wave_factor * wave).astype(second.dtype)


def join_kernel(factors, sigma_own, *refs):
    pieces, (out, held, sems) = refs[:-3], refs[-3:]
    _, share, columns = pieces[0].shape
    place = lax.axis_index("ops")
    scale = jnp.broadcast_to(factors[0][:1, :1], (share, columns))
    shift = jnp.broadcast_to(factors[1][:1, :1], (share, columns))
    copies = []
    for step, piece in zip(reversed(range(len(pieces))), pieces):
        rows = pl.ds(pl.multiple_of((place ^ step) * share, share), share)
        moved = shift * sigma_own[0, rows, :].astype(jnp.float32)
        held[step] = scale * piece[0].astype(jnp.float32) - moved
        copies.append(pltpu.make_async_copy(held.at[step], out.at[0, rows], sems.at[step]))
        copies[-1].start()
    for copy in copies:
        copy.wait()


def partner(value, steps):
    steps = {axis: step for axis, step in steps.items() if step}
    if not steps:
        return value
    axes = tuple(steps)
    places = [()]
    for axis in axes:
        places = [place + (i,) for place in places for i in range(lax.axis_size(axis))]
    index = {place: i for i, place in enumerate(places)}
    pairs = [
        (index[tuple(i ^ steps[axis] for i, axis in zip(place, axes))], index[place])
        for place in places
    ]
    return lax.ppermute(value, axes, pairs)


def local(wavefunction, sector_sizes, left_blocks, right_blocks, sector_pairs, pair_weights):
    sectors = sector_sizes.shape[0]
    ops_count = lax.axis_size("ops")
    _, rows, columns = wavefunction.shape
    terms, side = left_blocks.shape[0], left_blocks.shape[1]
    share = rows // ops_count
    bf16, f32 = jnp.bfloat16, jnp.float32
    smem = pl.BlockSpec(memory_space=pltpu.SMEM)
    outside = pl.BlockSpec(memory_space=pltpu.HBM)
    inside = pl.BlockSpec(memory_space=pltpu.VMEM)

    def shape(*dims, dtype=bf16):
        return jax.ShapeDtypeStruct(dims, dtype)

    def call(kernel, name, out_shape, in_specs, *operands, scratch=(), vmem=16, out=inside):
        return pl.pallas_call(
            kernel,
            out_shape=out_shape,
            in_specs=list(in_specs) + [inside] * (len(operands) - len(in_specs)),
            out_specs=jax.tree.map(lambda _: out, out_shape),
            scratch_shapes=list(scratch),
            compiler_params=pltpu.CompilerParams(vmem_limit_bytes=vmem * mebibyte),
            name=name,
        )(*operands)

    def summed(name, *pieces, after=(), handed=()):
        pieces = [piece if isinstance(piece, tuple) else (piece, 0) for piece in pieces]
        arrays, indices = zip(*pieces)
        sums = call(
            lambda *refs: sum_kernel(indices, len(handed), *refs),
            name,
            [shape(1, share, columns)] * (1 + len(handed)),
            [],
            *arrays,
            *handed,
            *after,
        )
        return sums if handed else sums[0]

    farthest_first = list(reversed(range(ops_count)))
    arrived = partner(wavefunction, {"rep": 1})
    early = terms // 2
    left_own, left_other, loaded = call(
        load_kernel,
        "load_operators",
        [
            shape(terms, rows, rows),
            shape(terms, rows, side - rows),
            shape(early, *right_blocks.shape[1:]),
        ],
        [outside] * 2,
        left_blocks,
        right_blocks,
        scratch=[pltpu.SemaphoreType.DMA((3,))],
        vmem=51,
    )
    pairs = jnp.swapaxes(sector_pairs, 1, 2)
    scalars = (sector_sizes, pairs, pair_weights)

    far = ops_count - 1
    direct = [(along,) for along in farthest_first[1:-1]]
    spots = [((far, 0), across) for across in range(sectors)]
    spots += [(along, across) for along in direct for across in range(sectors)]
    right, wave_own, wave_other, *rest = call(
        lambda *refs: first_kernel(spots, *refs),
        "first_sigma_terms",
        [shape(terms - early, *right_blocks.shape[1:]), shape(rows, columns), shape(rows, columns)]
        + [
            shape(len(along), share, columns, dtype=f32 if along == (far, 0) and across == 0 else bf16)
            for along, across in spots
        ],
        [smem] * 3 + [inside] * 3 + [outside],
        *scalars,
        left_own,
        left_other,
        loaded,
        right_blocks,
        wavefunction,
        arrived,
        scratch=[
            pltpu.VMEM((sectors, rows, columns), f32),
            pltpu.SemaphoreType.DMA((terms - early,)),
        ],
        vmem=49,
    )
    rest = dict(zip(spots, rest))
    met = [partner(rest[(far, 0), across], {"sec": across}) for across in range(sectors)]
    diagonal = [((1,), across) for across in range(1, sectors)]
    far_sum, *handed = summed("sum_far_share", *met, handed=[rest[spot] for spot in diagonal])
    rest.update(zip(diagonal, handed))
    received = [partner(far_sum, {"ops": far})]
    received += [
        partner(rest[along, across], {"ops": along[0], "sec": across})
        for along in direct
        for across in range(sectors)
    ]
    first_share = summed("sum_first_sigma", *[(piece, 1) for piece in met], *received)
    along_ops = {along: partner(first_share, {"ops": along}) for along in farthest_first}
    sigma_own = call(
        lambda *refs: place_kernel([(along, 0) for along in farthest_first], *refs),
        "place_own_sector",
        shape(1, rows, columns),
        [],
        *along_ops.values(),
    )
    sigma_other = partner(sigma_own, {"rep": 1})
    spots = [(along, across) for along in farthest_first for across in range(1, sectors)]
    pieces = [
        partner(first_share, {"ops": along, "sec": across})
        if along < 2
        else partner(along_ops[along], {"sec": across})
        for along, across in spots
    ]
    across_own = call(
        lambda *refs: place_kernel([(along, across - 1) for along, across in spots], *refs),
        "place_other_sectors",
        shape(sectors - 1, rows, columns),
        [],
        *pieces,
    )
    across_other = partner(across_own, {"rep": 1})

    products = call(
        left_kernel,
        "left_products",
        shape(terms, rows, columns, dtype=f32),
        [smem] * 2,
        *scalars[1:],
        left_own,
        left_other,
        sigma_own,
        sigma_other,
        across_own,
    )
    shares = []
    for side, steps in ((1, farthest_first[: ops_count // 2]), (0, farthest_first[ops_count // 2 :])):
        shares += call(
            lambda *refs, side=side, steps=steps: second_kernel(side, steps, *refs),
            "second_sigma_far" if side else "second_sigma_near",
            [shape(1, share, columns, dtype=bf16 if step else f32) for step in steps],
            [smem] * 3,
            *scalars,
            left_other,
            loaded,
            right,
            products,
            across_other,
            scratch=[pltpu.VMEM((rows // 2, columns), f32)],
        )
    shares = dict(zip(farthest_first, shares))
    received = [partner(shares[step], {"ops": step}) for step in farthest_first[:-1]]
    sums = call(
        sums_kernel,
        "sums_for_rayleigh",
        shape(3, 8, 128, dtype=f32),
        [],
        wave_own,
        wave_other,
        sigma_own,
        sigma_other,
    )
    sums = [partner(sums, {"sec": step}) for step in range(sectors)]
    second_share = summed("sum_second_sigma", shares[0], *received, after=sums)
    second_wave, factors = call(
        wave_kernel,
        "second_wave",
        [shape(1, rows, columns), shape(2, 8, 128, dtype=f32)],
        [smem],
        sector_sizes,
        wave_own,
        sigma_own,
        *sums,
    )
    second_sigma = call(
        join_kernel,
        "join_second_sigma",
        shape(1, rows, columns, dtype=f32),
        [],
        factors,
        sigma_own,
        *[partner(second_share, {"ops": step}) for step in farthest_first],
        scratch=[
            pltpu.VMEM((ops_count, share, columns), f32),
            pltpu.SemaphoreType.DMA((ops_count,)),
        ],
        out=outside,
    )
    return (second_wave, second_sigma)


def solution(mesh):
    return jax.shard_map(
        local,
        mesh=mesh,
        in_specs=(
            P(("grp", "sec"), "rep", None),
            P("grp", None),
            P(("grp", "ops"), None, None),
            P(("grp", "ops"), None, None),
            P(("grp", "ops"), None, None),
            P(("grp", "ops"), None),
        ),
        out_specs=(P(("grp", "sec"), "rep", None), P(("grp", "sec"), "rep", None)),
        check_vma=False,
    )
```

```python
import jax
import jax.numpy as jnp
from jax import lax
from jax.experimental import pallas as pl
from jax.experimental.pallas import tpu as pltpu
from jax.sharding import PartitionSpec as P

epsilon = 1e-06
mebibyte = 1024 * 1024


def mixing_scalar(pairs_ref, weights_ref, term, target, source):
    value = jnp.float32(0.0)
    for pair in range(weights_ref.shape[1]):
        hit = (pairs_ref[term, 1, pair] == target) & (pairs_ref[term, 0, pair] == source)
        value = value + jnp.where(hit, weights_ref[term, pair], jnp.float32(0.0))
    return value


def live_cells(sizes_ref, sector, row_start, rows, columns):
    row = row_start + lax.broadcasted_iota(jnp.int32, (rows, columns), 0)
    column = lax.broadcasted_iota(jnp.int32, (rows, columns), 1)
    return (row < sizes_ref[sector, 0]) & (column < sizes_ref[sector, 1])


def masked(values, live):
    return jnp.where(live, values.astype(jnp.float32), 0.0).astype(values.dtype)


def left_times(left_own, left_other, own, other):
    terms, rows, depth = left_own.shape
    product = jnp.dot(
        left_own[...].reshape(terms * rows, depth), own, preferred_element_type=jnp.float32
    ) + jnp.dot(
        left_other[...].reshape(terms * rows, depth), other, preferred_element_type=jnp.float32
    )
    return product.reshape(terms, rows, -1)


def times_right(values, right, term):
    return lax.dot_general(
        values.astype(jnp.bfloat16),
        right[term],
        (((1,), (1,)), ((), ())),
        preferred_element_type=jnp.float32,
    )


def load_kernel(left_ref, right_ref, left_own, left_other, right, sems):
    rows = left_own.shape[1]
    core = lax.axis_index("rep")
    copies = []
    for index, (half, place) in enumerate(((left_own, core), (left_other, core ^ 1))):
        mine = pl.ds(pl.multiple_of(core * rows, rows), rows)
        columns = pl.ds(pl.multiple_of(place * rows, rows), rows)
        copies.append(pltpu.make_async_copy(left_ref.at[:, mine, columns], half, sems.at[index]))
    copies.append(pltpu.make_async_copy(right_ref, right, sems.at[2]))
    for copy in copies:
        copy.start()
    for copy in copies:
        copy.wait()


def first_kernel(shares, *refs):
    sizes_ref, pairs_ref, weights_ref, left_own, left_other, right, wave, arrived = refs[:8]
    own, other, *parts = refs[8:-1]
    held = refs[-1]
    rows, columns = own.shape
    share = parts[0].shape[-2]
    sectors = held.shape[0]
    sector = lax.axis_index("sec")
    core = lax.axis_index("rep")
    place = lax.axis_index("ops")
    live = live_cells(sizes_ref, sector, core * rows, rows, columns)
    own[...] = masked(wave[0], live)
    live = live_cells(sizes_ref, sector, (core ^ 1) * rows, rows, columns)
    other[...] = masked(arrived[0], live)
    totals = [None] * sectors
    products = left_times(left_own, left_other, own[...], other[...])
    for term in range(right.shape[0]):
        product = times_right(products[term], right, term)
        for step in range(sectors):
            weight = mixing_scalar(pairs_ref, weights_ref, term, sector ^ step, sector)
            part = weight * product
            totals[step] = part if totals[step] is None else totals[step] + part
    for step in range(sectors):
        live = live_cells(sizes_ref, sector ^ step, core * rows, rows, columns)
        held[step] = jnp.where(live, totals[step], 0.0)
    for (steps, across), out in zip(shares, parts):
        for index, along in enumerate(steps):
            start = pl.multiple_of((place ^ along) * share, share)
            out[index] = held[across, pl.ds(start, share), :].astype(out.dtype)


def sum_kernel(indices, *refs):
    total = refs[0][indices[0]].astype(jnp.float32)
    for index, piece in zip(indices[1:], refs[1:]):
        total = total + piece[index].astype(jnp.float32)
    refs[-1][0] = total.astype(refs[-1].dtype)


def place_kernel(spots, *refs):
    pieces, half = refs[:-1], refs[-1]
    share = pieces[0].shape[1]
    place = lax.axis_index("ops")
    for (along, index), piece in zip(spots, pieces):
        start = pl.multiple_of((place ^ along) * share, share)
        half[index, pl.ds(start, share), :] = piece[0]


def left_kernel(left_own, left_other, own, other, out):
    out[...] = left_times(left_own, left_other, own[0], other[0])


def second_kernel(
    sizes_ref, pairs_ref, weights_ref, left_own, left_other, right, products, own, other, *refs
):
    shares, held = refs[:-1], refs[-1]
    rows, columns = own.shape[1:]
    share = shares[0].shape[1]
    target = lax.axis_index("sec")
    core = lax.axis_index("rep")
    place = lax.axis_index("ops")
    total = None
    across = [
        left_times(left_own, left_other, own[step], other[step]) for step in range(own.shape[0])
    ]
    for term in range(right.shape[0]):
        weight = mixing_scalar(pairs_ref, weights_ref, term, target, target)
        combined = weight * products[term]
        for step, part in enumerate(across, 1):
            weight = mixing_scalar(pairs_ref, weights_ref, term, target, target ^ step)
            combined = combined + weight * part[term]
        part = times_right(combined, right, term)
        total = part if total is None else total + part
    live = live_cells(sizes_ref, target, core * rows, rows, columns)
    held[...] = jnp.where(live, total, 0.0)
    for step, out in enumerate(shares):
        start = pl.multiple_of((place ^ step) * share, share)
        out[0] = held[pl.ds(start, share), :].astype(out.dtype)


def sums_kernel(wave_own, wave_other, sigma_own, sigma_other, out):
    step, columns = 16, wave_own.shape[1]
    sums = (jnp.zeros((step, columns), jnp.float32),) * 3
    for wave, sigma in ((wave_own, sigma_own), (wave_other, sigma_other)):

        def add_rows(block, carry):
            start = pl.multiple_of(block * step, step)
            w = wave[pl.ds(start, step), :].astype(jnp.float32)
            s = sigma[0, pl.ds(start, step), :].astype(jnp.float32)
            return (carry[0] + w * s, carry[1] + w * w, carry[2] + s * s)

        sums = lax.fori_loop(0, wave.shape[0] // step, add_rows, sums, unroll=2)
    for index, value in enumerate(sums):
        out[index] = jnp.broadcast_to(jnp.sum(value, keepdims=True), out.shape[1:])


def wave_kernel(sizes_ref, wave_own, sigma_own, *refs):
    sums, (second, factors) = refs[:-2], refs[-2:]
    rows, columns = wave_own.shape
    live_count = jnp.float32(0.0)
    for sector in range(sizes_ref.shape[0]):
        live_count = live_count + sizes_ref[sector, 0].astype(jnp.float32) * sizes_ref[
            sector, 1
        ].astype(jnp.float32)
    total = sums[0][...]
    for other in sums[1:]:
        total = total + other[...]
    correlation, norm_square, sigma_square = total[0], total[1], total[2]
    rayleigh = correlation / norm_square
    residual_square = (
        sigma_square - 2.0 * rayleigh * correlation + rayleigh * rayleigh * norm_square
    )
    residual_square = jnp.maximum(residual_square, 0.0)
    scale = 1.0 / jnp.sqrt(residual_square / live_count + epsilon)
    factors[0] = scale
    factors[1] = rayleigh * scale
    sigma_factor = jnp.broadcast_to(scale[:1, :1], (rows, columns))
    wave_factor = jnp.broadcast_to((rayleigh * scale)[:1, :1], (rows, columns))
    sigma = sigma_own[0].astype(jnp.float32)
    wave = wave_own[...].astype(jnp.float32)
    second[0] = (sigma_factor * sigma - wave_factor * wave).astype(second.dtype)


def join_kernel(factors, sigma_own, *refs):
    pieces, (out, held, sems) = refs[:-3], refs[-3:]
    _, share, columns = pieces[0].shape
    place = lax.axis_index("ops")
    scale = jnp.broadcast_to(factors[0][:1, :1], (share, columns))
    shift = jnp.broadcast_to(factors[1][:1, :1], (share, columns))
    copies = []
    for step, piece in enumerate(pieces):
        rows = pl.ds(pl.multiple_of((place ^ step) * share, share), share)
        moved = shift * sigma_own[0, rows, :].astype(jnp.float32)
        held[step] = scale * piece[0].astype(jnp.float32) - moved
        copies.append(pltpu.make_async_copy(held.at[step], out.at[0, rows], sems.at[step]))
        copies[-1].start()
    for copy in copies:
        copy.wait()


def partner(value, steps):
    steps = {axis: step for axis, step in steps.items() if step}
    if not steps:
        return value
    axes = tuple(steps)
    places = [()]
    for axis in axes:
        places = [place + (i,) for place in places for i in range(lax.axis_size(axis))]
    index = {place: i for i, place in enumerate(places)}
    pairs = [
        (index[tuple(i ^ steps[axis] for i, axis in zip(place, axes))], index[place])
        for place in places
    ]
    return lax.ppermute(value, axes, pairs)


def local(wavefunction, sector_sizes, left_blocks, right_blocks, sector_pairs, pair_weights):
    sectors = sector_sizes.shape[0]
    ops_count = lax.axis_size("ops")
    _, rows, columns = wavefunction.shape
    terms, side = left_blocks.shape[0], left_blocks.shape[1]
    share = rows // ops_count
    bf16, f32 = jnp.bfloat16, jnp.float32
    smem = pl.BlockSpec(memory_space=pltpu.SMEM)
    outside = pl.BlockSpec(memory_space=pltpu.HBM)
    inside = pl.BlockSpec(memory_space=pltpu.VMEM)

    def shape(*dims, dtype=bf16):
        return jax.ShapeDtypeStruct(dims, dtype)

    def call(kernel, name, out_shape, in_specs, *operands, scratch=(), vmem=16, out=inside):
        return pl.pallas_call(
            kernel,
            out_shape=out_shape,
            in_specs=list(in_specs) + [inside] * (len(operands) - len(in_specs)),
            out_specs=jax.tree.map(lambda _: out, out_shape),
            scratch_shapes=list(scratch),
            compiler_params=pltpu.CompilerParams(vmem_limit_bytes=vmem * mebibyte),
            name=name,
        )(*operands)

    def summed(name, *pieces, after=()):
        pieces = [piece if isinstance(piece, tuple) else (piece, 0) for piece in pieces]
        arrays, indices = zip(*pieces)
        return call(
            lambda *refs: sum_kernel(indices, *refs),
            name,
            shape(1, share, columns),
            [],
            *arrays,
            *after,
        )

    farthest_first = list(reversed(range(ops_count)))
    arrived = partner(wavefunction, {"rep": 1})
    left_own, left_other, right = call(
        load_kernel,
        "load_operators",
        [
            shape(terms, rows, rows),
            shape(terms, rows, side - rows),
            shape(*right_blocks.shape),
        ],
        [outside] * 2,
        left_blocks,
        right_blocks,
        scratch=[pltpu.SemaphoreType.DMA((3,))],
        vmem=49,
    )
    pairs = jnp.swapaxes(sector_pairs, 1, 2)
    operators = (sector_sizes, pairs, pair_weights, left_own, left_other, right)

    far = ops_count - 1
    direct = [(along,) for along in farthest_first[1:-1]]
    spots = [((far, 0), across) for across in range(sectors)]
    spots += [(along, across) for along in direct for across in range(sectors)]
    wave_own, wave_other, *rest = call(
        lambda *refs: first_kernel(spots, *refs),
        "first_sigma_terms",
        [shape(rows, columns)] * 2
        + [
            shape(len(along), share, columns, dtype=f32 if along == (far, 0) and across == 0 else bf16)
            for along, across in spots
        ],
        [smem] * 3,
        *operators,
        wavefunction,
        arrived,
        scratch=[pltpu.VMEM((sectors, rows, columns), f32)],
    )
    rest = dict(zip(spots, rest))
    met = [partner(rest[(far, 0), across], {"sec": across}) for across in range(sectors)]
    received = [partner(summed("sum_far_share", *met), {"ops": far})]
    received += [
        partner(rest[along, across], {"ops": along[0], "sec": across})
        for along in direct
        for across in range(sectors)
    ]
    first_share = summed("sum_first_sigma", *[(piece, 1) for piece in met], *received)
    along_ops = {along: partner(first_share, {"ops": along}) for along in farthest_first}
    sigma_own = call(
        lambda *refs: place_kernel([(along, 0) for along in farthest_first], *refs),
        "place_own_sector",
        shape(1, rows, columns),
        [],
        *along_ops.values(),
    )
    sigma_other = partner(sigma_own, {"rep": 1})
    spots = [(along, across) for along in farthest_first for across in range(1, sectors)]
    pieces = [
        partner(first_share, {"ops": along, "sec": across})
        if along < 2
        else partner(along_ops[along], {"sec": across})
        for along, across in spots
    ]
    across_own = call(
        lambda *refs: place_kernel([(along, across - 1) for along, across in spots], *refs),
        "place_other_sectors",
        shape(sectors - 1, rows, columns),
        [],
        *pieces,
    )
    across_other = partner(across_own, {"rep": 1})

    products = call(
        left_kernel,
        "left_products",
        shape(terms, rows, columns, dtype=f32),
        [],
        left_own,
        left_other,
        sigma_own,
        sigma_other,
    )
    shares = call(
        second_kernel,
        "second_sigma_terms",
        [shape(1, share, columns, dtype=f32)] + [shape(1, share, columns)] * (ops_count - 1),
        [smem] * 3,
        *operators,
        products,
        across_own,
        across_other,
        scratch=[pltpu.VMEM((rows, columns), f32)],
    )
    received = [partner(shares[step], {"ops": step}) for step in farthest_first[:-1]]
    sums = call(
        sums_kernel,
        "sums_for_rayleigh",
        shape(3, 8, 128, dtype=f32),
        [],
        wave_own,
        wave_other,
        sigma_own,
        sigma_other,
    )
    sums = [partner(sums, {"sec": step}) for step in range(sectors)]
    second_share = summed("sum_second_sigma", shares[0], *received, after=sums)
    second_wave, factors = call(
        wave_kernel,
        "second_wave",
        [shape(1, rows, columns), shape(2, 8, 128, dtype=f32)],
        [smem],
        sector_sizes,
        wave_own,
        sigma_own,
        *sums,
    )
    second_sigma = call(
        join_kernel,
        "join_second_sigma",
        shape(1, rows, columns, dtype=f32),
        [],
        factors,
        sigma_own,
        *[partner(second_share, {"ops": step}) for step in range(ops_count)],
        scratch=[
            pltpu.VMEM((ops_count, share, columns), f32),
            pltpu.SemaphoreType.DMA((ops_count,)),
        ],
        out=outside,
    )
    return (second_wave, second_sigma)


def solution(mesh):
    return jax.shard_map(
        local,
        mesh=mesh,
        in_specs=(
            P(("grp", "sec"), "rep", None),
            P("grp", None),
            P(("grp", "ops"), None, None),
            P(("grp", "ops"), None, None),
            P(("grp", "ops"), None, None),
            P(("grp", "ops"), None),
        ),
        out_specs=(P(("grp", "sec"), "rep", None), P(("grp", "sec"), "rep", None)),
        check_vma=False,
    )
```

```python
import jax
import jax.numpy as jnp
from jax import lax
from jax.experimental import pallas as pl
from jax.experimental.pallas import tpu as pltpu
from jax.sharding import PartitionSpec as P

epsilon = 1e-06
mebibyte = 1024 * 1024


def mixing_scalar(pairs_ref, weights_ref, term, target, source):
    value = jnp.float32(0.0)
    for pair in range(weights_ref.shape[1]):
        hit = (pairs_ref[term, 1, pair] == target) & (pairs_ref[term, 0, pair] == source)
        value = value + jnp.where(hit, weights_ref[term, pair], jnp.float32(0.0))
    return value


def live_cells(sizes_ref, sector, row_start, rows, columns):
    row = row_start + lax.broadcasted_iota(jnp.int32, (rows, columns), 0)
    column = lax.broadcasted_iota(jnp.int32, (rows, columns), 1)
    return (row < sizes_ref[sector, 0]) & (column < sizes_ref[sector, 1])


def masked(values, live):
    return jnp.where(live, values.astype(jnp.float32), 0.0).astype(values.dtype)


def left_times(lefts, blocks):
    total = None
    for left, block in zip(lefts, blocks):
        terms, rows, depth = left.shape
        stacked = left[...].reshape(terms * rows, depth)
        part = jnp.dot(stacked, block, preferred_element_type=jnp.float32)
        total = part if total is None else total + part
    return total.reshape(terms, rows, -1)


def times_right(values, right, term):
    return lax.dot_general(
        values.astype(jnp.bfloat16),
        right[term],
        (((1,), (1,)), ((), ())),
        preferred_element_type=jnp.float32,
    )


def load_kernel(left_ref, right_ref, left_own, left_other, right, sems):
    rows = left_own.shape[1]
    core = lax.axis_index("rep")
    copies = []
    for index, (half, place) in enumerate(((left_own, core), (left_other, core ^ 1))):
        mine = pl.ds(pl.multiple_of(core * rows, rows), rows)
        columns = pl.ds(pl.multiple_of(place * rows, rows), rows)
        copies.append(pltpu.make_async_copy(left_ref.at[:, mine, columns], half, sems.at[index]))
    copies.append(pltpu.make_async_copy(right_ref, right, sems.at[2]))
    for copy in copies:
        copy.start()
    for copy in copies:
        copy.wait()


def first_kernel(shares, *refs):
    sizes_ref, pairs_ref, weights_ref, left_own, left_other, right, wave, arrived = refs[:8]
    own, other, *parts = refs[8:-1]
    held = refs[-1]
    rows, columns = own.shape
    share = parts[0].shape[-2]
    sectors = held.shape[0]
    sector = lax.axis_index("sec")
    core = lax.axis_index("rep")
    place = lax.axis_index("ops")
    live = live_cells(sizes_ref, sector, core * rows, rows, columns)
    own[...] = masked(wave[0], live)
    live = live_cells(sizes_ref, sector, (core ^ 1) * rows, rows, columns)
    other[...] = masked(arrived[0], live)
    totals = [None] * sectors
    products = left_times((left_own, left_other), (own[...], other[...]))
    for term in range(right.shape[0]):
        product = times_right(products[term], right, term)
        for step in range(sectors):
            weight = mixing_scalar(pairs_ref, weights_ref, term, sector ^ step, sector)
            part = weight * product
            totals[step] = part if totals[step] is None else totals[step] + part
    for step in range(sectors):
        live = live_cells(sizes_ref, sector ^ step, core * rows, rows, columns)
        held[step] = jnp.where(live, totals[step], 0.0)
    for (steps, across), out in zip(shares, parts):
        for index, along in enumerate(steps):
            start = pl.multiple_of((place ^ along) * share, share)
            out[index] = held[across, pl.ds(start, share), :].astype(out.dtype)


def sum_kernel(indices, *refs):
    total = refs[0][indices[0]].astype(jnp.float32)
    for index, piece in zip(indices[1:], refs[1:]):
        total = total + piece[index].astype(jnp.float32)
    refs[-1][0] = total.astype(refs[-1].dtype)


def place_kernel(spots, *refs):
    pieces, half = refs[:-1], refs[-1]
    share = pieces[0].shape[1]
    place = lax.axis_index("ops")
    for (along, index), piece in zip(spots, pieces):
        start = pl.multiple_of((place ^ along) * share, share)
        half[index, pl.ds(start, share), :] = piece[0]


def left_kernel(left_own, left_other, own, other, across_own, out, across_out):
    out[...] = left_times((left_own, left_other), (own[0], other[0]))
    for step in range(across_own.shape[0]):
        across_out[step] = left_times((left_own,), (across_own[step],))


def second_kernel(
    sizes_ref, pairs_ref, weights_ref, left_other, right, products, across_products, other, *refs
):
    shares, held = refs[:-1], refs[-1]
    rows, columns = products.shape[1:]
    share = shares[0].shape[1]
    target = lax.axis_index("sec")
    core = lax.axis_index("rep")
    place = lax.axis_index("ops")
    total = None
    across = [left_times((left_other,), (other[step],)) for step in range(other.shape[0])]
    for term in range(right.shape[0]):
        weight = mixing_scalar(pairs_ref, weights_ref, term, target, target)
        combined = weight * products[term]
        for step, part in enumerate(across, 1):
            weight = mixing_scalar(pairs_ref, weights_ref, term, target, target ^ step)
            combined = combined + weight * (across_products[step - 1, term] + part[term])
        part = times_right(combined, right, term)
        total = part if total is None else total + part
    live = live_cells(sizes_ref, target, core * rows, rows, columns)
    held[...] = jnp.where(live, total, 0.0)
    for step, out in enumerate(shares):
        start = pl.multiple_of((place ^ step) * share, share)
        out[0] = held[pl.ds(start, share), :].astype(out.dtype)


def sums_kernel(wave_own, wave_other, sigma_own, sigma_other, out):
    step, columns = 16, wave_own.shape[1]
    sums = (jnp.zeros((step, columns), jnp.float32),) * 3
    for wave, sigma in ((wave_own, sigma_own), (wave_other, sigma_other)):

        def add_rows(block, carry):
            start = pl.multiple_of(block * step, step)
            w = wave[pl.ds(start, step), :].astype(jnp.float32)
            s = sigma[0, pl.ds(start, step), :].astype(jnp.float32)
            return (carry[0] + w * s, carry[1] + w * w, carry[2] + s * s)

        sums = lax.fori_loop(0, wave.shape[0] // step, add_rows, sums, unroll=2)
    for index, value in enumerate(sums):
        out[index] = jnp.broadcast_to(jnp.sum(value, keepdims=True), out.shape[1:])


def wave_kernel(sizes_ref, wave_own, sigma_own, *refs):
    sums, (second, factors) = refs[:-2], refs[-2:]
    rows, columns = wave_own.shape
    live_count = jnp.float32(0.0)
    for sector in range(sizes_ref.shape[0]):
        live_count = live_count + sizes_ref[sector, 0].astype(jnp.float32) * sizes_ref[
            sector, 1
        ].astype(jnp.float32)
    total = sums[0][...]
    for other in sums[1:]:
        total = total + other[...]
    correlation, norm_square, sigma_square = total[0], total[1], total[2]
    rayleigh = correlation / norm_square
    residual_square = (
        sigma_square - 2.0 * rayleigh * correlation + rayleigh * rayleigh * norm_square
    )
    residual_square = jnp.maximum(residual_square, 0.0)
    scale = 1.0 / jnp.sqrt(residual_square / live_count + epsilon)
    factors[0] = scale
    factors[1] = rayleigh * scale
    sigma_factor = jnp.broadcast_to(scale[:1, :1], (rows, columns))
    wave_factor = jnp.broadcast_to((rayleigh * scale)[:1, :1], (rows, columns))
    sigma = sigma_own[0].astype(jnp.float32)
    wave = wave_own[...].astype(jnp.float32)
    second[0] = (sigma_factor * sigma - wave_factor * wave).astype(second.dtype)


def join_kernel(factors, sigma_own, *refs):
    pieces, (out, held, sems) = refs[:-3], refs[-3:]
    _, share, columns = pieces[0].shape
    place = lax.axis_index("ops")
    scale = jnp.broadcast_to(factors[0][:1, :1], (share, columns))
    shift = jnp.broadcast_to(factors[1][:1, :1], (share, columns))
    copies = []
    for step, piece in zip(reversed(range(len(pieces))), pieces):
        rows = pl.ds(pl.multiple_of((place ^ step) * share, share), share)
        moved = shift * sigma_own[0, rows, :].astype(jnp.float32)
        held[step] = scale * piece[0].astype(jnp.float32) - moved
        copies.append(pltpu.make_async_copy(held.at[step], out.at[0, rows], sems.at[step]))
        copies[-1].start()
    for copy in copies:
        copy.wait()


def partner(value, steps):
    steps = {axis: step for axis, step in steps.items() if step}
    if not steps:
        return value
    axes = tuple(steps)
    places = [()]
    for axis in axes:
        places = [place + (i,) for place in places for i in range(lax.axis_size(axis))]
    index = {place: i for i, place in enumerate(places)}
    pairs = [
        (index[tuple(i ^ steps[axis] for i, axis in zip(place, axes))], index[place])
        for place in places
    ]
    return lax.ppermute(value, axes, pairs)


def local(wavefunction, sector_sizes, left_blocks, right_blocks, sector_pairs, pair_weights):
    sectors = sector_sizes.shape[0]
    ops_count = lax.axis_size("ops")
    _, rows, columns = wavefunction.shape
    terms, side = left_blocks.shape[0], left_blocks.shape[1]
    share = rows // ops_count
    bf16, f32 = jnp.bfloat16, jnp.float32
    smem = pl.BlockSpec(memory_space=pltpu.SMEM)
    outside = pl.BlockSpec(memory_space=pltpu.HBM)
    inside = pl.BlockSpec(memory_space=pltpu.VMEM)

    def shape(*dims, dtype=bf16):
        return jax.ShapeDtypeStruct(dims, dtype)

    def call(kernel, name, out_shape, in_specs, *operands, scratch=(), vmem=16, out=inside):
        return pl.pallas_call(
            kernel,
            out_shape=out_shape,
            in_specs=list(in_specs) + [inside] * (len(operands) - len(in_specs)),
            out_specs=jax.tree.map(lambda _: out, out_shape),
            scratch_shapes=list(scratch),
            compiler_params=pltpu.CompilerParams(vmem_limit_bytes=vmem * mebibyte),
            name=name,
        )(*operands)

    def summed(name, *pieces, after=()):
        pieces = [piece if isinstance(piece, tuple) else (piece, 0) for piece in pieces]
        arrays, indices = zip(*pieces)
        return call(
            lambda *refs: sum_kernel(indices, *refs),
            name,
            shape(1, share, columns),
            [],
            *arrays,
            *after,
        )

    farthest_first = list(reversed(range(ops_count)))
    arrived = partner(wavefunction, {"rep": 1})
    left_own, left_other, right = call(
        load_kernel,
        "load_operators",
        [
            shape(terms, rows, rows),
            shape(terms, rows, side - rows),
            shape(*right_blocks.shape),
        ],
        [outside] * 2,
        left_blocks,
        right_blocks,
        scratch=[pltpu.SemaphoreType.DMA((3,))],
        vmem=49,
    )
    pairs = jnp.swapaxes(sector_pairs, 1, 2)
    scalars = (sector_sizes, pairs, pair_weights)

    far = ops_count - 1
    direct = [(along,) for along in farthest_first[1:-1]]
    spots = [((far, 0), across) for across in range(sectors)]
    spots += [(along, across) for along in direct for across in range(sectors)]
    wave_own, wave_other, *rest = call(
        lambda *refs: first_kernel(spots, *refs),
        "first_sigma_terms",
        [shape(rows, columns)] * 2
        + [
            shape(len(along), share, columns, dtype=f32 if along == (far, 0) and across == 0 else bf16)
            for along, across in spots
        ],
        [smem] * 3,
        *scalars,
        left_own,
        left_other,
        right,
        wavefunction,
        arrived,
        scratch=[pltpu.VMEM((sectors, rows, columns), f32)],
    )
    rest = dict(zip(spots, rest))
    met = [partner(rest[(far, 0), across], {"sec": across}) for across in range(sectors)]
    received = [partner(summed("sum_far_share", *met), {"ops": far})]
    received += [
        partner(rest[along, across], {"ops": along[0], "sec": across})
        for along in direct
        for across in range(sectors)
    ]
    first_share = summed("sum_first_sigma", *[(piece, 1) for piece in met], *received)
    crossed = {
        along: partner(first_share, {"ops": along}) for along in farthest_first if along % 2 == 0
    }
    pieces = {
        (along, across): partner(crossed[along // 2 * 2], {"ops": along % 2, "sec": across})
        for along in farthest_first
        for across in range(sectors)
    }
    sigma_own = call(
        lambda *refs: place_kernel([(along, 0) for along in farthest_first], *refs),
        "place_own_sector",
        shape(1, rows, columns),
        [],
        *[pieces[along, 0] for along in farthest_first],
        *[pieces[spot] for spot in pieces if spot[0] < 2 and spot[1]],
    )
    sigma_other = partner(sigma_own, {"rep": 1})
    spots = [(along, across) for along in farthest_first for across in range(1, sectors)]
    across_own = call(
        lambda *refs: place_kernel([(along, across - 1) for along, across in spots], *refs),
        "place_other_sectors",
        shape(sectors - 1, rows, columns),
        [],
        *[pieces[spot] for spot in spots],
    )
    across_other = partner(across_own, {"rep": 1})

    products, across_products = call(
        left_kernel,
        "left_products",
        [
            shape(terms, rows, columns, dtype=f32),
            shape(sectors - 1, terms, rows, columns, dtype=f32),
        ],
        [],
        left_own,
        left_other,
        sigma_own,
        sigma_other,
        across_own,
    )
    shares = call(
        second_kernel,
        "second_sigma_terms",
        [shape(1, share, columns, dtype=f32)] + [shape(1, share, columns)] * (ops_count - 1),
        [smem] * 3,
        *scalars,
        left_other,
        right,
        products,
        across_products,
        across_other,
        scratch=[pltpu.VMEM((rows, columns), f32)],
    )
    received = [partner(shares[step], {"ops": step}) for step in farthest_first[:-1]]
    sums = call(
        sums_kernel,
        "sums_for_rayleigh",
        shape(3, 8, 128, dtype=f32),
        [],
        wave_own,
        wave_other,
        sigma_own,
        sigma_other,
    )
    sums = [partner(sums, {"sec": step}) for step in range(sectors)]
    second_share = summed("sum_second_sigma", shares[0], *received, after=sums)
    second_wave, factors = call(
        wave_kernel,
        "second_wave",
        [shape(1, rows, columns), shape(2, 8, 128, dtype=f32)],
        [smem],
        sector_sizes,
        wave_own,
        sigma_own,
        *sums,
    )
    second_sigma = call(
        join_kernel,
        "join_second_sigma",
        shape(1, rows, columns, dtype=f32),
        [],
        factors,
        sigma_own,
        *[partner(second_share, {"ops": step}) for step in farthest_first],
        scratch=[
            pltpu.VMEM((ops_count, share, columns), f32),
            pltpu.SemaphoreType.DMA((ops_count,)),
        ],
        out=outside,
    )
    return (second_wave, second_sigma)


def solution(mesh):
    return jax.shard_map(
        local,
        mesh=mesh,
        in_specs=(
            P(("grp", "sec"), "rep", None),
            P("grp", None),
            P(("grp", "ops"), None, None),
            P(("grp", "ops"), None, None),
            P(("grp", "ops"), None, None),
            P(("grp", "ops"), None),
        ),
        out_specs=(P(("grp", "sec"), "rep", None), P(("grp", "sec"), "rep", None)),
        check_vma=False,
    )
```

```python
import jax
import jax.numpy as jnp
from jax import lax
from jax.experimental import pallas as pl
from jax.experimental.pallas import tpu as pltpu
from jax.sharding import PartitionSpec as P

epsilon = 1e-06
mebibyte = 1024 * 1024


def mixing_scalar(pairs_ref, weights_ref, term, target, source):
    value = jnp.float32(0.0)
    for pair in range(weights_ref.shape[1]):
        hit = (pairs_ref[term, 1, pair] == target) & (pairs_ref[term, 0, pair] == source)
        value = value + jnp.where(hit, weights_ref[term, pair], jnp.float32(0.0))
    return value


def live_cells(sizes_ref, sector, row_start, rows, columns):
    row = row_start + lax.broadcasted_iota(jnp.int32, (rows, columns), 0)
    column = lax.broadcasted_iota(jnp.int32, (rows, columns), 1)
    return (row < sizes_ref[sector, 0]) & (column < sizes_ref[sector, 1])


def masked(values, live):
    return jnp.where(live, values.astype(jnp.float32), 0.0).astype(values.dtype)


def left_times(lefts, blocks):
    total = None
    for left, block in zip(lefts, blocks):
        terms, rows, depth = left.shape
        stacked = left[...].reshape(terms * rows, depth)
        part = jnp.dot(stacked, block, preferred_element_type=jnp.float32)
        total = part if total is None else total + part
    return total.reshape(terms, rows, -1)


def times_right(values, right, term):
    return lax.dot_general(
        values.astype(jnp.bfloat16),
        right[term],
        (((1,), (1,)), ((), ())),
        preferred_element_type=jnp.float32,
    )


def load_kernel(left_ref, right_ref, left_own, left_other, right, sems):
    rows = left_own.shape[1]
    core = lax.axis_index("rep")
    copies = []
    for index, (half, place) in enumerate(((left_own, core), (left_other, core ^ 1))):
        mine = pl.ds(pl.multiple_of(core * rows, rows), rows)
        columns = pl.ds(pl.multiple_of(place * rows, rows), rows)
        copies.append(pltpu.make_async_copy(left_ref.at[:, mine, columns], half, sems.at[index]))
    copies.append(pltpu.make_async_copy(right_ref, right, sems.at[2]))
    for copy in copies:
        copy.start()
    for copy in copies:
        copy.wait()


def first_kernel(shares, *refs):
    sizes_ref, pairs_ref, weights_ref, left_own, left_other, right, wave, arrived = refs[:8]
    own, other, *parts = refs[8:-1]
    held = refs[-1]
    rows, columns = own.shape
    share = parts[0].shape[-2]
    sectors = held.shape[0]
    sector = lax.axis_index("sec")
    core = lax.axis_index("rep")
    place = lax.axis_index("ops")
    live = live_cells(sizes_ref, sector, core * rows, rows, columns)
    own[...] = masked(wave[0], live)
    live = live_cells(sizes_ref, sector, (core ^ 1) * rows, rows, columns)
    other[...] = masked(arrived[0], live)
    products = left_times((left_own, left_other), (own[...], other[...]))
    total = None
    for term in range(right.shape[0]):
        scaled = [
            mixing_scalar(pairs_ref, weights_ref, term, sector ^ step, sector) * products[term]
            for step in range(sectors)
        ]
        stacked = jnp.concatenate([part.astype(jnp.bfloat16) for part in scaled], axis=0)
        part = times_right(stacked, right, term)
        total = part if total is None else total + part
    for step in range(sectors):
        live = live_cells(sizes_ref, sector ^ step, core * rows, rows, columns)
        held[step] = jnp.where(live, total[step * rows : (step + 1) * rows], 0.0)
    for (steps, across), out in zip(shares, parts):
        for index, along in enumerate(steps):
            start = pl.multiple_of((place ^ along) * share, share)
            out[index] = held[across, pl.ds(start, share), :].astype(out.dtype)


def sum_kernel(indices, *refs):
    total = refs[0][indices[0]].astype(jnp.float32)
    for index, piece in zip(indices[1:], refs[1:]):
        total = total + piece[index].astype(jnp.float32)
    refs[-1][0] = total.astype(refs[-1].dtype)


def place_kernel(spots, *refs):
    pieces, half = refs[:-1], refs[-1]
    share = pieces[0].shape[1]
    place = lax.axis_index("ops")
    for (along, index), piece in zip(spots, pieces):
        start = pl.multiple_of((place ^ along) * share, share)
        half[index, pl.ds(start, share), :] = piece[0]


def left_kernel(left_own, left_other, own, other, across_own, out, across_out):
    out[...] = left_times((left_own, left_other), (own[0], other[0]))
    for step in range(across_own.shape[0]):
        across_out[step] = left_times((left_own,), (across_own[step],))


def tables_kernel(sizes_ref, pairs_ref, weights_ref, _, mixing, live):
    target = lax.axis_index("sec")
    for term in range(mixing.shape[0]):
        for step in range(mixing.shape[1]):
            weight = mixing_scalar(pairs_ref, weights_ref, term, target, target ^ step)
            mixing[term, step] = jnp.full(mixing.shape[2:], weight, jnp.float32)
    rows, columns = live.shape
    cells = live_cells(sizes_ref, target, lax.axis_index("rep") * rows, rows, columns)
    live[...] = jnp.where(cells, 1.0, 0.0)


def second_kernel(mixing, live, left_other, right, products, across_products, other, *refs):
    shares, held = refs[:-1], refs[-1]
    rows, columns = products.shape[1:]
    share = shares[0].shape[1]
    place = lax.axis_index("ops")
    total = None
    across = [left_times((left_other,), (other[step],)) for step in range(other.shape[0])]
    for term in range(right.shape[0]):
        weights = [
            jnp.broadcast_to(mixing[term, step][:1, :1], (rows, columns))
            for step in range(len(across) + 1)
        ]
        combined = weights[0] * products[term]
        for step, part in enumerate(across):
            combined = combined + weights[step + 1] * (across_products[step, term] + part[term])
        part = times_right(combined, right, term)
        total = part if total is None else total + part
    held[...] = total * live[...]
    for step, out in enumerate(shares):
        start = pl.multiple_of((place ^ step) * share, share)
        out[0] = held[pl.ds(start, share), :].astype(out.dtype)


def sums_kernel(wave_own, wave_other, sigma_own, sigma_other, out):
    step, columns = 16, wave_own.shape[1]
    sums = (jnp.zeros((step, columns), jnp.float32),) * 3
    for wave, sigma in ((wave_own, sigma_own), (wave_other, sigma_other)):

        def add_rows(block, carry):
            start = pl.multiple_of(block * step, step)
            w = wave[pl.ds(start, step), :].astype(jnp.float32)
            s = sigma[0, pl.ds(start, step), :].astype(jnp.float32)
            return (carry[0] + w * s, carry[1] + w * w, carry[2] + s * s)

        sums = lax.fori_loop(0, wave.shape[0] // step, add_rows, sums, unroll=2)
    for index, value in enumerate(sums):
        out[index] = jnp.broadcast_to(jnp.sum(value, keepdims=True), out.shape[1:])


def wave_kernel(sizes_ref, wave_own, sigma_own, *refs):
    sums, (second, factors) = refs[:-2], refs[-2:]
    rows, columns = wave_own.shape
    live_count = jnp.float32(0.0)
    for sector in range(sizes_ref.shape[0]):
        live_count = live_count + sizes_ref[sector, 0].astype(jnp.float32) * sizes_ref[
            sector, 1
        ].astype(jnp.float32)
    total = sums[0][...]
    for other in sums[1:]:
        total = total + other[...]
    correlation, norm_square, sigma_square = total[0], total[1], total[2]
    rayleigh = correlation / norm_square
    residual_square = (
        sigma_square - 2.0 * rayleigh * correlation + rayleigh * rayleigh * norm_square
    )
    residual_square = jnp.maximum(residual_square, 0.0)
    scale = 1.0 / jnp.sqrt(residual_square / live_count + epsilon)
    factors[0] = scale
    factors[1] = rayleigh * scale
    sigma_factor = jnp.broadcast_to(scale[:1, :1], (rows, columns))
    wave_factor = jnp.broadcast_to((rayleigh * scale)[:1, :1], (rows, columns))
    sigma = sigma_own[0].astype(jnp.float32)
    wave = wave_own[...].astype(jnp.float32)
    second[0] = (sigma_factor * sigma - wave_factor * wave).astype(second.dtype)


def join_kernel(factors, sigma_own, *refs):
    pieces, (out, held, sems) = refs[:-3], refs[-3:]
    _, share, columns = pieces[0].shape
    place = lax.axis_index("ops")
    scale = jnp.broadcast_to(factors[0][:1, :1], (share, columns))
    shift = jnp.broadcast_to(factors[1][:1, :1], (share, columns))
    copies = []
    for step, piece in zip(reversed(range(len(pieces))), pieces):
        rows = pl.ds(pl.multiple_of((place ^ step) * share, share), share)
        moved = shift * sigma_own[0, rows, :].astype(jnp.float32)
        held[step] = scale * piece[0].astype(jnp.float32) - moved
        copies.append(pltpu.make_async_copy(held.at[step], out.at[0, rows], sems.at[step]))
        copies[-1].start()
    for copy in copies:
        copy.wait()


def partner(value, steps):
    steps = {axis: step for axis, step in steps.items() if step}
    if not steps:
        return value
    axes = tuple(steps)
    places = [()]
    for axis in axes:
        places = [place + (i,) for place in places for i in range(lax.axis_size(axis))]
    index = {place: i for i, place in enumerate(places)}
    pairs = [
        (index[tuple(i ^ steps[axis] for i, axis in zip(place, axes))], index[place])
        for place in places
    ]
    return lax.ppermute(value, axes, pairs)


def local(wavefunction, sector_sizes, left_blocks, right_blocks, sector_pairs, pair_weights):
    sectors = sector_sizes.shape[0]
    ops_count = lax.axis_size("ops")
    _, rows, columns = wavefunction.shape
    terms, side = left_blocks.shape[0], left_blocks.shape[1]
    share = rows // ops_count
    bf16, f32 = jnp.bfloat16, jnp.float32
    smem = pl.BlockSpec(memory_space=pltpu.SMEM)
    outside = pl.BlockSpec(memory_space=pltpu.HBM)
    inside = pl.BlockSpec(memory_space=pltpu.VMEM)

    def shape(*dims, dtype=bf16):
        return jax.ShapeDtypeStruct(dims, dtype)

    def call(kernel, name, out_shape, in_specs, *operands, scratch=(), vmem=16, out=inside):
        return pl.pallas_call(
            kernel,
            out_shape=out_shape,
            in_specs=list(in_specs) + [inside] * (len(operands) - len(in_specs)),
            out_specs=jax.tree.map(lambda _: out, out_shape),
            scratch_shapes=list(scratch),
            compiler_params=pltpu.CompilerParams(vmem_limit_bytes=vmem * mebibyte),
            name=name,
        )(*operands)

    def summed(name, *pieces, after=()):
        pieces = [piece if isinstance(piece, tuple) else (piece, 0) for piece in pieces]
        arrays, indices = zip(*pieces)
        return call(
            lambda *refs: sum_kernel(indices, *refs),
            name,
            shape(1, share, columns),
            [],
            *arrays,
            *after,
        )

    farthest_first = list(reversed(range(ops_count)))
    arrived = partner(wavefunction, {"rep": 1})
    left_own, left_other, right = call(
        load_kernel,
        "load_operators",
        [
            shape(terms, rows, rows),
            shape(terms, rows, side - rows),
            shape(*right_blocks.shape),
        ],
        [outside] * 2,
        left_blocks,
        right_blocks,
        scratch=[pltpu.SemaphoreType.DMA((3,))],
        vmem=49,
    )
    pairs = jnp.swapaxes(sector_pairs, 1, 2)
    scalars = (sector_sizes, pairs, pair_weights)

    far = ops_count - 1
    direct = [(along,) for along in farthest_first[1:-1]]
    spots = [((far, 0), across) for across in range(sectors)]
    spots += [(along, across) for along in direct for across in range(sectors)]
    wave_own, wave_other, *rest = call(
        lambda *refs: first_kernel(spots, *refs),
        "first_sigma_terms",
        [shape(rows, columns)] * 2
        + [
            shape(len(along), share, columns, dtype=f32 if along == (far, 0) and across == 0 else bf16)
            for along, across in spots
        ],
        [smem] * 3,
        *scalars,
        left_own,
        left_other,
        right,
        wavefunction,
        arrived,
        scratch=[pltpu.VMEM((sectors, rows, columns), f32)],
    )
    rest = dict(zip(spots, rest))
    mixing, live = call(
        tables_kernel,
        "tables_for_second_sigma",
        [shape(terms, sectors, 8, 128, dtype=f32), shape(rows, columns, dtype=f32)],
        [smem] * 3,
        *scalars,
        wave_own,
    )
    met = [partner(rest[(far, 0), across], {"sec": across}) for across in range(sectors)]
    received = [partner(summed("sum_far_share", *met), {"ops": far})]
    received += [
        partner(rest[along, across], {"ops": along[0], "sec": across})
        for along in direct
        for across in range(sectors)
    ]
    first_share = summed("sum_first_sigma", *[(piece, 1) for piece in met], *received, after=(mixing,))
    along_ops = {along: partner(first_share, {"ops": along}) for along in farthest_first}
    sigma_own = call(
        lambda *refs: place_kernel([(along, 0) for along in farthest_first], *refs),
        "place_own_sector",
        shape(1, rows, columns),
        [],
        *along_ops.values(),
    )
    sigma_other = partner(sigma_own, {"rep": 1})
    spots = [(along, across) for along in farthest_first for across in range(1, sectors)]
    pieces = [
        partner(first_share, {"ops": along, "sec": across})
        if along < 2
        else partner(along_ops[along], {"sec": across})
        for along, across in spots
    ]
    across_own = call(
        lambda *refs: place_kernel([(along, across - 1) for along, across in spots], *refs),
        "place_other_sectors",
        shape(sectors - 1, rows, columns),
        [],
        *pieces,
    )
    across_other = partner(across_own, {"rep": 1})

    products, across_products = call(
        left_kernel,
        "left_products",
        [
            shape(terms, rows, columns, dtype=f32),
            shape(sectors - 1, terms, rows, columns, dtype=f32),
        ],
        [],
        left_own,
        left_other,
        sigma_own,
        sigma_other,
        across_own,
    )
    shares = call(
        second_kernel,
        "second_sigma_terms",
        [shape(1, share, columns, dtype=f32)] + [shape(1, share, columns)] * (ops_count - 1),
        [],
        mixing,
        live,
        left_other,
        right,
        products,
        across_products,
        across_other,
        scratch=[pltpu.VMEM((rows, columns), f32)],
    )
    received = [partner(shares[step], {"ops": step}) for step in farthest_first[:-1]]
    sums = call(
        sums_kernel,
        "sums_for_rayleigh",
        shape(3, 8, 128, dtype=f32),
        [],
        wave_own,
        wave_other,
        sigma_own,
        sigma_other,
    )
    sums = [partner(sums, {"sec": step}) for step in range(sectors)]
    second_share = summed("sum_second_sigma", shares[0], *received, after=sums)
    second_wave, factors = call(
        wave_kernel,
        "second_wave",
        [shape(1, rows, columns), shape(2, 8, 128, dtype=f32)],
        [smem],
        sector_sizes,
        wave_own,
        sigma_own,
        *sums,
    )
    second_sigma = call(
        join_kernel,
        "join_second_sigma",
        shape(1, rows, columns, dtype=f32),
        [],
        factors,
        sigma_own,
        *[partner(second_share, {"ops": step}) for step in farthest_first],
        scratch=[
            pltpu.VMEM((ops_count, share, columns), f32),
            pltpu.SemaphoreType.DMA((ops_count,)),
        ],
        out=outside,
    )
    return (second_wave, second_sigma)


def solution(mesh):
    return jax.shard_map(
        local,
        mesh=mesh,
        in_specs=(
            P(("grp", "sec"), "rep", None),
            P("grp", None),
            P(("grp", "ops"), None, None),
            P(("grp", "ops"), None, None),
            P(("grp", "ops"), None, None),
            P(("grp", "ops"), None),
        ),
        out_specs=(P(("grp", "sec"), "rep", None), P(("grp", "sec"), "rep", None)),
        check_vma=False,
    )
```

```python
import jax
import jax.numpy as jnp
from jax import lax
from jax.experimental import pallas as pl
from jax.experimental.pallas import tpu as pltpu
from jax.sharding import PartitionSpec as P

epsilon = 1e-06
mebibyte = 1024 * 1024


def mixing_scalar(pairs_ref, weights_ref, term, target, source):
    value = jnp.float32(0.0)
    for pair in range(weights_ref.shape[1]):
        hit = (pairs_ref[term, 1, pair] == target) & (pairs_ref[term, 0, pair] == source)
        value = value + jnp.where(hit, weights_ref[term, pair], jnp.float32(0.0))
    return value


def live_cells(sizes_ref, sector, row_start, rows, columns):
    row = row_start + lax.broadcasted_iota(jnp.int32, (rows, columns), 0)
    column = lax.broadcasted_iota(jnp.int32, (rows, columns), 1)
    return (row < sizes_ref[sector, 0]) & (column < sizes_ref[sector, 1])


def masked(values, live):
    return jnp.where(live, values.astype(jnp.float32), 0.0).astype(values.dtype)


def left_times(lefts, blocks):
    total = None
    for left, block in zip(lefts, blocks):
        terms, rows, depth = left.shape
        stacked = left[...].reshape(terms * rows, depth)
        part = jnp.dot(stacked, block, preferred_element_type=jnp.float32)
        total = part if total is None else total + part
    return total.reshape(terms, rows, -1)


def times_right(values, right, term):
    return lax.dot_general(
        values.astype(jnp.bfloat16),
        right[term],
        (((1,), (1,)), ((), ())),
        preferred_element_type=jnp.float32,
    )


def load_kernel(left_ref, left_own, left_other, sems):
    rows = left_own.shape[1]
    core = lax.axis_index("rep")
    copies = []
    for index, (half, place) in enumerate(((left_own, core), (left_other, core ^ 1))):
        mine = pl.ds(pl.multiple_of(core * rows, rows), rows)
        columns = pl.ds(pl.multiple_of(place * rows, rows), rows)
        copies.append(pltpu.make_async_copy(left_ref.at[:, mine, columns], half, sems.at[index]))
    for copy in copies:
        copy.start()
    for copy in copies:
        copy.wait()


def first_tables_kernel(sizes_ref, pairs_ref, weights_ref, wave, _, own, mixing, live):
    rows, columns = own.shape
    sector = lax.axis_index("sec")
    start = lax.axis_index("rep") * rows
    for term in range(mixing.shape[0]):
        for step in range(mixing.shape[1]):
            weight = mixing_scalar(pairs_ref, weights_ref, term, sector ^ step, sector)
            mixing[term, step] = jnp.full(mixing.shape[2:], weight, jnp.float32)
    for step in range(live.shape[0] - 1):
        cells = live_cells(sizes_ref, sector ^ step, start, rows, columns)
        live[step] = jnp.where(cells, 1.0, 0.0)
    own[...] = (wave[0].astype(jnp.float32) * live[0]).astype(own.dtype)
    start = (lax.axis_index("rep") ^ 1) * rows
    cells = live_cells(sizes_ref, sector, start, rows, columns)
    live[live.shape[0] - 1] = jnp.where(cells, 1.0, 0.0)


def first_kernel(shares, *refs):
    mixing, live, left_own, left_other, right, own, arrived = refs[:7]
    other, *parts = refs[7:-1]
    held = refs[-1]
    rows, columns = own.shape
    share = parts[0].shape[-2]
    sectors = held.shape[0]
    place = lax.axis_index("ops")
    other[...] = (arrived[0].astype(jnp.float32) * live[sectors]).astype(other.dtype)
    products = left_times((left_own, left_other), (own[...], other[...]))
    totals = [None] * sectors
    for term in range(right.shape[0]):
        product = times_right(products[term], right, term)
        for step in range(sectors):
            part = jnp.broadcast_to(mixing[term, step][:1, :1], (rows, columns)) * product
            totals[step] = part if totals[step] is None else totals[step] + part
    for step in range(sectors):
        held[step] = totals[step] * live[step]
    for (steps, across), out in zip(shares, parts):
        for index, along in enumerate(steps):
            start = pl.multiple_of((place ^ along) * share, share)
            out[index] = held[across, pl.ds(start, share), :].astype(out.dtype)


def sum_kernel(indices, *refs):
    total = refs[0][indices[0]].astype(jnp.float32)
    for index, piece in zip(indices[1:], refs[1:]):
        total = total + piece[index].astype(jnp.float32)
    refs[-1][0] = total.astype(refs[-1].dtype)


def place_kernel(spots, *refs):
    pieces, half = refs[:-1], refs[-1]
    share = pieces[0].shape[1]
    place = lax.axis_index("ops")
    for (along, index), piece in zip(spots, pieces):
        start = pl.multiple_of((place ^ along) * share, share)
        half[index, pl.ds(start, share), :] = piece[0]


def left_kernel(left_own, left_other, own, other, across_own, out, across_out):
    out[...] = left_times((left_own, left_other), (own[0], other[0]))
    for step in range(across_own.shape[0]):
        across_out[step] = left_times((left_own,), (across_own[step],))


def tables_kernel(sizes_ref, pairs_ref, weights_ref, _, mixing, live):
    target = lax.axis_index("sec")
    for term in range(mixing.shape[0]):
        for step in range(mixing.shape[1]):
            weight = mixing_scalar(pairs_ref, weights_ref, term, target, target ^ step)
            mixing[term, step] = jnp.full(mixing.shape[2:], weight, jnp.float32)
    rows, columns = live.shape
    cells = live_cells(sizes_ref, target, lax.axis_index("rep") * rows, rows, columns)
    live[...] = jnp.where(cells, 1.0, 0.0)


def second_kernel(mixing, live, left_other, right, products, across_products, other, *refs):
    shares, held = refs[:-1], refs[-1]
    rows, columns = products.shape[1:]
    share = shares[0].shape[1]
    place = lax.axis_index("ops")
    total = None
    across = [left_times((left_other,), (other[step],)) for step in range(other.shape[0])]
    for term in range(right.shape[0]):
        weights = [
            jnp.broadcast_to(mixing[term, step][:1, :1], (rows, columns))
            for step in range(len(across) + 1)
        ]
        combined = weights[0] * products[term]
        for step, part in enumerate(across):
            combined = combined + weights[step + 1] * (across_products[step, term] + part[term])
        part = times_right(combined, right, term)
        total = part if total is None else total + part
    held[...] = total * live[...]
    for step, out in enumerate(shares):
        start = pl.multiple_of((place ^ step) * share, share)
        out[0] = held[pl.ds(start, share), :].astype(out.dtype)


def sums_kernel(wave_own, wave_other, sigma_own, sigma_other, out):
    step, columns = 16, wave_own.shape[1]
    sums = (jnp.zeros((step, columns), jnp.float32),) * 3
    for wave, sigma in ((wave_own, sigma_own), (wave_other, sigma_other)):

        def add_rows(block, carry):
            start = pl.multiple_of(block * step, step)
            w = wave[pl.ds(start, step), :].astype(jnp.float32)
            s = sigma[0, pl.ds(start, step), :].astype(jnp.float32)
            return (carry[0] + w * s, carry[1] + w * w, carry[2] + s * s)

        sums = lax.fori_loop(0, wave.shape[0] // step, add_rows, sums, unroll=2)
    for index, value in enumerate(sums):
        out[index] = jnp.broadcast_to(jnp.sum(value, keepdims=True), out.shape[1:])


def wave_kernel(sizes_ref, wave_own, sigma_own, *refs):
    sums, (second, factors) = refs[:-2], refs[-2:]
    rows, columns = wave_own.shape
    live_count = jnp.float32(0.0)
    for sector in range(sizes_ref.shape[0]):
        live_count = live_count + sizes_ref[sector, 0].astype(jnp.float32) * sizes_ref[
            sector, 1
        ].astype(jnp.float32)
    total = sums[0][...]
    for other in sums[1:]:
        total = total + other[...]
    correlation, norm_square, sigma_square = total[0], total[1], total[2]
    rayleigh = correlation / norm_square
    residual_square = (
        sigma_square - 2.0 * rayleigh * correlation + rayleigh * rayleigh * norm_square
    )
    residual_square = jnp.maximum(residual_square, 0.0)
    scale = 1.0 / jnp.sqrt(residual_square / live_count + epsilon)
    factors[0] = scale
    factors[1] = rayleigh * scale
    sigma_factor = jnp.broadcast_to(scale[:1, :1], (rows, columns))
    wave_factor = jnp.broadcast_to((rayleigh * scale)[:1, :1], (rows, columns))
    sigma = sigma_own[0].astype(jnp.float32)
    wave = wave_own[...].astype(jnp.float32)
    second[0] = (sigma_factor * sigma - wave_factor * wave).astype(second.dtype)


def join_kernel(factors, sigma_own, *refs):
    pieces, (out, held, sems) = refs[:-3], refs[-3:]
    _, share, columns = pieces[0].shape
    place = lax.axis_index("ops")
    scale = jnp.broadcast_to(factors[0][:1, :1], (share, columns))
    shift = jnp.broadcast_to(factors[1][:1, :1], (share, columns))
    copies = []
    for step, piece in zip(reversed(range(len(pieces))), pieces):
        rows = pl.ds(pl.multiple_of((place ^ step) * share, share), share)
        moved = shift * sigma_own[0, rows, :].astype(jnp.float32)
        held[step] = scale * piece[0].astype(jnp.float32) - moved
        copies.append(pltpu.make_async_copy(held.at[step], out.at[0, rows], sems.at[step]))
        copies[-1].start()
    for copy in copies:
        copy.wait()


def partner(value, steps):
    steps = {axis: step for axis, step in steps.items() if step}
    if not steps:
        return value
    axes = tuple(steps)
    places = [()]
    for axis in axes:
        places = [place + (i,) for place in places for i in range(lax.axis_size(axis))]
    index = {place: i for i, place in enumerate(places)}
    pairs = [
        (index[tuple(i ^ steps[axis] for i, axis in zip(place, axes))], index[place])
        for place in places
    ]
    return lax.ppermute(value, axes, pairs)


def local(wavefunction, sector_sizes, left_blocks, right_blocks, sector_pairs, pair_weights):
    sectors = sector_sizes.shape[0]
    ops_count = lax.axis_size("ops")
    _, rows, columns = wavefunction.shape
    terms, side = left_blocks.shape[0], left_blocks.shape[1]
    share = rows // ops_count
    bf16, f32 = jnp.bfloat16, jnp.float32
    smem = pl.BlockSpec(memory_space=pltpu.SMEM)
    outside = pl.BlockSpec(memory_space=pltpu.HBM)
    inside = pl.BlockSpec(memory_space=pltpu.VMEM)

    def shape(*dims, dtype=bf16):
        return jax.ShapeDtypeStruct(dims, dtype)

    def call(kernel, name, out_shape, in_specs, *operands, scratch=(), vmem=16, out=inside):
        return pl.pallas_call(
            kernel,
            out_shape=out_shape,
            in_specs=list(in_specs) + [inside] * (len(operands) - len(in_specs)),
            out_specs=jax.tree.map(lambda _: out, out_shape),
            scratch_shapes=list(scratch),
            compiler_params=pltpu.CompilerParams(vmem_limit_bytes=vmem * mebibyte),
            name=name,
        )(*operands)

    def summed(name, *pieces, after=()):
        pieces = [piece if isinstance(piece, tuple) else (piece, 0) for piece in pieces]
        arrays, indices = zip(*pieces)
        return call(
            lambda *refs: sum_kernel(indices, *refs),
            name,
            shape(1, share, columns),
            [],
            *arrays,
            *after,
        )

    farthest_first = list(reversed(range(ops_count)))
    arrived = partner(wavefunction, {"rep": 1})
    left_own, left_other = call(
        load_kernel,
        "load_operators",
        [shape(terms, rows, rows), shape(terms, rows, side - rows)],
        [outside],
        left_blocks,
        scratch=[pltpu.SemaphoreType.DMA((2,))],
        vmem=51,
    )
    right = right_blocks
    pairs = jnp.swapaxes(sector_pairs, 1, 2)
    scalars = (sector_sizes, pairs, pair_weights)

    far = ops_count - 1
    direct = [(along,) for along in farthest_first[1:-1]]
    spots = [((far, 0), across) for across in range(sectors)]
    spots += [(along, across) for along in direct for across in range(sectors)]
    wave_own, mixing, live = call(
        first_tables_kernel,
        "tables_for_first_sigma",
        [
            shape(rows, columns),
            shape(terms, sectors, 8, 128, dtype=f32),
            shape(sectors + 1, rows, columns, dtype=f32),
        ],
        [smem] * 3,
        *scalars,
        wavefunction,
        left_own,
    )
    wave_other, *rest = call(
        lambda *refs: first_kernel(spots, *refs),
        "first_sigma_terms",
        [shape(rows, columns)]
        + [
            shape(len(along), share, columns, dtype=f32 if along == (far, 0) and across == 0 else bf16)
            for along, across in spots
        ],
        [],
        mixing,
        live,
        left_own,
        left_other,
        right,
        wave_own,
        arrived,
        scratch=[pltpu.VMEM((sectors, rows, columns), f32)],
    )
    rest = dict(zip(spots, rest))
    mixing, live = call(
        tables_kernel,
        "tables_for_second_sigma",
        [shape(terms, sectors, 8, 128, dtype=f32), shape(rows, columns, dtype=f32)],
        [smem] * 3,
        *scalars,
        wave_other,
    )
    met = [partner(rest[(far, 0), across], {"sec": across}) for across in range(sectors)]
    received = [partner(summed("sum_far_share", *met), {"ops": far})]
    received += [
        partner(rest[along, across], {"ops": along[0], "sec": across})
        for along in direct
        for across in range(sectors)
    ]
    first_share = summed("sum_first_sigma", *[(piece, 1) for piece in met], *received, after=(mixing,))
    along_ops = {along: partner(first_share, {"ops": along}) for along in farthest_first}
    sigma_own = call(
        lambda *refs: place_kernel([(along, 0) for along in farthest_first], *refs),
        "place_own_sector",
        shape(1, rows, columns),
        [],
        *along_ops.values(),
    )
    sigma_other = partner(sigma_own, {"rep": 1})
    spots = [(along, across) for along in farthest_first for across in range(1, sectors)]
    pieces = [
        partner(first_share, {"ops": along, "sec": across})
        if along < 2
        else partner(along_ops[along], {"sec": across})
        for along, across in spots
    ]
    across_own = call(
        lambda *refs: place_kernel([(along, across - 1) for along, across in spots], *refs),
        "place_other_sectors",
        shape(sectors - 1, rows, columns),
        [],
        *pieces,
    )
    across_other = partner(across_own, {"rep": 1})

    products, across_products = call(
        left_kernel,
        "left_products",
        [
            shape(terms, rows, columns, dtype=f32),
            shape(sectors - 1, terms, rows, columns, dtype=f32),
        ],
        [],
        left_own,
        left_other,
        sigma_own,
        sigma_other,
        across_own,
    )
    shares = call(
        second_kernel,
        "second_sigma_terms",
        [shape(1, share, columns, dtype=f32)] + [shape(1, share, columns)] * (ops_count - 1),
        [],
        mixing,
        live,
        left_other,
        right,
        products,
        across_products,
        across_other,
        scratch=[pltpu.VMEM((rows, columns), f32)],
    )
    received = [partner(shares[step], {"ops": step}) for step in farthest_first[:-1]]
    sums = call(
        sums_kernel,
        "sums_for_rayleigh",
        shape(3, 8, 128, dtype=f32),
        [],
        wave_own,
        wave_other,
        sigma_own,
        sigma_other,
    )
    sums = [partner(sums, {"sec": step}) for step in range(sectors)]
    second_share = summed("sum_second_sigma", shares[0], *received, after=sums)
    second_wave, factors = call(
        wave_kernel,
        "second_wave",
        [shape(1, rows, columns), shape(2, 8, 128, dtype=f32)],
        [smem],
        sector_sizes,
        wave_own,
        sigma_own,
        *sums,
    )
    second_sigma = call(
        join_kernel,
        "join_second_sigma",
        shape(1, rows, columns, dtype=f32),
        [],
        factors,
        sigma_own,
        *[partner(second_share, {"ops": step}) for step in farthest_first],
        scratch=[
            pltpu.VMEM((ops_count, share, columns), f32),
            pltpu.SemaphoreType.DMA((ops_count,)),
        ],
        out=outside,
    )
    return (second_wave, second_sigma)


def solution(mesh):
    return jax.shard_map(
        local,
        mesh=mesh,
        in_specs=(
            P(("grp", "sec"), "rep", None),
            P("grp", None),
            P(("grp", "ops"), None, None),
            P(("grp", "ops"), None, None),
            P(("grp", "ops"), None, None),
            P(("grp", "ops"), None),
        ),
        out_specs=(P(("grp", "sec"), "rep", None), P(("grp", "sec"), "rep", None)),
        check_vma=False,
    )
```

```python
import jax
import jax.numpy as jnp
from jax import lax
from jax.experimental import pallas as pl
from jax.experimental.pallas import tpu as pltpu
from jax.sharding import PartitionSpec as P

epsilon = 1e-06
mebibyte = 1024 * 1024


def mixing_scalar(pairs_ref, weights_ref, term, target, source):
    value = jnp.float32(0.0)
    for pair in range(weights_ref.shape[1]):
        hit = (pairs_ref[term, 1, pair] == target) & (pairs_ref[term, 0, pair] == source)
        value = value + jnp.where(hit, weights_ref[term, pair], jnp.float32(0.0))
    return value


def live_cells(sizes_ref, sector, row_start, rows, columns):
    row = row_start + lax.broadcasted_iota(jnp.int32, (rows, columns), 0)
    column = lax.broadcasted_iota(jnp.int32, (rows, columns), 1)
    return (row < sizes_ref[sector, 0]) & (column < sizes_ref[sector, 1])


def masked(values, live):
    return jnp.where(live, values.astype(jnp.float32), 0.0).astype(values.dtype)


def left_times(lefts, blocks):
    total = None
    for left, block in zip(lefts, blocks):
        terms, rows, depth = left.shape
        stacked = left[...].reshape(terms * rows, depth)
        part = jnp.dot(stacked, block, preferred_element_type=jnp.float32)
        total = part if total is None else total + part
    return total.reshape(terms, rows, -1)


def times_right(values, right, term):
    return lax.dot_general(
        values.astype(jnp.bfloat16),
        right[term],
        (((1,), (1,)), ((), ())),
        preferred_element_type=jnp.float32,
    )


def load_kernel(left_ref, left_own, left_other, sems):
    rows = left_own.shape[1]
    core = lax.axis_index("rep")
    copies = []
    for index, (half, place) in enumerate(((left_own, core), (left_other, core ^ 1))):
        mine = pl.ds(pl.multiple_of(core * rows, rows), rows)
        columns = pl.ds(pl.multiple_of(place * rows, rows), rows)
        copies.append(pltpu.make_async_copy(left_ref.at[:, mine, columns], half, sems.at[index]))
    for copy in copies:
        copy.start()
    for copy in copies:
        copy.wait()


def first_tables_kernel(sizes_ref, pairs_ref, weights_ref, wave, _, own, mixing, live):
    rows, columns = own.shape
    sector = lax.axis_index("sec")
    start = lax.axis_index("rep") * rows
    for term in range(mixing.shape[0]):
        for step in range(mixing.shape[1]):
            weight = mixing_scalar(pairs_ref, weights_ref, term, sector ^ step, sector)
            mixing[term, step] = jnp.full(mixing.shape[2:], weight, jnp.float32)
    for step in range(live.shape[0] - 1):
        cells = live_cells(sizes_ref, sector ^ step, start, rows, columns)
        live[step] = jnp.where(cells, 1.0, 0.0)
    own[...] = (wave[0].astype(jnp.float32) * live[0]).astype(own.dtype)
    start = (lax.axis_index("rep") ^ 1) * rows
    cells = live_cells(sizes_ref, sector, start, rows, columns)
    live[live.shape[0] - 1] = jnp.where(cells, 1.0, 0.0)


def first_kernel(shares, *refs):
    mixing, live, left_own, left_other, right, own, arrived = refs[:7]
    other, *parts = refs[7:-1]
    held = refs[-1]
    rows, columns = own.shape
    share = parts[0].shape[-2]
    sectors = held.shape[0]
    place = lax.axis_index("ops")
    other[...] = (arrived[0].astype(jnp.float32) * live[sectors]).astype(other.dtype)
    products = left_times((left_own, left_other), (own[...], other[...]))
    totals = [None] * sectors
    for term in range(right.shape[0]):
        product = times_right(products[term], right, term)
        for step in range(sectors):
            part = jnp.broadcast_to(mixing[term, step][:1, :1], (rows, columns)) * product
            totals[step] = part if totals[step] is None else totals[step] + part
    for step in range(sectors):
        held[step] = totals[step] * live[step]
    for (steps, across), out in zip(shares, parts):
        for index, along in enumerate(steps):
            start = pl.multiple_of((place ^ along) * share, share)
            out[index] = held[across, pl.ds(start, share), :].astype(out.dtype)


def sum_kernel(indices, *refs):
    total = refs[0][indices[0]].astype(jnp.float32)
    for index, piece in zip(indices[1:], refs[1:]):
        total = total + piece[index].astype(jnp.float32)
    refs[-1][0] = total.astype(refs[-1].dtype)


def place_kernel(spots, *refs):
    pieces, half = refs[:-1], refs[-1]
    share = pieces[0].shape[1]
    place = lax.axis_index("ops")
    for (along, index), piece in zip(spots, pieces):
        start = pl.multiple_of((place ^ along) * share, share)
        half[index, pl.ds(start, share), :] = piece[0]


def left_kernel(left_own, left_other, own, other, across_own, out, across_out):
    out[...] = left_times((left_own, left_other), (own[0], other[0]))
    for step in range(across_own.shape[0]):
        across_out[step] = left_times((left_own,), (across_own[step],))


def tables_kernel(sizes_ref, pairs_ref, weights_ref, _, mixing, live):
    target = lax.axis_index("sec")
    for term in range(mixing.shape[0]):
        for step in range(mixing.shape[1]):
            weight = mixing_scalar(pairs_ref, weights_ref, term, target, target ^ step)
            mixing[term, step] = jnp.full(mixing.shape[2:], weight, jnp.float32)
    rows, columns = live.shape
    cells = live_cells(sizes_ref, target, lax.axis_index("rep") * rows, rows, columns)
    live[...] = jnp.where(cells, 1.0, 0.0)


def second_kernel(mixing, live, left_other, right, products, across_products, other, *refs):
    shares, held = refs[:-1], refs[-1]
    rows, columns = products.shape[1:]
    share = shares[0].shape[1]
    place = lax.axis_index("ops")
    total = None
    across = [left_times((left_other,), (other[step],)) for step in range(other.shape[0])]
    for term in range(right.shape[0]):
        weights = [
            jnp.broadcast_to(mixing[term, step][:1, :1], (rows, columns))
            for step in range(len(across) + 1)
        ]
        combined = weights[0] * products[term]
        for step, part in enumerate(across):
            combined = combined + weights[step + 1] * (across_products[step, term] + part[term])
        part = times_right(combined, right, term)
        total = part if total is None else total + part
    held[...] = total * live[...]
    for step, out in enumerate(shares):
        start = pl.multiple_of((place ^ step) * share, share)
        out[0] = held[pl.ds(start, share), :].astype(out.dtype)


def sums_kernel(wave_own, wave_other, sigma_own, sigma_other, out):
    step, columns = 16, wave_own.shape[1]
    sums = (jnp.zeros((step, columns), jnp.float32),) * 3
    for wave, sigma in ((wave_own, sigma_own), (wave_other, sigma_other)):

        def add_rows(block, carry):
            start = pl.multiple_of(block * step, step)
            w = wave[pl.ds(start, step), :].astype(jnp.float32)
            s = sigma[0, pl.ds(start, step), :].astype(jnp.float32)
            return (carry[0] + w * s, carry[1] + w * w, carry[2] + s * s)

        sums = lax.fori_loop(0, wave.shape[0] // step, add_rows, sums, unroll=2)
    for index, value in enumerate(sums):
        out[index] = jnp.broadcast_to(jnp.sum(value, keepdims=True), out.shape[1:])


def wave_kernel(sizes_ref, wave_own, sigma_own, *refs):
    sums, (second, factors) = refs[:-2], refs[-2:]
    rows, columns = wave_own.shape
    live_count = jnp.float32(0.0)
    for sector in range(sizes_ref.shape[0]):
        live_count = live_count + sizes_ref[sector, 0].astype(jnp.float32) * sizes_ref[
            sector, 1
        ].astype(jnp.float32)
    total = sums[0][...]
    for other in sums[1:]:
        total = total + other[...]
    correlation, norm_square, sigma_square = total[0], total[1], total[2]
    rayleigh = correlation / norm_square
    residual_square = (
        sigma_square - 2.0 * rayleigh * correlation + rayleigh * rayleigh * norm_square
    )
    residual_square = jnp.maximum(residual_square, 0.0)
    scale = 1.0 / jnp.sqrt(residual_square / live_count + epsilon)
    factors[0] = scale
    factors[1] = rayleigh * scale
    sigma_factor = jnp.broadcast_to(scale[:1, :1], (rows, columns))
    wave_factor = jnp.broadcast_to((rayleigh * scale)[:1, :1], (rows, columns))
    sigma = sigma_own[0].astype(jnp.float32)
    wave = wave_own[...].astype(jnp.float32)
    second[0] = (sigma_factor * sigma - wave_factor * wave).astype(second.dtype)


def join_kernel(factors, sigma_own, *refs):
    pieces, (out, held, sems) = refs[:-3], refs[-3:]
    _, share, columns = pieces[0].shape
    place = lax.axis_index("ops")
    scale = jnp.broadcast_to(factors[0][:1, :1], (share, columns))
    shift = jnp.broadcast_to(factors[1][:1, :1], (share, columns))
    copies = []
    for step, piece in zip(reversed(range(len(pieces))), pieces):
        rows = pl.ds(pl.multiple_of((place ^ step) * share, share), share)
        moved = shift * sigma_own[0, rows, :].astype(jnp.float32)
        held[step] = scale * piece[0].astype(jnp.float32) - moved
        copies.append(pltpu.make_async_copy(held.at[step], out.at[0, rows], sems.at[step]))
        copies[-1].start()
    for copy in copies:
        copy.wait()


def partner(value, steps):
    steps = {axis: step for axis, step in steps.items() if step}
    if not steps:
        return value
    axes = tuple(steps)
    places = [()]
    for axis in axes:
        places = [place + (i,) for place in places for i in range(lax.axis_size(axis))]
    index = {place: i for i, place in enumerate(places)}
    pairs = [
        (index[tuple(i ^ steps[axis] for i, axis in zip(place, axes))], index[place])
        for place in places
    ]
    return lax.ppermute(value, axes, pairs)


def local(wavefunction, sector_sizes, left_blocks, right_blocks, sector_pairs, pair_weights):
    sectors = sector_sizes.shape[0]
    ops_count = lax.axis_size("ops")
    _, rows, columns = wavefunction.shape
    terms, side = left_blocks.shape[0], left_blocks.shape[1]
    share = rows // ops_count
    bf16, f32 = jnp.bfloat16, jnp.float32
    smem = pl.BlockSpec(memory_space=pltpu.SMEM)
    outside = pl.BlockSpec(memory_space=pltpu.HBM)
    inside = pl.BlockSpec(memory_space=pltpu.VMEM)

    def shape(*dims, dtype=bf16):
        return jax.ShapeDtypeStruct(dims, dtype)

    def call(kernel, name, out_shape, in_specs, *operands, scratch=(), vmem=16, out=inside):
        return pl.pallas_call(
            kernel,
            out_shape=out_shape,
            in_specs=list(in_specs) + [inside] * (len(operands) - len(in_specs)),
            out_specs=jax.tree.map(lambda _: out, out_shape),
            scratch_shapes=list(scratch),
            compiler_params=pltpu.CompilerParams(vmem_limit_bytes=vmem * mebibyte),
            name=name,
        )(*operands)

    def summed(name, *pieces, after=()):
        pieces = [piece if isinstance(piece, tuple) else (piece, 0) for piece in pieces]
        arrays, indices = zip(*pieces)
        return call(
            lambda *refs: sum_kernel(indices, *refs),
            name,
            shape(1, share, columns),
            [],
            *arrays,
            *after,
        )

    farthest_first = list(reversed(range(ops_count)))
    arrived = partner(wavefunction, {"rep": 1})
    left_own, left_other = call(
        load_kernel,
        "load_operators",
        [shape(terms, rows, rows), shape(terms, rows, side - rows)],
        [outside],
        left_blocks,
        scratch=[pltpu.SemaphoreType.DMA((2,))],
        vmem=51,
    )
    right = right_blocks
    pairs = jnp.swapaxes(sector_pairs, 1, 2)
    scalars = (sector_sizes, pairs, pair_weights)

    far = ops_count - 1
    direct = [(along,) for along in farthest_first[1:-1]]
    spots = [((far, 0), across) for across in range(sectors)]
    spots += [(along, across) for along in direct for across in range(sectors)]
    wave_own, mixing, live = call(
        first_tables_kernel,
        "tables_for_first_sigma",
        [
            shape(rows, columns),
            shape(terms, sectors, 8, 128, dtype=f32),
            shape(sectors + 1, rows, columns, dtype=f32),
        ],
        [smem] * 3,
        *scalars,
        wavefunction,
        left_own,
    )
    wave_other, *rest = call(
        lambda *refs: first_kernel(spots, *refs),
        "first_sigma_terms",
        [shape(rows, columns)]
        + [
            shape(len(along), share, columns, dtype=f32 if along == (far, 0) and across == 0 else bf16)
            for along, across in spots
        ],
        [],
        mixing,
        live,
        left_own,
        left_other,
        right,
        wave_own,
        arrived,
        scratch=[pltpu.VMEM((sectors, rows, columns), f32)],
    )
    rest = dict(zip(spots, rest))
    mixing, live = call(
        tables_kernel,
        "tables_for_second_sigma",
        [shape(terms, sectors, 8, 128, dtype=f32), shape(rows, columns, dtype=f32)],
        [smem] * 3,
        *scalars,
        wave_other,
    )
    met = [partner(rest[(far, 0), across], {"sec": across}) for across in range(sectors)]
    received = [partner(summed("sum_far_share", *met), {"ops": far})]
    nearest = ((1,), 0)
    order = [nearest] + [spot for spot in rest if spot[0] in direct and spot != nearest]
    received += [partner(rest[spot], {"ops": spot[0][0], "sec": spot[1]}) for spot in order]
    first_share = summed("sum_first_sigma", *[(piece, 1) for piece in met], *received, after=(mixing,))
    along_ops = {along: partner(first_share, {"ops": along}) for along in farthest_first}
    sigma_own = call(
        lambda *refs: place_kernel([(along, 0) for along in farthest_first], *refs),
        "place_own_sector",
        shape(1, rows, columns),
        [],
        *along_ops.values(),
    )
    sigma_other = partner(sigma_own, {"rep": 1})
    spots = [(along, across) for along in farthest_first for across in range(1, sectors)]
    pieces = [
        partner(first_share, {"ops": along, "sec": across})
        if along < 2
        else partner(along_ops[along], {"sec": across})
        for along, across in spots
    ]
    across_own = call(
        lambda *refs: place_kernel([(along, across - 1) for along, across in spots], *refs),
        "place_other_sectors",
        shape(sectors - 1, rows, columns),
        [],
        *pieces,
    )
    across_other = partner(across_own, {"rep": 1})

    products, across_products = call(
        left_kernel,
        "left_products",
        [
            shape(terms, rows, columns, dtype=f32),
            shape(sectors - 1, terms, rows, columns, dtype=f32),
        ],
        [],
        left_own,
        left_other,
        sigma_own,
        sigma_other,
        across_own,
    )
    shares = call(
        second_kernel,
        "second_sigma_terms",
        [shape(1, share, columns, dtype=f32)] + [shape(1, share, columns)] * (ops_count - 1),
        [],
        mixing,
        live,
        left_other,
        right,
        products,
        across_products,
        across_other,
        scratch=[pltpu.VMEM((rows, columns), f32)],
    )
    received = [partner(shares[step], {"ops": step}) for step in farthest_first[:-1]]
    sums = call(
        sums_kernel,
        "sums_for_rayleigh",
        shape(3, 8, 128, dtype=f32),
        [],
        wave_own,
        wave_other,
        sigma_own,
        sigma_other,
    )
    sums = [partner(sums, {"sec": step}) for step in range(sectors)]
    second_share = summed("sum_second_sigma", shares[0], *received, after=sums)
    second_wave, factors = call(
        wave_kernel,
        "second_wave",
        [shape(1, rows, columns), shape(2, 8, 128, dtype=f32)],
        [smem],
        sector_sizes,
        wave_own,
        sigma_own,
        *sums,
    )
    second_sigma = call(
        join_kernel,
        "join_second_sigma",
        shape(1, rows, columns, dtype=f32),
        [],
        factors,
        sigma_own,
        *[partner(second_share, {"ops": step}) for step in farthest_first],
        scratch=[
            pltpu.VMEM((ops_count, share, columns), f32),
            pltpu.SemaphoreType.DMA((ops_count,)),
        ],
        out=outside,
    )
    return (second_wave, second_sigma)


def solution(mesh):
    return jax.shard_map(
        local,
        mesh=mesh,
        in_specs=(
            P(("grp", "sec"), "rep", None),
            P("grp", None),
            P(("grp", "ops"), None, None),
            P(("grp", "ops"), None, None),
            P(("grp", "ops"), None, None),
            P(("grp", "ops"), None),
        ),
        out_specs=(P(("grp", "sec"), "rep", None), P(("grp", "sec"), "rep", None)),
        check_vma=False,
    )
```

```python
import jax
import jax.numpy as jnp
from jax import lax
from jax.experimental import pallas as pl
from jax.experimental.pallas import tpu as pltpu
from jax.sharding import PartitionSpec as P

epsilon = 1e-06
mebibyte = 1024 * 1024


def mixing_scalar(pairs_ref, weights_ref, term, target, source):
    value = jnp.float32(0.0)
    for pair in range(weights_ref.shape[1]):
        hit = (pairs_ref[term, 1, pair] == target) & (pairs_ref[term, 0, pair] == source)
        value = value + jnp.where(hit, weights_ref[term, pair], jnp.float32(0.0))
    return value


def live_cells(sizes_ref, sector, row_start, rows, columns):
    row = row_start + lax.broadcasted_iota(jnp.int32, (rows, columns), 0)
    column = lax.broadcasted_iota(jnp.int32, (rows, columns), 1)
    return (row < sizes_ref[sector, 0]) & (column < sizes_ref[sector, 1])


def masked(values, live):
    return jnp.where(live, values.astype(jnp.float32), 0.0).astype(values.dtype)


def left_times(lefts, blocks):
    total = None
    for left, block in zip(lefts, blocks):
        terms, rows, depth = left.shape
        stacked = left[...].reshape(terms * rows, depth)
        part = jnp.dot(stacked, block, preferred_element_type=jnp.float32)
        total = part if total is None else total + part
    return total.reshape(terms, rows, -1)


def times_right(values, right, term):
    return lax.dot_general(
        values.astype(jnp.bfloat16),
        right[term],
        (((1,), (1,)), ((), ())),
        preferred_element_type=jnp.float32,
    )


def load_kernel(left_ref, left_own, left_other, sems):
    rows = left_own.shape[1]
    core = lax.axis_index("rep")
    copies = []
    for index, (half, place) in enumerate(((left_own, core), (left_other, core ^ 1))):
        mine = pl.ds(pl.multiple_of(core * rows, rows), rows)
        columns = pl.ds(pl.multiple_of(place * rows, rows), rows)
        copies.append(pltpu.make_async_copy(left_ref.at[:, mine, columns], half, sems.at[index]))
    for copy in copies:
        copy.start()
    for copy in copies:
        copy.wait()


def live_rows(sizes, sector, row_start, rows, columns):
    bounds = sizes[pl.ds(sector, 1), :]
    row = row_start + lax.broadcasted_iota(jnp.int32, (rows, columns), 0)
    column = lax.broadcasted_iota(jnp.int32, (rows, columns), 1)
    inside = (row < bounds[:, 0:1]) & (column < bounds[:, 1:2])
    return jnp.where(inside, 1.0, 0.0)


def first_tables_kernel(sizes, pairs, weights, wave, _, own, mixing):
    rows, columns = own.shape
    sector = lax.axis_index("sec")
    live = live_rows(sizes, sector, lax.axis_index("rep") * rows, rows, columns)
    own[...] = (wave[0].astype(jnp.float32) * live).astype(own.dtype)
    source, target = pairs[:, 0, :], pairs[:, 1, :]
    for step in range(mixing.shape[0]):
        hits = (source == sector) & (target == (sector ^ step))
        total = jnp.sum(jnp.where(hits, weights[...], 0.0), axis=1, keepdims=True)
        mixing[step] = jnp.broadcast_to(total, mixing.shape[1:])


def first_kernel(shares, *refs):
    sizes, mixing, left_own, left_other, right, own, arrived = refs[:7]
    other, *parts = refs[7:-1]
    held = refs[-1]
    rows, columns = own.shape
    share = parts[0].shape[-2]
    sectors = held.shape[0]
    sector = lax.axis_index("sec")
    core = lax.axis_index("rep")
    place = lax.axis_index("ops")
    live = live_rows(sizes, sector, (core ^ 1) * rows, rows, columns)
    other[...] = (arrived[0].astype(jnp.float32) * live).astype(other.dtype)
    products = left_times((left_own, left_other), (own[...], other[...]))
    totals = [None] * sectors
    for term in range(right.shape[0]):
        product = times_right(products[term], right, term)
        for step in range(sectors):
            weight = jnp.broadcast_to(mixing[step][term : term + 1, :1], (rows, columns))
            part = weight * product
            totals[step] = part if totals[step] is None else totals[step] + part
    for step in range(sectors):
        live = live_rows(sizes, sector ^ step, core * rows, rows, columns)
        held[step] = totals[step] * live
    for (steps, across), out in zip(shares, parts):
        for index, along in enumerate(steps):
            start = pl.multiple_of((place ^ along) * share, share)
            out[index] = held[across, pl.ds(start, share), :].astype(out.dtype)


def sum_kernel(indices, *refs):
    total = refs[0][indices[0]].astype(jnp.float32)
    for index, piece in zip(indices[1:], refs[1:]):
        total = total + piece[index].astype(jnp.float32)
    refs[-1][0] = total.astype(refs[-1].dtype)


def place_kernel(spots, *refs):
    pieces, half = refs[:-1], refs[-1]
    share = pieces[0].shape[1]
    place = lax.axis_index("ops")
    for (along, index), piece in zip(spots, pieces):
        start = pl.multiple_of((place ^ along) * share, share)
        half[index, pl.ds(start, share), :] = piece[0]


def left_kernel(left_own, left_other, own, other, across_own, out, across_out):
    out[...] = left_times((left_own, left_other), (own[0], other[0]))
    for step in range(across_own.shape[0]):
        across_out[step] = left_times((left_own,), (across_own[step],))


def tables_kernel(sizes_ref, pairs_ref, weights_ref, _, mixing, live):
    target = lax.axis_index("sec")
    for term in range(mixing.shape[0]):
        for step in range(mixing.shape[1]):
            weight = mixing_scalar(pairs_ref, weights_ref, term, target, target ^ step)
            mixing[term, step] = jnp.full(mixing.shape[2:], weight, jnp.float32)
    rows, columns = live.shape
    cells = live_cells(sizes_ref, target, lax.axis_index("rep") * rows, rows, columns)
    live[...] = jnp.where(cells, 1.0, 0.0)


def second_kernel(mixing, live, left_other, right, products, across_products, other, *refs):
    shares, held = refs[:-1], refs[-1]
    rows, columns = products.shape[1:]
    share = shares[0].shape[1]
    place = lax.axis_index("ops")
    total = None
    across = [left_times((left_other,), (other[step],)) for step in range(other.shape[0])]
    for term in range(right.shape[0]):
        weights = [
            jnp.broadcast_to(mixing[term, step][:1, :1], (rows, columns))
            for step in range(len(across) + 1)
        ]
        combined = weights[0] * products[term]
        for step, part in enumerate(across):
            combined = combined + weights[step + 1] * (across_products[step, term] + part[term])
        part = times_right(combined, right, term)
        total = part if total is None else total + part
    held[...] = total * live[...]
    for step, out in enumerate(shares):
        start = pl.multiple_of((place ^ step) * share, share)
        out[0] = held[pl.ds(start, share), :].astype(out.dtype)


def sums_kernel(wave_own, wave_other, sigma_own, sigma_other, out):
    step, columns = 16, wave_own.shape[1]
    sums = (jnp.zeros((step, columns), jnp.float32),) * 3
    for wave, sigma in ((wave_own, sigma_own), (wave_other, sigma_other)):

        def add_rows(block, carry):
            start = pl.multiple_of(block * step, step)
            w = wave[pl.ds(start, step), :].astype(jnp.float32)
            s = sigma[0, pl.ds(start, step), :].astype(jnp.float32)
            return (carry[0] + w * s, carry[1] + w * w, carry[2] + s * s)

        sums = lax.fori_loop(0, wave.shape[0] // step, add_rows, sums, unroll=2)
    for index, value in enumerate(sums):
        out[index] = jnp.broadcast_to(jnp.sum(value, keepdims=True), out.shape[1:])


def wave_kernel(sizes_ref, wave_own, sigma_own, *refs):
    sums, (second, factors) = refs[:-2], refs[-2:]
    rows, columns = wave_own.shape
    live_count = jnp.float32(0.0)
    for sector in range(sizes_ref.shape[0]):
        live_count = live_count + sizes_ref[sector, 0].astype(jnp.float32) * sizes_ref[
            sector, 1
        ].astype(jnp.float32)
    total = sums[0][...]
    for other in sums[1:]:
        total = total + other[...]
    correlation, norm_square, sigma_square = total[0], total[1], total[2]
    rayleigh = correlation / norm_square
    residual_square = (
        sigma_square - 2.0 * rayleigh * correlation + rayleigh * rayleigh * norm_square
    )
    residual_square = jnp.maximum(residual_square, 0.0)
    scale = 1.0 / jnp.sqrt(residual_square / live_count + epsilon)
    factors[0] = scale
    factors[1] = rayleigh * scale
    sigma_factor = jnp.broadcast_to(scale[:1, :1], (rows, columns))
    wave_factor = jnp.broadcast_to((rayleigh * scale)[:1, :1], (rows, columns))
    sigma = sigma_own[0].astype(jnp.float32)
    wave = wave_own[...].astype(jnp.float32)
    second[0] = (sigma_factor * sigma - wave_factor * wave).astype(second.dtype)


def join_kernel(factors, sigma_own, *refs):
    pieces, (out, held, sems) = refs[:-3], refs[-3:]
    _, share, columns = pieces[0].shape
    place = lax.axis_index("ops")
    scale = jnp.broadcast_to(factors[0][:1, :1], (share, columns))
    shift = jnp.broadcast_to(factors[1][:1, :1], (share, columns))
    copies = []
    for step, piece in zip(reversed(range(len(pieces))), pieces):
        rows = pl.ds(pl.multiple_of((place ^ step) * share, share), share)
        moved = shift * sigma_own[0, rows, :].astype(jnp.float32)
        held[step] = scale * piece[0].astype(jnp.float32) - moved
        copies.append(pltpu.make_async_copy(held.at[step], out.at[0, rows], sems.at[step]))
        copies[-1].start()
    for copy in copies:
        copy.wait()


def partner(value, steps):
    steps = {axis: step for axis, step in steps.items() if step}
    if not steps:
        return value
    axes = tuple(steps)
    places = [()]
    for axis in axes:
        places = [place + (i,) for place in places for i in range(lax.axis_size(axis))]
    index = {place: i for i, place in enumerate(places)}
    pairs = [
        (index[tuple(i ^ steps[axis] for i, axis in zip(place, axes))], index[place])
        for place in places
    ]
    return lax.ppermute(value, axes, pairs)


def local(wavefunction, sector_sizes, left_blocks, right_blocks, sector_pairs, pair_weights):
    sectors = sector_sizes.shape[0]
    ops_count = lax.axis_size("ops")
    _, rows, columns = wavefunction.shape
    terms, side = left_blocks.shape[0], left_blocks.shape[1]
    share = rows // ops_count
    bf16, f32 = jnp.bfloat16, jnp.float32
    smem = pl.BlockSpec(memory_space=pltpu.SMEM)
    outside = pl.BlockSpec(memory_space=pltpu.HBM)
    inside = pl.BlockSpec(memory_space=pltpu.VMEM)

    def shape(*dims, dtype=bf16):
        return jax.ShapeDtypeStruct(dims, dtype)

    def call(kernel, name, out_shape, in_specs, *operands, scratch=(), vmem=16, out=inside):
        return pl.pallas_call(
            kernel,
            out_shape=out_shape,
            in_specs=list(in_specs) + [inside] * (len(operands) - len(in_specs)),
            out_specs=jax.tree.map(lambda _: out, out_shape),
            scratch_shapes=list(scratch),
            compiler_params=pltpu.CompilerParams(vmem_limit_bytes=vmem * mebibyte),
            name=name,
        )(*operands)

    def summed(name, *pieces, after=()):
        pieces = [piece if isinstance(piece, tuple) else (piece, 0) for piece in pieces]
        arrays, indices = zip(*pieces)
        return call(
            lambda *refs: sum_kernel(indices, *refs),
            name,
            shape(1, share, columns),
            [],
            *arrays,
            *after,
        )

    farthest_first = list(reversed(range(ops_count)))
    arrived = partner(wavefunction, {"rep": 1})
    left_own, left_other = call(
        load_kernel,
        "load_operators",
        [shape(terms, rows, rows), shape(terms, rows, side - rows)],
        [outside],
        left_blocks,
        scratch=[pltpu.SemaphoreType.DMA((2,))],
        vmem=51,
    )
    right = right_blocks
    pairs = jnp.swapaxes(sector_pairs, 1, 2)
    scalars = (sector_sizes, pairs, pair_weights)

    far = ops_count - 1
    direct = [(along,) for along in farthest_first[1:-1]]
    spots = [((far, 0), across) for across in range(sectors)]
    spots += [(along, across) for along in direct for across in range(sectors)]
    wave_own, mixing = call(
        first_tables_kernel,
        "tables_for_first_sigma",
        [shape(rows, columns), shape(sectors, terms, 128, dtype=f32)],
        [],
        *scalars,
        wavefunction,
        left_own,
    )
    wave_other, *rest = call(
        lambda *refs: first_kernel(spots, *refs),
        "first_sigma_terms",
        [shape(rows, columns)]
        + [
            shape(len(along), share, columns, dtype=f32 if along == (far, 0) and across == 0 else bf16)
            for along, across in spots
        ],
        [],
        sector_sizes,
        mixing,
        left_own,
        left_other,
        right,
        wave_own,
        arrived,
        scratch=[pltpu.VMEM((sectors, rows, columns), f32)],
    )
    rest = dict(zip(spots, rest))
    mixing, live = call(
        tables_kernel,
        "tables_for_second_sigma",
        [shape(terms, sectors, 8, 128, dtype=f32), shape(rows, columns, dtype=f32)],
        [smem] * 3,
        *scalars,
        wave_other,
    )
    met = [partner(rest[(far, 0), across], {"sec": across}) for across in range(sectors)]
    received = [partner(summed("sum_far_share", *met), {"ops": far})]
    nearest = ((1,), 0)
    order = [nearest] + [spot for spot in rest if spot[0] in direct and spot != nearest]
    received += [partner(rest[spot], {"ops": spot[0][0], "sec": spot[1]}) for spot in order]
    first_share = summed("sum_first_sigma", *[(piece, 1) for piece in met], *received, after=(mixing,))
    along_ops = {along: partner(first_share, {"ops": along}) for along in farthest_first}
    sigma_own = call(
        lambda *refs: place_kernel([(along, 0) for along in farthest_first], *refs),
        "place_own_sector",
        shape(1, rows, columns),
        [],
        *along_ops.values(),
    )
    sigma_other = partner(sigma_own, {"rep": 1})
    spots = [(along, across) for along in farthest_first for across in range(1, sectors)]
    pieces = [
        partner(first_share, {"ops": along, "sec": across})
        if along < 2
        else partner(along_ops[along], {"sec": across})
        for along, across in spots
    ]
    across_own = call(
        lambda *refs: place_kernel([(along, across - 1) for along, across in spots], *refs),
        "place_other_sectors",
        shape(sectors - 1, rows, columns),
        [],
        *pieces,
    )
    across_other = partner(across_own, {"rep": 1})

    products, across_products = call(
        left_kernel,
        "left_products",
        [
            shape(terms, rows, columns, dtype=f32),
            shape(sectors - 1, terms, rows, columns, dtype=f32),
        ],
        [],
        left_own,
        left_other,
        sigma_own,
        sigma_other,
        across_own,
    )
    shares = call(
        second_kernel,
        "second_sigma_terms",
        [shape(1, share, columns, dtype=f32)] + [shape(1, share, columns)] * (ops_count - 1),
        [],
        mixing,
        live,
        left_other,
        right,
        products,
        across_products,
        across_other,
        scratch=[pltpu.VMEM((rows, columns), f32)],
    )
    received = [partner(shares[step], {"ops": step}) for step in farthest_first[:-1]]
    sums = call(
        sums_kernel,
        "sums_for_rayleigh",
        shape(3, 8, 128, dtype=f32),
        [],
        wave_own,
        wave_other,
        sigma_own,
        sigma_other,
    )
    sums = [partner(sums, {"sec": step}) for step in range(sectors)]
    second_share = summed("sum_second_sigma", shares[0], *received, after=sums)
    second_wave, factors = call(
        wave_kernel,
        "second_wave",
        [shape(1, rows, columns), shape(2, 8, 128, dtype=f32)],
        [smem],
        sector_sizes,
        wave_own,
        sigma_own,
        *sums,
    )
    second_sigma = call(
        join_kernel,
        "join_second_sigma",
        shape(1, rows, columns, dtype=f32),
        [],
        factors,
        sigma_own,
        *[partner(second_share, {"ops": step}) for step in farthest_first],
        scratch=[
            pltpu.VMEM((ops_count, share, columns), f32),
            pltpu.SemaphoreType.DMA((ops_count,)),
        ],
        out=outside,
    )
    return (second_wave, second_sigma)


def solution(mesh):
    return jax.shard_map(
        local,
        mesh=mesh,
        in_specs=(
            P(("grp", "sec"), "rep", None),
            P("grp", None),
            P(("grp", "ops"), None, None),
            P(("grp", "ops"), None, None),
            P(("grp", "ops"), None, None),
            P(("grp", "ops"), None),
        ),
        out_specs=(P(("grp", "sec"), "rep", None), P(("grp", "sec"), "rep", None)),
        check_vma=False,
    )
```

```python
import jax
import jax.numpy as jnp
from jax import lax
from jax.experimental import pallas as pl
from jax.experimental.pallas import tpu as pltpu
from jax.sharding import PartitionSpec as P

epsilon = 1e-06
mebibyte = 1024 * 1024


def mixing_scalar(pairs_ref, weights_ref, term, target, source):
    value = jnp.float32(0.0)
    for pair in range(weights_ref.shape[1]):
        hit = (pairs_ref[term, 1, pair] == target) & (pairs_ref[term, 0, pair] == source)
        value = value + jnp.where(hit, weights_ref[term, pair], jnp.float32(0.0))
    return value


def live_cells(sizes_ref, sector, row_start, rows, columns):
    row = row_start + lax.broadcasted_iota(jnp.int32, (rows, columns), 0)
    column = lax.broadcasted_iota(jnp.int32, (rows, columns), 1)
    return (row < sizes_ref[sector, 0]) & (column < sizes_ref[sector, 1])


def masked(values, live):
    return jnp.where(live, values.astype(jnp.float32), 0.0).astype(values.dtype)


def left_times(lefts, blocks):
    total = None
    for left, block in zip(lefts, blocks):
        terms, rows, depth = left.shape
        stacked = left[...].reshape(terms * rows, depth)
        part = jnp.dot(stacked, block, preferred_element_type=jnp.float32)
        total = part if total is None else total + part
    return total.reshape(terms, rows, -1)


def times_right(values, right, term):
    return lax.dot_general(
        values.astype(jnp.bfloat16),
        right[term],
        (((1,), (1,)), ((), ())),
        preferred_element_type=jnp.float32,
    )


def load_kernel(left_ref, left_own, left_other, sems):
    rows = left_own.shape[1]
    core = lax.axis_index("rep")
    copies = []
    for index, (half, place) in enumerate(((left_own, core), (left_other, core ^ 1))):
        mine = pl.ds(pl.multiple_of(core * rows, rows), rows)
        columns = pl.ds(pl.multiple_of(place * rows, rows), rows)
        copies.append(pltpu.make_async_copy(left_ref.at[:, mine, columns], half, sems.at[index]))
    for copy in copies:
        copy.start()
    for copy in copies:
        copy.wait()


def live_rows(sizes, sector, row_start, rows, columns):
    bounds = sizes[pl.ds(sector, 1), :]
    row = row_start + lax.broadcasted_iota(jnp.int32, (rows, columns), 0)
    column = lax.broadcasted_iota(jnp.int32, (rows, columns), 1)
    inside = (row < bounds[:, 0:1]) & (column < bounds[:, 1:2])
    return jnp.where(inside, 1.0, 0.0)


def first_tables_kernel(sizes, pairs, weights, wave, _, own, mixing):
    rows, columns = own.shape
    sector = lax.axis_index("sec")
    live = live_rows(sizes, sector, lax.axis_index("rep") * rows, rows, columns)
    own[...] = (wave[0].astype(jnp.float32) * live).astype(own.dtype)
    source, target = pairs[:, 0, :], pairs[:, 1, :]
    for step in range(mixing.shape[0]):
        hits = (source == sector) & (target == (sector ^ step))
        total = jnp.sum(jnp.where(hits, weights[...], 0.0), axis=1, keepdims=True)
        mixing[step] = jnp.broadcast_to(total, mixing.shape[1:])


def first_kernel(shares, *refs):
    sizes, mixing, left_own, left_other, right, own, arrived = refs[:7]
    other, *parts = refs[7:-1]
    held = refs[-1]
    rows, columns = own.shape
    share = parts[0].shape[-2]
    sectors = held.shape[0]
    sector = lax.axis_index("sec")
    core = lax.axis_index("rep")
    place = lax.axis_index("ops")
    live = live_rows(sizes, sector, (core ^ 1) * rows, rows, columns)
    other[...] = (arrived[0].astype(jnp.float32) * live).astype(other.dtype)
    products = left_times((left_own, left_other), (own[...], other[...]))
    totals = [None] * sectors
    for term in range(right.shape[0]):
        product = times_right(products[term], right, term)
        for step in range(sectors):
            weight = jnp.broadcast_to(mixing[step][term : term + 1, :1], (rows, columns))
            part = weight * product
            totals[step] = part if totals[step] is None else totals[step] + part
    for step in range(sectors):
        live = live_rows(sizes, sector ^ step, core * rows, rows, columns)
        held[step] = totals[step] * live
    for (steps, across), out in zip(shares, parts):
        for index, along in enumerate(steps):
            start = pl.multiple_of((place ^ along) * share, share)
            out[index] = held[across, pl.ds(start, share), :].astype(out.dtype)


def sum_kernel(indices, *refs):
    total = refs[0][indices[0]].astype(jnp.float32)
    for index, piece in zip(indices[1:], refs[1:]):
        total = total + piece[index].astype(jnp.float32)
    refs[-1][0] = total.astype(refs[-1].dtype)


def place_kernel(spots, *refs):
    pieces, half = refs[:-1], refs[-1]
    share = pieces[0].shape[1]
    place = lax.axis_index("ops")
    for (along, index), piece in zip(spots, pieces):
        start = pl.multiple_of((place ^ along) * share, share)
        half[index, pl.ds(start, share), :] = piece[0]


def left_kernel(left_own, left_other, own, other, across_own, out, across_out):
    out[...] = left_times((left_own, left_other), (own[0], other[0]))
    for step in range(across_own.shape[0]):
        across_out[step] = left_times((left_own,), (across_own[step],))


def tables_kernel(sizes_ref, pairs_ref, weights_ref, _, mixing, live):
    target = lax.axis_index("sec")
    for term in range(mixing.shape[0]):
        for step in range(mixing.shape[1]):
            weight = mixing_scalar(pairs_ref, weights_ref, term, target, target ^ step)
            mixing[term, step] = jnp.full(mixing.shape[2:], weight, jnp.float32)
    rows, columns = live.shape
    cells = live_cells(sizes_ref, target, lax.axis_index("rep") * rows, rows, columns)
    live[...] = jnp.where(cells, 1.0, 0.0)


def second_kernel(mixing, live, left_other, right, products, across_products, other, *refs):
    shares, held = refs[:-1], refs[-1]
    rows, columns = products.shape[1:]
    share = shares[0].shape[1]
    place = lax.axis_index("ops")
    total = None
    across = [left_times((left_other,), (other[step],)) for step in range(other.shape[0])]
    for term in range(right.shape[0]):
        weights = [
            jnp.broadcast_to(mixing[term, step][:1, :1], (rows, columns))
            for step in range(len(across) + 1)
        ]
        combined = weights[0] * products[term]
        for step, part in enumerate(across):
            combined = combined + weights[step + 1] * (across_products[step, term] + part[term])
        part = times_right(combined, right, term)
        total = part if total is None else total + part
    held[...] = total * live[...]
    for step, out in enumerate(shares):
        start = pl.multiple_of((place ^ step) * share, share)
        out[0] = held[pl.ds(start, share), :].astype(out.dtype)


def sums_kernel(wave_own, wave_other, sigma_own, sigma_other, out):
    step, columns = 16, wave_own.shape[1]
    sums = (jnp.zeros((step, columns), jnp.float32),) * 3
    for wave, sigma in ((wave_own, sigma_own), (wave_other, sigma_other)):

        def add_rows(block, carry):
            start = pl.multiple_of(block * step, step)
            w = wave[pl.ds(start, step), :].astype(jnp.float32)
            s = sigma[0, pl.ds(start, step), :].astype(jnp.float32)
            return (carry[0] + w * s, carry[1] + w * w, carry[2] + s * s)

        sums = lax.fori_loop(0, wave.shape[0] // step, add_rows, sums, unroll=2)
    for index, value in enumerate(sums):
        out[index] = jnp.broadcast_to(jnp.sum(value, keepdims=True), out.shape[1:])


def wave_kernel(sizes_ref, wave_own, sigma_own, *refs):
    sums, (second, factors) = refs[:-2], refs[-2:]
    rows, columns = wave_own.shape
    live_count = jnp.float32(0.0)
    for sector in range(sizes_ref.shape[0]):
        live_count = live_count + sizes_ref[sector, 0].astype(jnp.float32) * sizes_ref[
            sector, 1
        ].astype(jnp.float32)
    total = sums[0][...]
    for other in sums[1:]:
        total = total + other[...]
    correlation, norm_square, sigma_square = total[0], total[1], total[2]
    rayleigh = correlation / norm_square
    residual_square = (
        sigma_square - 2.0 * rayleigh * correlation + rayleigh * rayleigh * norm_square
    )
    residual_square = jnp.maximum(residual_square, 0.0)
    scale = 1.0 / jnp.sqrt(residual_square / live_count + epsilon)
    factors[0] = scale
    factors[1] = rayleigh * scale
    sigma_factor = jnp.broadcast_to(scale[:1, :1], (rows, columns))
    wave_factor = jnp.broadcast_to((rayleigh * scale)[:1, :1], (rows, columns))
    sigma = sigma_own[0].astype(jnp.float32)
    wave = wave_own[...].astype(jnp.float32)
    second[0] = (sigma_factor * sigma - wave_factor * wave).astype(second.dtype)


def join_kernel(factors, sigma_own, *refs):
    pieces, (out, held, sems) = refs[:-3], refs[-3:]
    _, share, columns = pieces[0].shape
    place = lax.axis_index("ops")
    scale = jnp.broadcast_to(factors[0][:1, :1], (share, columns))
    shift = jnp.broadcast_to(factors[1][:1, :1], (share, columns))
    copies = []
    for step, piece in zip(reversed(range(len(pieces))), pieces):
        rows = pl.ds(pl.multiple_of((place ^ step) * share, share), share)
        moved = shift * sigma_own[0, rows, :].astype(jnp.float32)
        held[step] = scale * piece[0].astype(jnp.float32) - moved
        copies.append(pltpu.make_async_copy(held.at[step], out.at[0, rows], sems.at[step]))
        copies[-1].start()
    for copy in copies:
        copy.wait()


def partner(value, steps):
    steps = {axis: step for axis, step in steps.items() if step}
    if not steps:
        return value
    axes = tuple(steps)
    places = [()]
    for axis in axes:
        places = [place + (i,) for place in places for i in range(lax.axis_size(axis))]
    index = {place: i for i, place in enumerate(places)}
    pairs = [
        (index[tuple(i ^ steps[axis] for i, axis in zip(place, axes))], index[place])
        for place in places
    ]
    return lax.ppermute(value, axes, pairs)


def local(wavefunction, sector_sizes, left_blocks, right_blocks, sector_pairs, pair_weights):
    sectors = sector_sizes.shape[0]
    ops_count = lax.axis_size("ops")
    _, rows, columns = wavefunction.shape
    terms, side = left_blocks.shape[0], left_blocks.shape[1]
    share = rows // ops_count
    bf16, f32 = jnp.bfloat16, jnp.float32
    smem = pl.BlockSpec(memory_space=pltpu.SMEM)
    outside = pl.BlockSpec(memory_space=pltpu.HBM)
    inside = pl.BlockSpec(memory_space=pltpu.VMEM)

    def shape(*dims, dtype=bf16):
        return jax.ShapeDtypeStruct(dims, dtype)

    def call(kernel, name, out_shape, in_specs, *operands, scratch=(), vmem=16, out=inside):
        return pl.pallas_call(
            kernel,
            out_shape=out_shape,
            in_specs=list(in_specs) + [inside] * (len(operands) - len(in_specs)),
            out_specs=jax.tree.map(lambda _: out, out_shape),
            scratch_shapes=list(scratch),
            compiler_params=pltpu.CompilerParams(vmem_limit_bytes=vmem * mebibyte),
            name=name,
        )(*operands)

    def summed(name, *pieces, after=()):
        pieces = [piece if isinstance(piece, tuple) else (piece, 0) for piece in pieces]
        arrays, indices = zip(*pieces)
        return call(
            lambda *refs: sum_kernel(indices, *refs),
            name,
            shape(1, share, columns),
            [],
            *arrays,
            *after,
        )

    farthest_first = list(reversed(range(ops_count)))
    arrived = partner(wavefunction, {"rep": 1})
    left_own, left_other = call(
        load_kernel,
        "load_operators",
        [shape(terms, rows, rows), shape(terms, rows, side - rows)],
        [outside],
        left_blocks,
        scratch=[pltpu.SemaphoreType.DMA((2,))],
        vmem=51,
    )
    right = right_blocks
    pairs = jnp.swapaxes(sector_pairs, 1, 2)
    scalars = (sector_sizes, pairs, pair_weights)

    far = ops_count - 1
    groups = [(far, 0), (1,)] + [(along,) for along in farthest_first[1:-2]]
    spots = [(along, across) for along in groups for across in range(sectors)]
    wave_own, mixing = call(
        first_tables_kernel,
        "tables_for_first_sigma",
        [shape(rows, columns), shape(sectors, terms, 128, dtype=f32)],
        [],
        *scalars,
        wavefunction,
        left_own,
    )
    wave_other, *rest = call(
        lambda *refs: first_kernel(spots, *refs),
        "first_sigma_terms",
        [shape(rows, columns)]
        + [
            shape(len(along), share, columns, dtype=f32 if along in groups[:2] and across == 0 else bf16)
            for along, across in spots
        ],
        [],
        sector_sizes,
        mixing,
        left_own,
        left_other,
        right,
        wave_own,
        arrived,
        scratch=[pltpu.VMEM((sectors, rows, columns), f32)],
    )
    rest = dict(zip(spots, rest))
    mixing, live = call(
        tables_kernel,
        "tables_for_second_sigma",
        [shape(terms, sectors, 8, 128, dtype=f32), shape(rows, columns, dtype=f32)],
        [smem] * 3,
        *scalars,
        wave_other,
    )
    met = {
        along: [partner(rest[along, across], {"sec": across}) for across in range(sectors)]
        for along in groups[:2]
    }
    far_sum = summed("sum_far_share", *met[far, 0])
    received = [partner(far_sum, {"ops": far})]
    received += [
        partner(rest[along, across], {"ops": along[0], "sec": across})
        for along in groups[2:]
        for across in range(sectors)
    ]
    near_sum = summed("sum_near_share", *met[1,], after=(far_sum,))
    received.append(partner(near_sum, {"ops": 1}))
    kept = [(piece, 1) for piece in met[far, 0]]
    first_share = summed("sum_first_sigma", *kept, *received, after=(mixing,))
    along_ops = {along: partner(first_share, {"ops": along}) for along in farthest_first}
    sigma_own = call(
        lambda *refs: place_kernel([(along, 0) for along in farthest_first], *refs),
        "place_own_sector",
        shape(1, rows, columns),
        [],
        *along_ops.values(),
    )
    sigma_other = partner(sigma_own, {"rep": 1})
    spots = [(along, across) for along in farthest_first for across in range(1, sectors)]
    pieces = [
        partner(first_share, {"ops": along, "sec": across})
        if along < 2
        else partner(along_ops[along], {"sec": across})
        for along, across in spots
    ]
    across_own = call(
        lambda *refs: place_kernel([(along, across - 1) for along, across in spots], *refs),
        "place_other_sectors",
        shape(sectors - 1, rows, columns),
        [],
        *pieces,
    )
    across_other = partner(across_own, {"rep": 1})

    products, across_products = call(
        left_kernel,
        "left_products",
        [
            shape(terms, rows, columns, dtype=f32),
            shape(sectors - 1, terms, rows, columns, dtype=f32),
        ],
        [],
        left_own,
        left_other,
        sigma_own,
        sigma_other,
        across_own,
    )
    shares = call(
        second_kernel,
        "second_sigma_terms",
        [shape(1, share, columns, dtype=f32)] + [shape(1, share, columns)] * (ops_count - 1),
        [],
        mixing,
        live,
        left_other,
        right,
        products,
        across_products,
        across_other,
        scratch=[pltpu.VMEM((rows, columns), f32)],
    )
    received = [partner(shares[step], {"ops": step}) for step in farthest_first[:-1]]
    sums = call(
        sums_kernel,
        "sums_for_rayleigh",
        shape(3, 8, 128, dtype=f32),
        [],
        wave_own,
        wave_other,
        sigma_own,
        sigma_other,
    )
    sums = [partner(sums, {"sec": step}) for step in range(sectors)]
    second_share = summed("sum_second_sigma", shares[0], *received, after=sums)
    second_wave, factors = call(
        wave_kernel,
        "second_wave",
        [shape(1, rows, columns), shape(2, 8, 128, dtype=f32)],
        [smem],
        sector_sizes,
        wave_own,
        sigma_own,
        *sums,
    )
    second_sigma = call(
        join_kernel,
        "join_second_sigma",
        shape(1, rows, columns, dtype=f32),
        [],
        factors,
        sigma_own,
        *[partner(second_share, {"ops": step}) for step in farthest_first],
        scratch=[
            pltpu.VMEM((ops_count, share, columns), f32),
            pltpu.SemaphoreType.DMA((ops_count,)),
        ],
        out=outside,
    )
    return (second_wave, second_sigma)


def solution(mesh):
    return jax.shard_map(
        local,
        mesh=mesh,
        in_specs=(
            P(("grp", "sec"), "rep", None),
            P("grp", None),
            P(("grp", "ops"), None, None),
            P(("grp", "ops"), None, None),
            P(("grp", "ops"), None, None),
            P(("grp", "ops"), None),
        ),
        out_specs=(P(("grp", "sec"), "rep", None), P(("grp", "sec"), "rep", None)),
        check_vma=False,
    )
```

```python
import jax
import jax.numpy as jnp
from jax import lax
from jax.experimental import pallas as pl
from jax.experimental.pallas import tpu as pltpu
from jax.sharding import PartitionSpec as P

epsilon = 1e-06
mebibyte = 1024 * 1024


def mixing_scalar(pairs_ref, weights_ref, term, target, source):
    value = jnp.float32(0.0)
    for pair in range(weights_ref.shape[1]):
        hit = (pairs_ref[term, 1, pair] == target) & (pairs_ref[term, 0, pair] == source)
        value = value + jnp.where(hit, weights_ref[term, pair], jnp.float32(0.0))
    return value


def live_cells(sizes_ref, sector, row_start, rows, columns):
    row = row_start + lax.broadcasted_iota(jnp.int32, (rows, columns), 0)
    column = lax.broadcasted_iota(jnp.int32, (rows, columns), 1)
    return (row < sizes_ref[sector, 0]) & (column < sizes_ref[sector, 1])


def masked(values, live):
    return jnp.where(live, values.astype(jnp.float32), 0.0).astype(values.dtype)


def left_times(lefts, blocks):
    total = None
    for left, block in zip(lefts, blocks):
        terms, rows, depth = left.shape
        stacked = left[...].reshape(terms * rows, depth)
        part = jnp.dot(stacked, block, preferred_element_type=jnp.float32)
        total = part if total is None else total + part
    return total.reshape(terms, rows, -1)


def times_right(values, right, term):
    return lax.dot_general(
        values.astype(jnp.bfloat16),
        right[term],
        (((1,), (1,)), ((), ())),
        preferred_element_type=jnp.float32,
    )


def load_kernel(left_ref, left_own, left_other, sems):
    rows = left_own.shape[1]
    core = lax.axis_index("rep")
    copies = []
    for index, (half, place) in enumerate(((left_own, core), (left_other, core ^ 1))):
        mine = pl.ds(pl.multiple_of(core * rows, rows), rows)
        columns = pl.ds(pl.multiple_of(place * rows, rows), rows)
        copies.append(pltpu.make_async_copy(left_ref.at[:, mine, columns], half, sems.at[index]))
    for copy in copies:
        copy.start()
    for copy in copies:
        copy.wait()


def live_rows(sizes, sector, row_start, rows, columns):
    bounds = sizes[pl.ds(sector, 1), :]
    row = row_start + lax.broadcasted_iota(jnp.int32, (rows, columns), 0)
    column = lax.broadcasted_iota(jnp.int32, (rows, columns), 1)
    inside = (row < bounds[:, 0:1]) & (column < bounds[:, 1:2])
    return jnp.where(inside, 1.0, 0.0)


def first_tables_kernel(sizes, pairs, weights, wave, _, own, mixing):
    rows, columns = own.shape
    sector = lax.axis_index("sec")
    live = live_rows(sizes, sector, lax.axis_index("rep") * rows, rows, columns)
    own[...] = (wave[0].astype(jnp.float32) * live).astype(own.dtype)
    source, target = pairs[:, 0, :], pairs[:, 1, :]
    for step in range(mixing.shape[0]):
        hits = (source == sector) & (target == (sector ^ step))
        total = jnp.sum(jnp.where(hits, weights[...], 0.0), axis=1, keepdims=True)
        mixing[step] = jnp.broadcast_to(total, mixing.shape[1:])


def first_kernel(shares, *refs):
    sizes, mixing, left_own, left_other, right, own, arrived = refs[:7]
    other, *parts = refs[7:-1]
    held = refs[-1]
    rows, columns = own.shape
    share = parts[0].shape[-2]
    sectors = held.shape[0]
    sector = lax.axis_index("sec")
    core = lax.axis_index("rep")
    place = lax.axis_index("ops")
    live = live_rows(sizes, sector, (core ^ 1) * rows, rows, columns)
    other[...] = (arrived[0].astype(jnp.float32) * live).astype(other.dtype)
    products = left_times((left_own, left_other), (own[...], other[...]))
    totals = [None] * sectors
    for term in range(right.shape[0]):
        product = times_right(products[term], right, term)
        for step in range(sectors):
            weight = jnp.broadcast_to(mixing[step][term : term + 1, :1], (rows, columns))
            part = weight * product
            totals[step] = part if totals[step] is None else totals[step] + part
    for step in range(sectors):
        live = live_rows(sizes, sector ^ step, core * rows, rows, columns)
        held[step] = totals[step] * live
    for (steps, across), out in zip(shares, parts):
        for index, along in enumerate(steps):
            start = pl.multiple_of((place ^ along) * share, share)
            out[index] = held[across, pl.ds(start, share), :].astype(out.dtype)


def sum_kernel(indices, *refs):
    total = refs[0][indices[0]].astype(jnp.float32)
    for index, piece in zip(indices[1:], refs[1:]):
        total = total + piece[index].astype(jnp.float32)
    refs[-1][0] = total.astype(refs[-1].dtype)


def place_kernel(spots, *refs):
    pieces, half = refs[:-1], refs[-1]
    share = pieces[0].shape[1]
    place = lax.axis_index("ops")
    for (along, index), piece in zip(spots, pieces):
        start = pl.multiple_of((place ^ along) * share, share)
        half[index, pl.ds(start, share), :] = piece[0]


def left_kernel(left_own, left_other, own, other, across_own, out, across_out):
    out[...] = left_times((left_own, left_other), (own[0], other[0]))
    for step in range(across_own.shape[0]):
        across_out[step] = left_times((left_own,), (across_own[step],))


def tables_kernel(sizes_ref, pairs_ref, weights_ref, _, mixing, live):
    target = lax.axis_index("sec")
    for term in range(mixing.shape[0]):
        for step in range(mixing.shape[1]):
            weight = mixing_scalar(pairs_ref, weights_ref, term, target, target ^ step)
            mixing[term, step] = jnp.full(mixing.shape[2:], weight, jnp.float32)
    rows, columns = live.shape
    cells = live_cells(sizes_ref, target, lax.axis_index("rep") * rows, rows, columns)
    live[...] = jnp.where(cells, 1.0, 0.0)


def second_kernel(mixing, live, left_other, right, products, across_products, other, *refs):
    shares, held = refs[:-1], refs[-1]
    rows, columns = products.shape[1:]
    share = shares[0].shape[1]
    place = lax.axis_index("ops")
    total = None
    across = [left_times((left_other,), (other[step],)) for step in range(other.shape[0])]
    for term in range(right.shape[0]):
        weights = [
            jnp.broadcast_to(mixing[term, step][:1, :1], (rows, columns))
            for step in range(len(across) + 1)
        ]
        combined = weights[0] * products[term]
        for step, part in enumerate(across):
            combined = combined + weights[step + 1] * (across_products[step, term] + part[term])
        part = times_right(combined, right, term)
        total = part if total is None else total + part
    held[...] = total * live[...]
    for step, out in enumerate(shares):
        start = pl.multiple_of((place ^ step) * share, share)
        out[0] = held[pl.ds(start, share), :].astype(out.dtype)


def sums_kernel(wave_own, wave_other, sigma_own, sigma_other, out):
    step, columns = 16, wave_own.shape[1]
    sums = (jnp.zeros((step, columns), jnp.float32),) * 3
    for wave, sigma in ((wave_own, sigma_own), (wave_other, sigma_other)):

        def add_rows(block, carry):
            start = pl.multiple_of(block * step, step)
            w = wave[pl.ds(start, step), :].astype(jnp.float32)
            s = sigma[0, pl.ds(start, step), :].astype(jnp.float32)
            return (carry[0] + w * s, carry[1] + w * w, carry[2] + s * s)

        sums = lax.fori_loop(0, wave.shape[0] // step, add_rows, sums, unroll=2)
    for index, value in enumerate(sums):
        out[index] = jnp.broadcast_to(jnp.sum(value, keepdims=True), out.shape[1:])


def wave_kernel(sizes_ref, wave_own, sigma_own, *refs):
    sums, (second, factors) = refs[:-2], refs[-2:]
    rows, columns = wave_own.shape
    live_count = jnp.float32(0.0)
    for sector in range(sizes_ref.shape[0]):
        live_count = live_count + sizes_ref[sector, 0].astype(jnp.float32) * sizes_ref[
            sector, 1
        ].astype(jnp.float32)
    total = sums[0][...]
    for other in sums[1:]:
        total = total + other[...]
    correlation, norm_square, sigma_square = total[0], total[1], total[2]
    rayleigh = correlation / norm_square
    residual_square = (
        sigma_square - 2.0 * rayleigh * correlation + rayleigh * rayleigh * norm_square
    )
    residual_square = jnp.maximum(residual_square, 0.0)
    scale = 1.0 / jnp.sqrt(residual_square / live_count + epsilon)
    factors[0] = scale
    factors[1] = rayleigh * scale
    sigma_factor = jnp.broadcast_to(scale[:1, :1], (rows, columns))
    wave_factor = jnp.broadcast_to((rayleigh * scale)[:1, :1], (rows, columns))
    sigma = sigma_own[0].astype(jnp.float32)
    wave = wave_own[...].astype(jnp.float32)
    second[0] = (sigma_factor * sigma - wave_factor * wave).astype(second.dtype)


def join_kernel(order, factors, sigma_own, *refs):
    pieces, (out, held, sems) = refs[:-3], refs[-3:]
    _, share, columns = pieces[0].shape
    place = lax.axis_index("ops")
    scale = jnp.broadcast_to(factors[0][:1, :1], (share, columns))
    shift = jnp.broadcast_to(factors[1][:1, :1], (share, columns))
    copies = []
    for step, piece in zip(order, pieces):
        rows = pl.ds(pl.multiple_of((place ^ step) * share, share), share)
        moved = shift * sigma_own[0, rows, :].astype(jnp.float32)
        held[step] = scale * piece[0].astype(jnp.float32) - moved
        copies.append(pltpu.make_async_copy(held.at[step], out.at[0, rows], sems.at[step]))
        copies[-1].start()
    for copy in copies:
        copy.wait()


def partner(value, steps):
    steps = {axis: step for axis, step in steps.items() if step}
    if not steps:
        return value
    axes = tuple(steps)
    places = [()]
    for axis in axes:
        places = [place + (i,) for place in places for i in range(lax.axis_size(axis))]
    index = {place: i for i, place in enumerate(places)}
    pairs = [
        (index[tuple(i ^ steps[axis] for i, axis in zip(place, axes))], index[place])
        for place in places
    ]
    return lax.ppermute(value, axes, pairs)


def local(wavefunction, sector_sizes, left_blocks, right_blocks, sector_pairs, pair_weights):
    sectors = sector_sizes.shape[0]
    ops_count = lax.axis_size("ops")
    _, rows, columns = wavefunction.shape
    terms, side = left_blocks.shape[0], left_blocks.shape[1]
    share = rows // ops_count
    bf16, f32 = jnp.bfloat16, jnp.float32
    smem = pl.BlockSpec(memory_space=pltpu.SMEM)
    outside = pl.BlockSpec(memory_space=pltpu.HBM)
    inside = pl.BlockSpec(memory_space=pltpu.VMEM)

    def shape(*dims, dtype=bf16):
        return jax.ShapeDtypeStruct(dims, dtype)

    def call(kernel, name, out_shape, in_specs, *operands, scratch=(), vmem=16, out=inside):
        return pl.pallas_call(
            kernel,
            out_shape=out_shape,
            in_specs=list(in_specs) + [inside] * (len(operands) - len(in_specs)),
            out_specs=jax.tree.map(lambda _: out, out_shape),
            scratch_shapes=list(scratch),
            compiler_params=pltpu.CompilerParams(vmem_limit_bytes=vmem * mebibyte),
            name=name,
        )(*operands)

    def summed(name, *pieces, after=()):
        pieces = [piece if isinstance(piece, tuple) else (piece, 0) for piece in pieces]
        arrays, indices = zip(*pieces)
        return call(
            lambda *refs: sum_kernel(indices, *refs),
            name,
            shape(1, share, columns),
            [],
            *arrays,
            *after,
        )

    farthest_first = list(reversed(range(ops_count)))
    send_order = farthest_first[1:2] + farthest_first[:1] + farthest_first[2:]
    arrived = partner(wavefunction, {"rep": 1})
    left_own, left_other = call(
        load_kernel,
        "load_operators",
        [shape(terms, rows, rows), shape(terms, rows, side - rows)],
        [outside],
        left_blocks,
        scratch=[pltpu.SemaphoreType.DMA((2,))],
        vmem=51,
    )
    right = right_blocks
    pairs = jnp.swapaxes(sector_pairs, 1, 2)
    scalars = (sector_sizes, pairs, pair_weights)

    far = ops_count - 1
    direct = [(along,) for along in farthest_first[1:-1]]
    spots = [((far, 0), across) for across in range(sectors)]
    spots += [(along, across) for along in direct for across in range(sectors)]
    wave_own, mixing = call(
        first_tables_kernel,
        "tables_for_first_sigma",
        [shape(rows, columns), shape(sectors, terms, 128, dtype=f32)],
        [],
        *scalars,
        wavefunction,
        left_own,
    )
    wave_other, *rest = call(
        lambda *refs: first_kernel(spots, *refs),
        "first_sigma_terms",
        [shape(rows, columns)]
        + [
            shape(len(along), share, columns, dtype=f32 if along == (far, 0) and across == 0 else bf16)
            for along, across in spots
        ],
        [],
        sector_sizes,
        mixing,
        left_own,
        left_other,
        right,
        wave_own,
        arrived,
        scratch=[pltpu.VMEM((sectors, rows, columns), f32)],
    )
    rest = dict(zip(spots, rest))
    mixing, live = call(
        tables_kernel,
        "tables_for_second_sigma",
        [shape(terms, sectors, 8, 128, dtype=f32), shape(rows, columns, dtype=f32)],
        [smem] * 3,
        *scalars,
        wave_other,
    )
    met = [partner(rest[(far, 0), across], {"sec": across}) for across in range(sectors)]
    received = [partner(summed("sum_far_share", *met), {"ops": far})]
    nearest = ((1,), 0)
    order = [nearest] + [spot for spot in rest if spot[0] in direct and spot != nearest]
    received += [partner(rest[spot], {"ops": spot[0][0], "sec": spot[1]}) for spot in order]
    first_share = summed("sum_first_sigma", *[(piece, 1) for piece in met], *received, after=(mixing,))
    along_ops = {along: partner(first_share, {"ops": along}) for along in send_order}
    sigma_own = call(
        lambda *refs: place_kernel([(along, 0) for along in send_order], *refs),
        "place_own_sector",
        shape(1, rows, columns),
        [],
        *along_ops.values(),
    )
    sigma_other = partner(sigma_own, {"rep": 1})
    spots = [(along, across) for along in send_order for across in range(1, sectors)]
    pieces = [
        partner(first_share, {"ops": along, "sec": across})
        if along < 2
        else partner(along_ops[along], {"sec": across})
        for along, across in spots
    ]
    across_own = call(
        lambda *refs: place_kernel([(along, across - 1) for along, across in spots], *refs),
        "place_other_sectors",
        shape(sectors - 1, rows, columns),
        [],
        *pieces,
    )
    across_other = partner(across_own, {"rep": 1})

    products, across_products = call(
        left_kernel,
        "left_products",
        [
            shape(terms, rows, columns, dtype=f32),
            shape(sectors - 1, terms, rows, columns, dtype=f32),
        ],
        [],
        left_own,
        left_other,
        sigma_own,
        sigma_other,
        across_own,
    )
    shares = call(
        second_kernel,
        "second_sigma_terms",
        [shape(1, share, columns, dtype=f32)] + [shape(1, share, columns)] * (ops_count - 1),
        [],
        mixing,
        live,
        left_other,
        right,
        products,
        across_products,
        across_other,
        scratch=[pltpu.VMEM((rows, columns), f32)],
    )
    received = [partner(shares[step], {"ops": step}) for step in send_order[:-1]]
    sums = call(
        sums_kernel,
        "sums_for_rayleigh",
        shape(3, 8, 128, dtype=f32),
        [],
        wave_own,
        wave_other,
        sigma_own,
        sigma_other,
    )
    sums = [partner(sums, {"sec": step}) for step in range(sectors)]
    second_share = summed("sum_second_sigma", shares[0], *received, after=sums)
    second_wave, factors = call(
        wave_kernel,
        "second_wave",
        [shape(1, rows, columns), shape(2, 8, 128, dtype=f32)],
        [smem],
        sector_sizes,
        wave_own,
        sigma_own,
        *sums,
    )
    second_sigma = call(
        lambda *refs: join_kernel(send_order, *refs),
        "join_second_sigma",
        shape(1, rows, columns, dtype=f32),
        [],
        factors,
        sigma_own,
        *[partner(second_share, {"ops": step}) for step in send_order],
        scratch=[
            pltpu.VMEM((ops_count, share, columns), f32),
            pltpu.SemaphoreType.DMA((ops_count,)),
        ],
        out=outside,
    )
    return (second_wave, second_sigma)


def solution(mesh):
    return jax.shard_map(
        local,
        mesh=mesh,
        in_specs=(
            P(("grp", "sec"), "rep", None),
            P("grp", None),
            P(("grp", "ops"), None, None),
            P(("grp", "ops"), None, None),
            P(("grp", "ops"), None, None),
            P(("grp", "ops"), None),
        ),
        out_specs=(P(("grp", "sec"), "rep", None), P(("grp", "sec"), "rep", None)),
        check_vma=False,
    )
```

```python
import jax
import jax.numpy as jnp
from jax import lax
from jax.experimental import pallas as pl
from jax.experimental.pallas import tpu as pltpu
from jax.sharding import PartitionSpec as P

epsilon = 1e-06
mebibyte = 1024 * 1024


def mixing_scalar(pairs_ref, weights_ref, term, target, source):
    value = jnp.float32(0.0)
    for pair in range(weights_ref.shape[1]):
        hit = (pairs_ref[term, 1, pair] == target) & (pairs_ref[term, 0, pair] == source)
        value = value + jnp.where(hit, weights_ref[term, pair], jnp.float32(0.0))
    return value


def live_cells(sizes_ref, sector, row_start, rows, columns):
    row = row_start + lax.broadcasted_iota(jnp.int32, (rows, columns), 0)
    column = lax.broadcasted_iota(jnp.int32, (rows, columns), 1)
    return (row < sizes_ref[sector, 0]) & (column < sizes_ref[sector, 1])


def masked(values, live):
    return jnp.where(live, values.astype(jnp.float32), 0.0).astype(values.dtype)


def left_times(lefts, blocks):
    total = None
    for left, block in zip(lefts, blocks):
        terms, rows, depth = left.shape
        stacked = left[...].reshape(terms * rows, depth)
        part = jnp.dot(stacked, block, preferred_element_type=jnp.float32)
        total = part if total is None else total + part
    return total.reshape(terms, rows, -1)


def times_right(values, right, term):
    return lax.dot_general(
        values.astype(jnp.bfloat16),
        right[term],
        (((1,), (1,)), ((), ())),
        preferred_element_type=jnp.float32,
    )


def load_kernel(left_ref, left_own, left_other, sems):
    rows = left_own.shape[1]
    core = lax.axis_index("rep")
    copies = []
    for index, (half, place) in enumerate(((left_own, core), (left_other, core ^ 1))):
        mine = pl.ds(pl.multiple_of(core * rows, rows), rows)
        columns = pl.ds(pl.multiple_of(place * rows, rows), rows)
        copies.append(pltpu.make_async_copy(left_ref.at[:, mine, columns], half, sems.at[index]))
    for copy in copies:
        copy.start()
    for copy in copies:
        copy.wait()


def live_rows(sizes, sector, row_start, rows, columns):
    bounds = sizes[pl.ds(sector, 1), :]
    row = row_start + lax.broadcasted_iota(jnp.int32, (rows, columns), 0)
    column = lax.broadcasted_iota(jnp.int32, (rows, columns), 1)
    inside = (row < bounds[:, 0:1]) & (column < bounds[:, 1:2])
    return jnp.where(inside, 1.0, 0.0)


def first_tables_kernel(sizes, pairs, weights, wave, _, own, mixing):
    rows, columns = own.shape
    sector = lax.axis_index("sec")
    live = live_rows(sizes, sector, lax.axis_index("rep") * rows, rows, columns)
    own[...] = (wave[0].astype(jnp.float32) * live).astype(own.dtype)
    source, target = pairs[:, 0, :], pairs[:, 1, :]
    for step in range(mixing.shape[0]):
        hits = (source == sector) & (target == (sector ^ step))
        total = jnp.sum(jnp.where(hits, weights[...], 0.0), axis=1, keepdims=True)
        mixing[step] = jnp.broadcast_to(total, mixing.shape[1:])


def first_kernel(shares, *refs):
    sizes, mixing, left_own, left_other, right, own, arrived = refs[:7]
    other, *parts = refs[7:-1]
    held = refs[-1]
    rows, columns = own.shape
    share = parts[0].shape[-2]
    sectors = held.shape[0]
    sector = lax.axis_index("sec")
    core = lax.axis_index("rep")
    place = lax.axis_index("ops")
    live = live_rows(sizes, sector, (core ^ 1) * rows, rows, columns)
    other[...] = (arrived[0].astype(jnp.float32) * live).astype(other.dtype)
    products = left_times((left_own, left_other), (own[...], other[...]))
    totals = [None] * sectors
    for term in range(right.shape[0]):
        product = times_right(products[term], right, term)
        for step in range(sectors):
            weight = jnp.broadcast_to(mixing[step][term : term + 1, :1], (rows, columns))
            part = weight * product
            totals[step] = part if totals[step] is None else totals[step] + part
    for step in range(sectors):
        live = live_rows(sizes, sector ^ step, core * rows, rows, columns)
        held[step] = totals[step] * live
    for (steps, across), out in zip(shares, parts):
        for index, along in enumerate(steps):
            start = pl.multiple_of((place ^ along) * share, share)
            out[index] = held[across, pl.ds(start, share), :].astype(out.dtype)


def sum_kernel(indices, *refs):
    total = refs[0][indices[0]].astype(jnp.float32)
    for index, piece in zip(indices[1:], refs[1:]):
        total = total + piece[index].astype(jnp.float32)
    refs[-1][0] = total.astype(refs[-1].dtype)


def place_kernel(spots, *refs):
    pieces, half = refs[:-1], refs[-1]
    share = pieces[0].shape[1]
    place = lax.axis_index("ops")
    for (along, index), piece in zip(spots, pieces):
        start = pl.multiple_of((place ^ along) * share, share)
        half[index, pl.ds(start, share), :] = piece[0]


def left_kernel(left_own, left_other, own, other, across_own, out, across_out):
    out[...] = left_times((left_own, left_other), (own[0], other[0]))
    for step in range(across_own.shape[0]):
        across_out[step] = left_times((left_own,), (across_own[step],))


def tables_kernel(sizes_ref, pairs_ref, weights_ref, _, mixing, live):
    target = lax.axis_index("sec")
    for term in range(mixing.shape[0]):
        for step in range(mixing.shape[1]):
            weight = mixing_scalar(pairs_ref, weights_ref, term, target, target ^ step)
            mixing[term, step] = jnp.full(mixing.shape[2:], weight, jnp.float32)
    rows, columns = live.shape
    cells = live_cells(sizes_ref, target, lax.axis_index("rep") * rows, rows, columns)
    live[...] = jnp.where(cells, 1.0, 0.0)


def second_kernel(mixing, live, left_other, right, products, across_products, other, *refs):
    shares, held = refs[:-1], refs[-1]
    rows, columns = products.shape[1:]
    share = shares[0].shape[1]
    place = lax.axis_index("ops")
    total = None
    across = [left_times((left_other,), (other[step],)) for step in range(other.shape[0])]
    for term in range(right.shape[0]):
        weights = [
            jnp.broadcast_to(mixing[term, step][:1, :1], (rows, columns))
            for step in range(len(across) + 1)
        ]
        combined = weights[0] * products[term]
        for step, part in enumerate(across):
            combined = combined + weights[step + 1] * (across_products[step, term] + part[term])
        part = times_right(combined, right, term)
        total = part if total is None else total + part
    held[...] = total * live[...]
    for step, out in enumerate(shares):
        start = pl.multiple_of((place ^ step) * share, share)
        out[0] = held[pl.ds(start, share), :].astype(out.dtype)


def sums_kernel(wave_own, wave_other, sigma_own, sigma_other, out):
    step, columns = 16, wave_own.shape[1]
    sums = (jnp.zeros((step, columns), jnp.float32),) * 3
    for wave, sigma in ((wave_own, sigma_own), (wave_other, sigma_other)):

        def add_rows(block, carry):
            start = pl.multiple_of(block * step, step)
            w = wave[pl.ds(start, step), :].astype(jnp.float32)
            s = sigma[0, pl.ds(start, step), :].astype(jnp.float32)
            return (carry[0] + w * s, carry[1] + w * w, carry[2] + s * s)

        sums = lax.fori_loop(0, wave.shape[0] // step, add_rows, sums, unroll=2)
    for index, value in enumerate(sums):
        out[index] = jnp.broadcast_to(jnp.sum(value, keepdims=True), out.shape[1:])


def wave_kernel(sizes_ref, wave_own, sigma_own, *refs):
    sums, (second, factors) = refs[:-2], refs[-2:]
    rows, columns = wave_own.shape
    live_count = jnp.float32(0.0)
    for sector in range(sizes_ref.shape[0]):
        live_count = live_count + sizes_ref[sector, 0].astype(jnp.float32) * sizes_ref[
            sector, 1
        ].astype(jnp.float32)
    total = sums[0][...]
    for other in sums[1:]:
        total = total + other[...]
    correlation, norm_square, sigma_square = total[0], total[1], total[2]
    rayleigh = correlation / norm_square
    residual_square = (
        sigma_square - 2.0 * rayleigh * correlation + rayleigh * rayleigh * norm_square
    )
    residual_square = jnp.maximum(residual_square, 0.0)
    scale = 1.0 / jnp.sqrt(residual_square / live_count + epsilon)
    factors[0] = scale
    factors[1] = rayleigh * scale
    sigma_factor = jnp.broadcast_to(scale[:1, :1], (rows, columns))
    wave_factor = jnp.broadcast_to((rayleigh * scale)[:1, :1], (rows, columns))
    sigma = sigma_own[0].astype(jnp.float32)
    wave = wave_own[...].astype(jnp.float32)
    second[0] = (sigma_factor * sigma - wave_factor * wave).astype(second.dtype)


def join_kernel(order, factors, sigma_own, *refs):
    pieces, (out, held, sems) = refs[:-3], refs[-3:]
    _, share, columns = pieces[0].shape
    place = lax.axis_index("ops")
    scale = jnp.broadcast_to(factors[0][:1, :1], (share, columns))
    shift = jnp.broadcast_to(factors[1][:1, :1], (share, columns))
    copies = []
    for step, piece in zip(order, pieces):
        rows = pl.ds(pl.multiple_of((place ^ step) * share, share), share)
        moved = shift * sigma_own[0, rows, :].astype(jnp.float32)
        held[step] = scale * piece[0].astype(jnp.float32) - moved
        copies.append(pltpu.make_async_copy(held.at[step], out.at[0, rows], sems.at[step]))
        copies[-1].start()
    for copy in copies:
        copy.wait()


def partner(value, steps):
    steps = {axis: step for axis, step in steps.items() if step}
    if not steps:
        return value
    axes = tuple(steps)
    places = [()]
    for axis in axes:
        places = [place + (i,) for place in places for i in range(lax.axis_size(axis))]
    index = {place: i for i, place in enumerate(places)}
    pairs = [
        (index[tuple(i ^ steps[axis] for i, axis in zip(place, axes))], index[place])
        for place in places
    ]
    return lax.ppermute(value, axes, pairs)


def local(wavefunction, sector_sizes, left_blocks, right_blocks, sector_pairs, pair_weights):
    sectors = sector_sizes.shape[0]
    ops_count = lax.axis_size("ops")
    _, rows, columns = wavefunction.shape
    terms, side = left_blocks.shape[0], left_blocks.shape[1]
    share = rows // ops_count
    bf16, f32 = jnp.bfloat16, jnp.float32
    smem = pl.BlockSpec(memory_space=pltpu.SMEM)
    outside = pl.BlockSpec(memory_space=pltpu.HBM)
    inside = pl.BlockSpec(memory_space=pltpu.VMEM)

    def shape(*dims, dtype=bf16):
        return jax.ShapeDtypeStruct(dims, dtype)

    def call(kernel, name, out_shape, in_specs, *operands, scratch=(), vmem=16, out=inside):
        return pl.pallas_call(
            kernel,
            out_shape=out_shape,
            in_specs=list(in_specs) + [inside] * (len(operands) - len(in_specs)),
            out_specs=jax.tree.map(lambda _: out, out_shape),
            scratch_shapes=list(scratch),
            compiler_params=pltpu.CompilerParams(vmem_limit_bytes=vmem * mebibyte),
            name=name,
        )(*operands)

    def summed(name, *pieces, after=()):
        pieces = [piece if isinstance(piece, tuple) else (piece, 0) for piece in pieces]
        arrays, indices = zip(*pieces)
        return call(
            lambda *refs: sum_kernel(indices, *refs),
            name,
            shape(1, share, columns),
            [],
            *arrays,
            *after,
        )

    farthest_first = list(reversed(range(ops_count)))
    send_order = farthest_first[1:2] + farthest_first[:1] + farthest_first[2:]
    arrived = partner(wavefunction, {"rep": 1})
    left_own, left_other = call(
        load_kernel,
        "load_operators",
        [shape(terms, rows, rows), shape(terms, rows, side - rows)],
        [outside],
        left_blocks,
        scratch=[pltpu.SemaphoreType.DMA((2,))],
        vmem=51,
    )
    right = right_blocks
    pairs = jnp.swapaxes(sector_pairs, 1, 2)
    scalars = (sector_sizes, pairs, pair_weights)

    far = ops_count - 1
    direct = [(along,) for along in farthest_first[1:-1]]
    spots = [((far, 0), across) for across in range(sectors)]
    spots += [(along, across) for along in direct for across in range(sectors)]
    wave_own, mixing = call(
        first_tables_kernel,
        "tables_for_first_sigma",
        [shape(rows, columns), shape(sectors, terms, 128, dtype=f32)],
        [],
        *scalars,
        wavefunction,
        left_own,
    )
    wave_other, *rest = call(
        lambda *refs: first_kernel(spots, *refs),
        "first_sigma_terms",
        [shape(rows, columns)]
        + [
            shape(len(along), share, columns, dtype=f32 if along == (far, 0) and across == 0 else bf16)
            for along, across in spots
        ],
        [],
        sector_sizes,
        mixing,
        left_own,
        left_other,
        right,
        wave_own,
        arrived,
        scratch=[pltpu.VMEM((sectors, rows, columns), f32)],
    )
    rest = dict(zip(spots, rest))
    mixing, live = call(
        tables_kernel,
        "tables_for_second_sigma",
        [shape(terms, sectors, 8, 128, dtype=f32), shape(rows, columns, dtype=f32)],
        [smem] * 3,
        *scalars,
        wave_other,
    )
    met = [partner(rest[(far, 0), across], {"sec": across}) for across in range(sectors)]
    received = [partner(summed("sum_far_share", *met), {"ops": far})]
    nearest = ((1,), 0)
    order = [nearest] + [spot for spot in rest if spot[0] in direct and spot != nearest]
    received += [partner(rest[spot], {"ops": spot[0][0], "sec": spot[1]}) for spot in order]
    first_share = summed("sum_first_sigma", *[(piece, 1) for piece in met], *received, after=(mixing,))
    along_ops = {along: partner(first_share, {"ops": along}) for along in send_order}
    sigma_own = call(
        lambda *refs: place_kernel([(along, 0) for along in send_order], *refs),
        "place_own_sector",
        shape(1, rows, columns),
        [],
        *along_ops.values(),
    )
    sigma_other = partner(sigma_own, {"rep": 1})
    spots = [(along, across) for along in send_order for across in range(1, sectors)]
    pieces = [
        partner(first_share, {"ops": along, "sec": across})
        if along < 2
        else partner(along_ops[along], {"sec": across})
        for along, across in spots
    ]
    across_own = call(
        lambda *refs: place_kernel([(along, across - 1) for along, across in spots], *refs),
        "place_other_sectors",
        shape(sectors - 1, rows, columns),
        [],
        *pieces,
    )
    across_other = partner(across_own, {"rep": 1})

    products, across_products = call(
        left_kernel,
        "left_products",
        [
            shape(terms, rows, columns, dtype=f32),
            shape(sectors - 1, terms, rows, columns, dtype=f32),
        ],
        [],
        left_own,
        left_other,
        sigma_own,
        sigma_other,
        across_own,
    )
    shares = call(
        second_kernel,
        "second_sigma_terms",
        [shape(1, share, columns, dtype=f32)] + [shape(1, share, columns)] * (ops_count - 1),
        [],
        mixing,
        live,
        left_other,
        right,
        products,
        across_products,
        across_other,
        scratch=[pltpu.VMEM((rows, columns), f32)],
    )
    received = [partner(shares[step], {"ops": step}) for step in farthest_first[:-1]]
    sums = call(
        sums_kernel,
        "sums_for_rayleigh",
        shape(3, 8, 128, dtype=f32),
        [],
        wave_own,
        wave_other,
        sigma_own,
        sigma_other,
    )
    sums = [partner(sums, {"sec": step}) for step in range(sectors)]
    second_share = summed("sum_second_sigma", shares[0], *received, after=sums)
    second_wave, factors = call(
        wave_kernel,
        "second_wave",
        [shape(1, rows, columns), shape(2, 8, 128, dtype=f32)],
        [smem],
        sector_sizes,
        wave_own,
        sigma_own,
        *sums,
    )
    second_sigma = call(
        lambda *refs: join_kernel(farthest_first, *refs),
        "join_second_sigma",
        shape(1, rows, columns, dtype=f32),
        [],
        factors,
        sigma_own,
        *[partner(second_share, {"ops": step}) for step in farthest_first],
        scratch=[
            pltpu.VMEM((ops_count, share, columns), f32),
            pltpu.SemaphoreType.DMA((ops_count,)),
        ],
        out=outside,
    )
    return (second_wave, second_sigma)


def solution(mesh):
    return jax.shard_map(
        local,
        mesh=mesh,
        in_specs=(
            P(("grp", "sec"), "rep", None),
            P("grp", None),
            P(("grp", "ops"), None, None),
            P(("grp", "ops"), None, None),
            P(("grp", "ops"), None, None),
            P(("grp", "ops"), None),
        ),
        out_specs=(P(("grp", "sec"), "rep", None), P(("grp", "sec"), "rep", None)),
        check_vma=False,
    )
```

```python
import jax
import jax.numpy as jnp
from jax import lax
from jax.experimental import pallas as pl
from jax.experimental.pallas import tpu as pltpu
from jax.sharding import PartitionSpec as P

epsilon = 1e-06
mebibyte = 1024 * 1024


def mixing_scalar(pairs_ref, weights_ref, term, target, source):
    value = jnp.float32(0.0)
    for pair in range(weights_ref.shape[1]):
        hit = (pairs_ref[term, 1, pair] == target) & (pairs_ref[term, 0, pair] == source)
        value = value + jnp.where(hit, weights_ref[term, pair], jnp.float32(0.0))
    return value


def live_cells(sizes_ref, sector, row_start, rows, columns):
    row = row_start + lax.broadcasted_iota(jnp.int32, (rows, columns), 0)
    column = lax.broadcasted_iota(jnp.int32, (rows, columns), 1)
    return (row < sizes_ref[sector, 0]) & (column < sizes_ref[sector, 1])


def masked(values, live):
    return jnp.where(live, values.astype(jnp.float32), 0.0).astype(values.dtype)


def left_times(lefts, blocks):
    total = None
    for left, block in zip(lefts, blocks):
        terms, rows, depth = left.shape
        stacked = left[...].reshape(terms * rows, depth)
        part = jnp.dot(stacked, block, preferred_element_type=jnp.float32)
        total = part if total is None else total + part
    return total.reshape(terms, rows, -1)


def times_right(values, right, term):
    return lax.dot_general(
        values.astype(jnp.bfloat16),
        right[term],
        (((1,), (1,)), ((), ())),
        preferred_element_type=jnp.float32,
    )


def load_kernel(left_ref, left_own, left_other, sems):
    rows = left_own.shape[1]
    core = lax.axis_index("rep")
    copies = []
    for index, (half, place) in enumerate(((left_own, core), (left_other, core ^ 1))):
        mine = pl.ds(pl.multiple_of(core * rows, rows), rows)
        columns = pl.ds(pl.multiple_of(place * rows, rows), rows)
        copies.append(pltpu.make_async_copy(left_ref.at[:, mine, columns], half, sems.at[index]))
    for copy in copies:
        copy.start()
    for copy in copies:
        copy.wait()


def live_rows(sizes, sector, row_start, rows, columns):
    bounds = sizes[pl.ds(sector, 1), :]
    row = row_start + lax.broadcasted_iota(jnp.int32, (rows, columns), 0)
    column = lax.broadcasted_iota(jnp.int32, (rows, columns), 1)
    inside = (row < bounds[:, 0:1]) & (column < bounds[:, 1:2])
    return jnp.where(inside, 1.0, 0.0)


def first_tables_kernel(sizes, pairs, weights, wave, _, own, mixing):
    rows, columns = own.shape
    sector = lax.axis_index("sec")
    live = live_rows(sizes, sector, lax.axis_index("rep") * rows, rows, columns)
    own[...] = (wave[0].astype(jnp.float32) * live).astype(own.dtype)
    source, target = pairs[:, 0, :], pairs[:, 1, :]
    for step in range(mixing.shape[0]):
        hits = (source == sector) & (target == (sector ^ step))
        total = jnp.sum(jnp.where(hits, weights[...], 0.0), axis=1, keepdims=True)
        mixing[step] = jnp.broadcast_to(total, mixing.shape[1:])


def first_kernel(shares, *refs):
    sizes, mixing, left_own, left_other, right, own, arrived = refs[:7]
    other, *parts = refs[7:-1]
    held = refs[-1]
    rows, columns = own.shape
    share = parts[0].shape[-2]
    sectors = held.shape[0]
    sector = lax.axis_index("sec")
    core = lax.axis_index("rep")
    place = lax.axis_index("ops")
    live = live_rows(sizes, sector, (core ^ 1) * rows, rows, columns)
    other[...] = (arrived[0].astype(jnp.float32) * live).astype(other.dtype)
    products = left_times((left_own, left_other), (own[...], other[...]))
    totals = [None] * sectors
    for term in range(right.shape[0]):
        product = times_right(products[term], right, term)
        for step in range(sectors):
            weight = jnp.broadcast_to(mixing[step][term : term + 1, :1], (rows, columns))
            part = weight * product
            totals[step] = part if totals[step] is None else totals[step] + part
    for step in range(sectors):
        live = live_rows(sizes, sector ^ step, core * rows, rows, columns)
        held[step] = totals[step] * live
    for (steps, across), out in zip(shares, parts):
        for index, along in enumerate(steps):
            start = pl.multiple_of((place ^ along) * share, share)
            out[index] = held[across, pl.ds(start, share), :].astype(out.dtype)


def sum_kernel(indices, *refs):
    total = refs[0][indices[0]].astype(jnp.float32)
    for index, piece in zip(indices[1:], refs[1:]):
        total = total + piece[index].astype(jnp.float32)
    refs[-1][0] = total.astype(refs[-1].dtype)


def place_kernel(spots, *refs):
    pieces, half = refs[:-1], refs[-1]
    share = pieces[0].shape[1]
    place = lax.axis_index("ops")
    for (along, index), piece in zip(spots, pieces):
        start = pl.multiple_of((place ^ along) * share, share)
        half[index, pl.ds(start, share), :] = piece[0]


def left_kernel(left_own, left_other, own, other, across_own, out, across_out):
    out[...] = left_times((left_own, left_other), (own[0], other[0]))
    for step in range(across_own.shape[0]):
        across_out[step] = left_times((left_own,), (across_own[step],))


def tables_kernel(sizes_ref, pairs_ref, weights_ref, _, mixing, live):
    target = lax.axis_index("sec")
    for term in range(mixing.shape[0]):
        for step in range(mixing.shape[1]):
            weight = mixing_scalar(pairs_ref, weights_ref, term, target, target ^ step)
            mixing[term, step] = jnp.full(mixing.shape[2:], weight, jnp.float32)
    rows, columns = live.shape
    cells = live_cells(sizes_ref, target, lax.axis_index("rep") * rows, rows, columns)
    live[...] = jnp.where(cells, 1.0, 0.0)


def second_kernel(mixing, live, left_other, right, products, across_products, other, *refs):
    shares, held = refs[:-1], refs[-1]
    rows, columns = products.shape[1:]
    share = shares[0].shape[1]
    place = lax.axis_index("ops")
    total = None
    across = [left_times((left_other,), (other[step],)) for step in range(other.shape[0])]
    for term in range(right.shape[0]):
        weights = [
            jnp.broadcast_to(mixing[term, step][:1, :1], (rows, columns))
            for step in range(len(across) + 1)
        ]
        combined = weights[0] * products[term]
        for step, part in enumerate(across):
            combined = combined + weights[step + 1] * (across_products[step, term] + part[term])
        part = times_right(combined, right, term)
        total = part if total is None else total + part
    held[...] = total * live[...]
    for step, out in enumerate(shares):
        start = pl.multiple_of((place ^ step) * share, share)
        out[0] = held[pl.ds(start, share), :].astype(out.dtype)


def sums_kernel(wave_own, wave_other, sigma_own, sigma_other, out):
    step, columns = 16, wave_own.shape[1]
    sums = (jnp.zeros((step, columns), jnp.float32),) * 3
    for wave, sigma in ((wave_own, sigma_own), (wave_other, sigma_other)):

        def add_rows(block, carry):
            start = pl.multiple_of(block * step, step)
            w = wave[pl.ds(start, step), :].astype(jnp.float32)
            s = sigma[0, pl.ds(start, step), :].astype(jnp.float32)
            return (carry[0] + w * s, carry[1] + w * w, carry[2] + s * s)

        sums = lax.fori_loop(0, wave.shape[0] // step, add_rows, sums, unroll=2)
    for index, value in enumerate(sums):
        out[index] = jnp.broadcast_to(jnp.sum(value, keepdims=True), out.shape[1:])


def wave_kernel(sizes_ref, wave_own, sigma_own, *refs):
    sums, (second, factors) = refs[:-2], refs[-2:]
    rows, columns = wave_own.shape
    live_count = jnp.float32(0.0)
    for sector in range(sizes_ref.shape[0]):
        live_count = live_count + sizes_ref[sector, 0].astype(jnp.float32) * sizes_ref[
            sector, 1
        ].astype(jnp.float32)
    total = sums[0][...]
    for other in sums[1:]:
        total = total + other[...]
    correlation, norm_square, sigma_square = total[0], total[1], total[2]
    rayleigh = correlation / norm_square
    residual_square = (
        sigma_square - 2.0 * rayleigh * correlation + rayleigh * rayleigh * norm_square
    )
    residual_square = jnp.maximum(residual_square, 0.0)
    scale = 1.0 / jnp.sqrt(residual_square / live_count + epsilon)
    factors[0] = scale
    factors[1] = rayleigh * scale
    sigma_factor = jnp.broadcast_to(scale[:1, :1], (rows, columns))
    wave_factor = jnp.broadcast_to((rayleigh * scale)[:1, :1], (rows, columns))
    sigma = sigma_own[0].astype(jnp.float32)
    wave = wave_own[...].astype(jnp.float32)
    second[0] = (sigma_factor * sigma - wave_factor * wave).astype(second.dtype)


def join_kernel(order, factors, sigma_own, *refs):
    pieces, (out, held, sems) = refs[:-3], refs[-3:]
    _, share, columns = pieces[0].shape
    place = lax.axis_index("ops")
    scale = jnp.broadcast_to(factors[0][:1, :1], (share, columns))
    shift = jnp.broadcast_to(factors[1][:1, :1], (share, columns))
    copies = []
    for step, piece in zip(order, pieces):
        rows = pl.ds(pl.multiple_of((place ^ step) * share, share), share)
        moved = shift * sigma_own[0, rows, :].astype(jnp.float32)
        held[step] = scale * piece[0].astype(jnp.float32) - moved
        copies.append(pltpu.make_async_copy(held.at[step], out.at[0, rows], sems.at[step]))
        copies[-1].start()
    for copy in copies:
        copy.wait()


def partner(value, steps):
    steps = {axis: step for axis, step in steps.items() if step}
    if not steps:
        return value
    axes = tuple(steps)
    places = [()]
    for axis in axes:
        places = [place + (i,) for place in places for i in range(lax.axis_size(axis))]
    index = {place: i for i, place in enumerate(places)}
    pairs = [
        (index[tuple(i ^ steps[axis] for i, axis in zip(place, axes))], index[place])
        for place in places
    ]
    return lax.ppermute(value, axes, pairs)


def local(wavefunction, sector_sizes, left_blocks, right_blocks, sector_pairs, pair_weights):
    sectors = sector_sizes.shape[0]
    ops_count = lax.axis_size("ops")
    _, rows, columns = wavefunction.shape
    terms, side = left_blocks.shape[0], left_blocks.shape[1]
    share = rows // ops_count
    bf16, f32 = jnp.bfloat16, jnp.float32
    smem = pl.BlockSpec(memory_space=pltpu.SMEM)
    outside = pl.BlockSpec(memory_space=pltpu.HBM)
    inside = pl.BlockSpec(memory_space=pltpu.VMEM)

    def shape(*dims, dtype=bf16):
        return jax.ShapeDtypeStruct(dims, dtype)

    def call(kernel, name, out_shape, in_specs, *operands, scratch=(), vmem=16, out=inside):
        return pl.pallas_call(
            kernel,
            out_shape=out_shape,
            in_specs=list(in_specs) + [inside] * (len(operands) - len(in_specs)),
            out_specs=jax.tree.map(lambda _: out, out_shape),
            scratch_shapes=list(scratch),
            compiler_params=pltpu.CompilerParams(vmem_limit_bytes=vmem * mebibyte),
            name=name,
        )(*operands)

    def summed(name, *pieces, after=()):
        pieces = [piece if isinstance(piece, tuple) else (piece, 0) for piece in pieces]
        arrays, indices = zip(*pieces)
        return call(
            lambda *refs: sum_kernel(indices, *refs),
            name,
            shape(1, share, columns),
            [],
            *arrays,
            *after,
        )

    farthest_first = list(reversed(range(ops_count)))
    send_order = farthest_first[1:2] + farthest_first[:1] + farthest_first[2:]
    arrived = partner(wavefunction, {"rep": 1})
    left_own, left_other = call(
        load_kernel,
        "load_operators",
        [shape(terms, rows, rows), shape(terms, rows, side - rows)],
        [outside],
        left_blocks,
        scratch=[pltpu.SemaphoreType.DMA((2,))],
        vmem=51,
    )
    right = right_blocks
    pairs = jnp.swapaxes(sector_pairs, 1, 2)
    scalars = (sector_sizes, pairs, pair_weights)

    far = ops_count - 1
    direct = [(along,) for along in farthest_first[1:-1]]
    spots = [((far, 0), across) for across in range(sectors)]
    spots += [(along, across) for along in direct for across in range(sectors)]
    wave_own, mixing = call(
        first_tables_kernel,
        "tables_for_first_sigma",
        [shape(rows, columns), shape(sectors, terms, 128, dtype=f32)],
        [],
        *scalars,
        wavefunction,
        left_own,
    )
    wave_other, *rest = call(
        lambda *refs: first_kernel(spots, *refs),
        "first_sigma_terms",
        [shape(rows, columns)]
        + [
            shape(len(along), share, columns, dtype=f32 if along == (far, 0) and across == 0 else bf16)
            for along, across in spots
        ],
        [],
        sector_sizes,
        mixing,
        left_own,
        left_other,
        right,
        wave_own,
        arrived,
        scratch=[pltpu.VMEM((sectors, rows, columns), f32)],
    )
    rest = dict(zip(spots, rest))
    mixing, live = call(
        tables_kernel,
        "tables_for_second_sigma",
        [shape(terms, sectors, 8, 128, dtype=f32), shape(rows, columns, dtype=f32)],
        [smem] * 3,
        *scalars,
        wave_other,
    )
    met = [partner(rest[(far, 0), across], {"sec": across}) for across in range(sectors)]
    received = [partner(summed("sum_far_share", *met), {"ops": far})]
    nearest = ((1,), 0)
    order = [nearest] + [spot for spot in rest if spot[0] in direct and spot != nearest]
    received += [partner(rest[spot], {"ops": spot[0][0], "sec": spot[1]}) for spot in order]
    first_share = summed("sum_first_sigma", *[(piece, 1) for piece in met], *received, after=(mixing,))
    along_ops = {along: partner(first_share, {"ops": along}) for along in send_order}
    sigma_own = call(
        lambda *refs: place_kernel([(along, 0) for along in send_order], *refs),
        "place_own_sector",
        shape(1, rows, columns),
        [],
        *along_ops.values(),
    )
    sigma_other = partner(sigma_own, {"rep": 1})
    spots = [(along, across) for along in send_order for across in range(1, sectors)]
    beside = {across: partner(first_share, {"sec": across}) for across in range(1, sectors)}
    handed = dict(along_ops)
    handed[send_order[0]] = summed("hand_on", along_ops[send_order[0]], after=beside.values())
    pieces = [
        beside[across]
        if along == 0
        else partner(first_share, {"ops": along, "sec": across})
        if along == 1
        else partner(handed[along], {"sec": across})
        for along, across in spots
    ]
    across_own = call(
        lambda *refs: place_kernel([(along, across - 1) for along, across in spots], *refs),
        "place_other_sectors",
        shape(sectors - 1, rows, columns),
        [],
        *pieces,
    )
    across_other = partner(across_own, {"rep": 1})

    products, across_products = call(
        left_kernel,
        "left_products",
        [
            shape(terms, rows, columns, dtype=f32),
            shape(sectors - 1, terms, rows, columns, dtype=f32),
        ],
        [],
        left_own,
        left_other,
        sigma_own,
        sigma_other,
        across_own,
    )
    shares = call(
        second_kernel,
        "second_sigma_terms",
        [shape(1, share, columns, dtype=f32)] + [shape(1, share, columns)] * (ops_count - 1),
        [],
        mixing,
        live,
        left_other,
        right,
        products,
        across_products,
        across_other,
        scratch=[pltpu.VMEM((rows, columns), f32)],
    )
    received = [partner(shares[step], {"ops": step}) for step in farthest_first[:-1]]
    sums = call(
        sums_kernel,
        "sums_for_rayleigh",
        shape(3, 8, 128, dtype=f32),
        [],
        wave_own,
        wave_other,
        sigma_own,
        sigma_other,
    )
    sums = [partner(sums, {"sec": step}) for step in range(sectors)]
    second_share = summed("sum_second_sigma", shares[0], *received, after=sums)
    second_wave, factors = call(
        wave_kernel,
        "second_wave",
        [shape(1, rows, columns), shape(2, 8, 128, dtype=f32)],
        [smem],
        sector_sizes,
        wave_own,
        sigma_own,
        *sums,
    )
    second_sigma = call(
        lambda *refs: join_kernel(farthest_first, *refs),
        "join_second_sigma",
        shape(1, rows, columns, dtype=f32),
        [],
        factors,
        sigma_own,
        *[partner(second_share, {"ops": step}) for step in farthest_first],
        scratch=[
            pltpu.VMEM((ops_count, share, columns), f32),
            pltpu.SemaphoreType.DMA((ops_count,)),
        ],
        out=outside,
    )
    return (second_wave, second_sigma)


def solution(mesh):
    return jax.shard_map(
        local,
        mesh=mesh,
        in_specs=(
            P(("grp", "sec"), "rep", None),
            P("grp", None),
            P(("grp", "ops"), None, None),
            P(("grp", "ops"), None, None),
            P(("grp", "ops"), None, None),
            P(("grp", "ops"), None),
        ),
        out_specs=(P(("grp", "sec"), "rep", None), P(("grp", "sec"), "rep", None)),
        check_vma=False,
    )
```

```python
import jax
import jax.numpy as jnp
from jax import lax
from jax.experimental import pallas as pl
from jax.experimental.pallas import tpu as pltpu
from jax.sharding import PartitionSpec as P

epsilon = 1e-06
mebibyte = 1024 * 1024


def mixing_scalar(pairs_ref, weights_ref, term, target, source):
    value = jnp.float32(0.0)
    for pair in range(weights_ref.shape[1]):
        hit = (pairs_ref[term, 1, pair] == target) & (pairs_ref[term, 0, pair] == source)
        value = value + jnp.where(hit, weights_ref[term, pair], jnp.float32(0.0))
    return value


def live_cells(sizes_ref, sector, row_start, rows, columns):
    row = row_start + lax.broadcasted_iota(jnp.int32, (rows, columns), 0)
    column = lax.broadcasted_iota(jnp.int32, (rows, columns), 1)
    return (row < sizes_ref[sector, 0]) & (column < sizes_ref[sector, 1])


def masked(values, live):
    return jnp.where(live, values.astype(jnp.float32), 0.0).astype(values.dtype)


def left_times(lefts, blocks):
    total = None
    for left, block in zip(lefts, blocks):
        terms, rows, depth = left.shape
        stacked = left[...].reshape(terms * rows, depth)
        part = jnp.dot(stacked, block, preferred_element_type=jnp.float32)
        total = part if total is None else total + part
    return total.reshape(terms, rows, -1)


def times_right(values, right, term):
    return lax.dot_general(
        values.astype(jnp.bfloat16),
        right[term],
        (((1,), (1,)), ((), ())),
        preferred_element_type=jnp.float32,
    )


def load_kernel(left_ref, left_own, left_other, sems):
    rows = left_own.shape[1]
    core = lax.axis_index("rep")
    copies = []
    for index, (half, place) in enumerate(((left_own, core), (left_other, core ^ 1))):
        mine = pl.ds(pl.multiple_of(core * rows, rows), rows)
        columns = pl.ds(pl.multiple_of(place * rows, rows), rows)
        copies.append(pltpu.make_async_copy(left_ref.at[:, mine, columns], half, sems.at[index]))
    for copy in copies:
        copy.start()
    for copy in copies:
        copy.wait()


def live_rows(sizes, sector, row_start, rows, columns):
    bounds = sizes[pl.ds(sector, 1), :]
    row = row_start + lax.broadcasted_iota(jnp.int32, (rows, columns), 0)
    column = lax.broadcasted_iota(jnp.int32, (rows, columns), 1)
    inside = (row < bounds[:, 0:1]) & (column < bounds[:, 1:2])
    return jnp.where(inside, 1.0, 0.0)


def first_tables_kernel(sizes, pairs, weights, wave, _, own, mixing):
    rows, columns = own.shape
    sector = lax.axis_index("sec")
    live = live_rows(sizes, sector, lax.axis_index("rep") * rows, rows, columns)
    own[...] = (wave[0].astype(jnp.float32) * live).astype(own.dtype)
    source, target = pairs[:, 0, :], pairs[:, 1, :]
    for step in range(mixing.shape[0]):
        hits = (source == sector) & (target == (sector ^ step))
        total = jnp.sum(jnp.where(hits, weights[...], 0.0), axis=1, keepdims=True)
        mixing[step] = jnp.broadcast_to(total, mixing.shape[1:])


def first_kernel(shares, *refs):
    sizes, mixing, left_own, left_other, right, own, arrived = refs[:7]
    other, *parts = refs[7:-1]
    held = refs[-1]
    rows, columns = own.shape
    share = parts[0].shape[-2]
    sectors = held.shape[0]
    sector = lax.axis_index("sec")
    core = lax.axis_index("rep")
    place = lax.axis_index("ops")
    live = live_rows(sizes, sector, (core ^ 1) * rows, rows, columns)
    other[...] = (arrived[0].astype(jnp.float32) * live).astype(other.dtype)
    products = left_times((left_own, left_other), (own[...], other[...]))
    totals = [None] * sectors
    for term in range(right.shape[0]):
        product = times_right(products[term], right, term)
        for step in range(sectors):
            weight = jnp.broadcast_to(mixing[step][term : term + 1, :1], (rows, columns))
            part = weight * product
            totals[step] = part if totals[step] is None else totals[step] + part
    for step in range(sectors):
        held[step] = totals[step]
    for (steps, across), out in zip(shares, parts):
        for index, along in enumerate(steps):
            start = pl.multiple_of((place ^ along) * share, share)
            out[index] = held[across, pl.ds(start, share), :].astype(out.dtype)


def sum_kernel(indices, masked, *refs):
    total = refs[0][indices[0]].astype(jnp.float32)
    for index, piece in zip(indices[1:], refs[1:]):
        total = total + piece[index].astype(jnp.float32)
    if masked:
        share = total.shape[0]
        start = pl.multiple_of(lax.axis_index("ops") * share, share)
        total = total * refs[len(indices)][pl.ds(start, share), :]
    refs[-1][0] = total.astype(refs[-1].dtype)


def place_kernel(spots, *refs):
    pieces, half = refs[:-1], refs[-1]
    share = pieces[0].shape[1]
    place = lax.axis_index("ops")
    for (along, index), piece in zip(spots, pieces):
        start = pl.multiple_of((place ^ along) * share, share)
        half[index, pl.ds(start, share), :] = piece[0]


def left_kernel(left_own, left_other, own, other, across_own, out, across_out):
    out[...] = left_times((left_own, left_other), (own[0], other[0]))
    for step in range(across_own.shape[0]):
        across_out[step] = left_times((left_own,), (across_own[step],))


def tables_kernel(sizes_ref, pairs_ref, weights_ref, _, mixing, live):
    target = lax.axis_index("sec")
    for term in range(mixing.shape[0]):
        for step in range(mixing.shape[1]):
            weight = mixing_scalar(pairs_ref, weights_ref, term, target, target ^ step)
            mixing[term, step] = jnp.full(mixing.shape[2:], weight, jnp.float32)
    rows, columns = live.shape
    cells = live_cells(sizes_ref, target, lax.axis_index("rep") * rows, rows, columns)
    live[...] = jnp.where(cells, 1.0, 0.0)


def second_kernel(mixing, left_other, right, products, across_products, other, *refs):
    shares, held = refs[:-1], refs[-1]
    rows, columns = products.shape[1:]
    share = shares[0].shape[1]
    place = lax.axis_index("ops")
    total = None
    across = [left_times((left_other,), (other[step],)) for step in range(other.shape[0])]
    for term in range(right.shape[0]):
        weights = [
            jnp.broadcast_to(mixing[term, step][:1, :1], (rows, columns))
            for step in range(len(across) + 1)
        ]
        combined = weights[0] * products[term]
        for step, part in enumerate(across):
            combined = combined + weights[step + 1] * (across_products[step, term] + part[term])
        part = times_right(combined, right, term)
        total = part if total is None else total + part
    held[...] = total
    for step, out in enumerate(shares):
        start = pl.multiple_of((place ^ step) * share, share)
        out[0] = held[pl.ds(start, share), :].astype(out.dtype)


def sums_kernel(wave_own, wave_other, sigma_own, sigma_other, out):
    step, columns = 16, wave_own.shape[1]
    sums = (jnp.zeros((step, columns), jnp.float32),) * 3
    for wave, sigma in ((wave_own, sigma_own), (wave_other, sigma_other)):

        def add_rows(block, carry):
            start = pl.multiple_of(block * step, step)
            w = wave[pl.ds(start, step), :].astype(jnp.float32)
            s = sigma[0, pl.ds(start, step), :].astype(jnp.float32)
            return (carry[0] + w * s, carry[1] + w * w, carry[2] + s * s)

        sums = lax.fori_loop(0, wave.shape[0] // step, add_rows, sums, unroll=2)
    for index, value in enumerate(sums):
        out[index] = jnp.broadcast_to(jnp.sum(value, keepdims=True), out.shape[1:])


def wave_kernel(sizes_ref, wave_own, sigma_own, *refs):
    sums, (second, factors) = refs[:-2], refs[-2:]
    rows, columns = wave_own.shape
    live_count = jnp.float32(0.0)
    for sector in range(sizes_ref.shape[0]):
        live_count = live_count + sizes_ref[sector, 0].astype(jnp.float32) * sizes_ref[
            sector, 1
        ].astype(jnp.float32)
    total = sums[0][...]
    for other in sums[1:]:
        total = total + other[...]
    correlation, norm_square, sigma_square = total[0], total[1], total[2]
    rayleigh = correlation / norm_square
    residual_square = (
        sigma_square - 2.0 * rayleigh * correlation + rayleigh * rayleigh * norm_square
    )
    residual_square = jnp.maximum(residual_square, 0.0)
    scale = 1.0 / jnp.sqrt(residual_square / live_count + epsilon)
    factors[0] = scale
    factors[1] = rayleigh * scale
    sigma_factor = jnp.broadcast_to(scale[:1, :1], (rows, columns))
    wave_factor = jnp.broadcast_to((rayleigh * scale)[:1, :1], (rows, columns))
    sigma = sigma_own[0].astype(jnp.float32)
    wave = wave_own[...].astype(jnp.float32)
    second[0] = (sigma_factor * sigma - wave_factor * wave).astype(second.dtype)


def join_kernel(order, factors, sigma_own, *refs):
    pieces, (out, held, sems) = refs[:-3], refs[-3:]
    _, share, columns = pieces[0].shape
    place = lax.axis_index("ops")
    scale = jnp.broadcast_to(factors[0][:1, :1], (share, columns))
    shift = jnp.broadcast_to(factors[1][:1, :1], (share, columns))
    copies = []
    for step, piece in zip(order, pieces):
        rows = pl.ds(pl.multiple_of((place ^ step) * share, share), share)
        moved = shift * sigma_own[0, rows, :].astype(jnp.float32)
        held[step] = scale * piece[0].astype(jnp.float32) - moved
        copies.append(pltpu.make_async_copy(held.at[step], out.at[0, rows], sems.at[step]))
        copies[-1].start()
    for copy in copies:
        copy.wait()


def partner(value, steps):
    steps = {axis: step for axis, step in steps.items() if step}
    if not steps:
        return value
    axes = tuple(steps)
    places = [()]
    for axis in axes:
        places = [place + (i,) for place in places for i in range(lax.axis_size(axis))]
    index = {place: i for i, place in enumerate(places)}
    pairs = [
        (index[tuple(i ^ steps[axis] for i, axis in zip(place, axes))], index[place])
        for place in places
    ]
    return lax.ppermute(value, axes, pairs)


def local(wavefunction, sector_sizes, left_blocks, right_blocks, sector_pairs, pair_weights):
    sectors = sector_sizes.shape[0]
    ops_count = lax.axis_size("ops")
    _, rows, columns = wavefunction.shape
    terms, side = left_blocks.shape[0], left_blocks.shape[1]
    share = rows // ops_count
    bf16, f32 = jnp.bfloat16, jnp.float32
    smem = pl.BlockSpec(memory_space=pltpu.SMEM)
    outside = pl.BlockSpec(memory_space=pltpu.HBM)
    inside = pl.BlockSpec(memory_space=pltpu.VMEM)

    def shape(*dims, dtype=bf16):
        return jax.ShapeDtypeStruct(dims, dtype)

    def call(kernel, name, out_shape, in_specs, *operands, scratch=(), vmem=16, out=inside):
        return pl.pallas_call(
            kernel,
            out_shape=out_shape,
            in_specs=list(in_specs) + [inside] * (len(operands) - len(in_specs)),
            out_specs=jax.tree.map(lambda _: out, out_shape),
            scratch_shapes=list(scratch),
            compiler_params=pltpu.CompilerParams(vmem_limit_bytes=vmem * mebibyte),
            name=name,
        )(*operands)

    def summed(name, *pieces, live=None, after=()):
        pieces = [piece if isinstance(piece, tuple) else (piece, 0) for piece in pieces]
        arrays, indices = zip(*pieces)
        return call(
            lambda *refs: sum_kernel(indices, live is not None, *refs),
            name,
            shape(1, share, columns),
            [],
            *arrays,
            *([] if live is None else [live]),
            *after,
        )

    farthest_first = list(reversed(range(ops_count)))
    send_order = farthest_first[1:2] + farthest_first[:1] + farthest_first[2:]
    arrived = partner(wavefunction, {"rep": 1})
    left_own, left_other = call(
        load_kernel,
        "load_operators",
        [shape(terms, rows, rows), shape(terms, rows, side - rows)],
        [outside],
        left_blocks,
        scratch=[pltpu.SemaphoreType.DMA((2,))],
        vmem=51,
    )
    right = right_blocks
    pairs = jnp.swapaxes(sector_pairs, 1, 2)
    scalars = (sector_sizes, pairs, pair_weights)

    far = ops_count - 1
    direct = [(along,) for along in farthest_first[1:-1]]
    spots = [((far, 0), across) for across in range(sectors)]
    spots += [(along, across) for along in direct for across in range(sectors)]
    wave_own, mixing = call(
        first_tables_kernel,
        "tables_for_first_sigma",
        [shape(rows, columns), shape(sectors, terms, 128, dtype=f32)],
        [],
        *scalars,
        wavefunction,
        left_own,
    )
    wave_other, *rest = call(
        lambda *refs: first_kernel(spots, *refs),
        "first_sigma_terms",
        [shape(rows, columns)]
        + [
            shape(len(along), share, columns, dtype=f32 if along == (far, 0) and across == 0 else bf16)
            for along, across in spots
        ],
        [],
        sector_sizes,
        mixing,
        left_own,
        left_other,
        right,
        wave_own,
        arrived,
        scratch=[pltpu.VMEM((sectors, rows, columns), f32)],
    )
    rest = dict(zip(spots, rest))
    mixing, live = call(
        tables_kernel,
        "tables_for_second_sigma",
        [shape(terms, sectors, 8, 128, dtype=f32), shape(rows, columns, dtype=f32)],
        [smem] * 3,
        *scalars,
        wave_other,
    )
    met = [partner(rest[(far, 0), across], {"sec": across}) for across in range(sectors)]
    received = [partner(summed("sum_far_share", *met), {"ops": far})]
    first_two = [(direct[0], 0), (direct[-1], 0)]
    order = first_two + [spot for spot in rest if spot[0] in direct and spot not in first_two]
    received += [partner(rest[spot], {"ops": spot[0][0], "sec": spot[1]}) for spot in order]
    first_share = summed("sum_first_sigma", *[(piece, 1) for piece in met], *received, live=live)
    along_ops = {along: partner(first_share, {"ops": along}) for along in send_order}
    sigma_own = call(
        lambda *refs: place_kernel([(along, 0) for along in send_order], *refs),
        "place_own_sector",
        shape(1, rows, columns),
        [],
        *along_ops.values(),
    )
    sigma_other = partner(sigma_own, {"rep": 1})
    spots = [(along, across) for along in send_order for across in range(1, sectors)]
    pieces = [
        partner(first_share, {"ops": along, "sec": across})
        if along < 2
        else partner(along_ops[along], {"sec": across})
        for along, across in spots
    ]
    across_own = call(
        lambda *refs: place_kernel([(along, across - 1) for along, across in spots], *refs),
        "place_other_sectors",
        shape(sectors - 1, rows, columns),
        [],
        *pieces,
    )
    across_other = partner(across_own, {"rep": 1})

    products, across_products = call(
        left_kernel,
        "left_products",
        [
            shape(terms, rows, columns, dtype=f32),
            shape(sectors - 1, terms, rows, columns, dtype=f32),
        ],
        [],
        left_own,
        left_other,
        sigma_own,
        sigma_other,
        across_own,
    )
    shares = call(
        second_kernel,
        "second_sigma_terms",
        [shape(1, share, columns, dtype=f32)] + [shape(1, share, columns)] * (ops_count - 1),
        [],
        mixing,
        left_other,
        right,
        products,
        across_products,
        across_other,
        scratch=[pltpu.VMEM((rows, columns), f32)],
    )
    received = [partner(shares[step], {"ops": step}) for step in farthest_first[:-1]]
    sums = call(
        sums_kernel,
        "sums_for_rayleigh",
        shape(3, 8, 128, dtype=f32),
        [],
        wave_own,
        wave_other,
        sigma_own,
        sigma_other,
    )
    sums = [partner(sums, {"sec": step}) for step in range(sectors)]
    second_share = summed("sum_second_sigma", shares[0], *received, live=live, after=sums)
    second_wave, factors = call(
        wave_kernel,
        "second_wave",
        [shape(1, rows, columns), shape(2, 8, 128, dtype=f32)],
        [smem],
        sector_sizes,
        wave_own,
        sigma_own,
        *sums,
    )
    second_sigma = call(
        lambda *refs: join_kernel(farthest_first, *refs),
        "join_second_sigma",
        shape(1, rows, columns, dtype=f32),
        [],
        factors,
        sigma_own,
        *[partner(second_share, {"ops": step}) for step in farthest_first],
        scratch=[
            pltpu.VMEM((ops_count, share, columns), f32),
            pltpu.SemaphoreType.DMA((ops_count,)),
        ],
        out=outside,
    )
    return (second_wave, second_sigma)


def solution(mesh):
    return jax.shard_map(
        local,
        mesh=mesh,
        in_specs=(
            P(("grp", "sec"), "rep", None),
            P("grp", None),
            P(("grp", "ops"), None, None),
            P(("grp", "ops"), None, None),
            P(("grp", "ops"), None, None),
            P(("grp", "ops"), None),
        ),
        out_specs=(P(("grp", "sec"), "rep", None), P(("grp", "sec"), "rep", None)),
        check_vma=False,
    )
```

```python
import jax
import jax.numpy as jnp
from jax import lax
from jax.experimental import pallas as pl
from jax.experimental.pallas import tpu as pltpu
from jax.sharding import PartitionSpec as P

epsilon = 1e-06
mebibyte = 1024 * 1024


def mixing_scalar(pairs_ref, weights_ref, term, target, source):
    value = jnp.float32(0.0)
    for pair in range(weights_ref.shape[1]):
        hit = (pairs_ref[term, 1, pair] == target) & (pairs_ref[term, 0, pair] == source)
        value = value + jnp.where(hit, weights_ref[term, pair], jnp.float32(0.0))
    return value


def live_cells(sizes_ref, sector, row_start, rows, columns):
    row = row_start + lax.broadcasted_iota(jnp.int32, (rows, columns), 0)
    column = lax.broadcasted_iota(jnp.int32, (rows, columns), 1)
    return (row < sizes_ref[sector, 0]) & (column < sizes_ref[sector, 1])


def masked(values, live):
    return jnp.where(live, values.astype(jnp.float32), 0.0).astype(values.dtype)


def left_times(lefts, blocks):
    total = None
    for left, block in zip(lefts, blocks):
        terms, rows, depth = left.shape
        stacked = left[...].reshape(terms * rows, depth)
        part = jnp.dot(stacked, block, preferred_element_type=jnp.float32)
        total = part if total is None else total + part
    return total.reshape(terms, rows, -1)


def times_right(values, right, term):
    return lax.dot_general(
        values.astype(jnp.bfloat16),
        right[term],
        (((1,), (1,)), ((), ())),
        preferred_element_type=jnp.float32,
    )


def load_kernel(left_ref, left_own, left_other, sems):
    rows = left_own.shape[1]
    core = lax.axis_index("rep")
    copies = []
    for index, (half, place) in enumerate(((left_own, core), (left_other, core ^ 1))):
        mine = pl.ds(pl.multiple_of(core * rows, rows), rows)
        columns = pl.ds(pl.multiple_of(place * rows, rows), rows)
        copies.append(pltpu.make_async_copy(left_ref.at[:, mine, columns], half, sems.at[index]))
    for copy in copies:
        copy.start()
    for copy in copies:
        copy.wait()


def live_rows(sizes, sector, row_start, rows, columns):
    bounds = sizes[pl.ds(sector, 1), :]
    row = row_start + lax.broadcasted_iota(jnp.int32, (rows, columns), 0)
    column = lax.broadcasted_iota(jnp.int32, (rows, columns), 1)
    inside = (row < bounds[:, 0:1]) & (column < bounds[:, 1:2])
    return jnp.where(inside, 1.0, 0.0)


def first_tables_kernel(sizes, pairs, weights, wave, _, own, mixing):
    rows, columns = own.shape
    sector = lax.axis_index("sec")
    live = live_rows(sizes, sector, lax.axis_index("rep") * rows, rows, columns)
    own[...] = (wave[0].astype(jnp.float32) * live).astype(own.dtype)
    source, target = pairs[:, 0, :], pairs[:, 1, :]
    for step in range(mixing.shape[0]):
        hits = (source == sector) & (target == (sector ^ step))
        total = jnp.sum(jnp.where(hits, weights[...], 0.0), axis=1, keepdims=True)
        mixing[step] = jnp.broadcast_to(total, mixing.shape[1:])


def first_kernel(shares, *refs):
    sizes, mixing, left_own, left_other, right, own, arrived = refs[:7]
    other, *parts = refs[7:-1]
    held = refs[-1]
    rows, columns = own.shape
    share = parts[0].shape[-2]
    sectors = held.shape[0]
    sector = lax.axis_index("sec")
    core = lax.axis_index("rep")
    place = lax.axis_index("ops")
    live = live_rows(sizes, sector, (core ^ 1) * rows, rows, columns)
    other[...] = (arrived[0].astype(jnp.float32) * live).astype(other.dtype)
    products = left_times((left_own, left_other), (own[...], other[...]))
    totals = [None] * sectors
    for term in range(right.shape[0]):
        product = times_right(products[term], right, term)
        for step in range(sectors):
            weight = jnp.broadcast_to(mixing[step][term : term + 1, :1], (rows, columns))
            part = weight * product
            totals[step] = part if totals[step] is None else totals[step] + part
    for step in range(sectors):
        held[step] = totals[step]
    for (steps, across), out in zip(shares, parts):
        for index, along in enumerate(steps):
            start = pl.multiple_of((place ^ along) * share, share)
            out[index] = held[across, pl.ds(start, share), :].astype(out.dtype)


def sum_kernel(indices, masked, *refs):
    total = refs[0][indices[0]].astype(jnp.float32)
    for index, piece in zip(indices[1:], refs[1:]):
        total = total + piece[index].astype(jnp.float32)
    if masked:
        share = total.shape[0]
        start = pl.multiple_of(lax.axis_index("ops") * share, share)
        total = total * refs[len(indices)][pl.ds(start, share), :]
    refs[-1][0] = total.astype(refs[-1].dtype)


def place_kernel(spots, *refs):
    pieces, half = refs[:-1], refs[-1]
    share = pieces[0].shape[1]
    place = lax.axis_index("ops")
    for (along, index), piece in zip(spots, pieces):
        start = pl.multiple_of((place ^ along) * share, share)
        half[index, pl.ds(start, share), :] = piece[0]


def left_kernel(left_own, left_other, own, other, across_own, out, across_out):
    out[...] = left_times((left_own, left_other), (own[0], other[0]))
    for step in range(across_own.shape[0]):
        across_out[step] = left_times((left_own,), (across_own[step],))


def tables_kernel(sizes_ref, pairs_ref, weights_ref, _, mixing, live):
    target = lax.axis_index("sec")
    for term in range(mixing.shape[0]):
        for step in range(mixing.shape[1]):
            weight = mixing_scalar(pairs_ref, weights_ref, term, target, target ^ step)
            mixing[term, step] = jnp.full(mixing.shape[2:], weight, jnp.float32)
    rows, columns = live.shape
    cells = live_cells(sizes_ref, target, lax.axis_index("rep") * rows, rows, columns)
    live[...] = jnp.where(cells, 1.0, 0.0)


def second_kernel(mixing, left_other, right, products, across_products, other, *refs):
    shares, held = refs[:-1], refs[-1]
    rows, columns = products.shape[1:]
    share = shares[0].shape[1]
    place = lax.axis_index("ops")
    total = None
    across = [left_times((left_other,), (other[step],)) for step in range(other.shape[0])]
    for term in range(right.shape[0]):
        weights = [
            jnp.broadcast_to(mixing[term, step][:1, :1], (rows, columns))
            for step in range(len(across) + 1)
        ]
        combined = weights[0] * products[term]
        for step, part in enumerate(across):
            combined = combined + weights[step + 1] * (across_products[step, term] + part[term])
        part = times_right(combined, right, term)
        total = part if total is None else total + part
    held[...] = total
    for step, out in enumerate(shares):
        start = pl.multiple_of((place ^ step) * share, share)
        out[0] = held[pl.ds(start, share), :].astype(out.dtype)


def sums_kernel(wave_own, wave_other, sigma_own, sigma_other, out):
    step, columns = 16, wave_own.shape[1]
    sums = (jnp.zeros((step, columns), jnp.float32),) * 3
    for wave, sigma in ((wave_own, sigma_own), (wave_other, sigma_other)):

        def add_rows(block, carry):
            start = pl.multiple_of(block * step, step)
            w = wave[pl.ds(start, step), :].astype(jnp.float32)
            s = sigma[0, pl.ds(start, step), :].astype(jnp.float32)
            return (carry[0] + w * s, carry[1] + w * w, carry[2] + s * s)

        sums = lax.fori_loop(0, wave.shape[0] // step, add_rows, sums, unroll=2)
    for index, value in enumerate(sums):
        out[index] = jnp.broadcast_to(jnp.sum(value, keepdims=True), out.shape[1:])


def wave_kernel(sizes_ref, wave_own, sigma_own, *refs):
    sums, (second, factors) = refs[:-2], refs[-2:]
    rows, columns = wave_own.shape
    live_count = jnp.float32(0.0)
    for sector in range(sizes_ref.shape[0]):
        live_count = live_count + sizes_ref[sector, 0].astype(jnp.float32) * sizes_ref[
            sector, 1
        ].astype(jnp.float32)
    total = sums[0][...]
    for other in sums[1:]:
        total = total + other[...]
    correlation, norm_square, sigma_square = total[0], total[1], total[2]
    rayleigh = correlation / norm_square
    residual_square = (
        sigma_square - 2.0 * rayleigh * correlation + rayleigh * rayleigh * norm_square
    )
    residual_square = jnp.maximum(residual_square, 0.0)
    scale = 1.0 / jnp.sqrt(residual_square / live_count + epsilon)
    factors[0] = scale
    factors[1] = rayleigh * scale
    sigma_factor = jnp.broadcast_to(scale[:1, :1], (rows, columns))
    wave_factor = jnp.broadcast_to((rayleigh * scale)[:1, :1], (rows, columns))
    sigma = sigma_own[0].astype(jnp.float32)
    wave = wave_own[...].astype(jnp.float32)
    second[0] = (sigma_factor * sigma - wave_factor * wave).astype(second.dtype)


def join_kernel(order, factors, sigma_own, *refs):
    pieces, (out, held, sems) = refs[:-3], refs[-3:]
    _, share, columns = pieces[0].shape
    place = lax.axis_index("ops")
    scale = jnp.broadcast_to(factors[0][:1, :1], (share, columns))
    shift = jnp.broadcast_to(factors[1][:1, :1], (share, columns))
    copies = []
    for step, piece in zip(order, pieces):
        rows = pl.ds(pl.multiple_of((place ^ step) * share, share), share)
        moved = shift * sigma_own[0, rows, :].astype(jnp.float32)
        held[step] = scale * piece[0].astype(jnp.float32) - moved
        copies.append(pltpu.make_async_copy(held.at[step], out.at[0, rows], sems.at[step]))
        copies[-1].start()
    for copy in copies:
        copy.wait()


def partner(value, steps):
    steps = {axis: step for axis, step in steps.items() if step}
    if not steps:
        return value
    axes = tuple(steps)
    places = [()]
    for axis in axes:
        places = [place + (i,) for place in places for i in range(lax.axis_size(axis))]
    index = {place: i for i, place in enumerate(places)}
    pairs = [
        (index[tuple(i ^ steps[axis] for i, axis in zip(place, axes))], index[place])
        for place in places
    ]
    return lax.ppermute(value, axes, pairs)


def local(wavefunction, sector_sizes, left_blocks, right_blocks, sector_pairs, pair_weights):
    sectors = sector_sizes.shape[0]
    ops_count = lax.axis_size("ops")
    _, rows, columns = wavefunction.shape
    terms, side = left_blocks.shape[0], left_blocks.shape[1]
    share = rows // ops_count
    bf16, f32 = jnp.bfloat16, jnp.float32
    smem = pl.BlockSpec(memory_space=pltpu.SMEM)
    outside = pl.BlockSpec(memory_space=pltpu.HBM)
    inside = pl.BlockSpec(memory_space=pltpu.VMEM)

    def shape(*dims, dtype=bf16):
        return jax.ShapeDtypeStruct(dims, dtype)

    def call(kernel, name, out_shape, in_specs, *operands, scratch=(), vmem=16, out=inside):
        return pl.pallas_call(
            kernel,
            out_shape=out_shape,
            in_specs=list(in_specs) + [inside] * (len(operands) - len(in_specs)),
            out_specs=jax.tree.map(lambda _: out, out_shape),
            scratch_shapes=list(scratch),
            compiler_params=pltpu.CompilerParams(vmem_limit_bytes=vmem * mebibyte),
            name=name,
        )(*operands)

    def summed(name, *pieces, live=None, after=()):
        pieces = [piece if isinstance(piece, tuple) else (piece, 0) for piece in pieces]
        arrays, indices = zip(*pieces)
        return call(
            lambda *refs: sum_kernel(indices, live is not None, *refs),
            name,
            shape(1, share, columns),
            [],
            *arrays,
            *([] if live is None else [live]),
            *after,
        )

    farthest_first = list(reversed(range(ops_count)))
    send_order = farthest_first[1:2] + farthest_first[:1] + farthest_first[2:]
    arrived = partner(wavefunction, {"rep": 1})
    left_own, left_other = call(
        load_kernel,
        "load_operators",
        [shape(terms, rows, rows), shape(terms, rows, side - rows)],
        [outside],
        left_blocks,
        scratch=[pltpu.SemaphoreType.DMA((2,))],
        vmem=51,
    )
    right = right_blocks
    pairs = jnp.swapaxes(sector_pairs, 1, 2)
    scalars = (sector_sizes, pairs, pair_weights)

    far = ops_count - 1
    direct = [(along,) for along in farthest_first[1:-1]]
    spots = [((far, 0), across) for across in range(sectors)]
    spots += [(along, across) for along in direct for across in range(sectors)]
    wave_own, mixing = call(
        first_tables_kernel,
        "tables_for_first_sigma",
        [shape(rows, columns), shape(sectors, terms, 128, dtype=f32)],
        [],
        *scalars,
        wavefunction,
        left_own,
    )
    wave_other, *rest = call(
        lambda *refs: first_kernel(spots, *refs),
        "first_sigma_terms",
        [shape(rows, columns)]
        + [
            shape(len(along), share, columns, dtype=f32 if along == (far, 0) and across == 0 else bf16)
            for along, across in spots
        ],
        [],
        sector_sizes,
        mixing,
        left_own,
        left_other,
        right,
        wave_own,
        arrived,
        scratch=[pltpu.VMEM((sectors, rows, columns), f32)],
    )
    rest = dict(zip(spots, rest))
    mixing, live = call(
        tables_kernel,
        "tables_for_second_sigma",
        [shape(terms, sectors, 8, 128, dtype=f32), shape(rows, columns, dtype=f32)],
        [smem] * 3,
        *scalars,
        wave_other,
    )
    met = [partner(rest[(far, 0), across], {"sec": across}) for across in range(sectors)]
    received = [partner(summed("sum_far_share", *met), {"ops": far})]
    first_two = [(direct[0], 0), (direct[-1], 0)]
    order = first_two + [spot for spot in rest if spot[0] in direct and spot not in first_two]
    received += [partner(rest[spot], {"ops": spot[0][0], "sec": spot[1]}) for spot in order]
    first_share = summed("sum_first_sigma", *[(piece, 1) for piece in met], *received, live=live)
    along_ops = {along: partner(first_share, {"ops": along}) for along in send_order}
    spots = [(along, across) for along in send_order for across in range(1, sectors)]
    pieces = {
        (along, across): partner(first_share, {"ops": along, "sec": across})
        if along < 2
        else partner(along_ops[along], {"sec": across})
        for along, across in spots
    }
    ahead = [pieces[along, across] for along, across in spots if along < 2]
    sigma_own = call(
        lambda *refs: place_kernel([(along, 0) for along in send_order], *refs[len(ahead) :]),
        "place_own_sector",
        shape(1, rows, columns),
        [],
        *ahead,
        *along_ops.values(),
    )
    sigma_other = partner(sigma_own, {"rep": 1})
    across_own = call(
        lambda *refs: place_kernel([(along, across - 1) for along, across in spots], *refs),
        "place_other_sectors",
        shape(sectors - 1, rows, columns),
        [],
        *pieces.values(),
    )
    across_other = partner(across_own, {"rep": 1})

    products, across_products = call(
        left_kernel,
        "left_products",
        [
            shape(terms, rows, columns, dtype=f32),
            shape(sectors - 1, terms, rows, columns, dtype=f32),
        ],
        [],
        left_own,
        left_other,
        sigma_own,
        sigma_other,
        across_own,
    )
    shares = call(
        second_kernel,
        "second_sigma_terms",
        [shape(1, share, columns, dtype=f32)] + [shape(1, share, columns)] * (ops_count - 1),
        [],
        mixing,
        left_other,
        right,
        products,
        across_products,
        across_other,
        scratch=[pltpu.VMEM((rows, columns), f32)],
    )
    received = [partner(shares[step], {"ops": step}) for step in farthest_first[:-1]]
    sums = call(
        sums_kernel,
        "sums_for_rayleigh",
        shape(3, 8, 128, dtype=f32),
        [],
        wave_own,
        wave_other,
        sigma_own,
        sigma_other,
    )
    sums = [partner(sums, {"sec": step}) for step in range(sectors)]
    second_share = summed("sum_second_sigma", shares[0], *received, live=live, after=sums)
    second_wave, factors = call(
        wave_kernel,
        "second_wave",
        [shape(1, rows, columns), shape(2, 8, 128, dtype=f32)],
        [smem],
        sector_sizes,
        wave_own,
        sigma_own,
        *sums,
    )
    second_sigma = call(
        lambda *refs: join_kernel(farthest_first, *refs),
        "join_second_sigma",
        shape(1, rows, columns, dtype=f32),
        [],
        factors,
        sigma_own,
        *[partner(second_share, {"ops": step}) for step in farthest_first],
        scratch=[
            pltpu.VMEM((ops_count, share, columns), f32),
            pltpu.SemaphoreType.DMA((ops_count,)),
        ],
        out=outside,
    )
    return (second_wave, second_sigma)


def solution(mesh):
    return jax.shard_map(
        local,
        mesh=mesh,
        in_specs=(
            P(("grp", "sec"), "rep", None),
            P("grp", None),
            P(("grp", "ops"), None, None),
            P(("grp", "ops"), None, None),
            P(("grp", "ops"), None, None),
            P(("grp", "ops"), None),
        ),
        out_specs=(P(("grp", "sec"), "rep", None), P(("grp", "sec"), "rep", None)),
        check_vma=False,
    )
```

```python
import jax
import jax.numpy as jnp
from jax import lax
from jax.experimental import pallas as pl
from jax.experimental.pallas import tpu as pltpu
from jax.sharding import PartitionSpec as P

epsilon = 1e-06
mebibyte = 1024 * 1024


def mixing_scalar(pairs_ref, weights_ref, term, target, source):
    value = jnp.float32(0.0)
    for pair in range(weights_ref.shape[1]):
        hit = (pairs_ref[term, 1, pair] == target) & (pairs_ref[term, 0, pair] == source)
        value = value + jnp.where(hit, weights_ref[term, pair], jnp.float32(0.0))
    return value


def live_cells(sizes_ref, sector, row_start, rows, columns):
    row = row_start + lax.broadcasted_iota(jnp.int32, (rows, columns), 0)
    column = lax.broadcasted_iota(jnp.int32, (rows, columns), 1)
    return (row < sizes_ref[sector, 0]) & (column < sizes_ref[sector, 1])


def masked(values, live):
    return jnp.where(live, values.astype(jnp.float32), 0.0).astype(values.dtype)


def left_times(lefts, blocks):
    total = None
    for left, block in zip(lefts, blocks):
        terms, rows, depth = left.shape
        stacked = left[...].reshape(terms * rows, depth)
        part = jnp.dot(stacked, block, preferred_element_type=jnp.float32)
        total = part if total is None else total + part
    return total.reshape(terms, rows, -1)


def times_right(values, right, term):
    return lax.dot_general(
        values.astype(jnp.bfloat16),
        right[term],
        (((1,), (1,)), ((), ())),
        preferred_element_type=jnp.float32,
    )


def load_kernel(left_ref, left_own, left_other, sems):
    rows = left_own.shape[1]
    core = lax.axis_index("rep")
    copies = []
    for index, (half, place) in enumerate(((left_own, core), (left_other, core ^ 1))):
        mine = pl.ds(pl.multiple_of(core * rows, rows), rows)
        columns = pl.ds(pl.multiple_of(place * rows, rows), rows)
        copies.append(pltpu.make_async_copy(left_ref.at[:, mine, columns], half, sems.at[index]))
    for copy in copies:
        copy.start()
    for copy in copies:
        copy.wait()


def live_rows(sizes, sector, row_start, rows, columns):
    bounds = sizes[pl.ds(sector, 1), :]
    row = row_start + lax.broadcasted_iota(jnp.int32, (rows, columns), 0)
    column = lax.broadcasted_iota(jnp.int32, (rows, columns), 1)
    inside = (row < bounds[:, 0:1]) & (column < bounds[:, 1:2])
    return jnp.where(inside, 1.0, 0.0)


def first_tables_kernel(sizes, pairs, weights, wave, _, own, mixing):
    rows, columns = own.shape
    sector = lax.axis_index("sec")
    live = live_rows(sizes, sector, lax.axis_index("rep") * rows, rows, columns)
    own[...] = (wave[0].astype(jnp.float32) * live).astype(own.dtype)
    source, target = pairs[:, 0, :], pairs[:, 1, :]
    for step in range(mixing.shape[0]):
        hits = (source == sector) & (target == (sector ^ step))
        total = jnp.sum(jnp.where(hits, weights[...], 0.0), axis=1, keepdims=True)
        mixing[step] = jnp.broadcast_to(total, mixing.shape[1:])


def first_kernel(shares, *refs):
    sizes, mixing, left_own, left_other, right, own, arrived = refs[:7]
    other, *parts = refs[7:-1]
    held = refs[-1]
    rows, columns = own.shape
    share = parts[0].shape[-2]
    sectors = held.shape[0]
    sector = lax.axis_index("sec")
    core = lax.axis_index("rep")
    place = lax.axis_index("ops")
    live = live_rows(sizes, sector, (core ^ 1) * rows, rows, columns)
    other[...] = (arrived[0].astype(jnp.float32) * live).astype(other.dtype)
    products = left_times((left_own, left_other), (own[...], other[...]))
    totals = [None] * sectors
    for term in range(right.shape[0]):
        product = times_right(products[term], right, term)
        for step in range(sectors):
            weight = jnp.broadcast_to(mixing[step][term : term + 1, :1], (rows, columns))
            part = weight * product
            totals[step] = part if totals[step] is None else totals[step] + part
    for step in range(sectors):
        held[step] = totals[step]
    for (steps, across), out in zip(shares, parts):
        for index, along in enumerate(steps):
            start = pl.multiple_of((place ^ along) * share, share)
            out[index] = held[across, pl.ds(start, share), :].astype(out.dtype)


def sum_kernel(indices, masked, *refs):
    total = refs[0][indices[0]].astype(jnp.float32)
    for index, piece in zip(indices[1:], refs[1:]):
        total = total + piece[index].astype(jnp.float32)
    if masked:
        share = total.shape[0]
        start = pl.multiple_of(lax.axis_index("ops") * share, share)
        total = total * refs[len(indices)][pl.ds(start, share), :]
    refs[-1][0] = total.astype(refs[-1].dtype)


def place_kernel(spots, *refs):
    pieces, half = refs[:-1], refs[-1]
    share = pieces[0].shape[1]
    place = lax.axis_index("ops")
    for (along, index), piece in zip(spots, pieces):
        start = pl.multiple_of((place ^ along) * share, share)
        half[index, pl.ds(start, share), :] = piece[0]


def left_kernel(left_own, left_other, own, other, across_own, out, across_out):
    out[...] = left_times((left_own, left_other), (own[0], other[0]))
    for step in range(across_own.shape[0]):
        across_out[step] = left_times((left_own,), (across_own[step],))


def tables_kernel(sizes_ref, pairs_ref, weights_ref, _, mixing, live):
    target = lax.axis_index("sec")
    for term in range(mixing.shape[0]):
        for step in range(mixing.shape[1]):
            weight = mixing_scalar(pairs_ref, weights_ref, term, target, target ^ step)
            mixing[term, step] = jnp.full(mixing.shape[2:], weight, jnp.float32)
    rows, columns = live.shape
    cells = live_cells(sizes_ref, target, lax.axis_index("rep") * rows, rows, columns)
    live[...] = jnp.where(cells, 1.0, 0.0)


def second_kernel(mixing, left_other, right, products, across_products, other, *refs):
    shares, held = refs[:-1], refs[-1]
    rows, columns = products.shape[1:]
    share = shares[0].shape[1]
    place = lax.axis_index("ops")
    total = None
    across = [left_times((left_other,), (other[step],)) for step in range(other.shape[0])]
    for term in range(right.shape[0]):
        weights = [
            jnp.broadcast_to(mixing[term, step][:1, :1], (rows, columns))
            for step in range(len(across) + 1)
        ]
        combined = weights[0] * products[term]
        for step, part in enumerate(across):
            combined = combined + weights[step + 1] * (across_products[step, term] + part[term])
        part = times_right(combined, right, term)
        total = part if total is None else total + part
    held[...] = total
    for step, out in enumerate(shares):
        start = pl.multiple_of((place ^ step) * share, share)
        out[0] = held[pl.ds(start, share), :].astype(out.dtype)


def sums_kernel(wave_own, wave_other, sigma_own, sigma_other, out):
    step, columns = 16, wave_own.shape[1]
    sums = (jnp.zeros((step, columns), jnp.float32),) * 3
    for wave, sigma in ((wave_own, sigma_own), (wave_other, sigma_other)):

        def add_rows(block, carry):
            start = pl.multiple_of(block * step, step)
            w = wave[pl.ds(start, step), :].astype(jnp.float32)
            s = sigma[0, pl.ds(start, step), :].astype(jnp.float32)
            return (carry[0] + w * s, carry[1] + w * w, carry[2] + s * s)

        sums = lax.fori_loop(0, wave.shape[0] // step, add_rows, sums, unroll=2)
    for index, value in enumerate(sums):
        out[index] = jnp.broadcast_to(jnp.sum(value, keepdims=True), out.shape[1:])


def wave_kernel(sizes_ref, wave_own, sigma_own, *refs):
    sums, (second, factors) = refs[:-2], refs[-2:]
    rows, columns = wave_own.shape
    live_count = jnp.float32(0.0)
    for sector in range(sizes_ref.shape[0]):
        live_count = live_count + sizes_ref[sector, 0].astype(jnp.float32) * sizes_ref[
            sector, 1
        ].astype(jnp.float32)
    total = sums[0][...]
    for other in sums[1:]:
        total = total + other[...]
    correlation, norm_square, sigma_square = total[0], total[1], total[2]
    rayleigh = correlation / norm_square
    residual_square = (
        sigma_square - 2.0 * rayleigh * correlation + rayleigh * rayleigh * norm_square
    )
    residual_square = jnp.maximum(residual_square, 0.0)
    scale = 1.0 / jnp.sqrt(residual_square / live_count + epsilon)
    factors[0] = scale
    factors[1] = rayleigh * scale
    sigma_factor = jnp.broadcast_to(scale[:1, :1], (rows, columns))
    wave_factor = jnp.broadcast_to((rayleigh * scale)[:1, :1], (rows, columns))
    sigma = sigma_own[0].astype(jnp.float32)
    wave = wave_own[...].astype(jnp.float32)
    second[0] = (sigma_factor * sigma - wave_factor * wave).astype(second.dtype)


def join_kernel(order, factors, sigma_own, *refs):
    pieces, (out, held, sems) = refs[:-3], refs[-3:]
    _, share, columns = pieces[0].shape
    place = lax.axis_index("ops")
    scale = jnp.broadcast_to(factors[0][:1, :1], (share, columns))
    shift = jnp.broadcast_to(factors[1][:1, :1], (share, columns))
    copies = []
    for step, piece in zip(order, pieces):
        rows = pl.ds(pl.multiple_of((place ^ step) * share, share), share)
        moved = shift * sigma_own[0, rows, :].astype(jnp.float32)
        held[step] = scale * piece[0].astype(jnp.float32) - moved
        copies.append(pltpu.make_async_copy(held.at[step], out.at[0, rows], sems.at[step]))
        copies[-1].start()
    for copy in copies:
        copy.wait()


def partner(value, steps):
    steps = {axis: step for axis, step in steps.items() if step}
    if not steps:
        return value
    axes = tuple(steps)
    places = [()]
    for axis in axes:
        places = [place + (i,) for place in places for i in range(lax.axis_size(axis))]
    index = {place: i for i, place in enumerate(places)}
    pairs = [
        (index[tuple(i ^ steps[axis] for i, axis in zip(place, axes))], index[place])
        for place in places
    ]
    return lax.ppermute(value, axes, pairs)


def local(wavefunction, sector_sizes, left_blocks, right_blocks, sector_pairs, pair_weights):
    sectors = sector_sizes.shape[0]
    ops_count = lax.axis_size("ops")
    _, rows, columns = wavefunction.shape
    terms, side = left_blocks.shape[0], left_blocks.shape[1]
    share = rows // ops_count
    bf16, f32 = jnp.bfloat16, jnp.float32
    smem = pl.BlockSpec(memory_space=pltpu.SMEM)
    outside = pl.BlockSpec(memory_space=pltpu.HBM)
    inside = pl.BlockSpec(memory_space=pltpu.VMEM)

    def shape(*dims, dtype=bf16):
        return jax.ShapeDtypeStruct(dims, dtype)

    def call(kernel, name, out_shape, in_specs, *operands, scratch=(), vmem=16, out=inside):
        return pl.pallas_call(
            kernel,
            out_shape=out_shape,
            in_specs=list(in_specs) + [inside] * (len(operands) - len(in_specs)),
            out_specs=jax.tree.map(lambda _: out, out_shape),
            scratch_shapes=list(scratch),
            compiler_params=pltpu.CompilerParams(vmem_limit_bytes=vmem * mebibyte),
            name=name,
        )(*operands)

    def summed(name, *pieces, live=None, after=()):
        pieces = [piece if isinstance(piece, tuple) else (piece, 0) for piece in pieces]
        arrays, indices = zip(*pieces)
        return call(
            lambda *refs: sum_kernel(indices, live is not None, *refs),
            name,
            shape(1, share, columns),
            [],
            *arrays,
            *([] if live is None else [live]),
            *after,
        )

    farthest_first = list(reversed(range(ops_count)))
    send_order = farthest_first[1:2] + farthest_first[:1] + farthest_first[2:]
    arrived = partner(wavefunction, {"rep": 1})
    left_own, left_other = call(
        load_kernel,
        "load_operators",
        [shape(terms, rows, rows), shape(terms, rows, side - rows)],
        [outside],
        left_blocks,
        scratch=[pltpu.SemaphoreType.DMA((2,))],
        vmem=51,
    )
    right = right_blocks
    pairs = jnp.swapaxes(sector_pairs, 1, 2)
    scalars = (sector_sizes, pairs, pair_weights)

    far = ops_count - 1
    direct = [(along,) for along in farthest_first[1:-1]]
    spots = [((far, 0), across) for across in range(sectors)]
    spots += [(along, across) for along in direct for across in range(sectors)]
    wave_own, mixing = call(
        first_tables_kernel,
        "tables_for_first_sigma",
        [shape(rows, columns), shape(sectors, terms, 128, dtype=f32)],
        [],
        *scalars,
        wavefunction,
        left_own,
    )
    wave_other, *rest = call(
        lambda *refs: first_kernel(spots, *refs),
        "first_sigma_terms",
        [shape(rows, columns)]
        + [
            shape(len(along), share, columns, dtype=f32 if along == (far, 0) and across == 0 else bf16)
            for along, across in spots
        ],
        [],
        sector_sizes,
        mixing,
        left_own,
        left_other,
        right,
        wave_own,
        arrived,
        scratch=[pltpu.VMEM((sectors, rows, columns), f32)],
    )
    rest = dict(zip(spots, rest))
    mixing, live = call(
        tables_kernel,
        "tables_for_second_sigma",
        [shape(terms, sectors, 8, 128, dtype=f32), shape(rows, columns, dtype=f32)],
        [smem] * 3,
        *scalars,
        wave_other,
    )
    met = [partner(rest[(far, 0), across], {"sec": across}) for across in range(sectors)]
    far_sum = summed("sum_far_share", *met)
    received = [partner(far_sum, {"ops": far})]
    nearest = (direct[-1], 0)
    order = [spot for spot in rest if spot[0] in direct and spot != nearest]
    received += [partner(rest[spot], {"ops": spot[0][0], "sec": spot[1]}) for spot in order]
    last = summed("hand_on", rest[nearest], after=(far_sum,))
    received.append(partner(last, {"ops": nearest[0][0]}))
    first_share = summed("sum_first_sigma", *[(piece, 1) for piece in met], *received, live=live)
    along_ops = {along: partner(first_share, {"ops": along}) for along in send_order}
    spots = [(along, across) for along in send_order for across in range(1, sectors)]
    pieces = {
        (along, across): partner(first_share, {"ops": along, "sec": across})
        if along < 2
        else partner(along_ops[along], {"sec": across})
        for along, across in spots
    }
    ahead = [pieces[along, across] for along, across in spots if along < 2]
    sigma_own = call(
        lambda *refs: place_kernel([(along, 0) for along in send_order], *refs[len(ahead) :]),
        "place_own_sector",
        shape(1, rows, columns),
        [],
        *ahead,
        *along_ops.values(),
    )
    sigma_other = partner(sigma_own, {"rep": 1})
    across_own = call(
        lambda *refs: place_kernel([(along, across - 1) for along, across in spots], *refs),
        "place_other_sectors",
        shape(sectors - 1, rows, columns),
        [],
        *pieces.values(),
    )
    across_other = partner(across_own, {"rep": 1})

    products, across_products = call(
        left_kernel,
        "left_products",
        [
            shape(terms, rows, columns, dtype=f32),
            shape(sectors - 1, terms, rows, columns, dtype=f32),
        ],
        [],
        left_own,
        left_other,
        sigma_own,
        sigma_other,
        across_own,
    )
    shares = call(
        second_kernel,
        "second_sigma_terms",
        [shape(1, share, columns, dtype=f32)] + [shape(1, share, columns)] * (ops_count - 1),
        [],
        mixing,
        left_other,
        right,
        products,
        across_products,
        across_other,
        scratch=[pltpu.VMEM((rows, columns), f32)],
    )
    received = [partner(shares[step], {"ops": step}) for step in farthest_first[:-1]]
    sums = call(
        sums_kernel,
        "sums_for_rayleigh",
        shape(3, 8, 128, dtype=f32),
        [],
        wave_own,
        wave_other,
        sigma_own,
        sigma_other,
    )
    sums = [partner(sums, {"sec": step}) for step in range(sectors)]
    second_share = summed("sum_second_sigma", shares[0], *received, live=live, after=sums)
    second_wave, factors = call(
        wave_kernel,
        "second_wave",
        [shape(1, rows, columns), shape(2, 8, 128, dtype=f32)],
        [smem],
        sector_sizes,
        wave_own,
        sigma_own,
        *sums,
    )
    second_sigma = call(
        lambda *refs: join_kernel(farthest_first, *refs),
        "join_second_sigma",
        shape(1, rows, columns, dtype=f32),
        [],
        factors,
        sigma_own,
        *[partner(second_share, {"ops": step}) for step in farthest_first],
        scratch=[
            pltpu.VMEM((ops_count, share, columns), f32),
            pltpu.SemaphoreType.DMA((ops_count,)),
        ],
        out=outside,
    )
    return (second_wave, second_sigma)


def solution(mesh):
    return jax.shard_map(
        local,
        mesh=mesh,
        in_specs=(
            P(("grp", "sec"), "rep", None),
            P("grp", None),
            P(("grp", "ops"), None, None),
            P(("grp", "ops"), None, None),
            P(("grp", "ops"), None, None),
            P(("grp", "ops"), None),
        ),
        out_specs=(P(("grp", "sec"), "rep", None), P(("grp", "sec"), "rep", None)),
        check_vma=False,
    )
```

```python
import jax
import jax.numpy as jnp
from jax import lax
from jax.experimental import pallas as pl
from jax.experimental.pallas import tpu as pltpu
from jax.sharding import PartitionSpec as P

epsilon = 1e-06
mebibyte = 1024 * 1024


def mixing_scalar(pairs_ref, weights_ref, term, target, source):
    value = jnp.float32(0.0)
    for pair in range(weights_ref.shape[1]):
        hit = (pairs_ref[term, 1, pair] == target) & (pairs_ref[term, 0, pair] == source)
        value = value + jnp.where(hit, weights_ref[term, pair], jnp.float32(0.0))
    return value


def live_cells(sizes_ref, sector, row_start, rows, columns):
    row = row_start + lax.broadcasted_iota(jnp.int32, (rows, columns), 0)
    column = lax.broadcasted_iota(jnp.int32, (rows, columns), 1)
    return (row < sizes_ref[sector, 0]) & (column < sizes_ref[sector, 1])


def left_times(lefts, blocks):
    total = None
    for left, block in zip(lefts, blocks):
        terms, rows, depth = left.shape
        stacked = left[...].reshape(terms * rows, depth)
        part = jnp.dot(stacked, block, preferred_element_type=jnp.float32)
        total = part if total is None else total + part
    return total.reshape(terms, rows, -1)


def times_right(values, right, term):
    return lax.dot_general(
        values.astype(jnp.bfloat16),
        right[term],
        (((1,), (1,)), ((), ())),
        preferred_element_type=jnp.float32,
    )


def load_kernel(left_ref, left_own, left_other, sems):
    rows = left_own.shape[1]
    core = lax.axis_index("rep")
    copies = []
    for index, (half, place) in enumerate(((left_own, core), (left_other, core ^ 1))):
        mine = pl.ds(pl.multiple_of(core * rows, rows), rows)
        columns = pl.ds(pl.multiple_of(place * rows, rows), rows)
        copies.append(pltpu.make_async_copy(left_ref.at[:, mine, columns], half, sems.at[index]))
    for copy in copies:
        copy.start()
    for copy in copies:
        copy.wait()


def live_rows(sizes, sector, row_start, rows, columns):
    bounds = sizes[pl.ds(sector, 1), :]
    row = row_start + lax.broadcasted_iota(jnp.int32, (rows, columns), 0)
    column = lax.broadcasted_iota(jnp.int32, (rows, columns), 1)
    inside = (row < bounds[:, 0:1]) & (column < bounds[:, 1:2])
    return jnp.where(inside, 1.0, 0.0)


def first_tables_kernel(sizes, pairs, weights, wave, _, own, mixing):
    rows, columns = own.shape
    sector = lax.axis_index("sec")
    live = live_rows(sizes, sector, lax.axis_index("rep") * rows, rows, columns)
    own[...] = (wave[0].astype(jnp.float32) * live).astype(own.dtype)
    source, target = pairs[:, 0, :], pairs[:, 1, :]
    for step in range(mixing.shape[0]):
        hits = (source == sector) & (target == (sector ^ step))
        total = jnp.sum(jnp.where(hits, weights[...], 0.0), axis=1, keepdims=True)
        mixing[step] = jnp.broadcast_to(total, mixing.shape[1:])


def first_kernel(shares, *refs):
    sizes, mixing, left_own, left_other, right, own, arrived = refs[:7]
    other, *parts = refs[7:-1]
    held = refs[-1]
    rows, columns = own.shape
    share = parts[0].shape[-2]
    sectors = held.shape[0]
    sector = lax.axis_index("sec")
    core = lax.axis_index("rep")
    place = lax.axis_index("ops")
    live = live_rows(sizes, sector, (core ^ 1) * rows, rows, columns)
    other[...] = (arrived[0].astype(jnp.float32) * live).astype(other.dtype)
    products = left_times((left_own, left_other), (own[...], other[...]))
    totals = [None] * sectors
    for term in range(right.shape[0]):
        product = times_right(products[term], right, term)
        for step in range(sectors):
            weight = jnp.broadcast_to(mixing[step][term : term + 1, :1], (rows, columns))
            part = weight * product
            totals[step] = part if totals[step] is None else totals[step] + part
    for step in range(sectors):
        held[step] = totals[step]
    for (steps, across), out in zip(shares, parts):
        for index, along in enumerate(steps):
            start = pl.multiple_of((place ^ along) * share, share)
            out[index] = held[across, pl.ds(start, share), :].astype(out.dtype)


def sum_kernel(indices, masked, *refs):
    total = refs[0][indices[0]].astype(jnp.float32)
    for index, piece in zip(indices[1:], refs[1:]):
        total = total + piece[index].astype(jnp.float32)
    if masked:
        share = total.shape[0]
        start = pl.multiple_of(lax.axis_index("ops") * share, share)
        total = total * refs[len(indices)][pl.ds(start, share), :]
    refs[-1][0] = total.astype(refs[-1].dtype)


def place_kernel(spots, *refs):
    pieces, half = refs[:-1], refs[-1]
    share = pieces[0].shape[1]
    place = lax.axis_index("ops")
    for (along, index), piece in zip(spots, pieces):
        start = pl.multiple_of((place ^ along) * share, share)
        half[index, pl.ds(start, share), :] = piece[0]


def left_kernel(left_own, left_other, own, other, across_own, out, across_out):
    out[...] = left_times((left_own, left_other), (own[0], other[0]))
    for step in range(across_own.shape[0]):
        across_out[step] = left_times((left_own,), (across_own[step],))


def tables_kernel(sizes_ref, pairs_ref, weights_ref, _, mixing, live):
    target = lax.axis_index("sec")
    for term in range(mixing.shape[0]):
        for step in range(mixing.shape[1]):
            weight = mixing_scalar(pairs_ref, weights_ref, term, target, target ^ step)
            mixing[term, step] = jnp.full(mixing.shape[2:], weight, jnp.float32)
    rows, columns = live.shape
    cells = live_cells(sizes_ref, target, lax.axis_index("rep") * rows, rows, columns)
    live[...] = jnp.where(cells, 1.0, 0.0)


def second_kernel(mixing, left_other, right, products, across_products, other, *refs):
    shares, held = refs[:-1], refs[-1]
    rows, columns = products.shape[1:]
    share = shares[0].shape[1]
    place = lax.axis_index("ops")
    total = None
    across = [left_times((left_other,), (other[step],)) for step in range(other.shape[0])]
    for term in range(right.shape[0]):
        weights = [
            jnp.broadcast_to(mixing[term, step][:1, :1], (rows, columns))
            for step in range(len(across) + 1)
        ]
        combined = weights[0] * products[term]
        for step, part in enumerate(across):
            combined = combined + weights[step + 1] * (across_products[step, term] + part[term])
        part = times_right(combined, right, term)
        total = part if total is None else total + part
    held[...] = total
    for step, out in enumerate(shares):
        start = pl.multiple_of((place ^ step) * share, share)
        out[0] = held[pl.ds(start, share), :].astype(out.dtype)


def sums_kernel(wave_own, wave_other, sigma_own, sigma_other, out):
    step, columns = 16, wave_own.shape[1]
    sums = (jnp.zeros((step, columns), jnp.float32),) * 3
    for wave, sigma in ((wave_own, sigma_own), (wave_other, sigma_other)):

        def add_rows(block, carry):
            start = pl.multiple_of(block * step, step)
            w = wave[pl.ds(start, step), :].astype(jnp.float32)
            s = sigma[0, pl.ds(start, step), :].astype(jnp.float32)
            return (carry[0] + w * s, carry[1] + w * w, carry[2] + s * s)

        sums = lax.fori_loop(0, wave.shape[0] // step, add_rows, sums, unroll=2)
    for index, value in enumerate(sums):
        out[index] = jnp.broadcast_to(jnp.sum(value, keepdims=True), out.shape[1:])


def wave_kernel(sizes_ref, wave_own, sigma_own, *refs):
    sums, (second, factors) = refs[:-2], refs[-2:]
    rows, columns = wave_own.shape
    live_count = jnp.float32(0.0)
    for sector in range(sizes_ref.shape[0]):
        live_count = live_count + sizes_ref[sector, 0].astype(jnp.float32) * sizes_ref[
            sector, 1
        ].astype(jnp.float32)
    total = sums[0][...]
    for other in sums[1:]:
        total = total + other[...]
    correlation, norm_square, sigma_square = total[0], total[1], total[2]
    rayleigh = correlation / norm_square
    residual_square = (
        sigma_square - 2.0 * rayleigh * correlation + rayleigh * rayleigh * norm_square
    )
    residual_square = jnp.maximum(residual_square, 0.0)
    scale = 1.0 / jnp.sqrt(residual_square / live_count + epsilon)
    factors[0] = scale
    factors[1] = rayleigh * scale
    sigma_factor = jnp.broadcast_to(scale[:1, :1], (rows, columns))
    wave_factor = jnp.broadcast_to((rayleigh * scale)[:1, :1], (rows, columns))
    sigma = sigma_own[0].astype(jnp.float32)
    wave = wave_own[...].astype(jnp.float32)
    second[0] = (sigma_factor * sigma - wave_factor * wave).astype(second.dtype)


def join_kernel(order, factors, sigma_own, *refs):
    pieces, (out, held, sems) = refs[:-3], refs[-3:]
    _, share, columns = pieces[0].shape
    place = lax.axis_index("ops")
    scale = jnp.broadcast_to(factors[0][:1, :1], (share, columns))
    shift = jnp.broadcast_to(factors[1][:1, :1], (share, columns))
    copies = []
    for step, piece in zip(order, pieces):
        rows = pl.ds(pl.multiple_of((place ^ step) * share, share), share)
        moved = shift * sigma_own[0, rows, :].astype(jnp.float32)
        held[step] = scale * piece[0].astype(jnp.float32) - moved
        copies.append(pltpu.make_async_copy(held.at[step], out.at[0, rows], sems.at[step]))
        copies[-1].start()
    for copy in copies:
        copy.wait()


def partner(value, steps):
    steps = {axis: step for axis, step in steps.items() if step}
    if not steps:
        return value
    axes = tuple(steps)
    places = [()]
    for axis in axes:
        places = [place + (i,) for place in places for i in range(lax.axis_size(axis))]
    index = {place: i for i, place in enumerate(places)}
    pairs = [
        (index[tuple(i ^ steps[axis] for i, axis in zip(place, axes))], index[place])
        for place in places
    ]
    return lax.ppermute(value, axes, pairs)


def local(wavefunction, sector_sizes, left_blocks, right_blocks, sector_pairs, pair_weights):
    sectors = sector_sizes.shape[0]
    ops_count = lax.axis_size("ops")
    _, rows, columns = wavefunction.shape
    terms, side = left_blocks.shape[0], left_blocks.shape[1]
    share = rows // ops_count
    bf16, f32 = jnp.bfloat16, jnp.float32
    smem = pl.BlockSpec(memory_space=pltpu.SMEM)
    outside = pl.BlockSpec(memory_space=pltpu.HBM)
    inside = pl.BlockSpec(memory_space=pltpu.VMEM)

    def shape(*dims, dtype=bf16):
        return jax.ShapeDtypeStruct(dims, dtype)

    def call(kernel, name, out_shape, in_specs, *operands, scratch=(), vmem=16, out=inside):
        return pl.pallas_call(
            kernel,
            out_shape=out_shape,
            in_specs=list(in_specs) + [inside] * (len(operands) - len(in_specs)),
            out_specs=jax.tree.map(lambda _: out, out_shape),
            scratch_shapes=list(scratch),
            compiler_params=pltpu.CompilerParams(vmem_limit_bytes=vmem * mebibyte),
            name=name,
        )(*operands)

    def summed(name, *pieces, live=None, after=()):
        pieces = [piece if isinstance(piece, tuple) else (piece, 0) for piece in pieces]
        arrays, indices = zip(*pieces)
        return call(
            lambda *refs: sum_kernel(indices, live is not None, *refs),
            name,
            shape(1, share, columns),
            [],
            *arrays,
            *([] if live is None else [live]),
            *after,
        )

    farthest_first = list(reversed(range(ops_count)))
    send_order = farthest_first[1:2] + farthest_first[:1] + farthest_first[2:]
    arrived = partner(wavefunction, {"rep": 1})
    left_own, left_other = call(
        load_kernel,
        "load_operators",
        [shape(terms, rows, rows), shape(terms, rows, side - rows)],
        [outside],
        left_blocks,
        scratch=[pltpu.SemaphoreType.DMA((2,))],
        vmem=51,
    )
    right = right_blocks
    pairs = jnp.swapaxes(sector_pairs, 1, 2)
    scalars = (sector_sizes, pairs, pair_weights)

    far = ops_count - 1
    direct = [(along,) for along in farthest_first[1:-1]]
    spots = [((far, 0), across) for across in range(sectors)]
    spots += [(along, across) for along in direct for across in range(sectors)]
    wave_own, mixing = call(
        first_tables_kernel,
        "tables_for_first_sigma",
        [shape(rows, columns), shape(sectors, terms, 128, dtype=f32)],
        [],
        *scalars,
        wavefunction,
        left_own,
    )
    wave_other, *rest = call(
        lambda *refs: first_kernel(spots, *refs),
        "first_sigma_terms",
        [shape(rows, columns)]
        + [
            shape(len(along), share, columns, dtype=f32 if along == (far, 0) and across == 0 else bf16)
            for along, across in spots
        ],
        [],
        sector_sizes,
        mixing,
        left_own,
        left_other,
        right,
        wave_own,
        arrived,
        scratch=[pltpu.VMEM((sectors, rows, columns), f32)],
    )
    rest = dict(zip(spots, rest))
    mixing, live = call(
        tables_kernel,
        "tables_for_second_sigma",
        [shape(terms, sectors, 8, 128, dtype=f32), shape(rows, columns, dtype=f32)],
        [smem] * 3,
        *scalars,
        wave_other,
    )
    met = [partner(rest[(far, 0), across], {"sec": across}) for across in range(sectors)]
    received = [partner(summed("sum_far_share", *met), {"ops": far})]
    first_two = [(direct[0], 0), (direct[-1], 0)]
    order = first_two + [spot for spot in rest if spot[0] in direct and spot not in first_two]
    received += [partner(rest[spot], {"ops": spot[0][0], "sec": spot[1]}) for spot in order]
    first_share = summed("sum_first_sigma", *[(piece, 1) for piece in met], *received, live=live)
    crossed = {
        along: partner(first_share, {"ops": along}) for along in send_order if along % 2 == 0
    }
    spots = [(along, across) for along in send_order for across in range(1, sectors)]
    pieces = {
        (along, across): partner(crossed[along // 2 * 2], {"ops": along % 2, "sec": across})
        for along, across in spots
    }
    along_ops = {
        along: partner(crossed[along // 2 * 2], {"ops": along % 2}) for along in send_order
    }
    ahead = [pieces[along, across] for along, across in spots if along < 2]
    sigma_own = call(
        lambda *refs: place_kernel([(along, 0) for along in send_order], *refs[len(ahead) :]),
        "place_own_sector",
        shape(1, rows, columns),
        [],
        *ahead,
        *along_ops.values(),
    )
    sigma_other = partner(sigma_own, {"rep": 1})
    across_own = call(
        lambda *refs: place_kernel([(along, across - 1) for along, across in spots], *refs),
        "place_other_sectors",
        shape(sectors - 1, rows, columns),
        [],
        *pieces.values(),
    )
    across_other = partner(across_own, {"rep": 1})

    products, across_products = call(
        left_kernel,
        "left_products",
        [
            shape(terms, rows, columns, dtype=f32),
            shape(sectors - 1, terms, rows, columns, dtype=f32),
        ],
        [],
        left_own,
        left_other,
        sigma_own,
        sigma_other,
        across_own,
    )
    shares = call(
        second_kernel,
        "second_sigma_terms",
        [shape(1, share, columns, dtype=f32)] + [shape(1, share, columns)] * (ops_count - 1),
        [],
        mixing,
        left_other,
        right,
        products,
        across_products,
        across_other,
        scratch=[pltpu.VMEM((rows, columns), f32)],
    )
    received = [partner(shares[step], {"ops": step}) for step in farthest_first[:-1]]
    sums = call(
        sums_kernel,
        "sums_for_rayleigh",
        shape(3, 8, 128, dtype=f32),
        [],
        wave_own,
        wave_other,
        sigma_own,
        sigma_other,
    )
    sums = [partner(sums, {"sec": step}) for step in range(sectors)]
    second_share = summed("sum_second_sigma", shares[0], *received, live=live, after=sums)
    second_wave, factors = call(
        wave_kernel,
        "second_wave",
        [shape(1, rows, columns), shape(2, 8, 128, dtype=f32)],
        [smem],
        sector_sizes,
        wave_own,
        sigma_own,
        *sums,
    )
    second_sigma = call(
        lambda *refs: join_kernel(farthest_first, *refs),
        "join_second_sigma",
        shape(1, rows, columns, dtype=f32),
        [],
        factors,
        sigma_own,
        *[partner(second_share, {"ops": step}) for step in farthest_first],
        scratch=[
            pltpu.VMEM((ops_count, share, columns), f32),
            pltpu.SemaphoreType.DMA((ops_count,)),
        ],
        out=outside,
    )
    return (second_wave, second_sigma)


def solution(mesh):
    return jax.shard_map(
        local,
        mesh=mesh,
        in_specs=(
            P(("grp", "sec"), "rep", None),
            P("grp", None),
            P(("grp", "ops"), None, None),
            P(("grp", "ops"), None, None),
            P(("grp", "ops"), None, None),
            P(("grp", "ops"), None),
        ),
        out_specs=(P(("grp", "sec"), "rep", None), P(("grp", "sec"), "rep", None)),
        check_vma=False,
    )
```

```python
import jax
import jax.numpy as jnp
from jax import lax
from jax.experimental import pallas as pl
from jax.experimental.pallas import tpu as pltpu
from jax.sharding import PartitionSpec as P

epsilon = 1e-06
mebibyte = 1024 * 1024


def mixing_scalar(pairs_ref, weights_ref, term, target, source):
    value = jnp.float32(0.0)
    for pair in range(weights_ref.shape[1]):
        hit = (pairs_ref[term, 1, pair] == target) & (pairs_ref[term, 0, pair] == source)
        value = value + jnp.where(hit, weights_ref[term, pair], jnp.float32(0.0))
    return value


def live_cells(sizes_ref, sector, row_start, rows, columns):
    row = row_start + lax.broadcasted_iota(jnp.int32, (rows, columns), 0)
    column = lax.broadcasted_iota(jnp.int32, (rows, columns), 1)
    return (row < sizes_ref[sector, 0]) & (column < sizes_ref[sector, 1])


def masked(values, live):
    return jnp.where(live, values.astype(jnp.float32), 0.0).astype(values.dtype)


def left_times(lefts, blocks):
    total = None
    for left, block in zip(lefts, blocks):
        terms, rows, depth = left.shape
        stacked = left[...].reshape(terms * rows, depth)
        part = jnp.dot(stacked, block, preferred_element_type=jnp.float32)
        total = part if total is None else total + part
    return total.reshape(terms, rows, -1)


def times_right(values, right, term):
    return lax.dot_general(
        values.astype(jnp.bfloat16),
        right[term],
        (((1,), (1,)), ((), ())),
        preferred_element_type=jnp.float32,
    )


def load_kernel(left_ref, left_own, left_other, sems):
    rows = left_own.shape[1]
    core = lax.axis_index("rep")
    copies = []
    for index, (half, place) in enumerate(((left_own, core), (left_other, core ^ 1))):
        mine = pl.ds(pl.multiple_of(core * rows, rows), rows)
        columns = pl.ds(pl.multiple_of(place * rows, rows), rows)
        copies.append(pltpu.make_async_copy(left_ref.at[:, mine, columns], half, sems.at[index]))
    for copy in copies:
        copy.start()
    for copy in copies:
        copy.wait()


def live_rows(sizes, sector, row_start, rows, columns):
    bounds = sizes[pl.ds(sector, 1), :]
    row = row_start + lax.broadcasted_iota(jnp.int32, (rows, columns), 0)
    column = lax.broadcasted_iota(jnp.int32, (rows, columns), 1)
    inside = (row < bounds[:, 0:1]) & (column < bounds[:, 1:2])
    return jnp.where(inside, 1.0, 0.0)


def first_tables_kernel(sizes, pairs, weights, wave, _, own, mixing):
    rows, columns = own.shape
    sector = lax.axis_index("sec")
    live = live_rows(sizes, sector, lax.axis_index("rep") * rows, rows, columns)
    own[...] = (wave[0].astype(jnp.float32) * live).astype(own.dtype)
    source, target = pairs[:, 0, :], pairs[:, 1, :]
    for step in range(mixing.shape[0]):
        hits = (source == sector) & (target == (sector ^ step))
        total = jnp.sum(jnp.where(hits, weights[...], 0.0), axis=1, keepdims=True)
        mixing[step] = jnp.broadcast_to(total, mixing.shape[1:])


def first_kernel(shares, *refs):
    sizes, mixing, left_own, left_other, right, own, arrived = refs[:7]
    other, *parts = refs[7:-1]
    held = refs[-1]
    rows, columns = own.shape
    share = parts[0].shape[-2]
    sectors = held.shape[0]
    sector = lax.axis_index("sec")
    core = lax.axis_index("rep")
    place = lax.axis_index("ops")
    live = live_rows(sizes, sector, (core ^ 1) * rows, rows, columns)
    other[...] = (arrived[0].astype(jnp.float32) * live).astype(other.dtype)
    products = left_times((left_own, left_other), (own[...], other[...]))
    totals = [None] * sectors
    for term in range(right.shape[0]):
        product = times_right(products[term], right, term)
        for step in range(sectors):
            weight = jnp.broadcast_to(mixing[step][term : term + 1, :1], (rows, columns))
            part = weight * product
            totals[step] = part if totals[step] is None else totals[step] + part
    for step in range(sectors):
        held[step] = totals[step]
    for (steps, across), out in zip(shares, parts):
        for index, along in enumerate(steps):
            start = pl.multiple_of((place ^ along) * share, share)
            out[index] = held[across, pl.ds(start, share), :].astype(out.dtype)


def sum_kernel(indices, masked, *refs):
    total = refs[0][indices[0]].astype(jnp.float32)
    for index, piece in zip(indices[1:], refs[1:]):
        total = total + piece[index].astype(jnp.float32)
    if masked:
        share = total.shape[0]
        start = pl.multiple_of(lax.axis_index("ops") * share, share)
        total = total * refs[len(indices)][pl.ds(start, share), :]
    refs[-1][0] = total.astype(refs[-1].dtype)


def place_kernel(spots, *refs):
    pieces, half = refs[:-1], refs[-1]
    share = pieces[0].shape[1]
    place = lax.axis_index("ops")
    for (along, index), piece in zip(spots, pieces):
        start = pl.multiple_of((place ^ along) * share, share)
        half[index, pl.ds(start, share), :] = piece[0]


def left_kernel(left_own, left_other, own, other, across_own, out, across_out):
    out[...] = left_times((left_own, left_other), (own[0], other[0]))
    for step in range(across_own.shape[0]):
        across_out[step] = left_times((left_own,), (across_own[step],))


def tables_kernel(sizes_ref, pairs_ref, weights_ref, _, mixing, live):
    target = lax.axis_index("sec")
    for term in range(mixing.shape[0]):
        for step in range(mixing.shape[1]):
            weight = mixing_scalar(pairs_ref, weights_ref, term, target, target ^ step)
            mixing[term, step] = jnp.full(mixing.shape[2:], weight, jnp.float32)
    rows, columns = live.shape
    cells = live_cells(sizes_ref, target, lax.axis_index("rep") * rows, rows, columns)
    live[...] = jnp.where(cells, 1.0, 0.0)


def second_kernel(mixing, left_other, right, products, across_products, other, *refs):
    shares, held = refs[:-1], refs[-1]
    rows, columns = products.shape[1:]
    share = shares[0].shape[1]
    place = lax.axis_index("ops")
    total = None
    across = [left_times((left_other,), (other[step],)) for step in range(other.shape[0])]
    for term in range(right.shape[0]):
        weights = [
            jnp.broadcast_to(mixing[term, step][:1, :1], (rows, columns))
            for step in range(len(across) + 1)
        ]
        combined = weights[0] * products[term]
        for step, part in enumerate(across):
            combined = combined + weights[step + 1] * (across_products[step, term] + part[term])
        part = times_right(combined, right, term)
        total = part if total is None else total + part
    held[...] = total
    for step, out in enumerate(shares):
        start = pl.multiple_of((place ^ step) * share, share)
        out[0] = held[pl.ds(start, share), :].astype(out.dtype)


def sums_kernel(wave_own, wave_other, sigma_own, sigma_other, out):
    step, columns = 16, wave_own.shape[1]
    sums = (jnp.zeros((step, columns), jnp.float32),) * 3
    for wave, sigma in ((wave_own, sigma_own), (wave_other, sigma_other)):

        def add_rows(block, carry):
            start = pl.multiple_of(block * step, step)
            w = wave[pl.ds(start, step), :].astype(jnp.float32)
            s = sigma[0, pl.ds(start, step), :].astype(jnp.float32)
            return (carry[0] + w * s, carry[1] + w * w, carry[2] + s * s)

        sums = lax.fori_loop(0, wave.shape[0] // step, add_rows, sums, unroll=2)
    for index, value in enumerate(sums):
        out[index] = jnp.broadcast_to(jnp.sum(value, keepdims=True), out.shape[1:])


def wave_kernel(sizes_ref, wave_own, sigma_own, *refs):
    sums, (second, factors) = refs[:-2], refs[-2:]
    rows, columns = wave_own.shape
    live_count = jnp.float32(0.0)
    for sector in range(sizes_ref.shape[0]):
        live_count = live_count + sizes_ref[sector, 0].astype(jnp.float32) * sizes_ref[
            sector, 1
        ].astype(jnp.float32)
    total = sums[0][...]
    for other in sums[1:]:
        total = total + other[...]
    correlation, norm_square, sigma_square = total[0], total[1], total[2]
    rayleigh = correlation / norm_square
    residual_square = (
        sigma_square - 2.0 * rayleigh * correlation + rayleigh * rayleigh * norm_square
    )
    residual_square = jnp.maximum(residual_square, 0.0)
    scale = 1.0 / jnp.sqrt(residual_square / live_count + epsilon)
    factors[0] = scale
    factors[1] = rayleigh * scale
    sigma_factor = jnp.broadcast_to(scale[:1, :1], (rows, columns))
    wave_factor = jnp.broadcast_to((rayleigh * scale)[:1, :1], (rows, columns))
    sigma = sigma_own[0].astype(jnp.float32)
    wave = wave_own[...].astype(jnp.float32)
    second[0] = (sigma_factor * sigma - wave_factor * wave).astype(second.dtype)


def join_kernel(steps, factors, sigma_own, *refs):
    pieces, (out, held, sems) = refs[: len(steps)], refs[-3:]
    _, share, columns = pieces[0].shape
    place = lax.axis_index("ops")
    scale = jnp.broadcast_to(factors[0][:1, :1], (share, columns))
    shift = jnp.broadcast_to(factors[1][:1, :1], (share, columns))
    copies = []
    for index, (step, piece) in enumerate(zip(steps, pieces)):
        rows = pl.ds(pl.multiple_of((place ^ step) * share, share), share)
        moved = shift * sigma_own[0, rows, :].astype(jnp.float32)
        held[index] = scale * piece[0].astype(jnp.float32) - moved
        copies.append(pltpu.make_async_copy(held.at[index], out.at[0, rows], sems.at[index]))
        copies[-1].start()
    for copy in copies:
        copy.wait()


def partner(value, steps):
    steps = {axis: step for axis, step in steps.items() if step}
    if not steps:
        return value
    axes = tuple(steps)
    places = [()]
    for axis in axes:
        places = [place + (i,) for place in places for i in range(lax.axis_size(axis))]
    index = {place: i for i, place in enumerate(places)}
    pairs = [
        (index[tuple(i ^ steps[axis] for i, axis in zip(place, axes))], index[place])
        for place in places
    ]
    return lax.ppermute(value, axes, pairs)


def local(wavefunction, sector_sizes, left_blocks, right_blocks, sector_pairs, pair_weights):
    sectors = sector_sizes.shape[0]
    ops_count = lax.axis_size("ops")
    _, rows, columns = wavefunction.shape
    terms, side = left_blocks.shape[0], left_blocks.shape[1]
    share = rows // ops_count
    bf16, f32 = jnp.bfloat16, jnp.float32
    smem = pl.BlockSpec(memory_space=pltpu.SMEM)
    outside = pl.BlockSpec(memory_space=pltpu.HBM)
    inside = pl.BlockSpec(memory_space=pltpu.VMEM)

    def shape(*dims, dtype=bf16):
        return jax.ShapeDtypeStruct(dims, dtype)

    def call(kernel, name, out_shape, in_specs, *operands, scratch=(), vmem=16, out=inside):
        return pl.pallas_call(
            kernel,
            out_shape=out_shape,
            in_specs=list(in_specs) + [inside] * (len(operands) - len(in_specs)),
            out_specs=jax.tree.map(lambda _: out, out_shape),
            scratch_shapes=list(scratch),
            compiler_params=pltpu.CompilerParams(vmem_limit_bytes=vmem * mebibyte),
            name=name,
        )(*operands)

    def summed(name, *pieces, live=None, after=()):
        pieces = [piece if isinstance(piece, tuple) else (piece, 0) for piece in pieces]
        arrays, indices = zip(*pieces)
        return call(
            lambda *refs: sum_kernel(indices, live is not None, *refs),
            name,
            shape(1, share, columns),
            [],
            *arrays,
            *([] if live is None else [live]),
            *after,
        )

    farthest_first = list(reversed(range(ops_count)))
    send_order = farthest_first[1:2] + farthest_first[:1] + farthest_first[2:]
    arrived = partner(wavefunction, {"rep": 1})
    left_own, left_other = call(
        load_kernel,
        "load_operators",
        [shape(terms, rows, rows), shape(terms, rows, side - rows)],
        [outside],
        left_blocks,
        scratch=[pltpu.SemaphoreType.DMA((2,))],
        vmem=51,
    )
    right = right_blocks
    pairs = jnp.swapaxes(sector_pairs, 1, 2)
    scalars = (sector_sizes, pairs, pair_weights)

    far = ops_count - 1
    direct = [(along,) for along in farthest_first[1:-1]]
    spots = [((far, 0), across) for across in range(sectors)]
    spots += [(along, across) for along in direct for across in range(sectors)]
    wave_own, mixing = call(
        first_tables_kernel,
        "tables_for_first_sigma",
        [shape(rows, columns), shape(sectors, terms, 128, dtype=f32)],
        [],
        *scalars,
        wavefunction,
        left_own,
    )
    wave_other, *rest = call(
        lambda *refs: first_kernel(spots, *refs),
        "first_sigma_terms",
        [shape(rows, columns)]
        + [
            shape(len(along), share, columns, dtype=f32 if along == (far, 0) and across == 0 else bf16)
            for along, across in spots
        ],
        [],
        sector_sizes,
        mixing,
        left_own,
        left_other,
        right,
        wave_own,
        arrived,
        scratch=[pltpu.VMEM((sectors, rows, columns), f32)],
    )
    rest = dict(zip(spots, rest))
    mixing, live = call(
        tables_kernel,
        "tables_for_second_sigma",
        [shape(terms, sectors, 8, 128, dtype=f32), shape(rows, columns, dtype=f32)],
        [smem] * 3,
        *scalars,
        wave_other,
    )
    met = [partner(rest[(far, 0), across], {"sec": across}) for across in range(sectors)]
    received = [partner(summed("sum_far_share", *met), {"ops": far})]
    first_two = [(direct[0], 0), (direct[-1], 0)]
    order = first_two + [spot for spot in rest if spot[0] in direct and spot not in first_two]
    received += [partner(rest[spot], {"ops": spot[0][0], "sec": spot[1]}) for spot in order]
    first_share = summed("sum_first_sigma", *[(piece, 1) for piece in met], *received, live=live)
    along_ops = {along: partner(first_share, {"ops": along}) for along in send_order}
    sigma_own = call(
        lambda *refs: place_kernel([(along, 0) for along in send_order], *refs),
        "place_own_sector",
        shape(1, rows, columns),
        [],
        *along_ops.values(),
    )
    sigma_other = partner(sigma_own, {"rep": 1})
    spots = [(along, across) for along in send_order for across in range(1, sectors)]
    pieces = [
        partner(first_share, {"ops": along, "sec": across})
        if along < 2
        else partner(along_ops[along], {"sec": across})
        for along, across in spots
    ]
    across_own = call(
        lambda *refs: place_kernel([(along, across - 1) for along, across in spots], *refs),
        "place_other_sectors",
        shape(sectors - 1, rows, columns),
        [],
        *pieces,
    )
    across_other = partner(across_own, {"rep": 1})

    products, across_products = call(
        left_kernel,
        "left_products",
        [
            shape(terms, rows, columns, dtype=f32),
            shape(sectors - 1, terms, rows, columns, dtype=f32),
        ],
        [],
        left_own,
        left_other,
        sigma_own,
        sigma_other,
        across_own,
    )
    shares = call(
        second_kernel,
        "second_sigma_terms",
        [shape(1, share, columns, dtype=f32)] + [shape(1, share, columns)] * (ops_count - 1),
        [],
        mixing,
        left_other,
        right,
        products,
        across_products,
        across_other,
        scratch=[pltpu.VMEM((rows, columns), f32)],
    )
    received = [partner(shares[step], {"ops": step}) for step in farthest_first[:-1]]
    sums = call(
        sums_kernel,
        "sums_for_rayleigh",
        shape(3, 8, 128, dtype=f32),
        [],
        wave_own,
        wave_other,
        sigma_own,
        sigma_other,
    )
    sums = [partner(sums, {"sec": step}) for step in range(sectors)]
    second_share = summed("sum_second_sigma", shares[0], *received, live=live, after=sums)
    second_wave, factors = call(
        wave_kernel,
        "second_wave",
        [shape(1, rows, columns), shape(2, 8, 128, dtype=f32)],
        [smem],
        sector_sizes,
        wave_own,
        sigma_own,
        *sums,
    )
    arrived = {along: partner(second_share, {"ops": along}) for along in farthest_first}
    early = [farthest_first[0], 0]
    late = farthest_first[1:-1]
    second_sigma = None
    for steps, name in ((early, "join_early_shares"), (late, "join_late_shares")):
        operands = [factors, sigma_own, *[arrived[along] for along in steps]]
        specs = [inside] * len(operands)
        aliases = {}
        if second_sigma is not None:
            aliases = {len(operands): 0}
            operands.append(second_sigma)
            specs.append(outside)
        second_sigma = pl.pallas_call(
            lambda *refs, steps=steps: join_kernel(steps, *refs),
            out_shape=shape(1, rows, columns, dtype=f32),
            in_specs=specs,
            out_specs=outside,
            input_output_aliases=aliases,
            scratch_shapes=[
                pltpu.VMEM((len(steps), share, columns), f32),
                pltpu.SemaphoreType.DMA((len(steps),)),
            ],
            compiler_params=pltpu.CompilerParams(vmem_limit_bytes=16 * mebibyte),
            name=name,
        )(*operands)
    return (second_wave, second_sigma)


def solution(mesh):
    return jax.shard_map(
        local,
        mesh=mesh,
        in_specs=(
            P(("grp", "sec"), "rep", None),
            P("grp", None),
            P(("grp", "ops"), None, None),
            P(("grp", "ops"), None, None),
            P(("grp", "ops"), None, None),
            P(("grp", "ops"), None),
        ),
        out_specs=(P(("grp", "sec"), "rep", None), P(("grp", "sec"), "rep", None)),
        check_vma=False,
    )
```

```python
import jax
import jax.numpy as jnp
from jax import lax
from jax.experimental import pallas as pl
from jax.experimental.pallas import tpu as pltpu
from jax.sharding import PartitionSpec as P

epsilon = 1e-06
mebibyte = 1024 * 1024


def mixing_scalar(pairs_ref, weights_ref, term, target, source):
    value = jnp.float32(0.0)
    for pair in range(weights_ref.shape[1]):
        hit = (pairs_ref[term, 1, pair] == target) & (pairs_ref[term, 0, pair] == source)
        value = value + jnp.where(hit, weights_ref[term, pair], jnp.float32(0.0))
    return value


def live_cells(sizes_ref, sector, row_start, rows, columns):
    row = row_start + lax.broadcasted_iota(jnp.int32, (rows, columns), 0)
    column = lax.broadcasted_iota(jnp.int32, (rows, columns), 1)
    return (row < sizes_ref[sector, 0]) & (column < sizes_ref[sector, 1])


def left_times(lefts, blocks):
    total = None
    for left, block in zip(lefts, blocks):
        terms, rows, depth = left.shape
        stacked = left[...].reshape(terms * rows, depth)
        part = jnp.dot(stacked, block, preferred_element_type=jnp.float32)
        total = part if total is None else total + part
    return total.reshape(terms, rows, -1)


def times_right(values, right, term):
    return lax.dot_general(
        values.astype(jnp.bfloat16),
        right[term],
        (((1,), (1,)), ((), ())),
        preferred_element_type=jnp.float32,
    )


def load_kernel(left_ref, left_own, left_other, sems):
    rows = left_own.shape[1]
    core = lax.axis_index("rep")
    copies = []
    for index, (half, place) in enumerate(((left_own, core), (left_other, core ^ 1))):
        mine = pl.ds(pl.multiple_of(core * rows, rows), rows)
        columns = pl.ds(pl.multiple_of(place * rows, rows), rows)
        copies.append(pltpu.make_async_copy(left_ref.at[:, mine, columns], half, sems.at[index]))
    for copy in copies:
        copy.start()
    for copy in copies:
        copy.wait()


def live_rows(sizes, sector, row_start, rows, columns):
    bounds = sizes[pl.ds(sector, 1), :]
    row = row_start + lax.broadcasted_iota(jnp.int32, (rows, columns), 0)
    column = lax.broadcasted_iota(jnp.int32, (rows, columns), 1)
    inside = (row < bounds[:, 0:1]) & (column < bounds[:, 1:2])
    return jnp.where(inside, 1.0, 0.0)


def first_tables_kernel(sizes, pairs, weights, wave, _, own, mixing):
    rows, columns = own.shape
    sector = lax.axis_index("sec")
    live = live_rows(sizes, sector, lax.axis_index("rep") * rows, rows, columns)
    own[...] = (wave[0].astype(jnp.float32) * live).astype(own.dtype)
    source, target = pairs[:, 0, :], pairs[:, 1, :]
    for step in range(mixing.shape[0]):
        hits = (source == sector) & (target == (sector ^ step))
        total = jnp.sum(jnp.where(hits, weights[...], 0.0), axis=1, keepdims=True)
        mixing[step] = jnp.broadcast_to(total, mixing.shape[1:])


def first_kernel(shares, *refs):
    sizes, mixing, left_own, left_other, right, own, arrived = refs[:7]
    other, *parts = refs[7:-1]
    held = refs[-1]
    rows, columns = own.shape
    share = parts[0].shape[-2]
    sectors = held.shape[0]
    sector = lax.axis_index("sec")
    core = lax.axis_index("rep")
    place = lax.axis_index("ops")
    live = live_rows(sizes, sector, (core ^ 1) * rows, rows, columns)
    other[...] = (arrived[0].astype(jnp.float32) * live).astype(other.dtype)
    products = left_times((left_own, left_other), (own[...], other[...]))
    totals = [None] * sectors
    for term in range(right.shape[0]):
        product = times_right(products[term], right, term)
        for step in range(sectors):
            weight = jnp.broadcast_to(mixing[step][term : term + 1, :1], (rows, columns))
            part = weight * product
            totals[step] = part if totals[step] is None else totals[step] + part
    for step in range(sectors):
        held[step] = totals[step]
    for (steps, across), out in zip(shares, parts):
        for index, along in enumerate(steps):
            start = pl.multiple_of((place ^ along) * share, share)
            out[index] = held[across, pl.ds(start, share), :].astype(out.dtype)


def sum_kernel(indices, masked, *refs):
    total = refs[0][indices[0]].astype(jnp.float32)
    for index, piece in zip(indices[1:], refs[1:]):
        total = total + piece[index].astype(jnp.float32)
    if masked:
        share = total.shape[0]
        start = pl.multiple_of(lax.axis_index("ops") * share, share)
        total = total * refs[len(indices)][pl.ds(start, share), :]
    refs[-1][0] = total.astype(refs[-1].dtype)


def place_kernel(spots, *refs):
    pieces, half = refs[:-1], refs[-1]
    share = pieces[0].shape[1]
    place = lax.axis_index("ops")
    for (along, index), piece in zip(spots, pieces):
        start = pl.multiple_of((place ^ along) * share, share)
        half[index, pl.ds(start, share), :] = piece[0]


def left_kernel(left_own, left_other, own, other, across_own, out, across_out):
    out[...] = left_times((left_own, left_other), (own[0], other[0]))
    for step in range(across_own.shape[0]):
        across_out[step] = left_times((left_own,), (across_own[step],))


def tables_kernel(sizes_ref, pairs_ref, weights_ref, _, mixing, live):
    target = lax.axis_index("sec")
    for term in range(mixing.shape[0]):
        for step in range(mixing.shape[1]):
            weight = mixing_scalar(pairs_ref, weights_ref, term, target, target ^ step)
            mixing[term, step] = jnp.full(mixing.shape[2:], weight, jnp.float32)
    rows, columns = live.shape
    cells = live_cells(sizes_ref, target, lax.axis_index("rep") * rows, rows, columns)
    live[...] = jnp.where(cells, 1.0, 0.0)


def second_kernel(mixing, left_other, right, products, across_products, other, *refs):
    shares, held = refs[:-1], refs[-1]
    rows, columns = products.shape[1:]
    share = shares[0].shape[1]
    place = lax.axis_index("ops")
    total = None
    across = [left_times((left_other,), (other[step],)) for step in range(other.shape[0])]
    for term in range(right.shape[0]):
        weights = [
            jnp.broadcast_to(mixing[term, step][:1, :1], (rows, columns))
            for step in range(len(across) + 1)
        ]
        combined = weights[0] * products[term]
        for step, part in enumerate(across):
            combined = combined + weights[step + 1] * (across_products[step, term] + part[term])
        part = times_right(combined, right, term)
        total = part if total is None else total + part
    held[...] = total
    for step, out in enumerate(shares):
        start = pl.multiple_of((place ^ step) * share, share)
        out[0] = held[pl.ds(start, share), :].astype(out.dtype)


def sums_kernel(wave_own, wave_other, sigma_own, sigma_other, out):
    step, columns = 16, wave_own.shape[1]
    sums = (jnp.zeros((step, columns), jnp.float32),) * 3
    for wave, sigma in ((wave_own, sigma_own), (wave_other, sigma_other)):

        def add_rows(block, carry):
            start = pl.multiple_of(block * step, step)
            w = wave[pl.ds(start, step), :].astype(jnp.float32)
            s = sigma[0, pl.ds(start, step), :].astype(jnp.float32)
            return (carry[0] + w * s, carry[1] + w * w, carry[2] + s * s)

        sums = lax.fori_loop(0, wave.shape[0] // step, add_rows, sums, unroll=2)
    for index, value in enumerate(sums):
        out[index] = jnp.broadcast_to(jnp.sum(value, keepdims=True), out.shape[1:])


def wave_kernel(sizes_ref, wave_own, sigma_own, *refs):
    sums, (second, factors) = refs[:-2], refs[-2:]
    rows, columns = wave_own.shape
    live_count = jnp.float32(0.0)
    for sector in range(sizes_ref.shape[0]):
        live_count = live_count + sizes_ref[sector, 0].astype(jnp.float32) * sizes_ref[
            sector, 1
        ].astype(jnp.float32)
    total = sums[0][...]
    for other in sums[1:]:
        total = total + other[...]
    correlation, norm_square, sigma_square = total[0], total[1], total[2]
    rayleigh = correlation / norm_square
    residual_square = (
        sigma_square - 2.0 * rayleigh * correlation + rayleigh * rayleigh * norm_square
    )
    residual_square = jnp.maximum(residual_square, 0.0)
    scale = 1.0 / jnp.sqrt(residual_square / live_count + epsilon)
    factors[0] = scale
    factors[1] = rayleigh * scale
    sigma_factor = jnp.broadcast_to(scale[:1, :1], (rows, columns))
    wave_factor = jnp.broadcast_to((rayleigh * scale)[:1, :1], (rows, columns))
    sigma = sigma_own[0].astype(jnp.float32)
    wave = wave_own[...].astype(jnp.float32)
    second[0] = (sigma_factor * sigma - wave_factor * wave).astype(second.dtype)


def join_kernel(steps, factors, sigma_own, *refs):
    pieces, (out, held, sems) = refs[: len(steps)], refs[-3:]
    _, share, columns = pieces[0].shape
    place = lax.axis_index("ops")
    scale = jnp.broadcast_to(factors[0][:1, :1], (share, columns))
    shift = jnp.broadcast_to(factors[1][:1, :1], (share, columns))
    copies = []
    for index, (step, piece) in enumerate(zip(steps, pieces)):
        rows = pl.ds(pl.multiple_of((place ^ step) * share, share), share)
        moved = shift * sigma_own[0, rows, :].astype(jnp.float32)
        held[index] = scale * piece[0].astype(jnp.float32) - moved
        copies.append(pltpu.make_async_copy(held.at[index], out.at[0, rows], sems.at[index]))
        copies[-1].start()
    for copy in copies:
        copy.wait()


def partner(value, steps):
    steps = {axis: step for axis, step in steps.items() if step}
    if not steps:
        return value
    axes = tuple(steps)
    places = [()]
    for axis in axes:
        places = [place + (i,) for place in places for i in range(lax.axis_size(axis))]
    index = {place: i for i, place in enumerate(places)}
    pairs = [
        (index[tuple(i ^ steps[axis] for i, axis in zip(place, axes))], index[place])
        for place in places
    ]
    return lax.ppermute(value, axes, pairs)


def local(wavefunction, sector_sizes, left_blocks, right_blocks, sector_pairs, pair_weights):
    sectors = sector_sizes.shape[0]
    ops_count = lax.axis_size("ops")
    _, rows, columns = wavefunction.shape
    terms, side = left_blocks.shape[0], left_blocks.shape[1]
    share = rows // ops_count
    bf16, f32 = jnp.bfloat16, jnp.float32
    smem = pl.BlockSpec(memory_space=pltpu.SMEM)
    outside = pl.BlockSpec(memory_space=pltpu.HBM)
    inside = pl.BlockSpec(memory_space=pltpu.VMEM)

    def shape(*dims, dtype=bf16):
        return jax.ShapeDtypeStruct(dims, dtype)

    def call(kernel, name, out_shape, in_specs, *operands, scratch=(), vmem=16, out=inside):
        return pl.pallas_call(
            kernel,
            out_shape=out_shape,
            in_specs=list(in_specs) + [inside] * (len(operands) - len(in_specs)),
            out_specs=jax.tree.map(lambda _: out, out_shape),
            scratch_shapes=list(scratch),
            compiler_params=pltpu.CompilerParams(vmem_limit_bytes=vmem * mebibyte),
            name=name,
        )(*operands)

    def summed(name, *pieces, live=None, after=()):
        pieces = [piece if isinstance(piece, tuple) else (piece, 0) for piece in pieces]
        arrays, indices = zip(*pieces)
        return call(
            lambda *refs: sum_kernel(indices, live is not None, *refs),
            name,
            shape(1, share, columns),
            [],
            *arrays,
            *([] if live is None else [live]),
            *after,
        )

    farthest_first = list(reversed(range(ops_count)))
    send_order = farthest_first[1:2] + farthest_first[:1] + farthest_first[2:]
    arrived = partner(wavefunction, {"rep": 1})
    left_own, left_other = call(
        load_kernel,
        "load_operators",
        [shape(terms, rows, rows), shape(terms, rows, side - rows)],
        [outside],
        left_blocks,
        scratch=[pltpu.SemaphoreType.DMA((2,))],
        vmem=51,
    )
    right = right_blocks
    pairs = jnp.swapaxes(sector_pairs, 1, 2)
    scalars = (sector_sizes, pairs, pair_weights)

    far = ops_count - 1
    direct = [(along,) for along in farthest_first[1:-1]]
    spots = [((far, 0), across) for across in range(sectors)]
    spots += [(along, across) for along in direct for across in range(sectors)]
    wave_own, mixing = call(
        first_tables_kernel,
        "tables_for_first_sigma",
        [shape(rows, columns), shape(sectors, terms, 128, dtype=f32)],
        [],
        *scalars,
        wavefunction,
        left_own,
    )
    wave_other, *rest = call(
        lambda *refs: first_kernel(spots, *refs),
        "first_sigma_terms",
        [shape(rows, columns)]
        + [
            shape(len(along), share, columns, dtype=f32 if along == (far, 0) and across == 0 else bf16)
            for along, across in spots
        ],
        [],
        sector_sizes,
        mixing,
        left_own,
        left_other,
        right,
        wave_own,
        arrived,
        scratch=[pltpu.VMEM((sectors, rows, columns), f32)],
    )
    rest = dict(zip(spots, rest))
    mixing, live = call(
        tables_kernel,
        "tables_for_second_sigma",
        [shape(terms, sectors, 8, 128, dtype=f32), shape(rows, columns, dtype=f32)],
        [smem] * 3,
        *scalars,
        wave_other,
    )
    met = [partner(rest[(far, 0), across], {"sec": across}) for across in range(sectors)]
    received = [partner(summed("sum_far_share", *met), {"ops": far})]
    first_two = [(direct[0], 0), (direct[-1], 0)]
    order = first_two + [spot for spot in rest if spot[0] in direct and spot not in first_two]
    received += [partner(rest[spot], {"ops": spot[0][0], "sec": spot[1]}) for spot in order]
    first_share = summed("sum_first_sigma", *[(piece, 1) for piece in met], *received, live=live)
    along_ops = {along: partner(first_share, {"ops": along}) for along in send_order}
    spots = [(along, across) for along in send_order for across in range(1, sectors)]
    pieces = {
        (along, across): partner(first_share, {"ops": along, "sec": across})
        if along < 2
        else partner(along_ops[along], {"sec": across})
        for along, across in spots
    }
    ahead = [pieces[along, across] for along, across in spots if along < 2]
    sigma_own = call(
        lambda *refs: place_kernel([(along, 0) for along in send_order], *refs[len(ahead) :]),
        "place_own_sector",
        shape(1, rows, columns),
        [],
        *ahead,
        *along_ops.values(),
    )
    sigma_other = partner(sigma_own, {"rep": 1})
    across_own = call(
        lambda *refs: place_kernel([(along, across - 1) for along, across in spots], *refs),
        "place_other_sectors",
        shape(sectors - 1, rows, columns),
        [],
        *pieces.values(),
    )
    across_other = partner(across_own, {"rep": 1})

    products, across_products = call(
        left_kernel,
        "left_products",
        [
            shape(terms, rows, columns, dtype=f32),
            shape(sectors - 1, terms, rows, columns, dtype=f32),
        ],
        [],
        left_own,
        left_other,
        sigma_own,
        sigma_other,
        across_own,
    )
    shares = call(
        second_kernel,
        "second_sigma_terms",
        [shape(1, share, columns, dtype=f32)] + [shape(1, share, columns)] * (ops_count - 1),
        [],
        mixing,
        left_other,
        right,
        products,
        across_products,
        across_other,
        scratch=[pltpu.VMEM((rows, columns), f32)],
    )
    received = [partner(shares[step], {"ops": step}) for step in farthest_first[:-1]]
    sums = call(
        sums_kernel,
        "sums_for_rayleigh",
        shape(3, 8, 128, dtype=f32),
        [],
        wave_own,
        wave_other,
        sigma_own,
        sigma_other,
    )
    sums = [partner(sums, {"sec": step}) for step in range(sectors)]
    second_share = summed("sum_second_sigma", shares[0], *received, live=live, after=sums)
    second_wave, factors = call(
        wave_kernel,
        "second_wave",
        [shape(1, rows, columns), shape(2, 8, 128, dtype=f32)],
        [smem],
        sector_sizes,
        wave_own,
        sigma_own,
        *sums,
    )
    arrived = {along: partner(second_share, {"ops": along}) for along in farthest_first}
    early = [farthest_first[0], 0]
    late = farthest_first[1:-1]
    second_sigma = None
    for steps, name in ((early, "join_early_shares"), (late, "join_late_shares")):
        operands = [factors, sigma_own, *[arrived[along] for along in steps]]
        specs = [inside] * len(operands)
        aliases = {}
        if second_sigma is not None:
            aliases = {len(operands): 0}
            operands.append(second_sigma)
            specs.append(outside)
        second_sigma = pl.pallas_call(
            lambda *refs, steps=steps: join_kernel(steps, *refs),
            out_shape=shape(1, rows, columns, dtype=f32),
            in_specs=specs,
            out_specs=outside,
            input_output_aliases=aliases,
            scratch_shapes=[
                pltpu.VMEM((len(steps), share, columns), f32),
                pltpu.SemaphoreType.DMA((len(steps),)),
            ],
            compiler_params=pltpu.CompilerParams(vmem_limit_bytes=16 * mebibyte),
            name=name,
        )(*operands)
    return (second_wave, second_sigma)


def solution(mesh):
    return jax.shard_map(
        local,
        mesh=mesh,
        in_specs=(
            P(("grp", "sec"), "rep", None),
            P("grp", None),
            P(("grp", "ops"), None, None),
            P(("grp", "ops"), None, None),
            P(("grp", "ops"), None, None),
            P(("grp", "ops"), None),
        ),
        out_specs=(P(("grp", "sec"), "rep", None), P(("grp", "sec"), "rep", None)),
        check_vma=False,
    )
```

```python
import jax
import jax.numpy as jnp
from jax import lax
from jax.experimental import pallas as pl
from jax.experimental.pallas import tpu as pltpu
from jax.sharding import PartitionSpec as P

epsilon = 1e-06
mebibyte = 1024 * 1024


def mixing_scalar(pairs_ref, weights_ref, term, target, source):
    value = jnp.float32(0.0)
    for pair in range(weights_ref.shape[1]):
        hit = (pairs_ref[term, 1, pair] == target) & (pairs_ref[term, 0, pair] == source)
        value = value + jnp.where(hit, weights_ref[term, pair], jnp.float32(0.0))
    return value


def live_cells(sizes_ref, sector, row_start, rows, columns):
    row = row_start + lax.broadcasted_iota(jnp.int32, (rows, columns), 0)
    column = lax.broadcasted_iota(jnp.int32, (rows, columns), 1)
    return (row < sizes_ref[sector, 0]) & (column < sizes_ref[sector, 1])


def left_times(lefts, blocks):
    total = None
    for left, block in zip(lefts, blocks):
        terms, rows, depth = left.shape
        stacked = left[...].reshape(terms * rows, depth)
        part = jnp.dot(stacked, block, preferred_element_type=jnp.float32)
        total = part if total is None else total + part
    return total.reshape(terms, rows, -1)


def times_right(values, right, term):
    return lax.dot_general(
        values.astype(jnp.bfloat16),
        right[term],
        (((1,), (1,)), ((), ())),
        preferred_element_type=jnp.float32,
    )


def load_kernel(left_ref, left_own, left_other, sems):
    rows = left_own.shape[1]
    core = lax.axis_index("rep")
    copies = []
    for index, (half, place) in enumerate(((left_own, core), (left_other, core ^ 1))):
        mine = pl.ds(pl.multiple_of(core * rows, rows), rows)
        columns = pl.ds(pl.multiple_of(place * rows, rows), rows)
        copies.append(pltpu.make_async_copy(left_ref.at[:, mine, columns], half, sems.at[index]))
    for copy in copies:
        copy.start()
    for copy in copies:
        copy.wait()


def live_rows(sizes, sector, row_start, rows, columns):
    bounds = sizes[pl.ds(sector, 1), :]
    row = row_start + lax.broadcasted_iota(jnp.int32, (rows, columns), 0)
    column = lax.broadcasted_iota(jnp.int32, (rows, columns), 1)
    inside = (row < bounds[:, 0:1]) & (column < bounds[:, 1:2])
    return jnp.where(inside, 1.0, 0.0)


def first_tables_kernel(sizes, pairs, weights, wave, _, own, mixing):
    rows, columns = own.shape
    sector = lax.axis_index("sec")
    live = live_rows(sizes, sector, lax.axis_index("rep") * rows, rows, columns)
    own[...] = (wave[0].astype(jnp.float32) * live).astype(own.dtype)
    source, target = pairs[:, 0, :], pairs[:, 1, :]
    for step in range(mixing.shape[0]):
        hits = (source == sector) & (target == (sector ^ step))
        total = jnp.sum(jnp.where(hits, weights[...], 0.0), axis=1, keepdims=True)
        mixing[step] = jnp.broadcast_to(total, mixing.shape[1:])


def first_kernel(shares, *refs):
    sizes, mixing, left_own, left_other, right, own, arrived = refs[:7]
    other, *parts = refs[7:-1]
    held = refs[-1]
    rows, columns = own.shape
    share = parts[0].shape[-2]
    sectors = held.shape[0]
    sector = lax.axis_index("sec")
    core = lax.axis_index("rep")
    place = lax.axis_index("ops")
    live = live_rows(sizes, sector, (core ^ 1) * rows, rows, columns)
    other[...] = (arrived[0].astype(jnp.float32) * live).astype(other.dtype)
    products = left_times((left_own, left_other), (own[...], other[...]))
    totals = [None] * sectors
    for term in range(right.shape[0]):
        product = times_right(products[term], right, term)
        for step in range(sectors):
            weight = jnp.broadcast_to(mixing[step][term : term + 1, :1], (rows, columns))
            part = weight * product
            totals[step] = part if totals[step] is None else totals[step] + part
    for step in range(sectors):
        held[step] = totals[step]
    for (steps, across), out in zip(shares, parts):
        for index, along in enumerate(steps):
            start = pl.multiple_of((place ^ along) * share, share)
            out[index] = held[across, pl.ds(start, share), :].astype(out.dtype)


def sum_kernel(indices, masked, *refs):
    total = refs[0][indices[0]].astype(jnp.float32)
    for index, piece in zip(indices[1:], refs[1:]):
        total = total + piece[index].astype(jnp.float32)
    if masked:
        share = total.shape[0]
        start = pl.multiple_of(lax.axis_index("ops") * share, share)
        total = total * refs[len(indices)][pl.ds(start, share), :]
    refs[-1][0] = total.astype(refs[-1].dtype)


def place_kernel(spots, *refs):
    pieces, half = refs[:-1], refs[-1]
    share = pieces[0].shape[1]
    place = lax.axis_index("ops")
    for (along, index), piece in zip(spots, pieces):
        start = pl.multiple_of((place ^ along) * share, share)
        half[index, pl.ds(start, share), :] = piece[0]


def left_kernel(left_own, left_other, own, other, across_own, out, across_out):
    out[...] = left_times((left_own, left_other), (own[0], other[0]))
    for step in range(across_own.shape[0]):
        across_out[step] = left_times((left_own,), (across_own[step],))


def tables_kernel(sizes_ref, pairs_ref, weights_ref, _, mixing, live):
    target = lax.axis_index("sec")
    for term in range(mixing.shape[0]):
        for step in range(mixing.shape[1]):
            weight = mixing_scalar(pairs_ref, weights_ref, term, target, target ^ step)
            mixing[term, step] = jnp.full(mixing.shape[2:], weight, jnp.float32)
    rows, columns = live.shape
    cells = live_cells(sizes_ref, target, lax.axis_index("rep") * rows, rows, columns)
    live[...] = jnp.where(cells, 1.0, 0.0)


def second_kernel(mixing, left_other, right, products, across_products, other, *refs):
    shares, held = refs[:-1], refs[-1]
    rows, columns = products.shape[1:]
    share = shares[0].shape[1]
    place = lax.axis_index("ops")
    total = None
    across = [left_times((left_other,), (other[step],)) for step in range(other.shape[0])]
    for term in range(right.shape[0]):
        weights = [
            jnp.broadcast_to(mixing[term, step][:1, :1], (rows, columns))
            for step in range(len(across) + 1)
        ]
        combined = weights[0] * products[term]
        for step, part in enumerate(across):
            combined = combined + weights[step + 1] * (across_products[step, term] + part[term])
        part = times_right(combined, right, term)
        total = part if total is None else total + part
    held[...] = total
    for step, out in enumerate(shares):
        start = pl.multiple_of((place ^ step) * share, share)
        out[0] = held[pl.ds(start, share), :].astype(out.dtype)


def sums_kernel(wave_own, wave_other, sigma_own, sigma_other, out):
    step, columns = 16, wave_own.shape[1]
    sums = (jnp.zeros((step, columns), jnp.float32),) * 3
    for wave, sigma in ((wave_own, sigma_own), (wave_other, sigma_other)):

        def add_rows(block, carry):
            start = pl.multiple_of(block * step, step)
            w = wave[pl.ds(start, step), :].astype(jnp.float32)
            s = sigma[0, pl.ds(start, step), :].astype(jnp.float32)
            return (carry[0] + w * s, carry[1] + w * w, carry[2] + s * s)

        sums = lax.fori_loop(0, wave.shape[0] // step, add_rows, sums, unroll=2)
    for index, value in enumerate(sums):
        out[index] = jnp.broadcast_to(jnp.sum(value, keepdims=True), out.shape[1:])


def wave_kernel(sizes_ref, wave_own, sigma_own, *refs):
    sums, (second, factors) = refs[:-2], refs[-2:]
    rows, columns = wave_own.shape
    live_count = jnp.float32(0.0)
    for sector in range(sizes_ref.shape[0]):
        live_count = live_count + sizes_ref[sector, 0].astype(jnp.float32) * sizes_ref[
            sector, 1
        ].astype(jnp.float32)
    total = sums[0][...]
    for other in sums[1:]:
        total = total + other[...]
    correlation, norm_square, sigma_square = total[0], total[1], total[2]
    rayleigh = correlation / norm_square
    residual_square = (
        sigma_square - 2.0 * rayleigh * correlation + rayleigh * rayleigh * norm_square
    )
    residual_square = jnp.maximum(residual_square, 0.0)
    scale = 1.0 / jnp.sqrt(residual_square / live_count + epsilon)
    factors[0] = scale
    factors[1] = rayleigh * scale
    sigma_factor = jnp.broadcast_to(scale[:1, :1], (rows, columns))
    wave_factor = jnp.broadcast_to((rayleigh * scale)[:1, :1], (rows, columns))
    sigma = sigma_own[0].astype(jnp.float32)
    wave = wave_own[...].astype(jnp.float32)
    second[0] = (sigma_factor * sigma - wave_factor * wave).astype(second.dtype)


def join_kernel(steps, factors, sigma_own, *refs):
    pieces, (out, held, sems) = refs[: len(steps)], refs[-3:]
    _, share, columns = pieces[0].shape
    place = lax.axis_index("ops")
    scale = jnp.broadcast_to(factors[0][:1, :1], (share, columns))
    shift = jnp.broadcast_to(factors[1][:1, :1], (share, columns))
    copies = []
    for index, (step, piece) in enumerate(zip(steps, pieces)):
        rows = pl.ds(pl.multiple_of((place ^ step) * share, share), share)
        moved = shift * sigma_own[0, rows, :].astype(jnp.float32)
        held[index] = scale * piece[0].astype(jnp.float32) - moved
        copies.append(pltpu.make_async_copy(held.at[index], out.at[0, rows], sems.at[index]))
        copies[-1].start()
    for copy in copies:
        copy.wait()


def partner(value, steps):
    steps = {axis: step for axis, step in steps.items() if step}
    if not steps:
        return value
    axes = tuple(steps)
    places = [()]
    for axis in axes:
        places = [place + (i,) for place in places for i in range(lax.axis_size(axis))]
    index = {place: i for i, place in enumerate(places)}
    pairs = [
        (index[tuple(i ^ steps[axis] for i, axis in zip(place, axes))], index[place])
        for place in places
    ]
    return lax.ppermute(value, axes, pairs)


def local(wavefunction, sector_sizes, left_blocks, right_blocks, sector_pairs, pair_weights):
    sectors = sector_sizes.shape[0]
    ops_count = lax.axis_size("ops")
    _, rows, columns = wavefunction.shape
    terms, side = left_blocks.shape[0], left_blocks.shape[1]
    share = rows // ops_count
    bf16, f32 = jnp.bfloat16, jnp.float32
    smem = pl.BlockSpec(memory_space=pltpu.SMEM)
    outside = pl.BlockSpec(memory_space=pltpu.HBM)
    inside = pl.BlockSpec(memory_space=pltpu.VMEM)

    def shape(*dims, dtype=bf16):
        return jax.ShapeDtypeStruct(dims, dtype)

    def call(kernel, name, out_shape, in_specs, *operands, scratch=(), vmem=16, out=inside):
        return pl.pallas_call(
            kernel,
            out_shape=out_shape,
            in_specs=list(in_specs) + [inside] * (len(operands) - len(in_specs)),
            out_specs=jax.tree.map(lambda _: out, out_shape),
            scratch_shapes=list(scratch),
            compiler_params=pltpu.CompilerParams(vmem_limit_bytes=vmem * mebibyte),
            name=name,
        )(*operands)

    def summed(name, *pieces, live=None, after=()):
        pieces = [piece if isinstance(piece, tuple) else (piece, 0) for piece in pieces]
        arrays, indices = zip(*pieces)
        return call(
            lambda *refs: sum_kernel(indices, live is not None, *refs),
            name,
            shape(1, share, columns),
            [],
            *arrays,
            *([] if live is None else [live]),
            *after,
        )

    farthest_first = list(reversed(range(ops_count)))
    send_order = farthest_first[1:2] + farthest_first[:1] + farthest_first[2:]
    arrived = partner(wavefunction, {"rep": 1})
    left_own, left_other = call(
        load_kernel,
        "load_operators",
        [shape(terms, rows, rows), shape(terms, rows, side - rows)],
        [outside],
        left_blocks,
        scratch=[pltpu.SemaphoreType.DMA((2,))],
        vmem=51,
    )
    right = right_blocks
    pairs = jnp.swapaxes(sector_pairs, 1, 2)
    scalars = (sector_sizes, pairs, pair_weights)

    far = ops_count - 1
    direct = [(along,) for along in farthest_first[1:-1]]
    spots = [((far, 0), across) for across in range(sectors)]
    spots += [(along, across) for along in direct for across in range(sectors)]
    wave_own, mixing = call(
        first_tables_kernel,
        "tables_for_first_sigma",
        [shape(rows, columns), shape(sectors, terms, 128, dtype=f32)],
        [],
        *scalars,
        wavefunction,
        left_own,
    )
    wave_other, *rest = call(
        lambda *refs: first_kernel(spots, *refs),
        "first_sigma_terms",
        [shape(rows, columns)]
        + [
            shape(len(along), share, columns, dtype=f32 if along == (far, 0) and across == 0 else bf16)
            for along, across in spots
        ],
        [],
        sector_sizes,
        mixing,
        left_own,
        left_other,
        right,
        wave_own,
        arrived,
        scratch=[pltpu.VMEM((sectors, rows, columns), f32)],
    )
    rest = dict(zip(spots, rest))
    mixing, live = call(
        tables_kernel,
        "tables_for_second_sigma",
        [shape(terms, sectors, 8, 128, dtype=f32), shape(rows, columns, dtype=f32)],
        [smem] * 3,
        *scalars,
        wave_other,
    )
    met = [partner(rest[(far, 0), across], {"sec": across}) for across in range(sectors)]
    received = [partner(summed("sum_far_share", *met), {"ops": far})]
    first_two = [(direct[-1], 0), (direct[0], 0)]
    order = first_two + [spot for spot in rest if spot[0] in direct and spot not in first_two]
    received += [partner(rest[spot], {"ops": spot[0][0], "sec": spot[1]}) for spot in order]
    first_share = summed("sum_first_sigma", *[(piece, 1) for piece in met], *received, live=live)
    along_ops = {along: partner(first_share, {"ops": along}) for along in send_order}
    spots = [(along, across) for along in send_order for across in range(1, sectors)]
    pieces = {
        (along, across): partner(first_share, {"ops": along, "sec": across})
        if along < 2
        else partner(along_ops[along], {"sec": across})
        for along, across in spots
    }
    ahead = [pieces[along, across] for along, across in spots if along < 2]
    sigma_own = call(
        lambda *refs: place_kernel([(along, 0) for along in send_order], *refs[len(ahead) :]),
        "place_own_sector",
        shape(1, rows, columns),
        [],
        *ahead,
        *along_ops.values(),
    )
    sigma_other = partner(sigma_own, {"rep": 1})
    across_own = call(
        lambda *refs: place_kernel([(along, across - 1) for along, across in spots], *refs),
        "place_other_sectors",
        shape(sectors - 1, rows, columns),
        [],
        *pieces.values(),
    )
    across_other = partner(across_own, {"rep": 1})

    products, across_products = call(
        left_kernel,
        "left_products",
        [
            shape(terms, rows, columns, dtype=f32),
            shape(sectors - 1, terms, rows, columns, dtype=f32),
        ],
        [],
        left_own,
        left_other,
        sigma_own,
        sigma_other,
        across_own,
    )
    shares = call(
        second_kernel,
        "second_sigma_terms",
        [shape(1, share, columns, dtype=f32)] + [shape(1, share, columns)] * (ops_count - 1),
        [],
        mixing,
        left_other,
        right,
        products,
        across_products,
        across_other,
        scratch=[pltpu.VMEM((rows, columns), f32)],
    )
    received = [partner(shares[step], {"ops": step}) for step in farthest_first[:-1]]
    sums = call(
        sums_kernel,
        "sums_for_rayleigh",
        shape(3, 8, 128, dtype=f32),
        [],
        wave_own,
        wave_other,
        sigma_own,
        sigma_other,
    )
    sums = [partner(sums, {"sec": step}) for step in range(sectors)]
    second_share = summed("sum_second_sigma", shares[0], *received, live=live, after=sums)
    second_wave, factors = call(
        wave_kernel,
        "second_wave",
        [shape(1, rows, columns), shape(2, 8, 128, dtype=f32)],
        [smem],
        sector_sizes,
        wave_own,
        sigma_own,
        *sums,
    )
    arrived = {along: partner(second_share, {"ops": along}) for along in farthest_first}
    early = [farthest_first[0], 0]
    late = farthest_first[1:-1]
    second_sigma = None
    for steps, name in ((early, "join_early_shares"), (late, "join_late_shares")):
        operands = [factors, sigma_own, *[arrived[along] for along in steps]]
        specs = [inside] * len(operands)
        aliases = {}
        if second_sigma is not None:
            aliases = {len(operands): 0}
            operands.append(second_sigma)
            specs.append(outside)
        second_sigma = pl.pallas_call(
            lambda *refs, steps=steps: join_kernel(steps, *refs),
            out_shape=shape(1, rows, columns, dtype=f32),
            in_specs=specs,
            out_specs=outside,
            input_output_aliases=aliases,
            scratch_shapes=[
                pltpu.VMEM((len(steps), share, columns), f32),
                pltpu.SemaphoreType.DMA((len(steps),)),
            ],
            compiler_params=pltpu.CompilerParams(vmem_limit_bytes=16 * mebibyte),
            name=name,
        )(*operands)
    return (second_wave, second_sigma)


def solution(mesh):
    return jax.shard_map(
        local,
        mesh=mesh,
        in_specs=(
            P(("grp", "sec"), "rep", None),
            P("grp", None),
            P(("grp", "ops"), None, None),
            P(("grp", "ops"), None, None),
            P(("grp", "ops"), None, None),
            P(("grp", "ops"), None),
        ),
        out_specs=(P(("grp", "sec"), "rep", None), P(("grp", "sec"), "rep", None)),
        check_vma=False,
    )
```
